32 devices in a mesh: ctx: 8 (over z, x), tp: 4 (over y, core).
Axes of the slice: x: 2, y: 2, z: 4, core: 2. Of those that a mesh axis runs over, the one named last changes fastest.
Arguments:
- q_pre: bfloat16 [2, 512, 4096], P(None, 'ctx', 'tp'), may hold values from -8 to 8
- k_pre: bfloat16 [2, 512, 512], P(None, 'ctx', 'tp'), may hold values from -8 to 8
- value_before_filter: bfloat16 [2, 512, 512], P(None, 'ctx', 'tp'), may hold values from -8 to 8
- d_out: bfloat16 [2, 512, 4096], P(None, 'ctx', 'tp'), may hold values from -8 to 8
- filters: float32 [3, 3, 128], replicated, may hold values from 0.5 to 1.5
- doc_lengths: int32 [8], replicated, may hold values from 1 to 512, 1024 in all
Outputs:
- d_q_pre: float32 [2, 512, 4096], P(None, 'ctx', 'tp')
- d_k_pre: float32 [2, 512, 512], P(None, 'ctx', 'tp')
- d_v_pre: float32 [2, 512, 512], P(None, 'ctx', 'tp')
- d_filters: float32 [3, 3, 128], replicated
The draws below stay inside these ranges and needn't reach their ends.
Inputs may be any that keep to these rules, and one draw needn't show every extreme that they name: `doc_lengths`: the lengths sum to 1024, and the longest document has exactly 512 positions.
All inputs are finite; a program needn't handle non-finite values.
Results may differ from the reference program's by a relative error of at most 0.009.
The reference program's roundings to bfloat16 on the way count: a program that leaves them out, or rounds other values in their place, can miss the bound.
Values may be sent and summed in bfloat16 or wider, within the bound.
No kernel may reach another device: no remote copies, remote signals or barrier semaphores. Data moves between devices by JAX's collectives and lax.ppermute only.
A program may use at most 128 MiB of HBM per device.

```python
import math
import jax
import jax.numpy as jnp
import numpy as np
from jax import lax

HEAD_WIDTH = 128
HQ = 32
KEY_VALUE_HEADS = 4
QUERY_GROUP = 8
SPAN = 64
HALF_LENGTH = 512
PACKED_LENGTH = 1024
DOCS = 8
TAPS = 3
N_CTX = 8


def draw_q_pre(key, part):
    key = jax.random.fold_in(key, 3)
    sampled_values = jnp.clip(jax.random.normal(key, (2, HALF_LENGTH, HQ * HEAD_WIDTH)), -8.0, 8.0)
    return sampled_values.astype(jnp.bfloat16)


def draw_k_pre(key, part):
    key = jax.random.fold_in(key, 5)
    sampled_values = jnp.clip(jax.random.normal(key, (2, HALF_LENGTH, KEY_VALUE_HEADS * HEAD_WIDTH)), -8.0, 8.0)
    return sampled_values.astype(jnp.bfloat16)


def levels(rng, extent, cuts, smallest, largest):
    gain, own = 1.0, jax.random.fold_in(rng, 6)
    for axis_at, parts in cuts:
        steps = jnp.exp(jax.random.uniform(jax.random.fold_in(own, axis_at), (parts,), jnp.float32, smallest / len(cuts), largest / len(cuts)))
        gain = gain * jnp.repeat(steps, extent[axis_at] // parts).reshape([-1 if axis == axis_at else 1 for axis in range(len(extent))])
    return gain


def split_up(number_of, total, bound, lean):
    loads = [(1 << 20) // math.isqrt(rank ** lean) + 1 for rank in range(2, number_of + 1)]
    spare, given = total - bound - (number_of - 1), [1] * (number_of - 1)
    while spare > 0:
        candidates = [i for i in range(number_of - 1) if given[i] < bound]
        pool, remaining = sum([loads[i] for i in candidates]), spare
        for i in candidates:
            more = min(bound - given[i], max(1, remaining * loads[i] // pool), spare)
            given[i] = given[i] + more
            spare = spare - more
    return np.array([bound] + given)


def uneven_parts(stream_key, amount, total, limit, skew):
    if amount == 2:
        one = jax.random.randint(stream_key, (), max(1, total - limit), min(limit, total - 1) + 1)
        return jnp.stack([one, total - one])
    tallies = jnp.asarray(split_up(amount, total, limit, skew), jnp.int32)
    twos = (amount - 1) // 2
    giver, taker = tallies[1:1 + 2 * twos:2], tallies[2:2 + 2 * twos:2]
    room = jnp.minimum(giver - 1, limit - taker)
    passed = jax.random.randint(jax.random.fold_in(stream_key, 1), (twos,), 0, 1 << 20) % (room + 1)
    tallies = tallies.at[1:1 + 2 * twos:2].set(giver - passed).at[2:2 + 2 * twos:2].set(taker + passed)
    return tallies[jax.random.permutation(jax.random.fold_in(stream_key, 2), amount)]


def noise(key, extent, width, most, cuts=(), kind=jnp.bfloat16):
    factor_of = levels(key, extent, cuts, -0.22, 0.18) if cuts else 1.0
    array = jax.random.normal(key, extent, jnp.float32) * width * factor_of
    return jnp.minimum(jnp.maximum(array, -most), most).astype(kind)


def setup_inputs(seed: int = 0) -> dict:
    arg_keys = jax.random.split(jax.random.key(seed), 7)
    return {
        "q_pre": draw_q_pre(jax.random.fold_in(arg_keys[6], 71), 0),
        "k_pre": draw_k_pre(jax.random.fold_in(arg_keys[6], 71), 0),
        "value_before_filter": noise(arg_keys[2], (2, HALF_LENGTH, KEY_VALUE_HEADS * HEAD_WIDTH), 1.0, 8.0, ((1, 8), (2, 4))),
        "d_out": noise(arg_keys[3], (2, HALF_LENGTH, HQ * HEAD_WIDTH), 1.0, 8.0, ((1, 8), (2, 4))),
        "filters": jnp.clip(jax.random.uniform(arg_keys[4], (3, TAPS, HEAD_WIDTH), jnp.float32, 0.5, 1.5), 0.5, 1.5),
        "doc_lengths": uneven_parts(arg_keys[5], DOCS, PACKED_LENGTH, PACKED_LENGTH // 2, 2).astype(jnp.int32),
    }


def to_sequence(layout):
    late_rows = layout[1].reshape(N_CTX, SPAN, -1)[::-1].reshape(HALF_LENGTH, -1)
    return jnp.concatenate([layout[0], late_rows], axis=0)

def to_layout(sequence):
    late_rows = sequence[HALF_LENGTH:].reshape(N_CTX, SPAN, -1)[::-1].reshape(HALF_LENGTH, -1)
    return jnp.stack([sequence[:HALF_LENGTH], late_rows])

def doc_index(places, starts):
    return lax.optimization_barrier(jnp.sum((places[..., None] >= starts).astype(jnp.int32), axis=-1)) - 1

def convolve(source, weights, doc_ids):
    head_count = source.shape[1] // HEAD_WIDTH
    grid_rows = source.reshape(PACKED_LENGTH, head_count, HEAD_WIDTH)
    summed = jnp.zeros((PACKED_LENGTH, head_count, HEAD_WIDTH), jnp.float32)
    for tap_index in range(TAPS):
        earlier = jnp.concatenate([jnp.zeros((tap_index, head_count, HEAD_WIDTH), source.dtype), grid_rows[:PACKED_LENGTH - tap_index]], axis=0)
        earlier_docs = jnp.concatenate([jnp.full((tap_index,), -1, jnp.int32), doc_ids[:PACKED_LENGTH - tap_index]])
        same_doc = earlier_docs == doc_ids
        summed = summed + jnp.where(same_doc[:, None, None], weights[tap_index] * earlier, 0.0)
    return summed.reshape(PACKED_LENGTH, head_count * HEAD_WIDTH)

def attention_grads(query_full, key_full, value_full, output_gradient, doc_ids):
    query_head_rows = jnp.transpose(query_full.reshape(PACKED_LENGTH, KEY_VALUE_HEADS, QUERY_GROUP, HEAD_WIDTH), (1, 0, 2, 3))
    gradient_per_head = jnp.transpose(output_gradient.reshape(PACKED_LENGTH, KEY_VALUE_HEADS, QUERY_GROUP, HEAD_WIDTH), (1, 0, 2, 3))
    key_head_rows = jnp.transpose(key_full.reshape(PACKED_LENGTH, KEY_VALUE_HEADS, HEAD_WIDTH), (1, 0, 2))
    value_head_rows = jnp.transpose(value_full.reshape(PACKED_LENGTH, KEY_VALUE_HEADS, HEAD_WIDTH), (1, 0, 2))
    places = jnp.arange(PACKED_LENGTH, dtype=jnp.int32)
    block_size = math.gcd(PACKED_LENGTH, 512)
    score_scale = HEAD_WIDTH ** (-0.5)

    def per_head(operands):
        q_head, k_head, v_head, grad_head = operands
        dq_blocks = []
        dk_total = jnp.zeros((PACKED_LENGTH, HEAD_WIDTH), jnp.float32)
        dv_total = jnp.zeros((PACKED_LENGTH, HEAD_WIDTH), jnp.float32)
        for block_index in range(PACKED_LENGTH // block_size):
            row_lower = block_index * block_size
            row_upper = row_lower + block_size
            queries = q_head[row_lower:row_upper].astype(jnp.float32)
            grads_out = grad_head[row_lower:row_upper].astype(jnp.float32)
            key_rows = k_head[:row_upper].astype(jnp.float32)
            value_rows = v_head[:row_upper].astype(jnp.float32)
            allowed = (doc_ids[row_lower:row_upper, None] == doc_ids[None, :row_upper]) & (places[None, :row_upper] <= places[row_lower:row_upper, None])
            scores = jnp.einsum('cgd,nd->gcn', queries, key_rows) * score_scale
            row_max = lax.optimization_barrier(jnp.max(jnp.where(allowed, scores, -jnp.inf), axis=-1, keepdims=True))
            exp_total = lax.optimization_barrier(jnp.sum(jnp.where(allowed, jnp.exp(scores - row_max), 0.0), axis=-1, keepdims=True))
            log_total = row_max + jnp.log(exp_total)
            probabilities = jnp.where(allowed, jnp.exp(scores - log_total), 0.0)
            prob_grads = jnp.einsum('cgd,nd->gcn', grads_out, value_rows)
            row_sums = lax.optimization_barrier(jnp.sum(probabilities * prob_grads, axis=-1, keepdims=True))
            probs_low = lax.optimization_barrier(probabilities.astype(jnp.bfloat16)).astype(jnp.float32)
            score_grads = probabilities * (prob_grads - row_sums) * score_scale
            grads_low = lax.optimization_barrier(score_grads.astype(jnp.bfloat16)).astype(jnp.float32)
            dv_total = dv_total.at[:row_upper].add(jnp.einsum('gcn,cgd->nd', probs_low, grads_out))
            dk_total = dk_total.at[:row_upper].add(jnp.einsum('gcn,cgd->nd', grads_low, queries))
            dq_blocks.append(jnp.einsum('gcn,nd->cgd', grads_low, key_rows))
        return (jnp.concatenate(dq_blocks, axis=0), dk_total, dv_total)
    dq_heads, key_gradient_heads, value_gradient_heads = lax.map(per_head, (query_head_rows, key_head_rows, value_head_rows, gradient_per_head))
    dq_all = jnp.transpose(dq_heads, (1, 0, 2, 3)).reshape(PACKED_LENGTH, HQ * HEAD_WIDTH)
    key_gradient_full = jnp.transpose(key_gradient_heads, (1, 0, 2)).reshape(PACKED_LENGTH, KEY_VALUE_HEADS * HEAD_WIDTH)
    value_gradient_full = jnp.transpose(value_gradient_heads, (1, 0, 2)).reshape(PACKED_LENGTH, KEY_VALUE_HEADS * HEAD_WIDTH)
    return (dq_all, key_gradient_full, value_gradient_full)

def reference(q_pre, k_pre, value_before_filter, d_out, filters, doc_lengths):
    starts = jnp.cumsum(doc_lengths) - doc_lengths
    doc_ids = doc_index(jnp.arange(PACKED_LENGTH, dtype=jnp.int32), starts)
    sources = [to_sequence(array_in).astype(jnp.float32) for array_in in (q_pre, k_pre, value_before_filter)]
    projected = []
    pullbacks = []
    for tensor_index in range(3):
        conv_out, pullback = jax.vjp(lambda data, weights: convolve(data, weights, doc_ids), sources[tensor_index], filters[tensor_index])
        projected.append(conv_out.astype(jnp.bfloat16))
        pullbacks.append(pullback)
    grads_all = attention_grads(projected[0], projected[1], projected[2], to_sequence(d_out), doc_ids)
    results = [pullbacks[tensor_index](grads_all[tensor_index]) for tensor_index in range(3)]
    d_filters = jnp.stack([results[tensor_index][1] for tensor_index in range(3)])
    return (to_layout(results[0][0]), to_layout(results[1][0]), to_layout(results[2][0]), d_filters)
```

```python
import functools

import jax
import jax.numpy as jnp
import numpy as np
from jax import lax
from jax.experimental import pallas as pl
from jax.experimental.pallas import tpu as pltpu
from jax.sharding import PartitionSpec as P

LANES = 128
NT = (((1,), (1,)), ((), ()))
NN = (((1,), (0,)), ((), ()))
TN = (((0,), (0,)), ((), ()))
TAIL = 16
MAX_CHUNK = 640
MIB = 1 << 20


def loop(count, body, init, unrolled=16):
    if count <= unrolled:
        for step in range(count):
            init = body(step, init)
        return init
    return lax.fori_loop(0, count, body, init)


def aligned(start, multiple):
    return start if isinstance(start, int) else pl.multiple_of(start, multiple)


def doc_starts(lengths_ref):
    starts = [jnp.int32(0)]
    for index in range(lengths_ref.shape[0] - 1):
        starts.append(starts[-1] + lengths_ref[index])
    return starts


def fold_rows(terms):
    rows, lanes = terms.shape
    return jnp.sum(terms.reshape(rows // 8, 8, lanes), axis=0)


def pack_kernel(ctx_count, k_ref, v_ref, q_ref, out_ref):
    span = k_ref.shape[1]
    kv = jnp.concatenate([k_ref[...], v_ref[...]], axis=2).reshape(2 * span, 2 * LANES)
    tails = []
    for half in range(2):
        last = q_ref[half].astype(jnp.float32)[TAIL - 2 :]
        tails += [last[:, at : at + 2 * LANES] for at in range(0, last.shape[1], 2 * LANES)]
    tail = jnp.concatenate(tails, axis=0).astype(jnp.bfloat16)

    def store(index, carry):
        out_ref[index, : 2 * span] = kv
        out_ref[index, 2 * span :] = tail
        return carry

    loop(ctx_count, store, 0)


def grads_kernel(
    ctx_count,
    lengths_ref,
    filters_ref,
    q_ref,
    d_out_ref,
    msg_ref,
    dq_ref,
    out_ref,
    same_scr,
    kv_scr,
    conv_scr,
    dkv_scr,
    q_scr,
    qc_scr,
    do_scr,
    dq_scr,
    s_scr,
    dp_scr,
):
    f32, bf16 = jnp.float32, jnp.bfloat16
    span = q_ref.shape[1]
    heads = q_ref.shape[2] // LANES
    half_rows = span * ctx_count
    length = 2 * half_rows
    blocks = 2 * ctx_count
    me = lax.axis_index("ctx")
    scale = LANES**-0.5
    log2_scale = scale * 1.4426950408889634
    starts = doc_starts(lengths_ref)

    def fill_same(index, carry):
        place = index * span + lax.broadcasted_iota(jnp.int32, (span, LANES), 0)
        cut = place == starts[0]
        for start in starts[1:]:
            cut = cut | (place == start)
        same_scr[pl.ds(aligned(8 + index * span, 8), span)] = jnp.where(cut, 0.0, 1.0)
        return carry

    same_scr[:8] = jnp.zeros((8, LANES), f32)
    same_scr[8 + length :] = jnp.zeros((8, LANES), f32)
    loop(blocks, fill_same, 0)

    kv_scr[:8] = jnp.zeros((8, 2 * LANES), f32)
    kv_scr[8 + length :] = jnp.zeros((8, 2 * LANES), f32)

    def place_blocks(index, carry):
        early = aligned(8 + index * span, 8)
        late = aligned(8 + (blocks - 1 - index) * span, 8)
        kv_scr[pl.ds(early, span)] = msg_ref[index, :span].astype(f32)
        kv_scr[pl.ds(late, span)] = msg_ref[index, span : 2 * span].astype(f32)
        return carry

    loop(ctx_count, place_blocks, 0)

    def kv_taps(tap):
        return jnp.concatenate([filters_ref[1, tap : tap + 1], filters_ref[2, tap : tap + 1]], axis=1)

    def twice(mask):
        return jnp.concatenate([mask, mask], axis=1)

    def back_masks(same, first):
        one = same[first : first + span]
        return one, one * same[first - 1 : first - 1 + span]

    def convolve_kv(index, carry):
        rows = pl.ds(aligned(index * span, 8), span + 8)
        values = kv_scr[rows]
        one, two = back_masks(same_scr[rows], 8)
        total = kv_taps(0) * values[8:]
        total = total + twice(one) * (kv_taps(1) * values[7 : 7 + span])
        total = total + twice(two) * (kv_taps(2) * values[6 : 6 + span])
        conv_scr[pl.ds(aligned(index * span, 16), span)] = total.astype(bf16)
        return carry

    loop(blocks, convolve_kv, 0)

    before = jnp.maximum(me - 1, 0)
    after = jnp.minimum(me + 1, ctx_count - 1)
    middle = me == ctx_count - 1
    rim_before = msg_ref[before, 2 * span :].astype(f32)
    rim_after = msg_ref[after, 2 * span :].astype(f32)
    rim_rows = rim_before.shape[0] // 2
    late_rim = jnp.where(middle, rim_after[:rim_rows], rim_after[rim_rows:])
    rims = [rim_before[:rim_rows], late_rim]
    first_place = [me * span, (blocks - 1 - me) * span]

    for half in range(2):
        rows = [rims[half][2 * at : 2 * at + 2] for at in range(rim_rows // 2)]
        q_scr[half, 6:8] = jnp.concatenate(rows, axis=1)
        q_scr[half, 8:] = q_ref[half].astype(f32)
        same = same_scr[pl.ds(aligned(first_place[half], 8), span + 16)]
        one, two = back_masks(same, 8)
        for head in range(heads):
            lanes = slice(head * LANES, (head + 1) * LANES)
            total = filters_ref[0, 0:1] * q_scr[half, 8:, lanes]
            total = total + one * (filters_ref[0, 1:2] * q_scr[half, 7 : 7 + span, lanes])
            total = total + two * (filters_ref[0, 2:3] * q_scr[half, 6 : 6 + span, lanes])
            qc_scr[half, head * span : (head + 1) * span] = total.astype(bf16)
            do_scr[half, head * span : (head + 1) * span] = d_out_ref[half, :, lanes]

    def attend(half, window, first_key, add):
        chunks = 1
        while window // chunks > MAX_CHUNK or window % (16 * chunks):
            chunks += 1
        size = window // chunks
        query = first_place[half] + lax.rem(
            lax.broadcasted_iota(jnp.int32, (1, LANES), 1), jnp.int32(span)
        )
        lowest = jnp.zeros((1, LANES), jnp.int32)
        for start in starts[1:]:
            lowest = jnp.where(query >= start, start, lowest)
        group = 2 * LANES
        for at in range(heads * span // group):
            cols = slice(at * group, (at + 1) * group)
            queries = qc_scr[half, cols]
            grads = do_scr[half, cols]

            def key_rows(step):
                return pl.ds(aligned(first_key + step * size, 16), size)

            def score(step, top):
                places = first_key + step * size + lax.broadcasted_iota(jnp.int32, (size, LANES), 0)
                allowed = (places >= lowest) & (places <= query)
                bias = jnp.where(allowed, 0.0, -1e30)
                keys = conv_scr[key_rows(step), :LANES]
                scores = lax.dot_general(keys, queries, NT, preferred_element_type=f32)
                scores = scores + twice(bias)
                s_scr[pl.ds(aligned(step * size, 16), size)] = scores
                return jnp.maximum(top, jnp.max(scores, axis=0, keepdims=True))

            top = loop(chunks, score, jnp.full((1, group), -1e30, f32), 1)

            def weigh(step, carry):
                total, weighted = carry
                rows = pl.ds(aligned(step * size, 16), size)
                weights = jnp.exp2((s_scr[rows] - top) * log2_scale)
                values = conv_scr[key_rows(step), LANES:]
                prob_grads = lax.dot_general(values, grads, NT, preferred_element_type=f32)
                s_scr[rows] = weights
                dp_scr[rows] = prob_grads
                total = total + jnp.sum(weights, axis=0, keepdims=True)
                weighted = weighted + jnp.sum(weights * prob_grads, axis=0, keepdims=True)
                return total, weighted

            zeros = jnp.zeros((1, group), f32)
            total, weighted = loop(chunks, weigh, (zeros, zeros), 1)
            inverse = 1.0 / total
            mean = weighted * inverse
            slope = inverse * scale

            def accumulate(step, dq):
                rows = pl.ds(aligned(step * size, 16), size)
                weights = s_scr[rows]
                probs = (weights * inverse).astype(bf16)
                score_grads = (weights * slope * (dp_scr[rows] - mean)).astype(bf16)
                keys = conv_scr[key_rows(step), :LANES]
                dk = lax.dot_general(score_grads, queries, NN, preferred_element_type=f32)
                dv = lax.dot_general(probs, grads, NN, preferred_element_type=f32)
                terms = jnp.concatenate([dk, dv], axis=1)
                target = pl.ds(aligned(first_key + step * size, 16), size)
                if add or at:
                    dkv_scr[target] += terms
                else:
                    dkv_scr[target] = terms
                return dq + lax.dot_general(keys, score_grads, TN, preferred_element_type=f32)

            dq = loop(chunks, accumulate, jnp.zeros((LANES, group), f32), 1)
            dq = dq.T
            for part in range(group // span):
                head = at * (group // span) + part
                dq_scr[half, :span, head * LANES : (head + 1) * LANES] = dq[
                    part * span : (part + 1) * span
                ]

    dkv_scr[half_rows:] = jnp.zeros((half_rows + 8, 2 * LANES), f32)
    attend(0, half_rows, 0, False)
    attend(1, half_rows + span, (ctx_count - 1 - me) * span, True)

    next_rows = jnp.where(middle, dq_scr[1, :8], 0.0)
    dq_scr[0, span:] = next_rows
    dq_scr[1, span:] = jnp.zeros_like(next_rows)
    sums = [jnp.zeros((8, LANES), f32) for _ in range(3)]
    for half in range(2):
        same = same_scr[pl.ds(aligned(first_place[half], 8), span + 16)]
        one, two = back_masks(same, 8)
        ahead_one = same[9 : 9 + span]
        ahead_two = same[10 : 10 + span] * ahead_one
        for head in range(heads):
            lanes = slice(head * LANES, (head + 1) * LANES)
            grads = dq_scr[half, :span, lanes]
            out = filters_ref[0, 0:1] * grads
            out = out + ahead_one * (filters_ref[0, 1:2] * dq_scr[half, 1 : 1 + span, lanes])
            out = out + ahead_two * (filters_ref[0, 2:3] * dq_scr[half, 2 : 2 + span, lanes])
            dq_ref[half, :, lanes] = out
            sums[0] += fold_rows(grads * q_scr[half, 8:, lanes])
            sums[1] += fold_rows(grads * one * q_scr[half, 7 : 7 + span, lanes])
            sums[2] += fold_rows(grads * two * q_scr[half, 6 : 6 + span, lanes])
    q_sums = [jnp.sum(term, axis=0, keepdims=True) for term in sums]

    def finish_block(index, carry):
        base = aligned(index * span, 8)
        grads = dkv_scr[pl.ds(base, span + 8)]
        values = kv_scr[pl.ds(base, span + 8)]
        same = same_scr[pl.ds(base, span + 16)]
        one, two = back_masks(same, 8)
        ahead_one = same[9 : 9 + span]
        ahead_two = same[10 : 10 + span] * ahead_one
        out = kv_taps(0) * grads[:span]
        out = out + twice(ahead_one) * (kv_taps(1) * grads[1 : 1 + span])
        out = out + twice(ahead_two) * (kv_taps(2) * grads[2 : 2 + span])
        own = grads[:span]
        return out, (
            carry[0] + fold_rows(own * values[8:]),
            carry[1] + fold_rows(own * twice(one) * values[7 : 7 + span]),
            carry[2] + fold_rows(own * twice(two) * values[6 : 6 + span]),
        )

    def finish(index, carry):
        out_ref[index, :span], carry = finish_block(index, carry)
        out_ref[index, span : 2 * span], carry = finish_block(blocks - 1 - index, carry)
        return carry

    zeros = jnp.zeros((8, 2 * LANES), f32)
    kv_sums = loop(ctx_count, finish, (zeros, zeros, zeros))
    kv_sums = [jnp.sum(term, axis=0, keepdims=True) for term in kv_sums]

    sums_tile = jnp.concatenate(
        [jnp.concatenate([term, jnp.zeros_like(term)], axis=1) for term in q_sums]
        + kv_sums
        + [jnp.zeros((2, 2 * LANES), f32)],
        axis=0,
    )
    heads_tiles = []
    for half in range(2):
        rows = dq_scr[half, :2]
        heads_tiles.append(
            jnp.concatenate(
                [rows[:, at : at + 2 * LANES] for at in range(0, rows.shape[1], 2 * LANES)], axis=0
            )
        )

    def store_rim(index, carry):
        out_ref[index, 2 * span : 2 * span + 8] = jnp.where(index < me, heads_tiles[0], heads_tiles[1])
        out_ref[index, 2 * span + 8 :] = sums_tile
        return carry

    loop(ctx_count, store_rim, 0)


def finish_kernel(
    ctx_count, lengths_ref, filters_ref, msg_ref, dq_in_ref, dq_ref, dk_ref, dv_ref, sums_ref
):
    f32 = jnp.float32
    span = dk_ref.shape[1]
    me = lax.axis_index("ctx")
    starts = doc_starts(lengths_ref)
    blocks = 2 * ctx_count

    def add(index, carry):
        return carry + msg_ref[index].astype(f32)

    total = loop(ctx_count, add, jnp.zeros(msg_ref.shape[1:], f32))
    for half in range(2):
        dk_ref[half] = total[half * span : (half + 1) * span, :LANES]
        dv_ref[half] = total[half * span : (half + 1) * span, LANES:]
    sums = total[2 * span + 8 :]
    sums_ref[0] = sums[0:3, :LANES]
    sums_ref[1] = sums[3:6, :LANES]
    sums_ref[2] = sums[3:6, LANES:]

    def same(place):
        cut = place >= blocks * span
        for start in starts:
            cut = cut | (place == start)
        return jnp.where(cut, 0.0, 1.0).astype(f32)

    heads = dq_ref.shape[2] // LANES
    taps = [jnp.concatenate([filters_ref[0, tap : tap + 1]] * heads, axis=1) for tap in range(3)]
    row = lax.broadcasted_iota(jnp.int32, dq_ref.shape[1:], 0)
    sources = [jnp.minimum(me + 1, ctx_count - 1), jnp.maximum(me - 1, 0)]
    first_place = [me * span, (blocks - 1 - me) * span]
    present = [me < ctx_count - 1, me > 0]
    for half in range(2):
        rim = msg_ref[sources[half], 2 * span : 2 * span + 8].astype(f32)
        rows = jnp.concatenate([rim[2 * at : 2 * at + 2] for at in range(4)], axis=1)
        end = first_place[half] + span
        zero, one, two = same(end - 1), same(end), same(end + 1)
        one = jnp.where(present[half], one, 0.0)
        last_but_one = (zero * one) * (taps[2] * rows[0:1])
        last = one * (taps[1] * rows[0:1]) + (one * two) * (taps[2] * rows[1:2])
        extra = jnp.where(row == 6, last_but_one, jnp.where(row == 7, last, 0.0))
        dq_ref[half] = dq_in_ref[half] + extra


def shards(q_pre, k_pre, value_before_filter, d_out, filters, doc_lengths):
    f32, bf16 = jnp.float32, jnp.bfloat16
    ctx_count = lax.axis_size("ctx")
    span, width = q_pre.shape[1:]
    length = 2 * span * ctx_count
    rim = 4 * width // (2 * LANES)
    vmem = pl.BlockSpec(memory_space=pltpu.VMEM)
    smem = pl.BlockSpec(memory_space=pltpu.SMEM)

    packed = pl.pallas_call(
        functools.partial(pack_kernel, ctx_count),
        grid=(1,),
        out_shape=jax.ShapeDtypeStruct((ctx_count, 2 * span + rim, 2 * LANES), bf16),
        in_specs=[
            pl.BlockSpec(k_pre.shape, lambda i: (0, 0, 0)),
            pl.BlockSpec(k_pre.shape, lambda i: (0, 0, 0)),
            pl.BlockSpec((2, TAIL, width), lambda i: (0, span // TAIL - 1, 0)),
        ],
        out_specs=pl.BlockSpec((ctx_count, 2 * span + rim, 2 * LANES), lambda i: (0, 0, 0)),
        name="pack",
    )(k_pre, value_before_filter, q_pre)
    received = lax.all_to_all(packed, "ctx", 0, 0, tiled=True)

    window = span * ctx_count + span
    out_rows = 2 * span + 16
    scratch = [
        pltpu.VMEM((length + 16, LANES), f32),
        pltpu.VMEM((length + 16, 2 * LANES), f32),
        pltpu.VMEM((length, 2 * LANES), bf16),
        pltpu.VMEM((length + 8, 2 * LANES), f32),
        pltpu.VMEM((2, span + 8, width), f32),
        pltpu.VMEM((2, span * width // LANES, LANES), bf16),
        pltpu.VMEM((2, span * width // LANES, LANES), bf16),
        pltpu.VMEM((2, span + 8, width), f32),
        pltpu.VMEM((window, 2 * LANES), f32),
        pltpu.VMEM((window, 2 * LANES), f32),
    ]
    d_q_main, sent = pl.pallas_call(
        functools.partial(grads_kernel, ctx_count),
        out_shape=(
            jax.ShapeDtypeStruct(q_pre.shape, f32),
            jax.ShapeDtypeStruct((ctx_count, out_rows, 2 * LANES), f32),
        ),
        in_specs=[smem, vmem, vmem, vmem, vmem],
        out_specs=(vmem, vmem),
        scratch_shapes=scratch,
        compiler_params=pltpu.CompilerParams(vmem_limit_bytes=(24 if ctx_count <= 8 else 60) * MIB),
        name="grads",
    )(doc_lengths, filters, q_pre, d_out, received)
    terms = lax.all_to_all(sent, "ctx", 0, 0, tiled=True)

    def whole(shape):
        return pl.BlockSpec(shape, lambda i: (0,) * len(shape))

    last_rows = pl.BlockSpec((2, 8, width), lambda i: (0, span // 8 - 1, 0))
    d_q_pre, d_k_pre, d_v_pre, sums = pl.pallas_call(
        functools.partial(finish_kernel, ctx_count),
        grid=(1,),
        out_shape=(
            jax.ShapeDtypeStruct(q_pre.shape, f32),
            jax.ShapeDtypeStruct(k_pre.shape, f32),
            jax.ShapeDtypeStruct(k_pre.shape, f32),
            jax.ShapeDtypeStruct(filters.shape, f32),
        ),
        in_specs=[smem, whole(filters.shape), whole(terms.shape), last_rows],
        out_specs=(last_rows, whole(k_pre.shape), whole(k_pre.shape), whole(filters.shape)),
        input_output_aliases={3: 0},
        compiler_params=pltpu.CompilerParams(vmem_limit_bytes=(16 if ctx_count <= 8 else 40) * MIB),
        name="finish",
    )(doc_lengths, filters, terms, d_q_main)

    count = lax.axis_size("tp")
    level = [sums] + [
        lax.ppermute(sums, "tp", [(i, i ^ flip) for i in range(count)]) for flip in range(1, count)
    ]
    while len(level) > 1:
        level = [level[at] + level[at + 1] for at in range(0, len(level), 2)]
    d_filters = level[0]
    return (d_q_pre, d_k_pre, d_v_pre, d_filters)


def solution(mesh):
    split = P(None, "ctx", "tp")
    return jax.shard_map(
        shards,
        mesh=mesh,
        in_specs=(split, split, split, split, P(), P()),
        out_specs=(split, split, split, P()),
        check_vma=False,
    )
```

```python
import functools

import jax
import jax.numpy as jnp
import numpy as np
from jax import lax
from jax.experimental import pallas as pl
from jax.experimental.pallas import tpu as pltpu
from jax.sharding import PartitionSpec as P

LANES = 128
NT = (((1,), (1,)), ((), ()))
NN = (((1,), (0,)), ((), ()))
TN = (((0,), (0,)), ((), ()))
TAIL = 16
MAX_CHUNK = 640
MAX_TURNS = 8
MIB = 1 << 20


def loop(count, body, init, unrolled=16):
    if count <= unrolled:
        for step in range(count):
            init = body(step, init)
        return init
    return lax.fori_loop(0, count, body, init)


def aligned(start, multiple):
    return start if isinstance(start, int) else pl.multiple_of(start, multiple)


def doc_starts(lengths_ref):
    starts = [jnp.int32(0)]
    for index in range(lengths_ref.shape[0] - 1):
        starts.append(starts[-1] + lengths_ref[index])
    return starts


def fold_rows(terms):
    rows, lanes = terms.shape
    return jnp.sum(terms.reshape(rows // 8, 8, lanes), axis=0)


def split_bits(values):
    high = values.astype(jnp.bfloat16)
    low = (values - high.astype(jnp.float32)).astype(jnp.bfloat16)
    return high, low


def joined(pair):
    rows = pair.shape[0] // 2
    pair = pair.astype(jnp.float32)
    return pair[:rows] + pair[rows:]


class Slots:
    def __init__(self, refs, me, ctx_count, sign):
        self.refs, self.me, self.ctx_count, self.sign = refs, me, ctx_count, sign

    def device(self, turn):
        return lax.rem(self.me + self.sign * turn + self.ctx_count, self.ctx_count)

    def __getitem__(self, turn):
        if len(self.refs) == 1:
            return self.refs[0].at[self.device(turn)]
        return self.refs[turn]


def pack_kernel(k_ref, v_ref, q_ref, main_ref, rim_ref):
    span = k_ref.shape[1]
    kv = jnp.concatenate([k_ref[...], v_ref[...]], axis=2).reshape(2 * span, 2 * LANES)
    tails = []
    for half in range(2):
        last = q_ref[half].astype(jnp.float32)[TAIL - 2 :]
        tails += [last[:, at : at + 2 * LANES] for at in range(0, last.shape[1], 2 * LANES)]
    main_ref[...] = kv
    rim_ref[: 2 * span] = kv
    rim_ref[2 * span :] = jnp.concatenate(tails, axis=0).astype(jnp.bfloat16)


def grads_kernel(ctx_count, in_count, out_count, lengths_ref, filters_ref, q_ref, d_out_ref, *refs):
    msg_refs, refs = refs[:in_count], refs[in_count:]
    dq_ref, own_ref = refs[:2]
    out_refs, refs = refs[2 : 2 + out_count], refs[2 + out_count :]
    same_scr, kv_scr, conv_scr, dkv_scr, q_scr, qc_scr, do_scr, dq_scr, s_scr, dp_scr = refs
    f32, bf16 = jnp.float32, jnp.bfloat16
    span = q_ref.shape[1]
    heads = q_ref.shape[2] // LANES
    half_rows = span * ctx_count
    length = 2 * half_rows
    blocks = 2 * ctx_count
    me = lax.axis_index("ctx")
    received = Slots(msg_refs, me, ctx_count, -1)
    sent = Slots(out_refs if out_count == 1 else (own_ref,) + out_refs, me, ctx_count, 1)
    scale = LANES**-0.5
    log2_scale = scale * 1.4426950408889634
    starts = doc_starts(lengths_ref)

    def fill_same(index, carry):
        place = index * span + lax.broadcasted_iota(jnp.int32, (span, LANES), 0)
        cut = place == starts[0]
        for start in starts[1:]:
            cut = cut | (place == start)
        same_scr[pl.ds(aligned(8 + index * span, 8), span)] = jnp.where(cut, 0.0, 1.0)
        return carry

    same_scr[:8] = jnp.zeros((8, LANES), f32)
    same_scr[8 + length :] = jnp.zeros((8, LANES), f32)
    loop(blocks, fill_same, 0)

    kv_scr[:8] = jnp.zeros((8, 2 * LANES), f32)
    kv_scr[8 + length :] = jnp.zeros((8, 2 * LANES), f32)

    def place_blocks(turn, carry):
        index = received.device(turn)
        message = received[turn]
        early = aligned(8 + index * span, 8)
        late = aligned(8 + (blocks - 1 - index) * span, 8)
        kv_scr[pl.ds(early, span)] = message[:span].astype(f32)
        kv_scr[pl.ds(late, span)] = message[span : 2 * span].astype(f32)
        return carry

    loop(ctx_count, place_blocks, 0)

    def kv_taps(tap):
        return jnp.concatenate([filters_ref[1, tap : tap + 1], filters_ref[2, tap : tap + 1]], axis=1)

    def twice(mask):
        return jnp.concatenate([mask, mask], axis=1)

    def back_masks(same, first):
        one = same[first : first + span]
        return one, one * same[first - 1 : first - 1 + span]

    def convolve_kv(index, carry):
        rows = pl.ds(aligned(index * span, 8), span + 8)
        values = kv_scr[rows]
        one, two = back_masks(same_scr[rows], 8)
        total = kv_taps(0) * values[8:]
        total = total + twice(one) * (kv_taps(1) * values[7 : 7 + span])
        total = total + twice(two) * (kv_taps(2) * values[6 : 6 + span])
        conv_scr[pl.ds(aligned(index * span, 16), span)] = total.astype(bf16)
        return carry

    loop(blocks, convolve_kv, 0)

    middle = me == ctx_count - 1
    rim_own = received[0][2 * span :].astype(f32)
    rim_before = received[1][2 * span :].astype(f32)
    rim_after = received[ctx_count - 1][2 * span :].astype(f32)
    rim_rows = rim_own.shape[0] // 2
    late_rim = jnp.where(middle, rim_own[:rim_rows], rim_after[rim_rows:])
    rims = [rim_before[:rim_rows], late_rim]
    first_place = [me * span, (blocks - 1 - me) * span]

    for half in range(2):
        rows = [rims[half][2 * at : 2 * at + 2] for at in range(rim_rows // 2)]
        q_scr[half, 6:8] = jnp.concatenate(rows, axis=1)
        q_scr[half, 8:] = q_ref[half].astype(f32)
        same = same_scr[pl.ds(aligned(first_place[half], 8), span + 16)]
        one, two = back_masks(same, 8)
        for head in range(heads):
            lanes = slice(head * LANES, (head + 1) * LANES)
            total = filters_ref[0, 0:1] * q_scr[half, 8:, lanes]
            total = total + one * (filters_ref[0, 1:2] * q_scr[half, 7 : 7 + span, lanes])
            total = total + two * (filters_ref[0, 2:3] * q_scr[half, 6 : 6 + span, lanes])
            qc_scr[half, head * span : (head + 1) * span] = total.astype(bf16)
            do_scr[half, head * span : (head + 1) * span] = d_out_ref[half, :, lanes]

    def attend(half, window, first_key, add):
        chunks = 1
        while window // chunks > MAX_CHUNK or window % (16 * chunks):
            chunks += 1
        size = window // chunks
        query = first_place[half] + lax.rem(
            lax.broadcasted_iota(jnp.int32, (1, LANES), 1), jnp.int32(span)
        )
        lowest = jnp.zeros((1, LANES), jnp.int32)
        for start in starts[1:]:
            lowest = jnp.where(query >= start, start, lowest)
        group = 2 * LANES
        for at in range(heads * span // group):
            cols = slice(at * group, (at + 1) * group)
            queries = qc_scr[half, cols]
            grads = do_scr[half, cols]

            def key_rows(step):
                return pl.ds(aligned(first_key + step * size, 16), size)

            def score(step, top):
                places = first_key + step * size + lax.broadcasted_iota(jnp.int32, (size, LANES), 0)
                allowed = (places >= lowest) & (places <= query)
                bias = jnp.where(allowed, 0.0, -1e30)
                keys = conv_scr[key_rows(step), :LANES]
                scores = lax.dot_general(keys, queries, NT, preferred_element_type=f32)
                scores = scores + twice(bias)
                s_scr[pl.ds(aligned(step * size, 16), size)] = scores
                return jnp.maximum(top, jnp.max(scores, axis=0, keepdims=True))

            top = loop(chunks, score, jnp.full((1, group), -1e30, f32), 1)

            def weigh(step, carry):
                total, weighted = carry
                rows = pl.ds(aligned(step * size, 16), size)
                weights = jnp.exp2((s_scr[rows] - top) * log2_scale)
                values = conv_scr[key_rows(step), LANES:]
                prob_grads = lax.dot_general(values, grads, NT, preferred_element_type=f32)
                s_scr[rows] = weights
                dp_scr[rows] = prob_grads
                total = total + jnp.sum(weights, axis=0, keepdims=True)
                weighted = weighted + jnp.sum(weights * prob_grads, axis=0, keepdims=True)
                return total, weighted

            zeros = jnp.zeros((1, group), f32)
            total, weighted = loop(chunks, weigh, (zeros, zeros), 1)
            inverse = 1.0 / total
            mean = weighted * inverse
            slope = inverse * scale

            def accumulate(step, dq):
                rows = pl.ds(aligned(step * size, 16), size)
                weights = s_scr[rows]
                probs = (weights * inverse).astype(bf16)
                score_grads = (weights * slope * (dp_scr[rows] - mean)).astype(bf16)
                keys = conv_scr[key_rows(step), :LANES]
                dk = lax.dot_general(score_grads, queries, NN, preferred_element_type=f32)
                dv = lax.dot_general(probs, grads, NN, preferred_element_type=f32)
                terms = jnp.concatenate([dk, dv], axis=1)
                target = pl.ds(aligned(first_key + step * size, 16), size)
                if add or at:
                    dkv_scr[target] += terms
                else:
                    dkv_scr[target] = terms
                return dq + lax.dot_general(keys, score_grads, TN, preferred_element_type=f32)

            dq = loop(chunks, accumulate, jnp.zeros((LANES, group), f32), 1)
            dq = dq.T
            for part in range(group // span):
                head = at * (group // span) + part
                dq_scr[half, :span, head * LANES : (head + 1) * LANES] = dq[
                    part * span : (part + 1) * span
                ]

    dkv_scr[half_rows:] = jnp.zeros((half_rows + 8, 2 * LANES), f32)
    attend(0, half_rows, 0, False)
    attend(1, half_rows + span, (ctx_count - 1 - me) * span, True)

    next_rows = jnp.where(middle, dq_scr[1, :8], 0.0)
    dq_scr[0, span:] = next_rows
    dq_scr[1, span:] = jnp.zeros_like(next_rows)
    sums = [jnp.zeros((8, LANES), f32) for _ in range(3)]
    for half in range(2):
        same = same_scr[pl.ds(aligned(first_place[half], 8), span + 16)]
        one, two = back_masks(same, 8)
        ahead_one = same[9 : 9 + span]
        ahead_two = same[10 : 10 + span] * ahead_one
        for head in range(heads):
            lanes = slice(head * LANES, (head + 1) * LANES)
            grads = dq_scr[half, :span, lanes]
            out = filters_ref[0, 0:1] * grads
            out = out + ahead_one * (filters_ref[0, 1:2] * dq_scr[half, 1 : 1 + span, lanes])
            out = out + ahead_two * (filters_ref[0, 2:3] * dq_scr[half, 2 : 2 + span, lanes])
            dq_ref[half, :, lanes] = out
            sums[0] += fold_rows(grads * q_scr[half, 8:, lanes])
            sums[1] += fold_rows(grads * one * q_scr[half, 7 : 7 + span, lanes])
            sums[2] += fold_rows(grads * two * q_scr[half, 6 : 6 + span, lanes])
    q_sums = [jnp.sum(term, axis=0, keepdims=True) for term in sums]

    def finish_block(index, carry):
        base = aligned(index * span, 8)
        grads = dkv_scr[pl.ds(base, span + 8)]
        values = kv_scr[pl.ds(base, span + 8)]
        same = same_scr[pl.ds(base, span + 16)]
        one, two = back_masks(same, 8)
        ahead_one = same[9 : 9 + span]
        ahead_two = same[10 : 10 + span] * ahead_one
        out = kv_taps(0) * grads[:span]
        out = out + twice(ahead_one) * (kv_taps(1) * grads[1 : 1 + span])
        out = out + twice(ahead_two) * (kv_taps(2) * grads[2 : 2 + span])
        own = grads[:span]
        return out, (
            carry[0] + fold_rows(own * values[8:]),
            carry[1] + fold_rows(own * twice(one) * values[7 : 7 + span]),
            carry[2] + fold_rows(own * twice(two) * values[6 : 6 + span]),
        )

    def finish(turn, carry):
        index = sent.device(turn)
        message = sent[turn]
        out, carry = finish_block(index, carry)
        message[:span] = out.astype(bf16)
        out, carry = finish_block(blocks - 1 - index, carry)
        message[span : 2 * span] = out.astype(bf16)
        return carry

    zeros = jnp.zeros((8, 2 * LANES), f32)
    own_ref[:span], kv_sums = finish_block(me, (zeros, zeros, zeros))
    own_ref[span : 2 * span], kv_sums = finish_block(blocks - 1 - me, kv_sums)
    kv_sums = loop(ctx_count - 1, lambda turn, carry: finish(turn + 1, carry), kv_sums)
    kv_sums = [jnp.sum(term, axis=0, keepdims=True) for term in kv_sums]

    sums_tile = jnp.concatenate(
        [jnp.concatenate([term, jnp.zeros_like(term)], axis=1) for term in q_sums]
        + kv_sums
        + [jnp.zeros((2, 2 * LANES), f32)],
        axis=0,
    )
    sums_pair = jnp.concatenate(split_bits(sums_tile), axis=0)
    own_ref[2 * span :] = joined(sums_pair)

    def store_sums(turn, carry):
        sent[turn + 1][2 * span : 2 * span + 16] = sums_pair
        return carry

    loop(ctx_count - 1, store_sums, 0)
    for half, turn in ((0, ctx_count - 1), (1, 1)):
        rows = dq_scr[half, :2]
        rows = [rows[:, at : at + 2 * LANES] for at in range(0, rows.shape[1], 2 * LANES)]
        pair = jnp.concatenate(split_bits(jnp.concatenate(rows, axis=0)), axis=0)
        sent[turn][2 * span + 16 : 2 * span + 32] = pair


def finish_kernel(ctx_count, in_count, lengths_ref, filters_ref, dq_in_ref, own_ref, *refs):
    msg_refs, refs = refs[:in_count], refs[in_count:]
    dq_ref, dk_ref, dv_ref, sums_ref, sums_scr = refs
    f32 = jnp.float32
    span = dk_ref.shape[1]
    me = lax.axis_index("ctx")
    received = Slots(msg_refs if in_count == 1 else (own_ref,) + msg_refs, me, ctx_count, -1)
    starts = doc_starts(lengths_ref)
    blocks = 2 * ctx_count

    sums_scr[me] = own_ref[2 * span :]

    def add(turn, carry):
        message = received[turn + 1]
        sums_scr[received.device(turn + 1)] = joined(message[2 * span : 2 * span + 16])
        return carry + message[: 2 * span].astype(f32)

    total = loop(ctx_count - 1, add, own_ref[: 2 * span])
    for half in range(2):
        dk_ref[half] = total[half * span : (half + 1) * span, :LANES]
        dv_ref[half] = total[half * span : (half + 1) * span, LANES:]
    sums = loop(ctx_count, lambda index, carry: carry + sums_scr[index], jnp.zeros((8, 2 * LANES), f32))
    sums_ref[0] = sums[0:3, :LANES]
    sums_ref[1] = sums[3:6, :LANES]
    sums_ref[2] = sums[3:6, LANES:]

    def same(place):
        cut = place >= blocks * span
        for start in starts:
            cut = cut | (place == start)
        return jnp.where(cut, 0.0, 1.0).astype(f32)

    heads = dq_ref.shape[2] // LANES
    taps = [jnp.concatenate([filters_ref[0, tap : tap + 1]] * heads, axis=1) for tap in range(3)]
    row = lax.broadcasted_iota(jnp.int32, dq_ref.shape[1:], 0)
    turns = [ctx_count - 1, 1]
    first_place = [me * span, (blocks - 1 - me) * span]
    present = [me < ctx_count - 1, me > 0]
    for half in range(2):
        rim = joined(received[turns[half]][2 * span + 16 : 2 * span + 32])
        rows = jnp.concatenate([rim[2 * at : 2 * at + 2] for at in range(rim.shape[0] // 2)], axis=1)
        end = first_place[half] + span
        zero, one, two = same(end - 1), same(end), same(end + 1)
        one = jnp.where(present[half], one, 0.0)
        last_but_one = (zero * one) * (taps[2] * rows[0:1])
        last = one * (taps[1] * rows[0:1]) + (one * two) * (taps[2] * rows[1:2])
        extra = jnp.where(row == 6, last_but_one, jnp.where(row == 7, last, 0.0))
        dq_ref[half] = dq_in_ref[half] + extra


def shards(q_pre, k_pre, value_before_filter, d_out, filters, doc_lengths):
    f32, bf16 = jnp.float32, jnp.bfloat16
    ctx_count = lax.axis_size("ctx")
    span, width = q_pre.shape[1:]
    length = 2 * span * ctx_count
    rim = 4 * width // (2 * LANES)
    vmem = pl.BlockSpec(memory_space=pltpu.VMEM)
    smem = pl.BlockSpec(memory_space=pltpu.SMEM)

    def rows_of(turn):
        return 2 * span + (rim if turn in (1, ctx_count - 1) else 0)

    def whole(shape):
        return pl.BlockSpec(shape, lambda i: (0,) * len(shape))

    def turned(array, turn):
        return lax.ppermute(array, "ctx", [(i, (i + turn) % ctx_count) for i in range(ctx_count)])

    few = ctx_count <= MAX_TURNS
    main, rimmed = pl.pallas_call(
        pack_kernel,
        grid=(1,),
        out_shape=[jax.ShapeDtypeStruct((2 * span + more, 2 * LANES), bf16) for more in (0, rim)],
        in_specs=[
            whole(k_pre.shape),
            whole(k_pre.shape),
            pl.BlockSpec((2, TAIL, width), lambda i: (0, span // TAIL - 1, 0)),
        ],
        out_specs=[whole((2 * span + more, 2 * LANES)) for more in (0, rim)],
        name="pack",
    )(k_pre, value_before_filter, q_pre)
    if few:
        received = [rimmed] + [
            turned(main if rows_of(turn) == 2 * span else rimmed, turn)
            for turn in range(1, ctx_count)
        ]
    else:
        everywhere = jnp.broadcast_to(rimmed[None], (ctx_count,) + rimmed.shape)
        received = [lax.all_to_all(everywhere, "ctx", 0, 0, tiled=True)]

    window = span * ctx_count + span
    if few:
        sent_shapes = [
            (2 * span + (32 if turn in (1, ctx_count - 1) else 16), 2 * LANES)
            for turn in range(1, ctx_count)
        ]
    else:
        sent_shapes = [(ctx_count, 2 * span + 32, 2 * LANES)]
    scratch = [
        pltpu.VMEM((length + 16, LANES), f32),
        pltpu.VMEM((length + 16, 2 * LANES), f32),
        pltpu.VMEM((length, 2 * LANES), bf16),
        pltpu.VMEM((length + 8, 2 * LANES), f32),
        pltpu.VMEM((2, span + 8, width), f32),
        pltpu.VMEM((2, span * width // LANES, LANES), bf16),
        pltpu.VMEM((2, span * width // LANES, LANES), bf16),
        pltpu.VMEM((2, span + 8, width), f32),
        pltpu.VMEM((window, 2 * LANES), f32),
        pltpu.VMEM((window, 2 * LANES), f32),
    ]
    own_shape = (2 * span + 8, 2 * LANES)
    d_q_main, own, *sent = pl.pallas_call(
        functools.partial(grads_kernel, ctx_count, len(received), len(sent_shapes)),
        out_shape=[jax.ShapeDtypeStruct(q_pre.shape, f32), jax.ShapeDtypeStruct(own_shape, f32)]
        + [jax.ShapeDtypeStruct(shape, bf16) for shape in sent_shapes],
        in_specs=[smem] + [vmem] * (3 + len(received)),
        out_specs=[vmem] * (2 + len(sent_shapes)),
        scratch_shapes=scratch,
        compiler_params=pltpu.CompilerParams(vmem_limit_bytes=(24 if few else 60) * MIB),
        name="grads",
    )(doc_lengths, filters, q_pre, d_out, *received)
    if few:
        terms = [turned(array, turn + 1) for turn, array in enumerate(sent)]
    else:
        terms = [lax.all_to_all(sent[0], "ctx", 0, 0, tiled=True)]

    last_rows = pl.BlockSpec((2, 8, width), lambda i: (0, span // 8 - 1, 0))
    d_q_pre, d_k_pre, d_v_pre, sums = pl.pallas_call(
        functools.partial(finish_kernel, ctx_count, len(terms)),
        grid=(1,),
        out_shape=(
            jax.ShapeDtypeStruct(q_pre.shape, f32),
            jax.ShapeDtypeStruct(k_pre.shape, f32),
            jax.ShapeDtypeStruct(k_pre.shape, f32),
            jax.ShapeDtypeStruct(filters.shape, f32),
        ),
        in_specs=[smem, whole(filters.shape), last_rows, whole(own_shape)]
        + [whole(array.shape) for array in terms],
        out_specs=(last_rows, whole(k_pre.shape), whole(k_pre.shape), whole(filters.shape)),
        scratch_shapes=[pltpu.VMEM((ctx_count, 8, 2 * LANES), f32)],
        input_output_aliases={2: 0},
        compiler_params=pltpu.CompilerParams(vmem_limit_bytes=(16 if few else 40) * MIB),
        name="finish",
    )(doc_lengths, filters, d_q_main, own, *terms)

    count = lax.axis_size("tp")
    level = [sums] + [
        lax.ppermute(sums, "tp", [(i, i ^ flip) for i in range(count)]) for flip in range(1, count)
    ]
    while len(level) > 1:
        level = [level[at] + level[at + 1] for at in range(0, len(level), 2)]
    d_filters = level[0]
    return (d_q_pre, d_k_pre, d_v_pre, d_filters)


def solution(mesh):
    split = P(None, "ctx", "tp")
    return jax.shard_map(
        shards,
        mesh=mesh,
        in_specs=(split, split, split, split, P(), P()),
        out_specs=(split, split, split, P()),
        check_vma=False,
    )
```

```python
import functools

import jax
import jax.numpy as jnp
import numpy as np
from jax import lax
from jax.experimental import pallas as pl
from jax.experimental.pallas import tpu as pltpu
from jax.sharding import PartitionSpec as P

LANES = 128
NT = (((1,), (1,)), ((), ()))
NN = (((1,), (0,)), ((), ()))
TN = (((0,), (0,)), ((), ()))
TAIL = 16
MAX_CHUNK = 640
MAX_DIRECT = 4
MIB = 1 << 20


def loop(count, body, init, unrolled=16):
    if count <= unrolled:
        for step in range(count):
            init = body(step, init)
        return init
    return lax.fori_loop(0, count, body, init)


def aligned(start, multiple):
    return start if isinstance(start, int) else pl.multiple_of(start, multiple)


def doc_starts(lengths_ref):
    starts = [jnp.int32(0)]
    for index in range(lengths_ref.shape[0] - 1):
        starts.append(starts[-1] + lengths_ref[index])
    return starts


def fold_rows(terms):
    rows, lanes = terms.shape
    return jnp.sum(terms.reshape(rows // 8, 8, lanes), axis=0)


def split_bits(values):
    high = values.astype(jnp.bfloat16)
    low = (values - high.astype(jnp.float32)).astype(jnp.bfloat16)
    return high, low


def joined(pair):
    rows = pair.shape[0] // 2
    pair = pair.astype(jnp.float32)
    return pair[:rows] + pair[rows:]


class Slots:
    def __init__(self, refs, me):
        self.refs, self.me = refs, me

    def __getitem__(self, flip):
        if len(self.refs) == 1:
            place = lax.rem(self.me, jnp.int32(self.refs[0].shape[0]))
            return self.refs[0].at[partner(place, flip)]
        return self.refs[flip]


def partner(me, flip):
    return lax.bitwise_xor(me, jnp.int32(flip))


def pack_kernel(k_ref, v_ref, q_ref, out_ref):
    span = k_ref.shape[1]
    kv = jnp.concatenate([k_ref[...], v_ref[...]], axis=2).reshape(2 * span, 2 * LANES)
    tails = []
    for half in range(2):
        last = q_ref[half].astype(jnp.float32)[TAIL - 2 :]
        tails += [last[:, at : at + 2 * LANES] for at in range(0, last.shape[1], 2 * LANES)]
    out_ref[: 2 * span] = kv
    out_ref[2 * span :] = jnp.concatenate(tails, axis=0).astype(jnp.bfloat16)


def grads_kernel(ctx_count, direct, lengths_ref, filters_ref, q_ref, d_out_ref, *refs):
    group = ctx_count // 2
    arrays = group if direct else 1
    near_in, far_in, refs = refs[:arrays], refs[arrays : 2 * arrays], refs[2 * arrays :]
    dq_ref, own_near_ref, own_far_ref = refs[:3]
    arrays = group - 1 if direct else 1
    near_out, far_out = refs[3 : 3 + arrays], refs[3 + arrays : 3 + 2 * arrays]
    same_scr, kv_scr, conv_scr, dkv_scr, q_scr, qc_scr, do_scr, dq_scr, s_scr, dp_scr, rim_scr = refs[
        3 + 2 * arrays :
    ]
    f32, bf16 = jnp.float32, jnp.bfloat16
    span = q_ref.shape[1]
    heads = q_ref.shape[2] // LANES
    half_rows = span * ctx_count
    length = 2 * half_rows
    blocks = 2 * ctx_count
    me = lax.axis_index("ctx")
    near_in, far_in = Slots(near_in, me), Slots(far_in, me)
    near_out = Slots((own_near_ref,) + near_out if direct else near_out, me)
    far_out = Slots((own_far_ref,) + far_out if direct else far_out, me)
    scale = LANES**-0.5
    log2_scale = scale * 1.4426950408889634
    starts = doc_starts(lengths_ref)

    def fill_same(index, carry):
        place = index * span + lax.broadcasted_iota(jnp.int32, (span, LANES), 0)
        cut = place == starts[0]
        for start in starts[1:]:
            cut = cut | (place == start)
        same_scr[pl.ds(aligned(8 + index * span, 8), span)] = jnp.where(cut, 0.0, 1.0)
        return carry

    same_scr[:8] = jnp.zeros((8, LANES), f32)
    same_scr[8 + length :] = jnp.zeros((8, LANES), f32)
    loop(blocks, fill_same, 0)

    kv_scr[:8] = jnp.zeros((8, 2 * LANES), f32)
    kv_scr[8 + length :] = jnp.zeros((8, 2 * LANES), f32)

    def place_blocks(flip, carry):
        for message, index in (
            (near_in[flip], partner(me, flip)),
            (far_in[flip], partner(me, flip + group)),
        ):
            early = aligned(8 + index * span, 8)
            late = aligned(8 + (blocks - 1 - index) * span, 8)
            kv_scr[pl.ds(early, span)] = message[:span].astype(f32)
            kv_scr[pl.ds(late, span)] = message[span : 2 * span].astype(f32)
            rim_scr[index] = message[2 * span :].astype(f32)
        return carry

    loop(group, place_blocks, 0)

    def kv_taps(tap):
        return jnp.concatenate([filters_ref[1, tap : tap + 1], filters_ref[2, tap : tap + 1]], axis=1)

    def twice(mask):
        return jnp.concatenate([mask, mask], axis=1)

    def back_masks(same, first):
        one = same[first : first + span]
        return one, one * same[first - 1 : first - 1 + span]

    def convolve_kv(index, carry):
        rows = pl.ds(aligned(index * span, 8), span + 8)
        values = kv_scr[rows]
        one, two = back_masks(same_scr[rows], 8)
        total = kv_taps(0) * values[8:]
        total = total + twice(one) * (kv_taps(1) * values[7 : 7 + span])
        total = total + twice(two) * (kv_taps(2) * values[6 : 6 + span])
        conv_scr[pl.ds(aligned(index * span, 16), span)] = total.astype(bf16)
        return carry

    loop(blocks, convolve_kv, 0)

    middle = me == ctx_count - 1
    rim_rows = rim_scr.shape[1] // 2
    rim_before = rim_scr[jnp.maximum(me - 1, 0)]
    rim_after = rim_scr[jnp.minimum(me + 1, ctx_count - 1)]
    late_rim = jnp.where(middle, rim_after[:rim_rows], rim_after[rim_rows:])
    rims = [rim_before[:rim_rows], late_rim]
    first_place = [me * span, (blocks - 1 - me) * span]

    for half in range(2):
        rows = [rims[half][2 * at : 2 * at + 2] for at in range(rim_rows // 2)]
        q_scr[half, 6:8] = jnp.concatenate(rows, axis=1)
        q_scr[half, 8:] = q_ref[half].astype(f32)
        same = same_scr[pl.ds(aligned(first_place[half], 8), span + 16)]
        one, two = back_masks(same, 8)
        for head in range(heads):
            lanes = slice(head * LANES, (head + 1) * LANES)
            total = filters_ref[0, 0:1] * q_scr[half, 8:, lanes]
            total = total + one * (filters_ref[0, 1:2] * q_scr[half, 7 : 7 + span, lanes])
            total = total + two * (filters_ref[0, 2:3] * q_scr[half, 6 : 6 + span, lanes])
            qc_scr[half, head * span : (head + 1) * span] = total.astype(bf16)
            do_scr[half, head * span : (head + 1) * span] = d_out_ref[half, :, lanes]

    def attend(half, window, first_key, add):
        chunks = 1
        while window // chunks > MAX_CHUNK or window % (16 * chunks):
            chunks += 1
        size = window // chunks
        query = first_place[half] + lax.rem(
            lax.broadcasted_iota(jnp.int32, (1, LANES), 1), jnp.int32(span)
        )
        lowest = jnp.zeros((1, LANES), jnp.int32)
        for start in starts[1:]:
            lowest = jnp.where(query >= start, start, lowest)
        wide = 2 * LANES
        for at in range(heads * span // wide):
            cols = slice(at * wide, (at + 1) * wide)
            queries = qc_scr[half, cols]
            grads = do_scr[half, cols]

            def key_rows(step):
                return pl.ds(aligned(first_key + step * size, 16), size)

            def score(step, top):
                places = first_key + step * size + lax.broadcasted_iota(jnp.int32, (size, LANES), 0)
                allowed = (places >= lowest) & (places <= query)
                bias = jnp.where(allowed, 0.0, -1e30)
                keys = conv_scr[key_rows(step), :LANES]
                scores = lax.dot_general(keys, queries, NT, preferred_element_type=f32)
                scores = scores + twice(bias)
                s_scr[pl.ds(aligned(step * size, 16), size)] = scores
                return jnp.maximum(top, jnp.max(scores, axis=0, keepdims=True))

            top = loop(chunks, score, jnp.full((1, wide), -1e30, f32), 1)

            def weigh(step, carry):
                total, weighted = carry
                rows = pl.ds(aligned(step * size, 16), size)
                weights = jnp.exp2((s_scr[rows] - top) * log2_scale)
                values = conv_scr[key_rows(step), LANES:]
                prob_grads = lax.dot_general(values, grads, NT, preferred_element_type=f32)
                s_scr[rows] = weights
                dp_scr[rows] = prob_grads
                total = total + jnp.sum(weights, axis=0, keepdims=True)
                weighted = weighted + jnp.sum(weights * prob_grads, axis=0, keepdims=True)
                return total, weighted

            zeros = jnp.zeros((1, wide), f32)
            total, weighted = loop(chunks, weigh, (zeros, zeros), 1)
            inverse = 1.0 / total
            mean = weighted * inverse
            slope = inverse * scale

            def accumulate(step, dq):
                rows = pl.ds(aligned(step * size, 16), size)
                weights = s_scr[rows]
                probs = (weights * inverse).astype(bf16)
                score_grads = (weights * slope * (dp_scr[rows] - mean)).astype(bf16)
                keys = conv_scr[key_rows(step), :LANES]
                dk = lax.dot_general(score_grads, queries, NN, preferred_element_type=f32)
                dv = lax.dot_general(probs, grads, NN, preferred_element_type=f32)
                terms = jnp.concatenate([dk, dv], axis=1)
                target = pl.ds(aligned(first_key + step * size, 16), size)
                if add or at:
                    dkv_scr[target] += terms
                else:
                    dkv_scr[target] = terms
                return dq + lax.dot_general(keys, score_grads, TN, preferred_element_type=f32)

            dq = loop(chunks, accumulate, jnp.zeros((LANES, wide), f32), 1)
            dq = dq.T
            for part in range(wide // span):
                head = at * (wide // span) + part
                dq_scr[half, :span, head * LANES : (head + 1) * LANES] = dq[
                    part * span : (part + 1) * span
                ]

    dkv_scr[half_rows:] = jnp.zeros((half_rows + 8, 2 * LANES), f32)
    attend(0, half_rows, 0, False)
    attend(1, half_rows + span, (ctx_count - 1 - me) * span, True)

    next_rows = jnp.where(middle, dq_scr[1, :8], 0.0)
    dq_scr[0, span:] = next_rows
    dq_scr[1, span:] = jnp.zeros_like(next_rows)
    sums = [jnp.zeros((8, LANES), f32) for _ in range(3)]
    for half in range(2):
        same = same_scr[pl.ds(aligned(first_place[half], 8), span + 16)]
        one, two = back_masks(same, 8)
        ahead_one = same[9 : 9 + span]
        ahead_two = same[10 : 10 + span] * ahead_one
        for head in range(heads):
            lanes = slice(head * LANES, (head + 1) * LANES)
            grads = dq_scr[half, :span, lanes]
            out = filters_ref[0, 0:1] * grads
            out = out + ahead_one * (filters_ref[0, 1:2] * dq_scr[half, 1 : 1 + span, lanes])
            out = out + ahead_two * (filters_ref[0, 2:3] * dq_scr[half, 2 : 2 + span, lanes])
            dq_ref[half, :, lanes] = out
            sums[0] += fold_rows(grads * q_scr[half, 8:, lanes])
            sums[1] += fold_rows(grads * one * q_scr[half, 7 : 7 + span, lanes])
            sums[2] += fold_rows(grads * two * q_scr[half, 6 : 6 + span, lanes])
    q_sums = [jnp.sum(term, axis=0, keepdims=True) for term in sums]

    def finish_block(index, carry):
        base = aligned(index * span, 8)
        grads = dkv_scr[pl.ds(base, span + 8)]
        values = kv_scr[pl.ds(base, span + 8)]
        same = same_scr[pl.ds(base, span + 16)]
        one, two = back_masks(same, 8)
        ahead_one = same[9 : 9 + span]
        ahead_two = same[10 : 10 + span] * ahead_one
        out = kv_taps(0) * grads[:span]
        out = out + twice(ahead_one) * (kv_taps(1) * grads[1 : 1 + span])
        out = out + twice(ahead_two) * (kv_taps(2) * grads[2 : 2 + span])
        own = grads[:span]
        return out, (
            carry[0] + fold_rows(own * values[8:]),
            carry[1] + fold_rows(own * twice(one) * values[7 : 7 + span]),
            carry[2] + fold_rows(own * twice(two) * values[6 : 6 + span]),
        )

    def finish_pair(index, carry):
        early, carry = finish_block(index, carry)
        late, carry = finish_block(blocks - 1 - index, carry)
        return jnp.concatenate([early, late], axis=0), carry

    def finish(flip, carry):
        terms, carry = finish_pair(partner(me, flip + group), carry)
        far_out[flip][: 2 * span] = terms.astype(bf16)
        terms, carry = finish_pair(partner(me, flip), carry)
        near_out[flip][: 2 * span] = terms.astype(bf16)
        return carry

    zeros = jnp.zeros((8, 2 * LANES), f32)
    own_far_ref[: 2 * span], kv_sums = finish_pair(partner(me, group), (zeros, zeros, zeros))
    own_near_ref[...], kv_sums = finish_pair(me, kv_sums)
    kv_sums = loop(group - 1, lambda step, carry: finish(step + 1, carry), kv_sums)
    kv_sums = [jnp.sum(term, axis=0, keepdims=True) for term in kv_sums]

    sums_tile = jnp.concatenate(
        [jnp.concatenate([term, jnp.zeros_like(term)], axis=1) for term in q_sums]
        + kv_sums
        + [jnp.zeros((2, 2 * LANES), f32)],
        axis=0,
    )
    sums_pair = jnp.concatenate(split_bits(sums_tile), axis=0)
    own_far_ref[2 * span :] = joined(sums_pair)
    rims = []
    for half in range(2):
        rows = dq_scr[half, :2]
        rows = [rows[:, at : at + 2 * LANES] for at in range(0, rows.shape[1], 2 * LANES)]
        rims.append(jnp.concatenate(rows, axis=0))

    def rim_for(index):
        return jnp.concatenate(split_bits(jnp.where(index < me, rims[0], rims[1])), axis=0)

    def store_rims(step, carry):
        flip = step + 1
        far_out[flip][2 * span : 2 * span + 16] = sums_pair
        if not direct or flip == group - 1:
            far_out[flip][2 * span + 16 :] = rim_for(partner(me, flip + group))
        if not direct or flip & (flip + 1) == 0:
            near_out[flip][2 * span :] = rim_for(partner(me, flip))
        return carry

    loop(group - 1, store_rims, 0, 16 if direct else 1)


def merge_kernel(group, direct, own_ref, *refs):
    received_refs, (out_ref, half_sums_ref, sums_scr) = refs[:-3], refs[-3:]
    f32, bf16 = jnp.float32, jnp.bfloat16
    me = lax.axis_index("ctx")
    received = Slots((own_ref,) + received_refs if direct else received_refs, me)
    place = lax.rem(me, jnp.int32(group))
    rows = own_ref.shape[0] - 8
    sums_scr[place] = own_ref[rows:]

    def add(step, carry):
        message = received[step + 1]
        sums_scr[partner(place, step + 1)] = joined(message[rows : rows + 16])
        return carry + message[:rows].astype(f32)

    out_ref[:rows] = loop(group - 1, add, own_ref[:rows]).astype(bf16)
    sums = loop(group, lambda index, carry: carry + sums_scr[index], jnp.zeros((8, 2 * LANES), f32))
    pair = jnp.concatenate(split_bits(sums), axis=0)
    half_sums_ref[...] = joined(pair)
    out_ref[rows : rows + 16] = pair
    out_ref[rows + 16 :] = received[group - 1][rows + 16 :]


def finish_kernel(
    ctx_count, direct, lengths_ref, filters_ref, dq_in_ref, own_ref, half_sums_ref, far_ref, *refs
):
    near_refs, (dq_ref, dk_ref, dv_ref, sums_ref, rim_scr) = refs[:-5], refs[-5:]
    f32 = jnp.float32
    group = ctx_count // 2
    span = dk_ref.shape[1]
    me = lax.axis_index("ctx")
    near = Slots((own_ref,) + near_refs if direct else near_refs, me)
    starts = doc_starts(lengths_ref)
    blocks = 2 * ctx_count

    rim_scr[me] = jnp.zeros(rim_scr.shape[1:], f32)
    rim_scr[partner(me, ctx_count - 1)] = joined(far_ref[2 * span + 16 :])

    def add(step, carry):
        flip = step + 1
        message = near[flip]
        if not direct or flip & (flip + 1) == 0:
            rim_scr[partner(me, flip)] = joined(message[2 * span :])
        return carry + message[: 2 * span].astype(f32)

    total = own_ref[...] + far_ref[: 2 * span].astype(f32)
    total = loop(group - 1, add, total, 16 if direct else 1)
    for half in range(2):
        dk_ref[half] = total[half * span : (half + 1) * span, :LANES]
        dv_ref[half] = total[half * span : (half + 1) * span, LANES:]
    sums = half_sums_ref[...] + joined(far_ref[2 * span : 2 * span + 16])
    sums_ref[0] = sums[0:3, :LANES]
    sums_ref[1] = sums[3:6, :LANES]
    sums_ref[2] = sums[3:6, LANES:]

    def same(place):
        cut = place >= blocks * span
        for start in starts:
            cut = cut | (place == start)
        return jnp.where(cut, 0.0, 1.0).astype(f32)

    heads = dq_ref.shape[2] // LANES
    taps = [jnp.concatenate([filters_ref[0, tap : tap + 1]] * heads, axis=1) for tap in range(3)]
    row = lax.broadcasted_iota(jnp.int32, dq_ref.shape[1:], 0)
    sources = [jnp.minimum(me + 1, ctx_count - 1), jnp.maximum(me - 1, 0)]
    first_place = [me * span, (blocks - 1 - me) * span]
    present = [me < ctx_count - 1, me > 0]
    for half in range(2):
        rim = rim_scr[sources[half]]
        rows = jnp.concatenate([rim[2 * at : 2 * at + 2] for at in range(rim.shape[0] // 2)], axis=1)
        end = first_place[half] + span
        zero, one, two = same(end - 1), same(end), same(end + 1)
        one = jnp.where(present[half], one, 0.0)
        last_but_one = (zero * one) * (taps[2] * rows[0:1])
        last = one * (taps[1] * rows[0:1]) + (one * two) * (taps[2] * rows[1:2])
        extra = jnp.where(row == 6, last_but_one, jnp.where(row == 7, last, 0.0))
        dq_ref[half] = dq_in_ref[half] + extra


def shards(q_pre, k_pre, value_before_filter, d_out, filters, doc_lengths):
    f32, bf16 = jnp.float32, jnp.bfloat16
    ctx_count = lax.axis_size("ctx")
    span, width = q_pre.shape[1:]
    length = 2 * span * ctx_count
    rim = 4 * width // (2 * LANES)
    vmem = pl.BlockSpec(memory_space=pltpu.VMEM)
    smem = pl.BlockSpec(memory_space=pltpu.SMEM)

    group = ctx_count // 2
    direct = group <= MAX_DIRECT
    halves = [[half * group + at for at in range(group)] for half in range(2)]
    msg_rows = 2 * span + rim

    def whole(shape):
        return pl.BlockSpec(shape, lambda i: (0,) * len(shape))

    def flipped(array, flip):
        return lax.ppermute(array, "ctx", [(i, i ^ flip) for i in range(ctx_count)])

    def gathered(array):
        if direct:
            return [array] + [flipped(array, flip) for flip in range(1, group)]
        return [lax.all_gather(array, "ctx", axis_index_groups=halves)]

    def delivered(arrays):
        if direct:
            return [flipped(array, step + 1) for step, array in enumerate(arrays)]
        return [lax.all_to_all(arrays[0], "ctx", 0, 0, axis_index_groups=halves, tiled=True)]

    packed = pl.pallas_call(
        pack_kernel,
        grid=(1,),
        out_shape=jax.ShapeDtypeStruct((msg_rows, 2 * LANES), bf16),
        in_specs=[
            whole(k_pre.shape),
            whole(k_pre.shape),
            pl.BlockSpec((2, TAIL, width), lambda i: (0, span // TAIL - 1, 0)),
        ],
        out_specs=whole((msg_rows, 2 * LANES)),
        name="pack",
    )(k_pre, value_before_filter, q_pre)
    across = flipped(packed, group)
    received = gathered(packed) + gathered(across)

    window = span * ctx_count + span
    if direct:
        flips = range(1, group)
        near_shapes = [(2 * span + (16 if flip & (flip + 1) == 0 else 0), 2 * LANES) for flip in flips]
        far_shapes = [(2 * span + (32 if flip == group - 1 else 16), 2 * LANES) for flip in flips]
    else:
        near_shapes = [(group, 2 * span + 16, 2 * LANES)]
        far_shapes = [(group, 2 * span + 32, 2 * LANES)]
    scratch = [
        pltpu.VMEM((length + 16, LANES), f32),
        pltpu.VMEM((length + 16, 2 * LANES), f32),
        pltpu.VMEM((length, 2 * LANES), bf16),
        pltpu.VMEM((length + 8, 2 * LANES), f32),
        pltpu.VMEM((2, span + 8, width), f32),
        pltpu.VMEM((2, span * width // LANES, LANES), bf16),
        pltpu.VMEM((2, span * width // LANES, LANES), bf16),
        pltpu.VMEM((2, span + 8, width), f32),
        pltpu.VMEM((window, 2 * LANES), f32),
        pltpu.VMEM((window, 2 * LANES), f32),
        pltpu.VMEM((ctx_count, rim, 2 * LANES), f32),
    ]
    own_shapes = [(2 * span, 2 * LANES), (2 * span + 8, 2 * LANES)]
    d_q_main, own_near, own_far, *sent = pl.pallas_call(
        functools.partial(grads_kernel, ctx_count, direct),
        out_shape=[jax.ShapeDtypeStruct(q_pre.shape, f32)]
        + [jax.ShapeDtypeStruct(shape, f32) for shape in own_shapes]
        + [jax.ShapeDtypeStruct(shape, bf16) for shape in near_shapes + far_shapes],
        in_specs=[smem] + [vmem] * (3 + len(received)),
        out_specs=[vmem] * (3 + len(near_shapes) + len(far_shapes)),
        scratch_shapes=scratch,
        compiler_params=pltpu.CompilerParams(vmem_limit_bytes=(24 if direct else 60) * MIB),
        name="grads",
    )(doc_lengths, filters, q_pre, d_out, *received)
    far_terms = delivered(sent[len(near_shapes) :])
    merged, half_sums = pl.pallas_call(
        functools.partial(merge_kernel, group, direct),
        grid=(1,),
        out_shape=[
            jax.ShapeDtypeStruct((2 * span + 32, 2 * LANES), bf16),
            jax.ShapeDtypeStruct((8, 2 * LANES), f32),
        ],
        in_specs=[whole(array.shape) for array in [own_far] + far_terms],
        out_specs=[whole((2 * span + 32, 2 * LANES)), whole((8, 2 * LANES))],
        scratch_shapes=[pltpu.VMEM((group, 8, 2 * LANES), f32)],
        compiler_params=pltpu.CompilerParams(vmem_limit_bytes=(16 if direct else 40) * MIB),
        name="merge",
    )(own_far, *far_terms)
    from_half = flipped(merged, group)
    near_terms = delivered(sent[: len(near_shapes)])
    terms = [own_near, half_sums, from_half] + near_terms

    last_rows = pl.BlockSpec((2, 8, width), lambda i: (0, span // 8 - 1, 0))
    d_q_pre, d_k_pre, d_v_pre, sums = pl.pallas_call(
        functools.partial(finish_kernel, ctx_count, direct),
        grid=(1,),
        out_shape=(
            jax.ShapeDtypeStruct(q_pre.shape, f32),
            jax.ShapeDtypeStruct(k_pre.shape, f32),
            jax.ShapeDtypeStruct(k_pre.shape, f32),
            jax.ShapeDtypeStruct(filters.shape, f32),
        ),
        in_specs=[smem, whole(filters.shape), last_rows]
        + [whole(array.shape) for array in terms],
        out_specs=(last_rows, whole(k_pre.shape), whole(k_pre.shape), whole(filters.shape)),
        scratch_shapes=[pltpu.VMEM((ctx_count, rim // 2, 2 * LANES), f32)],
        input_output_aliases={2: 0},
        compiler_params=pltpu.CompilerParams(vmem_limit_bytes=(16 if direct else 40) * MIB),
        name="finish",
    )(doc_lengths, filters, d_q_main, *terms)

    count = lax.axis_size("tp")
    level = [sums] + [
        lax.ppermute(sums, "tp", [(i, i ^ flip) for i in range(count)]) for flip in range(1, count)
    ]
    while len(level) > 1:
        level = [level[at] + level[at + 1] for at in range(0, len(level), 2)]
    d_filters = level[0]
    return (d_q_pre, d_k_pre, d_v_pre, d_filters)


def solution(mesh):
    split = P(None, "ctx", "tp")
    return jax.shard_map(
        shards,
        mesh=mesh,
        in_specs=(split, split, split, split, P(), P()),
        out_specs=(split, split, split, P()),
        check_vma=False,
    )
```

```python
import functools

import jax
import jax.numpy as jnp
import numpy as np
from jax import lax
from jax.experimental import pallas as pl
from jax.experimental.pallas import tpu as pltpu
from jax.sharding import PartitionSpec as P

LANES = 128
NT = (((1,), (1,)), ((), ()))
NN = (((1,), (0,)), ((), ()))
TN = (((0,), (0,)), ((), ()))
TAIL = 16
MAX_CHUNK = 640
MAX_DIRECT = 4
MIB = 1 << 20


def loop(count, body, init, unrolled=16):
    if count <= unrolled:
        for step in range(count):
            init = body(step, init)
        return init
    return lax.fori_loop(0, count, body, init)


def aligned(start, multiple):
    return start if isinstance(start, int) else pl.multiple_of(start, multiple)


def doc_starts(lengths_ref):
    starts = [jnp.int32(0)]
    for index in range(lengths_ref.shape[0] - 1):
        starts.append(starts[-1] + lengths_ref[index])
    return starts


def fold_rows(terms):
    rows, lanes = terms.shape
    return jnp.sum(terms.reshape(rows // 8, 8, lanes), axis=0)


def split_bits(values):
    high = values.astype(jnp.bfloat16)
    low = (values - high.astype(jnp.float32)).astype(jnp.bfloat16)
    return high, low


def joined(pair):
    rows = pair.shape[0] // 2
    pair = pair.astype(jnp.float32)
    return pair[:rows] + pair[rows:]


class Slots:
    def __init__(self, refs, me):
        self.refs, self.me = refs, me

    def __getitem__(self, flip):
        if len(self.refs) == 1:
            place = lax.rem(self.me, jnp.int32(self.refs[0].shape[0]))
            return self.refs[0].at[partner(place, flip)]
        return self.refs[flip]


def partner(me, flip):
    return lax.bitwise_xor(me, jnp.int32(flip))


def pack_kernel(k_ref, v_ref, q_ref, out_ref):
    span = k_ref.shape[1]
    kv = jnp.concatenate([k_ref[...], v_ref[...]], axis=2).reshape(2 * span, 2 * LANES)
    tails = []
    for half in range(2):
        last = q_ref[half].astype(jnp.float32)[TAIL - 2 :]
        tails += [last[:, at : at + 2 * LANES] for at in range(0, last.shape[1], 2 * LANES)]
    out_ref[: 2 * span] = kv
    out_ref[2 * span :] = jnp.concatenate(tails, axis=0).astype(jnp.bfloat16)


def grads_kernel(ctx_count, direct, lengths_ref, filters_ref, q_hbm, d_out_hbm, *refs):
    group = ctx_count // 2
    arrays = group if direct else 1
    near_in, far_in, refs = refs[:arrays], refs[arrays : 2 * arrays], refs[2 * arrays :]
    dq_hbm, own_near_ref, own_far_ref = refs[:3]
    arrays = group - 1 if direct else 1
    near_out, far_out = refs[3 : 3 + arrays], refs[3 + arrays : 3 + 2 * arrays]
    same_scr, kv_scr, conv_scr, dkv_scr, q_scr, qc_scr, do_scr, dq_scr = refs[3 + 2 * arrays :][:8]
    s_scr, dp_scr, rim_scr, q_ref, d_out_ref, dq_ref, sems = refs[3 + 2 * arrays :][8:]
    f32, bf16 = jnp.float32, jnp.bfloat16
    loads = [
        pltpu.make_async_copy(q_hbm, q_ref, sems.at[0]),
        pltpu.make_async_copy(d_out_hbm, d_out_ref, sems.at[1]),
    ]
    for load in loads:
        load.start()
    span = q_ref.shape[1]
    heads = q_ref.shape[2] // LANES
    half_rows = span * ctx_count
    length = 2 * half_rows
    blocks = 2 * ctx_count
    me = lax.axis_index("ctx")
    near_in, far_in = Slots(near_in, me), Slots(far_in, me)
    near_out = Slots((own_near_ref,) + near_out if direct else near_out, me)
    far_out = Slots((own_far_ref,) + far_out if direct else far_out, me)
    scale = LANES**-0.5
    log2_scale = scale * 1.4426950408889634
    starts = doc_starts(lengths_ref)

    def fill_same(index, carry):
        place = index * span + lax.broadcasted_iota(jnp.int32, (span, LANES), 0)
        cut = place == starts[0]
        for start in starts[1:]:
            cut = cut | (place == start)
        same_scr[pl.ds(aligned(8 + index * span, 8), span)] = jnp.where(cut, 0.0, 1.0)
        return carry

    same_scr[:8] = jnp.zeros((8, LANES), f32)
    same_scr[8 + length :] = jnp.zeros((8, LANES), f32)
    loop(blocks, fill_same, 0)

    kv_scr[:8] = jnp.zeros((8, 2 * LANES), f32)
    kv_scr[8 + length :] = jnp.zeros((8, 2 * LANES), f32)

    def place_blocks(flip, carry):
        for message, index in (
            (near_in[flip], partner(me, flip)),
            (far_in[flip], partner(me, flip + group)),
        ):
            early = aligned(8 + index * span, 8)
            late = aligned(8 + (blocks - 1 - index) * span, 8)
            kv_scr[pl.ds(early, span)] = message[:span].astype(f32)
            kv_scr[pl.ds(late, span)] = message[span : 2 * span].astype(f32)
            rim_scr[index] = message[2 * span :].astype(f32)
        return carry

    loop(group, place_blocks, 0)

    def kv_taps(tap):
        return jnp.concatenate([filters_ref[1, tap : tap + 1], filters_ref[2, tap : tap + 1]], axis=1)

    def twice(mask):
        return jnp.concatenate([mask, mask], axis=1)

    def back_masks(same, first):
        one = same[first : first + span]
        return one, one * same[first - 1 : first - 1 + span]

    def convolve_kv(index, carry):
        rows = pl.ds(aligned(index * span, 8), span + 8)
        values = kv_scr[rows]
        one, two = back_masks(same_scr[rows], 8)
        total = kv_taps(0) * values[8:]
        total = total + twice(one) * (kv_taps(1) * values[7 : 7 + span])
        total = total + twice(two) * (kv_taps(2) * values[6 : 6 + span])
        conv_scr[pl.ds(aligned(index * span, 16), span)] = total.astype(bf16)
        return carry

    loop(blocks, convolve_kv, 0)

    middle = me == ctx_count - 1
    rim_rows = rim_scr.shape[1] // 2
    rim_before = rim_scr[jnp.maximum(me - 1, 0)]
    rim_after = rim_scr[jnp.minimum(me + 1, ctx_count - 1)]
    late_rim = jnp.where(middle, rim_after[:rim_rows], rim_after[rim_rows:])
    rims = [rim_before[:rim_rows], late_rim]
    first_place = [me * span, (blocks - 1 - me) * span]

    for load in loads:
        load.wait()
    for half in range(2):
        rows = [rims[half][2 * at : 2 * at + 2] for at in range(rim_rows // 2)]
        q_scr[half, 6:8] = jnp.concatenate(rows, axis=1)
        q_scr[half, 8:] = q_ref[half].astype(f32)
        same = same_scr[pl.ds(aligned(first_place[half], 8), span + 16)]
        one, two = back_masks(same, 8)
        for head in range(heads):
            lanes = slice(head * LANES, (head + 1) * LANES)
            total = filters_ref[0, 0:1] * q_scr[half, 8:, lanes]
            total = total + one * (filters_ref[0, 1:2] * q_scr[half, 7 : 7 + span, lanes])
            total = total + two * (filters_ref[0, 2:3] * q_scr[half, 6 : 6 + span, lanes])
            qc_scr[half, head * span : (head + 1) * span] = total.astype(bf16)
            do_scr[half, head * span : (head + 1) * span] = d_out_ref[half, :, lanes]

    def attend(half, window, first_key, add):
        chunks = 1
        while window // chunks > MAX_CHUNK or window % (16 * chunks):
            chunks += 1
        size = window // chunks
        query = first_place[half] + lax.rem(
            lax.broadcasted_iota(jnp.int32, (1, LANES), 1), jnp.int32(span)
        )
        lowest = jnp.zeros((1, LANES), jnp.int32)
        for start in starts[1:]:
            lowest = jnp.where(query >= start, start, lowest)
        wide = 2 * LANES
        whole_window = pl.ds(aligned(first_key, 16), window)
        keys_t = conv_scr[whole_window, :LANES].T if chunks == 1 else None
        for at in range(heads * span // wide):
            slot = (half * (heads * span // wide) + at) % s_scr.shape[0]
            cols = slice(at * wide, (at + 1) * wide)
            queries = qc_scr[half, cols]
            grads = do_scr[half, cols]

            def key_rows(step):
                return pl.ds(aligned(first_key + step * size, 16), size)

            def score(step, top):
                places = first_key + step * size + lax.broadcasted_iota(jnp.int32, (size, LANES), 0)
                allowed = (places >= lowest) & (places <= query)
                bias = jnp.where(allowed, 0.0, -1e30)
                keys = conv_scr[key_rows(step), :LANES]
                scores = lax.dot_general(keys, queries, NT, preferred_element_type=f32)
                scores = scores + twice(bias)
                s_scr[slot, pl.ds(aligned(step * size, 16), size)] = scores
                return jnp.maximum(top, jnp.max(scores, axis=0, keepdims=True))

            top = loop(chunks, score, jnp.full((1, wide), -1e30, f32), 1)

            def weigh(step, carry):
                total, weighted = carry
                rows = pl.ds(aligned(step * size, 16), size)
                weights = jnp.exp2((s_scr[slot, rows] - top) * log2_scale)
                values = conv_scr[key_rows(step), LANES:]
                prob_grads = lax.dot_general(values, grads, NT, preferred_element_type=f32)
                s_scr[slot, rows] = weights
                dp_scr[slot, rows] = prob_grads
                total = total + jnp.sum(weights, axis=0, keepdims=True)
                weighted = weighted + jnp.sum(weights * prob_grads, axis=0, keepdims=True)
                return total, weighted

            zeros = jnp.zeros((1, wide), f32)
            total, weighted = loop(chunks, weigh, (zeros, zeros), 1)
            inverse = 1.0 / total
            mean = weighted * inverse
            slope = inverse * scale

            def accumulate(step, dq):
                rows = pl.ds(aligned(step * size, 16), size)
                weights = s_scr[slot, rows]
                probs = (weights * inverse).astype(bf16)
                score_grads = (weights * slope * (dp_scr[slot, rows] - mean)).astype(bf16)
                dk = lax.dot_general(score_grads, queries, NN, preferred_element_type=f32)
                dv = lax.dot_general(probs, grads, NN, preferred_element_type=f32)
                terms = jnp.concatenate([dk, dv], axis=1)
                target = pl.ds(aligned(first_key + step * size, 16), size)
                if add or at:
                    dkv_scr[target] += terms
                else:
                    dkv_scr[target] = terms
                if keys_t is not None:
                    return lax.dot_general(keys_t, score_grads, NN, preferred_element_type=f32)
                keys = conv_scr[key_rows(step), :LANES]
                return dq + lax.dot_general(keys, score_grads, TN, preferred_element_type=f32)

            dq = loop(chunks, accumulate, jnp.zeros((LANES, wide), f32), 1)
            dq = dq.T
            for part in range(wide // span):
                head = at * (wide // span) + part
                dq_scr[half, :span, head * LANES : (head + 1) * LANES] = dq[
                    part * span : (part + 1) * span
                ]

    dkv_scr[half_rows:] = jnp.zeros((half_rows + 8, 2 * LANES), f32)
    attend(0, half_rows, 0, False)
    attend(1, half_rows + span, (ctx_count - 1 - me) * span, True)

    next_rows = jnp.where(middle, dq_scr[1, :8], 0.0)
    dq_scr[0, span:] = next_rows
    dq_scr[1, span:] = jnp.zeros_like(next_rows)
    sums = [jnp.zeros((8, LANES), f32) for _ in range(3)]
    for half in range(2):
        same = same_scr[pl.ds(aligned(first_place[half], 8), span + 16)]
        one, two = back_masks(same, 8)
        ahead_one = same[9 : 9 + span]
        ahead_two = same[10 : 10 + span] * ahead_one
        for head in range(heads):
            lanes = slice(head * LANES, (head + 1) * LANES)
            grads = dq_scr[half, :span, lanes]
            out = filters_ref[0, 0:1] * grads
            out = out + ahead_one * (filters_ref[0, 1:2] * dq_scr[half, 1 : 1 + span, lanes])
            out = out + ahead_two * (filters_ref[0, 2:3] * dq_scr[half, 2 : 2 + span, lanes])
            dq_ref[half, :, lanes] = out
            sums[0] += fold_rows(grads * q_scr[half, 8:, lanes])
            sums[1] += fold_rows(grads * one * q_scr[half, 7 : 7 + span, lanes])
            sums[2] += fold_rows(grads * two * q_scr[half, 6 : 6 + span, lanes])
    q_sums = [jnp.sum(term, axis=0, keepdims=True) for term in sums]
    store = pltpu.make_async_copy(dq_ref, dq_hbm, sems.at[2])
    store.start()

    def finish_block(index, carry):
        base = aligned(index * span, 8)
        grads = dkv_scr[pl.ds(base, span + 8)]
        values = kv_scr[pl.ds(base, span + 8)]
        same = same_scr[pl.ds(base, span + 16)]
        one, two = back_masks(same, 8)
        ahead_one = same[9 : 9 + span]
        ahead_two = same[10 : 10 + span] * ahead_one
        out = kv_taps(0) * grads[:span]
        out = out + twice(ahead_one) * (kv_taps(1) * grads[1 : 1 + span])
        out = out + twice(ahead_two) * (kv_taps(2) * grads[2 : 2 + span])
        own = grads[:span]
        return out, (
            carry[0] + fold_rows(own * values[8:]),
            carry[1] + fold_rows(own * twice(one) * values[7 : 7 + span]),
            carry[2] + fold_rows(own * twice(two) * values[6 : 6 + span]),
        )

    def finish_pair(index, carry):
        early, carry = finish_block(index, carry)
        late, carry = finish_block(blocks - 1 - index, carry)
        return jnp.concatenate([early, late], axis=0), carry

    def finish(flip, carry):
        terms, carry = finish_pair(partner(me, flip + group), carry)
        far_out[flip][: 2 * span] = terms.astype(bf16)
        terms, carry = finish_pair(partner(me, flip), carry)
        near_out[flip][: 2 * span] = terms.astype(bf16)
        return carry

    zeros = jnp.zeros((8, 2 * LANES), f32)
    own_far_ref[: 2 * span], kv_sums = finish_pair(partner(me, group), (zeros, zeros, zeros))
    own_near_ref[...], kv_sums = finish_pair(me, kv_sums)
    kv_sums = loop(group - 1, lambda step, carry: finish(step + 1, carry), kv_sums)
    kv_sums = [jnp.sum(term, axis=0, keepdims=True) for term in kv_sums]

    sums_tile = jnp.concatenate(
        [jnp.concatenate([term, jnp.zeros_like(term)], axis=1) for term in q_sums]
        + kv_sums
        + [jnp.zeros((2, 2 * LANES), f32)],
        axis=0,
    )
    sums_pair = jnp.concatenate(split_bits(sums_tile), axis=0)
    own_far_ref[2 * span :] = joined(sums_pair)
    rims = []
    for half in range(2):
        rows = dq_scr[half, :2]
        rows = [rows[:, at : at + 2 * LANES] for at in range(0, rows.shape[1], 2 * LANES)]
        rims.append(jnp.concatenate(rows, axis=0))

    def rim_for(index):
        return jnp.concatenate(split_bits(jnp.where(index < me, rims[0], rims[1])), axis=0)

    def store_rims(step, carry):
        flip = step + 1
        far_out[flip][2 * span : 2 * span + 16] = sums_pair
        if not direct or flip == group - 1:
            far_out[flip][2 * span + 16 :] = rim_for(partner(me, flip + group))
        if not direct or flip & (flip + 1) == 0:
            near_out[flip][2 * span :] = rim_for(partner(me, flip))
        return carry

    loop(group - 1, store_rims, 0, 16 if direct else 1)
    store.wait()


def merge_kernel(group, direct, own_ref, *refs):
    received_refs, (out_ref, half_sums_ref, sums_scr) = refs[:-3], refs[-3:]
    f32, bf16 = jnp.float32, jnp.bfloat16
    me = lax.axis_index("ctx")
    received = Slots((own_ref,) + received_refs if direct else received_refs, me)
    place = lax.rem(me, jnp.int32(group))
    rows = own_ref.shape[0] - 8
    sums_scr[place] = own_ref[rows:]

    def add(step, carry):
        message = received[step + 1]
        sums_scr[partner(place, step + 1)] = joined(message[rows : rows + 16])
        return carry + message[:rows].astype(f32)

    out_ref[:rows] = loop(group - 1, add, own_ref[:rows]).astype(bf16)
    sums = loop(group, lambda index, carry: carry + sums_scr[index], jnp.zeros((8, 2 * LANES), f32))
    pair = jnp.concatenate(split_bits(sums), axis=0)
    half_sums_ref[...] = joined(pair)
    out_ref[rows : rows + 16] = pair
    out_ref[rows + 16 :] = received[group - 1][rows + 16 :]


def sums_kernel(span, half_sums_ref, far_ref, out_ref):
    sums = half_sums_ref[...] + joined(far_ref[2 * span : 2 * span + 16])
    out_ref[0] = sums[0:3, :LANES]
    out_ref[1] = sums[3:6, :LANES]
    out_ref[2] = sums[3:6, LANES:]


def finish_kernel(
    ctx_count, direct, lengths_ref, filters_ref, dq_in_ref, own_ref, far_ref, *refs
):
    near_refs, (dq_ref, dk_ref, dv_ref, rim_scr) = refs[:-4], refs[-4:]
    f32 = jnp.float32
    group = ctx_count // 2
    span = dk_ref.shape[1]
    me = lax.axis_index("ctx")
    near = Slots((own_ref,) + near_refs if direct else near_refs, me)
    starts = doc_starts(lengths_ref)
    blocks = 2 * ctx_count

    rim_scr[me] = jnp.zeros(rim_scr.shape[1:], f32)
    rim_scr[partner(me, ctx_count - 1)] = joined(far_ref[2 * span + 16 :])

    def add(step, carry):
        flip = step + 1
        message = near[flip]
        if not direct or flip & (flip + 1) == 0:
            rim_scr[partner(me, flip)] = joined(message[2 * span :])
        return carry + message[: 2 * span].astype(f32)

    total = own_ref[...] + far_ref[: 2 * span].astype(f32)
    total = loop(group - 1, add, total, 16 if direct else 1)
    for half in range(2):
        dk_ref[half] = total[half * span : (half + 1) * span, :LANES]
        dv_ref[half] = total[half * span : (half + 1) * span, LANES:]

    def same(place):
        cut = place >= blocks * span
        for start in starts:
            cut = cut | (place == start)
        return jnp.where(cut, 0.0, 1.0).astype(f32)

    heads = dq_ref.shape[2] // LANES
    taps = [jnp.concatenate([filters_ref[0, tap : tap + 1]] * heads, axis=1) for tap in range(3)]
    row = lax.broadcasted_iota(jnp.int32, dq_ref.shape[1:], 0)
    sources = [jnp.minimum(me + 1, ctx_count - 1), jnp.maximum(me - 1, 0)]
    first_place = [me * span, (blocks - 1 - me) * span]
    present = [me < ctx_count - 1, me > 0]
    for half in range(2):
        rim = rim_scr[sources[half]]
        rows = jnp.concatenate([rim[2 * at : 2 * at + 2] for at in range(rim.shape[0] // 2)], axis=1)
        end = first_place[half] + span
        zero, one, two = same(end - 1), same(end), same(end + 1)
        one = jnp.where(present[half], one, 0.0)
        last_but_one = (zero * one) * (taps[2] * rows[0:1])
        last = one * (taps[1] * rows[0:1]) + (one * two) * (taps[2] * rows[1:2])
        extra = jnp.where(row == 6, last_but_one, jnp.where(row == 7, last, 0.0))
        dq_ref[half] = dq_in_ref[half] + extra


def shards(q_pre, k_pre, value_before_filter, d_out, filters, doc_lengths):
    f32, bf16 = jnp.float32, jnp.bfloat16
    ctx_count = lax.axis_size("ctx")
    span, width = q_pre.shape[1:]
    length = 2 * span * ctx_count
    rim = 4 * width // (2 * LANES)
    vmem = pl.BlockSpec(memory_space=pltpu.VMEM)
    smem = pl.BlockSpec(memory_space=pltpu.SMEM)
    hbm = pl.BlockSpec(memory_space=pltpu.HBM)

    group = ctx_count // 2
    direct = group <= MAX_DIRECT
    halves = [[half * group + at for at in range(group)] for half in range(2)]
    msg_rows = 2 * span + rim

    def whole(shape):
        return pl.BlockSpec(shape, lambda i: (0,) * len(shape))

    def flipped(array, flip):
        return lax.ppermute(array, "ctx", [(i, i ^ flip) for i in range(ctx_count)])

    def gathered(array):
        if direct:
            return [array] + [flipped(array, flip) for flip in range(1, group)]
        return [lax.all_gather(array, "ctx", axis_index_groups=halves)]

    def delivered(arrays):
        if direct:
            return [flipped(array, step + 1) for step, array in enumerate(arrays)]
        return [lax.all_to_all(arrays[0], "ctx", 0, 0, axis_index_groups=halves, tiled=True)]

    packed = pl.pallas_call(
        pack_kernel,
        grid=(1,),
        out_shape=jax.ShapeDtypeStruct((msg_rows, 2 * LANES), bf16),
        in_specs=[
            whole(k_pre.shape),
            whole(k_pre.shape),
            pl.BlockSpec((2, TAIL, width), lambda i: (0, span // TAIL - 1, 0)),
        ],
        out_specs=whole((msg_rows, 2 * LANES)),
        name="pack",
    )(k_pre, value_before_filter, q_pre)
    across = flipped(packed, group)
    received = gathered(packed) + gathered(across)

    window = span * ctx_count + span
    if direct:
        flips = range(1, group)
        near_shapes = [(2 * span + (16 if flip & (flip + 1) == 0 else 0), 2 * LANES) for flip in flips]
        far_shapes = [(2 * span + (32 if flip == group - 1 else 16), 2 * LANES) for flip in flips]
    else:
        near_shapes = [(group, 2 * span + 16, 2 * LANES)]
        far_shapes = [(group, 2 * span + 32, 2 * LANES)]
    scratch = [
        pltpu.VMEM((length + 16, LANES), f32),
        pltpu.VMEM((length + 16, 2 * LANES), f32),
        pltpu.VMEM((length, 2 * LANES), bf16),
        pltpu.VMEM((length + 8, 2 * LANES), f32),
        pltpu.VMEM((2, span + 8, width), f32),
        pltpu.VMEM((2, span * width // LANES, LANES), bf16),
        pltpu.VMEM((2, span * width // LANES, LANES), bf16),
        pltpu.VMEM((2, span + 8, width), f32),
        pltpu.VMEM((4 if direct else 1, window, 2 * LANES), f32),
        pltpu.VMEM((4 if direct else 1, window, 2 * LANES), f32),
        pltpu.VMEM((ctx_count, rim, 2 * LANES), f32),
        pltpu.VMEM(q_pre.shape, bf16),
        pltpu.VMEM(q_pre.shape, bf16),
        pltpu.VMEM(q_pre.shape, f32),
        pltpu.SemaphoreType.DMA((3,)),
    ]
    own_shapes = [(2 * span, 2 * LANES), (2 * span + 8, 2 * LANES)]
    d_q_main, own_near, own_far, *sent = pl.pallas_call(
        functools.partial(grads_kernel, ctx_count, direct),
        out_shape=[jax.ShapeDtypeStruct(q_pre.shape, f32)]
        + [jax.ShapeDtypeStruct(shape, f32) for shape in own_shapes]
        + [jax.ShapeDtypeStruct(shape, bf16) for shape in near_shapes + far_shapes],
        in_specs=[smem, vmem, hbm, hbm] + [vmem] * len(received),
        out_specs=[hbm] + [vmem] * (2 + len(near_shapes) + len(far_shapes)),
        scratch_shapes=scratch,
        compiler_params=pltpu.CompilerParams(vmem_limit_bytes=(32 if direct else 62) * MIB),
        name="grads",
    )(doc_lengths, filters, q_pre, d_out, *received)
    far_terms = delivered(sent[len(near_shapes) :])
    merged, half_sums = pl.pallas_call(
        functools.partial(merge_kernel, group, direct),
        grid=(1,),
        out_shape=[
            jax.ShapeDtypeStruct((2 * span + 32, 2 * LANES), bf16),
            jax.ShapeDtypeStruct((8, 2 * LANES), f32),
        ],
        in_specs=[whole(array.shape) for array in [own_far] + far_terms],
        out_specs=[whole((2 * span + 32, 2 * LANES)), whole((8, 2 * LANES))],
        scratch_shapes=[pltpu.VMEM((group, 8, 2 * LANES), f32)],
        compiler_params=pltpu.CompilerParams(vmem_limit_bytes=(16 if direct else 40) * MIB),
        name="merge",
    )(own_far, *far_terms)
    from_half = flipped(merged, group)
    near_terms = delivered(sent[: len(near_shapes)])
    terms = [own_near, from_half] + near_terms

    sums = pl.pallas_call(
        functools.partial(sums_kernel, span),
        out_shape=jax.ShapeDtypeStruct(filters.shape, f32),
        in_specs=[vmem, vmem],
        out_specs=vmem,
        name="sums",
    )(half_sums, from_half)
    count = lax.axis_size("tp")
    level = [sums] + [
        lax.ppermute(sums, "tp", [(i, i ^ flip) for i in range(count)]) for flip in range(1, count)
    ]

    last_rows = pl.BlockSpec((2, 8, width), lambda i: (0, span // 8 - 1, 0))
    d_q_pre, d_k_pre, d_v_pre = pl.pallas_call(
        functools.partial(finish_kernel, ctx_count, direct),
        grid=(1,),
        out_shape=(
            jax.ShapeDtypeStruct(q_pre.shape, f32),
            jax.ShapeDtypeStruct(k_pre.shape, f32),
            jax.ShapeDtypeStruct(k_pre.shape, f32),
        ),
        in_specs=[smem, whole(filters.shape), last_rows]
        + [whole(array.shape) for array in terms],
        out_specs=(last_rows, whole(k_pre.shape), whole(k_pre.shape)),
        scratch_shapes=[pltpu.VMEM((ctx_count, rim // 2, 2 * LANES), f32)],
        input_output_aliases={2: 0},
        compiler_params=pltpu.CompilerParams(vmem_limit_bytes=(16 if direct else 40) * MIB),
        name="finish",
    )(doc_lengths, filters, d_q_main, *terms)

    while len(level) > 1:
        level = [level[at] + level[at + 1] for at in range(0, len(level), 2)]
    d_filters = level[0]
    return (d_q_pre, d_k_pre, d_v_pre, d_filters)


def solution(mesh):
    split = P(None, "ctx", "tp")
    return jax.shard_map(
        shards,
        mesh=mesh,
        in_specs=(split, split, split, split, P(), P()),
        out_specs=(split, split, split, P()),
        check_vma=False,
    )
```

```python
import functools

import jax
import jax.numpy as jnp
import numpy as np
from jax import lax
from jax.experimental import pallas as pl
from jax.experimental.pallas import tpu as pltpu
from jax.sharding import PartitionSpec as P

LANES = 128
NT = (((1,), (1,)), ((), ()))
NN = (((1,), (0,)), ((), ()))
TN = (((0,), (0,)), ((), ()))
TAIL = 16
MAX_CHUNK = 640
MAX_DIRECT = 4
MIB = 1 << 20


def loop(count, body, init, unrolled=16):
    if count <= unrolled:
        for step in range(count):
            init = body(step, init)
        return init
    return lax.fori_loop(0, count, body, init)


def aligned(start, multiple):
    return start if isinstance(start, int) else pl.multiple_of(start, multiple)


def doc_starts(lengths_ref):
    starts = [jnp.int32(0)]
    for index in range(lengths_ref.shape[0] - 1):
        starts.append(starts[-1] + lengths_ref[index])
    return starts


def fold_rows(terms):
    rows, lanes = terms.shape
    return jnp.sum(terms.reshape(rows // 8, 8, lanes), axis=0)


def split_bits(values):
    high = values.astype(jnp.bfloat16)
    low = (values - high.astype(jnp.float32)).astype(jnp.bfloat16)
    return high, low


def joined(pair):
    rows = pair.shape[0] // 2
    pair = pair.astype(jnp.float32)
    return pair[:rows] + pair[rows:]


class Slots:
    def __init__(self, refs, me):
        self.refs, self.me = refs, me

    def __getitem__(self, flip):
        if len(self.refs) == 1:
            place = lax.rem(self.me, jnp.int32(self.refs[0].shape[0]))
            return self.refs[0].at[partner(place, flip)]
        return self.refs[flip]


def partner(me, flip):
    return lax.bitwise_xor(me, jnp.int32(flip))


def pack_kernel(k_ref, v_ref, q_ref, out_ref):
    span = k_ref.shape[1]
    kv = jnp.concatenate([k_ref[...], v_ref[...]], axis=2).reshape(2 * span, 2 * LANES)
    tails = []
    for half in range(2):
        last = q_ref[half].astype(jnp.float32)[TAIL - 2 :]
        tails += [last[:, at : at + 2 * LANES] for at in range(0, last.shape[1], 2 * LANES)]
    out_ref[: 2 * span] = kv
    out_ref[2 * span :] = jnp.concatenate(tails, axis=0).astype(jnp.bfloat16)


def grads_kernel(ctx_count, direct, lengths_ref, filters_ref, q_hbm, d_out_hbm, *refs):
    group = ctx_count // 2
    arrays = group if direct else 1
    near_in, far_in, refs = refs[:arrays], refs[arrays : 2 * arrays], refs[2 * arrays :]
    dq_hbm, own_near_ref, own_far_ref = refs[:3]
    arrays = group - 1 if direct else 1
    out_refs, refs = refs[3 : 3 + arrays], refs[3 + arrays :]
    same_scr, kv_scr, conv_scr, dkv_scr, q_scr, qc_scr, do_scr, dq_scr = refs[:8]
    s_scr, dp_scr, rim_scr, q_ref, d_out_ref, dq_ref, sems = refs[8:]
    f32, bf16 = jnp.float32, jnp.bfloat16
    loads = [
        pltpu.make_async_copy(q_hbm, q_ref, sems.at[0]),
        pltpu.make_async_copy(d_out_hbm, d_out_ref, sems.at[1]),
    ]
    for load in loads:
        load.start()
    span = q_ref.shape[1]
    heads = q_ref.shape[2] // LANES
    half_rows = span * ctx_count
    length = 2 * half_rows
    blocks = 2 * ctx_count
    me = lax.axis_index("ctx")
    near_in, far_in = Slots(near_in, me), Slots(far_in, me)
    sent = Slots((own_far_ref,) + out_refs if direct else out_refs, me)
    scale = LANES**-0.5
    log2_scale = scale * 1.4426950408889634
    starts = doc_starts(lengths_ref)

    def fill_same(index, carry):
        place = index * span + lax.broadcasted_iota(jnp.int32, (span, LANES), 0)
        cut = place == starts[0]
        for start in starts[1:]:
            cut = cut | (place == start)
        same_scr[pl.ds(aligned(8 + index * span, 8), span)] = jnp.where(cut, 0.0, 1.0)
        return carry

    same_scr[:8] = jnp.zeros((8, LANES), f32)
    same_scr[8 + length :] = jnp.zeros((8, LANES), f32)
    loop(blocks, fill_same, 0)

    kv_scr[:8] = jnp.zeros((8, 2 * LANES), f32)
    kv_scr[8 + length :] = jnp.zeros((8, 2 * LANES), f32)

    def place_blocks(flip, carry):
        for message, index in (
            (near_in[flip], partner(me, flip)),
            (far_in[flip], partner(me, flip + group)),
        ):
            early = aligned(8 + index * span, 8)
            late = aligned(8 + (blocks - 1 - index) * span, 8)
            kv_scr[pl.ds(early, span)] = message[:span].astype(f32)
            kv_scr[pl.ds(late, span)] = message[span : 2 * span].astype(f32)
            rim_scr[index] = message[2 * span :].astype(f32)
        return carry

    loop(group, place_blocks, 0)

    def kv_taps(tap):
        return jnp.concatenate([filters_ref[1, tap : tap + 1], filters_ref[2, tap : tap + 1]], axis=1)

    def twice(mask):
        return jnp.concatenate([mask, mask], axis=1)

    def back_masks(same, first):
        one = same[first : first + span]
        return one, one * same[first - 1 : first - 1 + span]

    def convolve_kv(index, carry):
        rows = pl.ds(aligned(index * span, 8), span + 8)
        values = kv_scr[rows]
        one, two = back_masks(same_scr[rows], 8)
        total = kv_taps(0) * values[8:]
        total = total + twice(one) * (kv_taps(1) * values[7 : 7 + span])
        total = total + twice(two) * (kv_taps(2) * values[6 : 6 + span])
        conv_scr[pl.ds(aligned(index * span, 16), span)] = total.astype(bf16)
        return carry

    loop(blocks, convolve_kv, 0)

    middle = me == ctx_count - 1
    rim_rows = rim_scr.shape[1] // 2
    rim_before = rim_scr[jnp.maximum(me - 1, 0)]
    rim_after = rim_scr[jnp.minimum(me + 1, ctx_count - 1)]
    late_rim = jnp.where(middle, rim_after[:rim_rows], rim_after[rim_rows:])
    rims = [rim_before[:rim_rows], late_rim]
    first_place = [me * span, (blocks - 1 - me) * span]

    for load in loads:
        load.wait()
    for half in range(2):
        rows = [rims[half][2 * at : 2 * at + 2] for at in range(rim_rows // 2)]
        q_scr[half, 6:8] = jnp.concatenate(rows, axis=1)
        q_scr[half, 8:] = q_ref[half].astype(f32)
        same = same_scr[pl.ds(aligned(first_place[half], 8), span + 16)]
        one, two = back_masks(same, 8)
        for head in range(heads):
            lanes = slice(head * LANES, (head + 1) * LANES)
            total = filters_ref[0, 0:1] * q_scr[half, 8:, lanes]
            total = total + one * (filters_ref[0, 1:2] * q_scr[half, 7 : 7 + span, lanes])
            total = total + two * (filters_ref[0, 2:3] * q_scr[half, 6 : 6 + span, lanes])
            qc_scr[half, head * span : (head + 1) * span] = total.astype(bf16)
            do_scr[half, head * span : (head + 1) * span] = d_out_ref[half, :, lanes]

    def attend(half, window, first_key, add):
        chunks = 1
        while window // chunks > MAX_CHUNK or window % (16 * chunks):
            chunks += 1
        size = window // chunks
        query = first_place[half] + lax.rem(
            lax.broadcasted_iota(jnp.int32, (1, LANES), 1), jnp.int32(span)
        )
        lowest = jnp.zeros((1, LANES), jnp.int32)
        for start in starts[1:]:
            lowest = jnp.where(query >= start, start, lowest)
        wide = 2 * LANES
        whole_window = pl.ds(aligned(first_key, 16), window)
        keys_t = conv_scr[whole_window, :LANES].T if chunks == 1 else None
        for at in range(heads * span // wide):
            slot = (half * (heads * span // wide) + at) % s_scr.shape[0]
            cols = slice(at * wide, (at + 1) * wide)
            queries = qc_scr[half, cols]
            grads = do_scr[half, cols]

            def key_rows(step):
                return pl.ds(aligned(first_key + step * size, 16), size)

            def score(step, top):
                places = first_key + step * size + lax.broadcasted_iota(jnp.int32, (size, LANES), 0)
                allowed = (places >= lowest) & (places <= query)
                bias = jnp.where(allowed, 0.0, -1e30)
                keys = conv_scr[key_rows(step), :LANES]
                scores = lax.dot_general(keys, queries, NT, preferred_element_type=f32)
                scores = scores + twice(bias)
                s_scr[slot, pl.ds(aligned(step * size, 16), size)] = scores
                return jnp.maximum(top, jnp.max(scores, axis=0, keepdims=True))

            top = loop(chunks, score, jnp.full((1, wide), -1e30, f32), 1)

            def weigh(step, carry):
                total, weighted = carry
                rows = pl.ds(aligned(step * size, 16), size)
                weights = jnp.exp2((s_scr[slot, rows] - top) * log2_scale)
                values = conv_scr[key_rows(step), LANES:]
                prob_grads = lax.dot_general(values, grads, NT, preferred_element_type=f32)
                s_scr[slot, rows] = weights
                dp_scr[slot, rows] = prob_grads
                total = total + jnp.sum(weights, axis=0, keepdims=True)
                weighted = weighted + jnp.sum(weights * prob_grads, axis=0, keepdims=True)
                return total, weighted

            zeros = jnp.zeros((1, wide), f32)
            total, weighted = loop(chunks, weigh, (zeros, zeros), 1)
            inverse = 1.0 / total
            mean = weighted * inverse
            slope = inverse * scale

            def accumulate(step, dq):
                rows = pl.ds(aligned(step * size, 16), size)
                weights = s_scr[slot, rows]
                probs = (weights * inverse).astype(bf16)
                score_grads = (weights * slope * (dp_scr[slot, rows] - mean)).astype(bf16)
                dk = lax.dot_general(score_grads, queries, NN, preferred_element_type=f32)
                dv = lax.dot_general(probs, grads, NN, preferred_element_type=f32)
                terms = jnp.concatenate([dk, dv], axis=1)
                target = pl.ds(aligned(first_key + step * size, 16), size)
                if add or at:
                    dkv_scr[target] += terms
                else:
                    dkv_scr[target] = terms
                if keys_t is not None:
                    return lax.dot_general(keys_t, score_grads, NN, preferred_element_type=f32)
                keys = conv_scr[key_rows(step), :LANES]
                return dq + lax.dot_general(keys, score_grads, TN, preferred_element_type=f32)

            dq = loop(chunks, accumulate, jnp.zeros((LANES, wide), f32), 1)
            dq = dq.T
            for part in range(wide // span):
                head = at * (wide // span) + part
                dq_scr[half, :span, head * LANES : (head + 1) * LANES] = dq[
                    part * span : (part + 1) * span
                ]

    dkv_scr[half_rows:] = jnp.zeros((half_rows + 8, 2 * LANES), f32)
    attend(0, half_rows, 0, False)
    attend(1, half_rows + span, (ctx_count - 1 - me) * span, True)

    next_rows = jnp.where(middle, dq_scr[1, :8], 0.0)
    dq_scr[0, span:] = next_rows
    dq_scr[1, span:] = jnp.zeros_like(next_rows)
    sums = [jnp.zeros((8, LANES), f32) for _ in range(3)]
    for half in range(2):
        same = same_scr[pl.ds(aligned(first_place[half], 8), span + 16)]
        one, two = back_masks(same, 8)
        ahead_one = same[9 : 9 + span]
        ahead_two = same[10 : 10 + span] * ahead_one
        for head in range(heads):
            lanes = slice(head * LANES, (head + 1) * LANES)
            grads = dq_scr[half, :span, lanes]
            out = filters_ref[0, 0:1] * grads
            out = out + ahead_one * (filters_ref[0, 1:2] * dq_scr[half, 1 : 1 + span, lanes])
            out = out + ahead_two * (filters_ref[0, 2:3] * dq_scr[half, 2 : 2 + span, lanes])
            dq_ref[half, :, lanes] = out
            sums[0] += fold_rows(grads * q_scr[half, 8:, lanes])
            sums[1] += fold_rows(grads * one * q_scr[half, 7 : 7 + span, lanes])
            sums[2] += fold_rows(grads * two * q_scr[half, 6 : 6 + span, lanes])
    q_sums = [jnp.sum(term, axis=0, keepdims=True) for term in sums]
    store = pltpu.make_async_copy(dq_ref, dq_hbm, sems.at[2])
    store.start()

    def finish_block(index, carry):
        base = aligned(index * span, 8)
        grads = dkv_scr[pl.ds(base, span + 8)]
        values = kv_scr[pl.ds(base, span + 8)]
        same = same_scr[pl.ds(base, span + 16)]
        one, two = back_masks(same, 8)
        ahead_one = same[9 : 9 + span]
        ahead_two = same[10 : 10 + span] * ahead_one
        out = kv_taps(0) * grads[:span]
        out = out + twice(ahead_one) * (kv_taps(1) * grads[1 : 1 + span])
        out = out + twice(ahead_two) * (kv_taps(2) * grads[2 : 2 + span])
        own = grads[:span]
        return out, (
            carry[0] + fold_rows(own * values[8:]),
            carry[1] + fold_rows(own * twice(one) * values[7 : 7 + span]),
            carry[2] + fold_rows(own * twice(two) * values[6 : 6 + span]),
        )

    def finish_pair(index, carry):
        early, carry = finish_block(index, carry)
        late, carry = finish_block(blocks - 1 - index, carry)
        return jnp.concatenate([early, late], axis=0), carry

    low = me < group

    def finish(step, carry):
        flip = step + 1
        owner = partner(me, flip)
        far_owner = partner(me, flip + group)
        near_late = blocks - 1 - owner
        places = [
            far_owner,
            jnp.where(low, blocks - 1 - far_owner, owner),
            jnp.where(low & (me > owner), owner, near_late),
        ]
        for at, place in enumerate(places):
            terms, carry = finish_block(place, carry)
            sent[flip][at * span : (at + 1) * span] = terms.astype(bf16)
        return carry

    zeros = jnp.zeros((8, 2 * LANES), f32)
    own_far_ref[: 2 * span], kv_sums = finish_pair(partner(me, group), (zeros, zeros, zeros))
    own_near_ref[...], kv_sums = finish_pair(me, kv_sums)
    kv_sums = loop(group - 1, finish, kv_sums)
    kv_sums = [jnp.sum(term, axis=0, keepdims=True) for term in kv_sums]

    sums_tile = jnp.concatenate(
        [jnp.concatenate([term, jnp.zeros_like(term)], axis=1) for term in q_sums]
        + kv_sums
        + [jnp.zeros((2, 2 * LANES), f32)],
        axis=0,
    )
    sums_pair = jnp.concatenate(split_bits(sums_tile), axis=0)
    own_far_ref[2 * span :] = joined(sums_pair)
    rims = []
    for half in range(2):
        rows = dq_scr[half, :2]
        rows = [rows[:, at : at + 2 * LANES] for at in range(0, rows.shape[1], 2 * LANES)]
        rims.append(jnp.concatenate(rows, axis=0))

    def rim_for(index):
        return jnp.concatenate(split_bits(jnp.where(index < me, rims[0], rims[1])), axis=0)

    def store_rims(step, carry):
        flip = step + 1
        owner = partner(me, flip)
        sent[flip][3 * span : 3 * span + 16] = sums_pair
        if not direct or flip & (flip + 1) == 0:
            across = (flip == group - 1) & (jnp.abs(owner - me) != 1)
            target = jnp.where(across, partner(owner, group), owner)
            sent[flip][3 * span + 16 :] = rim_for(target)
        return carry

    loop(group - 1, store_rims, 0, 16 if direct else 1)
    store.wait()


def merge_kernel(ctx_count, direct, own_near_ref, own_far_ref, *refs):
    received_refs = refs[:-6]
    near_ref, far_ref, half_sums_ref, rims_ref, sums_scr, rim_scr = refs[-6:]
    f32, bf16 = jnp.float32, jnp.bfloat16
    group = ctx_count // 2
    me = lax.axis_index("ctx")
    low = me < group
    received = Slots((own_far_ref,) + received_refs if direct else received_refs, me)
    place = lax.rem(me, jnp.int32(group))
    span = own_near_ref.shape[0] // 2
    rows = 2 * span
    sums_scr[place] = own_far_ref[rows:]
    neighbours = [jnp.minimum(me + 1, ctx_count - 1), jnp.maximum(me - 1, 0)]
    for index in neighbours:
        rim_scr[index] = jnp.zeros(rim_scr.shape[1:], f32)

    def add(step, carry):
        flip = step + 1
        source = partner(me, flip)
        message = received[flip]
        parts = [message[at * span : (at + 1) * span].astype(f32) for at in range(3)]
        near_early, near_late, far_early, far_late = carry
        sums_scr[partner(place, flip)] = joined(message[3 * span : 3 * span + 16])
        if not direct or flip & (flip + 1) == 0:
            rim_scr[source] = joined(message[3 * span + 16 :])
        to_early = low & (source > me)
        zero = jnp.zeros_like(parts[0])
        return (
            near_early + jnp.where(low, jnp.where(to_early, parts[2], zero), parts[1]),
            near_late + jnp.where(to_early, zero, parts[2]),
            far_early + parts[0],
            far_late + jnp.where(low, parts[1], zero),
        )

    init = (own_near_ref[:span], own_near_ref[span:], own_far_ref[:span], own_far_ref[span:rows])
    totals = loop(group - 1, add, init, 16 if direct else 1)
    near_ref[:span] = totals[0]
    near_ref[span:] = totals[1]
    far_ref[:span] = totals[2].astype(bf16)
    far_ref[span:rows] = totals[3].astype(bf16)
    sums = loop(group, lambda index, carry: carry + sums_scr[index], jnp.zeros((8, 2 * LANES), f32))
    pair = jnp.concatenate(split_bits(sums), axis=0)
    half_sums_ref[...] = joined(pair)
    far_ref[rows : rows + 16] = pair
    far_ref[rows + 16 :] = received[group - 1][3 * span + 16 :]
    for at, index in enumerate(neighbours):
        rims_ref[at] = rim_scr[index]


def sums_kernel(span, half_sums_ref, far_ref, out_ref):
    sums = half_sums_ref[...] + joined(far_ref[2 * span : 2 * span + 16])
    out_ref[0] = sums[0:3, :LANES]
    out_ref[1] = sums[3:6, :LANES]
    out_ref[2] = sums[3:6, LANES:]


def finish_kernel(
    ctx_count, lengths_ref, filters_ref, dq_in_ref, near_ref, far_ref, rims_ref, dq_ref, dk_ref, dv_ref
):
    f32 = jnp.float32
    group = ctx_count // 2
    span = dk_ref.shape[1]
    me = lax.axis_index("ctx")
    starts = doc_starts(lengths_ref)
    blocks = 2 * ctx_count

    total = near_ref[...] + far_ref[: 2 * span].astype(f32)
    for half in range(2):
        dk_ref[half] = total[half * span : (half + 1) * span, :LANES]
        dv_ref[half] = total[half * span : (half + 1) * span, LANES:]

    def same(place):
        cut = place >= blocks * span
        for start in starts:
            cut = cut | (place == start)
        return jnp.where(cut, 0.0, 1.0).astype(f32)

    heads = dq_ref.shape[2] // LANES
    taps = [jnp.concatenate([filters_ref[0, tap : tap + 1]] * heads, axis=1) for tap in range(3)]
    row = lax.broadcasted_iota(jnp.int32, dq_ref.shape[1:], 0)
    far_rim = joined(far_ref[2 * span + 16 :])
    crosses = [me == group - 1, me == group]
    first_place = [me * span, (blocks - 1 - me) * span]
    present = [me < ctx_count - 1, me > 0]
    for half in range(2):
        rim = jnp.where(crosses[half], far_rim, rims_ref[half])
        rows = jnp.concatenate([rim[2 * at : 2 * at + 2] for at in range(rim.shape[0] // 2)], axis=1)
        end = first_place[half] + span
        zero, one, two = same(end - 1), same(end), same(end + 1)
        one = jnp.where(present[half], one, 0.0)
        last_but_one = (zero * one) * (taps[2] * rows[0:1])
        last = one * (taps[1] * rows[0:1]) + (one * two) * (taps[2] * rows[1:2])
        extra = jnp.where(row == 6, last_but_one, jnp.where(row == 7, last, 0.0))
        dq_ref[half] = dq_in_ref[half] + extra


def shards(q_pre, k_pre, value_before_filter, d_out, filters, doc_lengths):
    f32, bf16 = jnp.float32, jnp.bfloat16
    ctx_count = lax.axis_size("ctx")
    span, width = q_pre.shape[1:]
    length = 2 * span * ctx_count
    rim = 4 * width // (2 * LANES)
    vmem = pl.BlockSpec(memory_space=pltpu.VMEM)
    smem = pl.BlockSpec(memory_space=pltpu.SMEM)
    hbm = pl.BlockSpec(memory_space=pltpu.HBM)

    group = ctx_count // 2
    direct = group <= MAX_DIRECT
    halves = [[half * group + at for at in range(group)] for half in range(2)]
    msg_rows = 2 * span + rim

    def whole(shape):
        return pl.BlockSpec(shape, lambda i: (0,) * len(shape))

    def flipped(array, flip):
        return lax.ppermute(array, "ctx", [(i, i ^ flip) for i in range(ctx_count)])

    def gathered(array):
        if direct:
            return [array] + [flipped(array, flip) for flip in range(1, group)]
        return [lax.all_gather(array, "ctx", axis_index_groups=halves)]

    def delivered(arrays):
        if direct:
            return [flipped(array, step + 1) for step, array in enumerate(arrays)]
        return [lax.all_to_all(arrays[0], "ctx", 0, 0, axis_index_groups=halves, tiled=True)]

    packed = pl.pallas_call(
        pack_kernel,
        grid=(1,),
        out_shape=jax.ShapeDtypeStruct((msg_rows, 2 * LANES), bf16),
        in_specs=[
            whole(k_pre.shape),
            whole(k_pre.shape),
            pl.BlockSpec((2, TAIL, width), lambda i: (0, span // TAIL - 1, 0)),
        ],
        out_specs=whole((msg_rows, 2 * LANES)),
        compiler_params=pltpu.CompilerParams(vmem_limit_bytes=4 * MIB),
        name="pack",
    )(k_pre, value_before_filter, q_pre)
    across = flipped(packed, group)
    received = gathered(packed) + gathered(across)

    window = span * ctx_count + span
    if direct:
        sent_shapes = [
            (3 * span + (32 if flip & (flip + 1) == 0 else 16), 2 * LANES) for flip in range(1, group)
        ]
    else:
        sent_shapes = [(group, 3 * span + 32, 2 * LANES)]
    scratch = [
        pltpu.VMEM((length + 16, LANES), f32),
        pltpu.VMEM((length + 16, 2 * LANES), f32),
        pltpu.VMEM((length, 2 * LANES), bf16),
        pltpu.VMEM((length + 8, 2 * LANES), f32),
        pltpu.VMEM((2, span + 8, width), f32),
        pltpu.VMEM((2, span * width // LANES, LANES), bf16),
        pltpu.VMEM((2, span * width // LANES, LANES), bf16),
        pltpu.VMEM((2, span + 8, width), f32),
        pltpu.VMEM((4 if direct else 1, window, 2 * LANES), f32),
        pltpu.VMEM((4 if direct else 1, window, 2 * LANES), f32),
        pltpu.VMEM((ctx_count, rim, 2 * LANES), f32),
        pltpu.VMEM(q_pre.shape, bf16),
        pltpu.VMEM(q_pre.shape, bf16),
        pltpu.VMEM(q_pre.shape, f32),
        pltpu.SemaphoreType.DMA((3,)),
    ]
    own_shapes = [(2 * span, 2 * LANES), (2 * span + 8, 2 * LANES)]
    d_q_main, own_near, own_far, *sent = pl.pallas_call(
        functools.partial(grads_kernel, ctx_count, direct),
        out_shape=[jax.ShapeDtypeStruct(q_pre.shape, f32)]
        + [jax.ShapeDtypeStruct(shape, f32) for shape in own_shapes]
        + [jax.ShapeDtypeStruct(shape, bf16) for shape in sent_shapes],
        in_specs=[smem, vmem, hbm, hbm] + [vmem] * len(received),
        out_specs=[hbm] + [vmem] * (2 + len(sent_shapes)),
        scratch_shapes=scratch,
        compiler_params=pltpu.CompilerParams(vmem_limit_bytes=(20 if direct else 62) * MIB),
        name="grads",
    )(doc_lengths, filters, q_pre, d_out, *received)
    half_terms = delivered(sent)
    merged_shapes = [
        jax.ShapeDtypeStruct((2 * span, 2 * LANES), f32),
        jax.ShapeDtypeStruct((2 * span + 32, 2 * LANES), bf16),
        jax.ShapeDtypeStruct((8, 2 * LANES), f32),
        jax.ShapeDtypeStruct((2, rim // 2, 2 * LANES), f32),
    ]
    near, far, half_sums, rims = pl.pallas_call(
        functools.partial(merge_kernel, ctx_count, direct),
        out_shape=merged_shapes,
        in_specs=[vmem] * (2 + len(half_terms)),
        out_specs=[vmem] * len(merged_shapes),
        scratch_shapes=[
            pltpu.VMEM((group, 8, 2 * LANES), f32),
            pltpu.VMEM((ctx_count, rim // 2, 2 * LANES), f32),
        ],
        compiler_params=pltpu.CompilerParams(vmem_limit_bytes=(4 if direct else 40) * MIB),
        name="merge",
    )(own_near, own_far, *half_terms)
    from_half = flipped(far, group)

    sums = pl.pallas_call(
        functools.partial(sums_kernel, span),
        out_shape=jax.ShapeDtypeStruct(filters.shape, f32),
        in_specs=[vmem, vmem],
        out_specs=vmem,
        compiler_params=pltpu.CompilerParams(vmem_limit_bytes=2 * MIB),
        name="sums",
    )(half_sums, from_half)
    count = lax.axis_size("tp")
    level = [sums] + [
        lax.ppermute(sums, "tp", [(i, i ^ flip) for i in range(count)]) for flip in range(1, count)
    ]

    last_rows = pl.BlockSpec((2, 8, width), lambda i: (0, span // 8 - 1, 0))
    d_q_pre, d_k_pre, d_v_pre = pl.pallas_call(
        functools.partial(finish_kernel, ctx_count),
        grid=(1,),
        out_shape=(
            jax.ShapeDtypeStruct(q_pre.shape, f32),
            jax.ShapeDtypeStruct(k_pre.shape, f32),
            jax.ShapeDtypeStruct(k_pre.shape, f32),
        ),
        in_specs=[smem, whole(filters.shape), last_rows]
        + [whole(array.shape) for array in (near, from_half, rims)],
        out_specs=(last_rows, whole(k_pre.shape), whole(k_pre.shape)),
        input_output_aliases={2: 0},
        compiler_params=pltpu.CompilerParams(vmem_limit_bytes=4 * MIB),
        name="finish",
    )(doc_lengths, filters, d_q_main, near, from_half, rims)

    while len(level) > 1:
        level = [level[at] + level[at + 1] for at in range(0, len(level), 2)]
    d_filters = level[0]
    return (d_q_pre, d_k_pre, d_v_pre, d_filters)


def solution(mesh):
    split = P(None, "ctx", "tp")
    return jax.shard_map(
        shards,
        mesh=mesh,
        in_specs=(split, split, split, split, P(), P()),
        out_specs=(split, split, split, P()),
        check_vma=False,
    )
```

```python
import functools

import jax
import jax.numpy as jnp
import numpy as np
from jax import lax
from jax.experimental import pallas as pl
from jax.experimental.pallas import tpu as pltpu
from jax.sharding import PartitionSpec as P

LANES = 128
NT = (((1,), (1,)), ((), ()))
NN = (((1,), (0,)), ((), ()))
TN = (((0,), (0,)), ((), ()))
TAIL = 16
MAX_CHUNK = 640
MAX_DIRECT = 4
MIB = 1 << 20


def loop(count, body, init, unrolled=16):
    if count <= unrolled:
        for step in range(count):
            init = body(step, init)
        return init
    return lax.fori_loop(0, count, body, init)


def aligned(start, multiple):
    return start if isinstance(start, int) else pl.multiple_of(start, multiple)


def doc_starts(lengths_ref):
    starts = [jnp.int32(0)]
    for index in range(lengths_ref.shape[0] - 1):
        starts.append(starts[-1] + lengths_ref[index])
    return starts


def fold_rows(terms):
    rows, lanes = terms.shape
    return jnp.sum(terms.reshape(rows // 8, 8, lanes), axis=0)


def split_bits(values):
    high = values.astype(jnp.bfloat16)
    low = (values - high.astype(jnp.float32)).astype(jnp.bfloat16)
    return high, low


def joined(pair):
    rows = pair.shape[0] // 2
    pair = pair.astype(jnp.float32)
    return pair[:rows] + pair[rows:]


class Slots:
    def __init__(self, refs, me):
        self.refs, self.me = refs, me

    def __getitem__(self, flip):
        if len(self.refs) == 1:
            place = lax.rem(self.me, jnp.int32(self.refs[0].shape[0]))
            return self.refs[0].at[partner(place, flip)]
        return self.refs[flip]


def partner(me, flip):
    return lax.bitwise_xor(me, jnp.int32(flip))


def pack_kernel(k_ref, v_ref, q_ref, out_ref):
    span = k_ref.shape[1]
    kv = jnp.concatenate([k_ref[...], v_ref[...]], axis=2).reshape(2 * span, 2 * LANES)
    tails = []
    for half in range(2):
        last = q_ref[half].astype(jnp.float32)[TAIL - 2 :]
        tails += [last[:, at : at + 2 * LANES] for at in range(0, last.shape[1], 2 * LANES)]
    out_ref[: 2 * span] = kv
    out_ref[2 * span :] = jnp.concatenate(tails, axis=0).astype(jnp.bfloat16)


def grads_kernel(ctx_count, direct, lengths_ref, filters_ref, q_hbm, d_out_hbm, *refs):
    group = ctx_count // 2
    arrays = group if direct else 1
    near_in, far_in, refs = refs[:arrays], refs[arrays : 2 * arrays], refs[2 * arrays :]
    dq_hbm, dq_tail_ref, own_near_ref, own_far_ref = refs[:4]
    arrays = group - 1 if direct else 1
    out_refs, refs = refs[4 : 4 + arrays], refs[4 + arrays :]
    same_scr, same_two_scr, kv_scr, conv_scr, dkv_scr, q_scr, qc_scr, do_scr, dq_scr = refs[:9]
    bias_scr, s_scr, dp_scr, rim_scr, q_ref, d_out_ref, dq_ref, sems = refs[9:]
    f32, bf16 = jnp.float32, jnp.bfloat16
    loads = [
        pltpu.make_async_copy(q_hbm, q_ref, sems.at[0]),
        pltpu.make_async_copy(d_out_hbm, d_out_ref, sems.at[1]),
    ]
    for load in loads:
        load.start()
    span = q_ref.shape[1]
    heads = q_ref.shape[2] // LANES
    half_rows = span * ctx_count
    length = 2 * half_rows
    blocks = 2 * ctx_count
    me = lax.axis_index("ctx")
    near_in, far_in = Slots(near_in, me), Slots(far_in, me)
    sent = Slots((own_far_ref,) + out_refs if direct else out_refs, me)
    scale = LANES**-0.5
    log2_scale = scale * 1.4426950408889634
    starts = doc_starts(lengths_ref)

    def fill(index, carry):
        rows = pl.ds(aligned(8 + index * span, 8), span)
        same_scr[rows] = jnp.ones((span, LANES), f32)
        same_two_scr[rows] = jnp.ones((span, LANES), f32)
        return carry

    loop(blocks, fill, 0)
    zeros = jnp.zeros((8, LANES), f32)
    for rows in (slice(0, 8), slice(8 + length, 16 + length)):
        same_scr[rows] = zeros
        same_two_scr[rows] = zeros
        for tensor in range(2):
            kv_scr[tensor, rows] = zeros
    for start in starts:
        same_scr[pl.ds(8 + start, 1)] = zeros[:1]
        same_two_scr[pl.ds(8 + start, 1)] = zeros[:1]
        same_two_scr[pl.ds(9 + start, 1)] = zeros[:1]

    def place_blocks(flip, carry):
        for message, index in (
            (near_in[flip], partner(me, flip)),
            (far_in[flip], partner(me, flip + group)),
        ):
            early = aligned(8 + index * span, 8)
            late = aligned(8 + (blocks - 1 - index) * span, 8)
            for tensor in range(2):
                lanes = slice(tensor * LANES, (tensor + 1) * LANES)
                kv_scr[tensor, pl.ds(early, span)] = message[:span, lanes].astype(f32)
                kv_scr[tensor, pl.ds(late, span)] = message[span : 2 * span, lanes].astype(f32)
            rim_scr[index] = message[2 * span :].astype(f32)
        return carry

    loop(group, place_blocks, 0)

    def taps(tensor):
        return [filters_ref[tensor, tap : tap + 1] for tap in range(3)]

    def masks(base, ahead):
        one = same_scr[pl.ds(base + 8 + min(ahead, 1), span)]
        return one, same_two_scr[pl.ds(base + 8 + ahead, span)]

    def convolve_kv(index, carry):
        base = index * span
        one, two = masks(base, 0)
        for tensor in range(2):
            zero_tap, one_tap, two_tap = taps(tensor + 1)
            total = zero_tap * kv_scr[tensor, pl.ds(aligned(base + 8, 8), span)]
            total = total + one * (one_tap * kv_scr[tensor, pl.ds(base + 7, span)])
            total = total + two * (two_tap * kv_scr[tensor, pl.ds(base + 6, span)])
            conv_scr[tensor, pl.ds(aligned(base, 16), span)] = total.astype(bf16)
        return carry

    loop(blocks, convolve_kv, 0)

    middle = me == ctx_count - 1
    rim_rows = rim_scr.shape[1] // 2
    rim_before = rim_scr[jnp.maximum(me - 1, 0)]
    rim_after = rim_scr[jnp.minimum(me + 1, ctx_count - 1)]
    late_rim = jnp.where(middle, rim_after[:rim_rows], rim_after[rim_rows:])
    rims = [rim_before[:rim_rows], late_rim]
    first_place = [me * span, (blocks - 1 - me) * span]

    for load in loads:
        load.wait()
    for half in range(2):
        one, two = masks(first_place[half], 0)
        zero_tap, one_tap, two_tap = taps(0)
        for head in range(heads):
            lanes = slice(head * LANES, (head + 1) * LANES)
            at = 2 * (head // 2)
            q_scr[half, head, 6:8] = rims[half][at : at + 2, (head % 2) * LANES : (head % 2 + 1) * LANES]
            q_scr[half, head, 8:] = q_ref[half, :, lanes].astype(f32)
            total = zero_tap * q_scr[half, head, 8:]
            total = total + one * (one_tap * q_scr[half, head, 7 : 7 + span])
            total = total + two * (two_tap * q_scr[half, head, 6 : 6 + span])
            qc_scr[half, head * span : (head + 1) * span] = total.astype(bf16)
            do_scr[half, head * span : (head + 1) * span] = d_out_ref[half, :, lanes]

    def attend(half, window, first_key, add):
        chunks = 1
        while window // chunks > MAX_CHUNK or window % (16 * chunks):
            chunks += 1
        size = window // chunks
        query = first_place[half] + lax.rem(
            lax.broadcasted_iota(jnp.int32, (1, LANES), 1), jnp.int32(span)
        )
        lowest = jnp.zeros((1, LANES), jnp.int32)
        for start in starts[1:]:
            lowest = jnp.where(query >= start, start, lowest)
        wide = 2 * LANES

        def fill_bias(step, carry):
            places = first_key + step * size + lax.broadcasted_iota(jnp.int32, (size, LANES), 0)
            allowed = (places >= lowest) & (places <= query)
            bias_scr[pl.ds(aligned(step * size, 16), size)] = jnp.where(allowed, 0.0, -1e30)
            return carry

        loop(chunks, fill_bias, 0, 1)
        whole_window = pl.ds(aligned(first_key, 16), window)
        keys_t = conv_scr[0, whole_window].T if chunks == 1 else None
        for at in range(heads * span // wide):
            slot = (half * (heads * span // wide) + at) % s_scr.shape[0]
            cols = slice(at * wide, (at + 1) * wide)
            queries = qc_scr[half, cols]
            grads = do_scr[half, cols]

            def key_rows(step):
                return pl.ds(aligned(first_key + step * size, 16), size)

            def score(step, top):
                keys = conv_scr[0, key_rows(step)]
                scores = lax.dot_general(keys, queries, NT, preferred_element_type=f32)
                bias = bias_scr[pl.ds(aligned(step * size, 16), size)]
                scores = scores + jnp.concatenate([bias, bias], axis=1)
                s_scr[slot, pl.ds(aligned(step * size, 16), size)] = scores
                return jnp.maximum(top, jnp.max(scores, axis=0, keepdims=True))

            top = loop(chunks, score, jnp.full((1, wide), -1e30, f32), 1)

            def weigh(step, carry):
                total, weighted = carry
                rows = pl.ds(aligned(step * size, 16), size)
                weights = jnp.exp2((s_scr[slot, rows] - top) * log2_scale)
                values = conv_scr[1, key_rows(step)]
                prob_grads = lax.dot_general(values, grads, NT, preferred_element_type=f32)
                s_scr[slot, rows] = weights
                dp_scr[slot, rows] = prob_grads
                total = total + jnp.sum(weights, axis=0, keepdims=True)
                weighted = weighted + jnp.sum(weights * prob_grads, axis=0, keepdims=True)
                return total, weighted

            zeros = jnp.zeros((1, wide), f32)
            total, weighted = loop(chunks, weigh, (zeros, zeros), 1)
            inverse = 1.0 / total
            mean = weighted * inverse
            slope = inverse * scale

            def accumulate(step, dq):
                rows = pl.ds(aligned(step * size, 16), size)
                weights = s_scr[slot, rows]
                probs = (weights * inverse).astype(bf16)
                score_grads = (weights * slope * (dp_scr[slot, rows] - mean)).astype(bf16)
                dk = lax.dot_general(score_grads, queries, NN, preferred_element_type=f32)
                dv = lax.dot_general(probs, grads, NN, preferred_element_type=f32)
                target = pl.ds(aligned(first_key + step * size, 16), size)
                for tensor, terms in enumerate((dk, dv)):
                    if add or at:
                        dkv_scr[tensor, target] += terms
                    else:
                        dkv_scr[tensor, target] = terms
                if keys_t is not None:
                    return lax.dot_general(keys_t, score_grads, NN, preferred_element_type=f32)
                keys = conv_scr[0, key_rows(step)]
                return dq + lax.dot_general(keys, score_grads, TN, preferred_element_type=f32)

            dq = loop(chunks, accumulate, jnp.zeros((LANES, wide), f32), 1)
            dq = dq.T
            for part in range(wide // span):
                head = at * (wide // span) + part
                dq_scr[half, head, :span] = dq[part * span : (part + 1) * span]

    for tensor in range(2):
        dkv_scr[tensor, half_rows:] = jnp.zeros((half_rows + 8, LANES), f32)
    attend(0, half_rows, 0, False)
    attend(1, half_rows + span, (ctx_count - 1 - me) * span, True)

    next_rows = jnp.where(middle, dq_scr[1, :, :8], 0.0)
    dq_scr[0, :, span:] = next_rows
    dq_scr[1, :, span:] = jnp.zeros_like(next_rows)
    sums = [jnp.zeros((8, LANES), f32) for _ in range(3)]
    for half in range(2):
        one, two = masks(first_place[half], 0)
        ahead_one = same_scr[pl.ds(first_place[half] + 9, span)]
        ahead_two = same_two_scr[pl.ds(first_place[half] + 10, span)]
        zero_tap, one_tap, two_tap = taps(0)
        for head in range(heads):
            lanes = slice(head * LANES, (head + 1) * LANES)
            grads = dq_scr[half, head, :span]
            out = zero_tap * grads
            out = out + ahead_one * (one_tap * dq_scr[half, head, 1 : 1 + span])
            out = out + ahead_two * (two_tap * dq_scr[half, head, 2 : 2 + span])
            dq_ref[half, :, lanes] = out
            dq_tail_ref[half, :, lanes] = out[span - 8 :]
            sums[0] += fold_rows(grads * q_scr[half, head, 8:])
            sums[1] += fold_rows(grads * one * q_scr[half, head, 7 : 7 + span])
            sums[2] += fold_rows(grads * two * q_scr[half, head, 6 : 6 + span])
    q_sums = [jnp.sum(term, axis=0, keepdims=True) for term in sums]
    store = pltpu.make_async_copy(dq_ref, dq_hbm, sems.at[2])
    store.start()

    def finish_block(index, carry, target, row):
        base = pl.multiple_of(index * span, 8)
        one, two = masks(base, 0)
        ahead_one = same_scr[pl.ds(base + 9, span)]
        ahead_two = same_two_scr[pl.ds(base + 10, span)]
        carry = list(carry)
        for tensor in range(2):
            zero_tap, one_tap, two_tap = taps(tensor + 1)
            own = dkv_scr[tensor, pl.ds(base, span)]
            out = zero_tap * own
            out = out + ahead_one * (one_tap * dkv_scr[tensor, pl.ds(base + 1, span)])
            out = out + ahead_two * (two_tap * dkv_scr[tensor, pl.ds(base + 2, span)])
            lanes = slice(tensor * LANES, (tensor + 1) * LANES)
            target[row : row + span, lanes] = out.astype(target.dtype)
            at = 3 * tensor
            carry[at] += fold_rows(own * kv_scr[tensor, pl.ds(base + 8, span)])
            carry[at + 1] += fold_rows(own * one * kv_scr[tensor, pl.ds(base + 7, span)])
            carry[at + 2] += fold_rows(own * two * kv_scr[tensor, pl.ds(base + 6, span)])
        return tuple(carry)

    low = me < group

    def finish(step, carry):
        flip = step + 1
        owner = partner(me, flip)
        far_owner = partner(me, flip + group)
        near_late = blocks - 1 - owner
        places = [
            far_owner,
            jnp.where(low, blocks - 1 - far_owner, owner),
            jnp.where(low & (me > owner), owner, near_late),
        ]
        for at, place in enumerate(places):
            carry = finish_block(place, carry, sent[flip], at * span)
        return carry

    kv_sums = (zeros,) * 6
    for target, index in ((own_far_ref, partner(me, group)), (own_near_ref, me)):
        kv_sums = finish_block(index, kv_sums, target, 0)
        kv_sums = finish_block(blocks - 1 - index, kv_sums, target, span)
    kv_sums = loop(group - 1, finish, kv_sums)
    kv_sums = [jnp.sum(term, axis=0, keepdims=True) for term in kv_sums]

    padding = [jnp.zeros((2, LANES), f32)]
    left = jnp.concatenate(q_sums + kv_sums[:3] + padding, axis=0)
    right = jnp.concatenate([jnp.zeros((3, LANES), f32)] + kv_sums[3:] + padding, axis=0)
    sums_tile = jnp.concatenate([left, right], axis=1)
    sums_pair = jnp.concatenate(split_bits(sums_tile), axis=0)
    own_far_ref[2 * span :] = joined(sums_pair)
    rims = []
    for half in range(2):
        rows = [dq_scr[half, head, :2] for head in range(heads)]
        rows = [jnp.concatenate(rows[at : at + 2], axis=1) for at in range(0, heads, 2)]
        rims.append(jnp.concatenate(rows, axis=0))

    def rim_for(index):
        return jnp.concatenate(split_bits(jnp.where(index < me, rims[0], rims[1])), axis=0)

    def store_rims(step, carry):
        flip = step + 1
        owner = partner(me, flip)
        sent[flip][3 * span : 3 * span + 16] = sums_pair
        if not direct or flip & (flip + 1) == 0:
            across = (flip == group - 1) & (jnp.abs(owner - me) != 1)
            target = jnp.where(across, partner(owner, group), owner)
            sent[flip][3 * span + 16 :] = rim_for(target)
        return carry

    loop(group - 1, store_rims, 0, 16 if direct else 1)
    store.wait()


def merge_kernel(ctx_count, direct, own_near_ref, own_far_ref, *refs):
    received_refs = refs[:-6]
    near_ref, far_ref, half_sums_ref, rims_ref, sums_scr, rim_scr = refs[-6:]
    f32, bf16 = jnp.float32, jnp.bfloat16
    group = ctx_count // 2
    me = lax.axis_index("ctx")
    low = me < group
    received = Slots((own_far_ref,) + received_refs if direct else received_refs, me)
    place = lax.rem(me, jnp.int32(group))
    span = own_near_ref.shape[0] // 2
    rows = 2 * span
    sums_scr[place] = own_far_ref[rows:]
    neighbours = [jnp.minimum(me + 1, ctx_count - 1), jnp.maximum(me - 1, 0)]
    for index in neighbours:
        rim_scr[index] = jnp.zeros(rim_scr.shape[1:], f32)

    def add(step, carry):
        flip = step + 1
        source = partner(me, flip)
        message = received[flip]
        parts = [message[at * span : (at + 1) * span].astype(f32) for at in range(3)]
        near_early, near_late, far_early, far_late = carry
        sums_scr[partner(place, flip)] = joined(message[3 * span : 3 * span + 16])
        if not direct or flip & (flip + 1) == 0:
            rim_scr[source] = joined(message[3 * span + 16 :])
        to_early = low & (source > me)
        zero = jnp.zeros_like(parts[0])
        return (
            near_early + jnp.where(low, jnp.where(to_early, parts[2], zero), parts[1]),
            near_late + jnp.where(to_early, zero, parts[2]),
            far_early + parts[0],
            far_late + jnp.where(low, parts[1], zero),
        )

    init = (own_near_ref[:span], own_near_ref[span:], own_far_ref[:span], own_far_ref[span:rows])
    totals = loop(group - 1, add, init, 16 if direct else 1)
    near_ref[:span] = totals[0]
    near_ref[span:] = totals[1]
    far_ref[:span] = totals[2].astype(bf16)
    far_ref[span:rows] = totals[3].astype(bf16)
    sums = loop(group, lambda index, carry: carry + sums_scr[index], jnp.zeros((8, 2 * LANES), f32))
    pair = jnp.concatenate(split_bits(sums), axis=0)
    half_sums_ref[...] = joined(pair)
    far_ref[rows : rows + 16] = pair
    far_ref[rows + 16 :] = received[group - 1][3 * span + 16 :]
    for at, index in enumerate(neighbours):
        rims_ref[at] = rim_scr[index]


def sums_kernel(span, half_sums_ref, far_ref, out_ref):
    sums = half_sums_ref[...] + joined(far_ref[2 * span : 2 * span + 16])
    out_ref[0] = sums[0:3, :LANES]
    out_ref[1] = sums[3:6, :LANES]
    out_ref[2] = sums[3:6, LANES:]


def finish_kernel(
    ctx_count, lengths_ref, filters_ref, dq_in_hbm, tail_ref, near_ref, far_ref, rims_ref, *refs
):
    dq_hbm, dk_hbm, dv_hbm, dq_ref, dk_ref, dv_ref, sems = refs
    f32 = jnp.float32
    group = ctx_count // 2
    span = dk_ref.shape[1]
    me = lax.axis_index("ctx")
    starts = doc_starts(lengths_ref)
    blocks = 2 * ctx_count

    total = near_ref[...] + far_ref[: 2 * span].astype(f32)
    for half in range(2):
        dk_ref[half] = total[half * span : (half + 1) * span, :LANES]
        dv_ref[half] = total[half * span : (half + 1) * span, LANES:]
    stores = [
        pltpu.make_async_copy(dk_ref, dk_hbm, sems.at[0]),
        pltpu.make_async_copy(dv_ref, dv_hbm, sems.at[1]),
        pltpu.make_async_copy(dq_ref, dq_hbm.at[:, pl.ds(span - 8, 8)], sems.at[2]),
    ]
    for store in stores[:2]:
        store.start()

    def same(place):
        cut = place >= blocks * span
        for start in starts:
            cut = cut | (place == start)
        return jnp.where(cut, 0.0, 1.0).astype(f32)

    heads = dq_ref.shape[2] // LANES
    taps = [jnp.concatenate([filters_ref[0, tap : tap + 1]] * heads, axis=1) for tap in range(3)]
    row = lax.broadcasted_iota(jnp.int32, dq_ref.shape[1:], 0)
    far_rim = joined(far_ref[2 * span + 16 :])
    crosses = [me == group - 1, me == group]
    first_place = [me * span, (blocks - 1 - me) * span]
    present = [me < ctx_count - 1, me > 0]
    for half in range(2):
        rim = jnp.where(crosses[half], far_rim, rims_ref[half])
        rows = jnp.concatenate([rim[2 * at : 2 * at + 2] for at in range(rim.shape[0] // 2)], axis=1)
        end = first_place[half] + span
        zero, one, two = same(end - 1), same(end), same(end + 1)
        one = jnp.where(present[half], one, 0.0)
        last_but_one = (zero * one) * (taps[2] * rows[0:1])
        last = one * (taps[1] * rows[0:1]) + (one * two) * (taps[2] * rows[1:2])
        extra = jnp.where(row == 6, last_but_one, jnp.where(row == 7, last, 0.0))
        dq_ref[half] = tail_ref[half] + extra
    stores[2].start()
    for store in stores:
        store.wait()


def shards(q_pre, k_pre, value_before_filter, d_out, filters, doc_lengths):
    f32, bf16 = jnp.float32, jnp.bfloat16
    ctx_count = lax.axis_size("ctx")
    span, width = q_pre.shape[1:]
    length = 2 * span * ctx_count
    rim = 4 * width // (2 * LANES)
    vmem = pl.BlockSpec(memory_space=pltpu.VMEM)
    smem = pl.BlockSpec(memory_space=pltpu.SMEM)
    hbm = pl.BlockSpec(memory_space=pltpu.HBM)

    group = ctx_count // 2
    direct = group <= MAX_DIRECT
    halves = [[half * group + at for at in range(group)] for half in range(2)]
    msg_rows = 2 * span + rim

    def whole(shape):
        return pl.BlockSpec(shape, lambda i: (0,) * len(shape))

    def in_hbm(array):
        return pltpu.with_memory_space_constraint(array, pltpu.HBM)

    def flipped(array, flip):
        return lax.ppermute(array, "ctx", [(i, i ^ flip) for i in range(ctx_count)])

    def gathered(array):
        if direct:
            return [array] + [flipped(array, flip) for flip in range(1, group)]
        return [lax.all_gather(array, "ctx", axis_index_groups=halves)]

    def delivered(arrays):
        if direct:
            return [flipped(array, step + 1) for step, array in enumerate(arrays)]
        return [lax.all_to_all(arrays[0], "ctx", 0, 0, axis_index_groups=halves, tiled=True)]

    packed = pl.pallas_call(
        pack_kernel,
        grid=(1,),
        out_shape=jax.ShapeDtypeStruct((msg_rows, 2 * LANES), bf16),
        in_specs=[
            whole(k_pre.shape),
            whole(k_pre.shape),
            pl.BlockSpec((2, TAIL, width), lambda i: (0, span // TAIL - 1, 0)),
        ],
        out_specs=whole((msg_rows, 2 * LANES)),
        compiler_params=pltpu.CompilerParams(vmem_limit_bytes=4 * MIB),
        name="pack",
    )(*[in_hbm(array) for array in (k_pre, value_before_filter, q_pre)])
    across = flipped(packed, group)
    received = gathered(packed) + gathered(across)

    window = span * ctx_count + span
    if direct:
        sent_shapes = [
            (3 * span + (32 if flip & (flip + 1) == 0 else 16), 2 * LANES) for flip in range(1, group)
        ]
    else:
        sent_shapes = [(group, 3 * span + 32, 2 * LANES)]
    slots = 4 if direct else 1
    heads = width // LANES
    scratch = [
        pltpu.VMEM((length + 16, LANES), f32),
        pltpu.VMEM((length + 16, LANES), f32),
        pltpu.VMEM((2, length + 16, LANES), f32),
        pltpu.VMEM((2, length, LANES), bf16),
        pltpu.VMEM((2, length + 8, LANES), f32),
        pltpu.VMEM((2, heads, span + 8, LANES), f32),
        pltpu.VMEM((2, span * heads, LANES), bf16),
        pltpu.VMEM((2, span * heads, LANES), bf16),
        pltpu.VMEM((2, heads, span + 8, LANES), f32),
        pltpu.VMEM((window, LANES), f32),
        pltpu.VMEM((slots, window, 2 * LANES), f32),
        pltpu.VMEM((slots, window, 2 * LANES), f32),
        pltpu.VMEM((ctx_count, rim, 2 * LANES), f32),
        pltpu.VMEM(q_pre.shape, bf16),
        pltpu.VMEM(q_pre.shape, bf16),
        pltpu.VMEM(q_pre.shape, f32),
        pltpu.SemaphoreType.DMA((3,)),
    ]
    own_shapes = [(2 * span, 2 * LANES), (2 * span + 8, 2 * LANES)]
    d_q_main, d_q_tail, own_near, own_far, *sent = pl.pallas_call(
        functools.partial(grads_kernel, ctx_count, direct),
        out_shape=[jax.ShapeDtypeStruct(q_pre.shape, f32)]
        + [jax.ShapeDtypeStruct(shape, f32) for shape in [(2, 8, width)] + own_shapes]
        + [jax.ShapeDtypeStruct(shape, bf16) for shape in sent_shapes],
        in_specs=[smem, vmem, hbm, hbm] + [vmem] * len(received),
        out_specs=[hbm] + [vmem] * (3 + len(sent_shapes)),
        scratch_shapes=scratch,
        compiler_params=pltpu.CompilerParams(vmem_limit_bytes=(20 if direct else 62) * MIB),
        name="grads",
    )(doc_lengths, filters, in_hbm(q_pre), in_hbm(d_out), *received)
    half_terms = delivered(sent)
    merged_shapes = [
        jax.ShapeDtypeStruct((2 * span, 2 * LANES), f32),
        jax.ShapeDtypeStruct((2 * span + 32, 2 * LANES), bf16),
        jax.ShapeDtypeStruct((8, 2 * LANES), f32),
        jax.ShapeDtypeStruct((2, rim // 2, 2 * LANES), f32),
    ]
    near, far, half_sums, rims = pl.pallas_call(
        functools.partial(merge_kernel, ctx_count, direct),
        out_shape=merged_shapes,
        in_specs=[vmem] * (2 + len(half_terms)),
        out_specs=[vmem] * len(merged_shapes),
        scratch_shapes=[
            pltpu.VMEM((group, 8, 2 * LANES), f32),
            pltpu.VMEM((ctx_count, rim // 2, 2 * LANES), f32),
        ],
        compiler_params=pltpu.CompilerParams(vmem_limit_bytes=(4 if direct else 40) * MIB),
        name="merge",
    )(own_near, own_far, *half_terms)
    from_half = flipped(far, group)

    sums = pl.pallas_call(
        functools.partial(sums_kernel, span),
        out_shape=jax.ShapeDtypeStruct(filters.shape, f32),
        in_specs=[vmem, vmem],
        out_specs=vmem,
        compiler_params=pltpu.CompilerParams(vmem_limit_bytes=2 * MIB),
        name="sums",
    )(half_sums, from_half)
    count = lax.axis_size("tp")
    level = [sums] + [
        lax.ppermute(sums, "tp", [(i, i ^ flip) for i in range(count)]) for flip in range(1, count)
    ]

    d_q_pre, d_k_pre, d_v_pre = pl.pallas_call(
        functools.partial(finish_kernel, ctx_count),
        out_shape=(
            jax.ShapeDtypeStruct(q_pre.shape, f32),
            jax.ShapeDtypeStruct(k_pre.shape, f32),
            jax.ShapeDtypeStruct(k_pre.shape, f32),
        ),
        in_specs=[smem, vmem, hbm, vmem, vmem, vmem, vmem],
        out_specs=(hbm, hbm, hbm),
        scratch_shapes=[
            pltpu.VMEM((2, 8, width), f32),
            pltpu.VMEM(k_pre.shape, f32),
            pltpu.VMEM(k_pre.shape, f32),
            pltpu.SemaphoreType.DMA((3,)),
        ],
        input_output_aliases={2: 0},
        compiler_params=pltpu.CompilerParams(vmem_limit_bytes=4 * MIB),
        name="finish",
    )(doc_lengths, filters, d_q_main, d_q_tail, near, from_half, rims)

    while len(level) > 1:
        level = [level[at] + level[at + 1] for at in range(0, len(level), 2)]
    d_filters = level[0]
    return (d_q_pre, d_k_pre, d_v_pre, d_filters)


def solution(mesh):
    split = P(None, "ctx", "tp")
    return jax.shard_map(
        shards,
        mesh=mesh,
        in_specs=(split, split, split, split, P(), P()),
        out_specs=(split, split, split, P()),
        check_vma=False,
    )
```

```python
import functools

import jax
import jax.numpy as jnp
import numpy as np
from jax import lax
from jax.experimental import pallas as pl
from jax.experimental.pallas import tpu as pltpu
from jax.sharding import PartitionSpec as P

LANES = 128
NT = (((1,), (1,)), ((), ()))
NN = (((1,), (0,)), ((), ()))
TN = (((0,), (0,)), ((), ()))
TAIL = 16
MAX_CHUNK = 640
MAX_DIRECT = 4
MIB = 1 << 20


def loop(count, body, init, unrolled=16):
    if count <= unrolled:
        for step in range(count):
            init = body(step, init)
        return init
    return lax.fori_loop(0, count, body, init)


def aligned(start, multiple):
    return start if isinstance(start, int) else pl.multiple_of(start, multiple)


def doc_starts(lengths_ref):
    starts = [jnp.int32(0)]
    for index in range(lengths_ref.shape[0] - 1):
        starts.append(starts[-1] + lengths_ref[index])
    return starts


def fold_rows(terms):
    rows, lanes = terms.shape
    return jnp.sum(terms.reshape(rows // 8, 8, lanes), axis=0)


def split_bits(values):
    high = values.astype(jnp.bfloat16)
    low = (values - high.astype(jnp.float32)).astype(jnp.bfloat16)
    return high, low


def joined(pair):
    rows = pair.shape[0] // 2
    pair = pair.astype(jnp.float32)
    return pair[:rows] + pair[rows:]


class Slots:
    def __init__(self, refs, me):
        self.refs, self.me = refs, me

    def __getitem__(self, flip):
        if len(self.refs) == 1:
            place = lax.rem(self.me, jnp.int32(self.refs[0].shape[0]))
            return self.refs[0].at[partner(place, flip)]
        return self.refs[flip]


def partner(me, flip):
    return lax.bitwise_xor(me, jnp.int32(flip))


def pack_kernel(k_ref, v_ref, q_ref, out_ref):
    span = k_ref.shape[1]
    kv = jnp.concatenate([k_ref[...], v_ref[...]], axis=2).reshape(2 * span, 2 * LANES)
    tails = []
    for half in range(2):
        last = q_ref[half].astype(jnp.float32)[TAIL - 2 :]
        tails += [last[:, at : at + 2 * LANES] for at in range(0, last.shape[1], 2 * LANES)]
    out_ref[: 2 * span] = kv
    out_ref[2 * span :] = jnp.concatenate(tails, axis=0).astype(jnp.bfloat16)


def relay_kernel(ctx_count, direct, own_ref, across_ref, *out_refs):
    group = ctx_count // 2
    me = lax.axis_index("ctx")
    low = me < group
    sent = Slots((None,) + out_refs if direct else out_refs, me)
    rows = own_ref.shape[0] - TAIL
    span = rows // 2

    def send(step, carry):
        flip = step + 1
        target = partner(me, flip)
        message = sent[flip]
        message[:span] = across_ref[:span]

        @pl.when(low)
        def _():
            message[span : 2 * span] = across_ref[span:rows]

            @pl.when(target > me)
            def _():
                message[2 * span : 3 * span] = own_ref[:span]

            @pl.when(target < me)
            def _():
                message[2 * span : 3 * span] = own_ref[span:rows]

        @pl.when(jnp.logical_not(low))
        def _():
            message[span : 3 * span] = own_ref[:rows]

        if not direct or flip & (flip + 1) == 0:

            @pl.when(jnp.abs(target - me) == 1)
            def _():
                message[3 * span :] = own_ref[rows:]

            @pl.when(jnp.abs(target - me) != 1)
            def _():
                message[3 * span :] = across_ref[rows:]

        return carry

    loop(group - 1, send, 0, 16 if direct else 1)


def grads_kernel(ctx_count, direct, lengths_ref, filters_ref, q_hbm, d_out_hbm, *refs):
    group = ctx_count // 2
    arrays = group - 1 if direct else 1
    own_ref, across_ref, received_refs, refs = refs[0], refs[1], refs[2 : 2 + arrays], refs[2 + arrays :]
    dq_hbm, dq_tail_ref, own_near_ref, own_far_ref = refs[:4]
    arrays = group - 1 if direct else 1
    out_refs, refs = refs[4 : 4 + arrays], refs[4 + arrays :]
    same_scr, same_two_scr, kv_scr, conv_scr, dkv_scr, q_scr, qc_scr, do_scr, dq_scr = refs[:9]
    bias_scr, s_scr, dp_scr, rim_scr, q_ref, d_out_ref, dq_ref, sems = refs[9:]
    f32, bf16 = jnp.float32, jnp.bfloat16
    loads = [
        pltpu.make_async_copy(q_hbm, q_ref, sems.at[0]),
        pltpu.make_async_copy(d_out_hbm, d_out_ref, sems.at[1]),
    ]
    for load in loads:
        load.start()
    span = q_ref.shape[1]
    heads = q_ref.shape[2] // LANES
    half_rows = span * ctx_count
    length = 2 * half_rows
    blocks = 2 * ctx_count
    me = lax.axis_index("ctx")
    received = Slots((None,) + received_refs if direct else received_refs, me)
    sent = Slots((own_far_ref,) + out_refs if direct else out_refs, me)
    scale = LANES**-0.5
    log2_scale = scale * 1.4426950408889634
    starts = doc_starts(lengths_ref)

    def fill(index, carry):
        rows = pl.ds(aligned(8 + index * span, 8), span)
        same_scr[rows] = jnp.ones((span, LANES), f32)
        same_two_scr[rows] = jnp.ones((span, LANES), f32)
        return carry

    loop(blocks, fill, 0)
    zeros = jnp.zeros((8, LANES), f32)
    for rows in (slice(0, 8), slice(8 + length, 16 + length)):
        same_scr[rows] = zeros
        same_two_scr[rows] = zeros
        for tensor in range(2):
            kv_scr[tensor, rows] = zeros
    for start in starts:
        same_scr[pl.ds(8 + start, 1)] = zeros[:1]
        same_two_scr[pl.ds(8 + start, 1)] = zeros[:1]
        same_two_scr[pl.ds(9 + start, 1)] = zeros[:1]

    def place(index, block):
        for tensor in range(2):
            lanes = slice(tensor * LANES, (tensor + 1) * LANES)
            kv_scr[tensor, pl.ds(aligned(8 + index * span, 8), span)] = block[:, lanes].astype(f32)

    def clear(index, carry):
        for tensor in range(2):
            kv_scr[tensor, pl.ds(aligned(8 + index * span, 8), span)] = jnp.zeros((span, LANES), f32)
        return carry

    low = me < group

    def place_received(step, carry):
        flip = step + 1
        source = partner(me, flip)
        across = partner(source, group)
        message = received[flip]
        late = blocks - 1 - source
        places = [
            across,
            jnp.where(low, blocks - 1 - across, source),
            jnp.where(low & (source < me), source, late),
        ]
        for at, index in enumerate(places):
            place(index, message[at * span : (at + 1) * span])
        if not direct or flip & (flip + 1) == 0:
            rim_scr[jnp.where(jnp.abs(source - me) == 1, source, across)] = message[3 * span :].astype(f32)
        return carry

    loop(blocks, clear, 0)
    for block_ref, index in ((own_ref, me), (across_ref, partner(me, group))):
        place(index, block_ref[:span])
        place(blocks - 1 - index, block_ref[span : 2 * span])
        rim_scr[index] = block_ref[2 * span :].astype(f32)
    loop(group - 1, place_received, 0, 16 if direct else 1)

    def taps(tensor):
        return [filters_ref[tensor, tap : tap + 1] for tap in range(3)]

    def masks(base, ahead):
        one = same_scr[pl.ds(base + 8 + min(ahead, 1), span)]
        return one, same_two_scr[pl.ds(base + 8 + ahead, span)]

    def convolve_kv(index, carry):
        base = index * span
        one, two = masks(base, 0)
        for tensor in range(2):
            zero_tap, one_tap, two_tap = taps(tensor + 1)
            total = zero_tap * kv_scr[tensor, pl.ds(aligned(base + 8, 8), span)]
            total = total + one * (one_tap * kv_scr[tensor, pl.ds(base + 7, span)])
            total = total + two * (two_tap * kv_scr[tensor, pl.ds(base + 6, span)])
            conv_scr[tensor, pl.ds(aligned(base, 16), span)] = total.astype(bf16)
        return carry

    loop(blocks, convolve_kv, 0)

    middle = me == ctx_count - 1
    rim_rows = rim_scr.shape[1] // 2
    rim_before = rim_scr[jnp.maximum(me - 1, 0)]
    rim_after = rim_scr[jnp.minimum(me + 1, ctx_count - 1)]
    late_rim = jnp.where(middle, rim_after[:rim_rows], rim_after[rim_rows:])
    rims = [rim_before[:rim_rows], late_rim]
    first_place = [me * span, (blocks - 1 - me) * span]

    for load in loads:
        load.wait()
    for half in range(2):
        one, two = masks(first_place[half], 0)
        zero_tap, one_tap, two_tap = taps(0)
        for head in range(heads):
            lanes = slice(head * LANES, (head + 1) * LANES)
            at = 2 * (head // 2)
            q_scr[half, head, 6:8] = rims[half][at : at + 2, (head % 2) * LANES : (head % 2 + 1) * LANES]
            q_scr[half, head, 8:] = q_ref[half, :, lanes].astype(f32)
            total = zero_tap * q_scr[half, head, 8:]
            total = total + one * (one_tap * q_scr[half, head, 7 : 7 + span])
            total = total + two * (two_tap * q_scr[half, head, 6 : 6 + span])
            qc_scr[half, head * span : (head + 1) * span] = total.astype(bf16)
            do_scr[half, head * span : (head + 1) * span] = d_out_ref[half, :, lanes]

    def attend(half, window, first_key, add):
        chunks = 1
        while window // chunks > MAX_CHUNK or window % (16 * chunks):
            chunks += 1
        size = window // chunks
        query = first_place[half] + lax.rem(
            lax.broadcasted_iota(jnp.int32, (1, LANES), 1), jnp.int32(span)
        )
        lowest = jnp.zeros((1, LANES), jnp.int32)
        for start in starts[1:]:
            lowest = jnp.where(query >= start, start, lowest)
        wide = 2 * LANES

        def fill_bias(step, carry):
            places = first_key + step * size + lax.broadcasted_iota(jnp.int32, (size, LANES), 0)
            allowed = (places >= lowest) & (places <= query)
            bias_scr[pl.ds(aligned(step * size, 16), size)] = jnp.where(allowed, 0.0, -1e30)
            return carry

        loop(chunks, fill_bias, 0, 1)
        whole_window = pl.ds(aligned(first_key, 16), window)
        keys_t = conv_scr[0, whole_window].T if chunks == 1 else None
        for at in range(heads * span // wide):
            slot = (half * (heads * span // wide) + at) % s_scr.shape[0]
            cols = slice(at * wide, (at + 1) * wide)
            queries = qc_scr[half, cols]
            grads = do_scr[half, cols]

            def key_rows(step):
                return pl.ds(aligned(first_key + step * size, 16), size)

            def score(step, top):
                keys = conv_scr[0, key_rows(step)]
                scores = lax.dot_general(keys, queries, NT, preferred_element_type=f32)
                bias = bias_scr[pl.ds(aligned(step * size, 16), size)]
                scores = scores + jnp.concatenate([bias, bias], axis=1)
                s_scr[slot, pl.ds(aligned(step * size, 16), size)] = scores
                return jnp.maximum(top, jnp.max(scores, axis=0, keepdims=True))

            top = loop(chunks, score, jnp.full((1, wide), -1e30, f32), 1)

            def weigh(step, carry):
                total, weighted = carry
                rows = pl.ds(aligned(step * size, 16), size)
                weights = jnp.exp2((s_scr[slot, rows] - top) * log2_scale)
                values = conv_scr[1, key_rows(step)]
                prob_grads = lax.dot_general(values, grads, NT, preferred_element_type=f32)
                s_scr[slot, rows] = weights
                dp_scr[slot, rows] = prob_grads
                total = total + jnp.sum(weights, axis=0, keepdims=True)
                weighted = weighted + jnp.sum(weights * prob_grads, axis=0, keepdims=True)
                return total, weighted

            zeros = jnp.zeros((1, wide), f32)
            total, weighted = loop(chunks, weigh, (zeros, zeros), 1)
            inverse = 1.0 / total
            mean = weighted * inverse
            slope = inverse * scale

            def accumulate(step, dq):
                rows = pl.ds(aligned(step * size, 16), size)
                weights = s_scr[slot, rows]
                probs = (weights * inverse).astype(bf16)
                score_grads = (weights * slope * (dp_scr[slot, rows] - mean)).astype(bf16)
                dk = lax.dot_general(score_grads, queries, NN, preferred_element_type=f32)
                dv = lax.dot_general(probs, grads, NN, preferred_element_type=f32)
                target = pl.ds(aligned(first_key + step * size, 16), size)
                for tensor, terms in enumerate((dk, dv)):
                    if add or at:
                        dkv_scr[tensor, target] += terms
                    else:
                        dkv_scr[tensor, target] = terms
                if keys_t is not None:
                    return lax.dot_general(keys_t, score_grads, NN, preferred_element_type=f32)
                keys = conv_scr[0, key_rows(step)]
                return dq + lax.dot_general(keys, score_grads, TN, preferred_element_type=f32)

            dq = loop(chunks, accumulate, jnp.zeros((LANES, wide), f32), 1)
            dq = dq.T
            for part in range(wide // span):
                head = at * (wide // span) + part
                dq_scr[half, head, :span] = dq[part * span : (part + 1) * span]

    for tensor in range(2):
        dkv_scr[tensor, half_rows:] = jnp.zeros((half_rows + 8, LANES), f32)
    attend(0, half_rows, 0, False)
    attend(1, half_rows + span, (ctx_count - 1 - me) * span, True)

    next_rows = jnp.where(middle, dq_scr[1, :, :8], 0.0)
    dq_scr[0, :, span:] = next_rows
    dq_scr[1, :, span:] = jnp.zeros_like(next_rows)
    sums = [jnp.zeros((8, LANES), f32) for _ in range(3)]
    for half in range(2):
        one, two = masks(first_place[half], 0)
        ahead_one = same_scr[pl.ds(first_place[half] + 9, span)]
        ahead_two = same_two_scr[pl.ds(first_place[half] + 10, span)]
        zero_tap, one_tap, two_tap = taps(0)
        for head in range(heads):
            lanes = slice(head * LANES, (head + 1) * LANES)
            grads = dq_scr[half, head, :span]
            out = zero_tap * grads
            out = out + ahead_one * (one_tap * dq_scr[half, head, 1 : 1 + span])
            out = out + ahead_two * (two_tap * dq_scr[half, head, 2 : 2 + span])
            dq_ref[half, :, lanes] = out
            dq_tail_ref[half, :, lanes] = out[span - 8 :]
            sums[0] += fold_rows(grads * q_scr[half, head, 8:])
            sums[1] += fold_rows(grads * one * q_scr[half, head, 7 : 7 + span])
            sums[2] += fold_rows(grads * two * q_scr[half, head, 6 : 6 + span])
    q_sums = [jnp.sum(term, axis=0, keepdims=True) for term in sums]
    store = pltpu.make_async_copy(dq_ref, dq_hbm, sems.at[2])
    store.start()

    def finish_block(index, carry, target, row):
        base = pl.multiple_of(index * span, 8)
        one, two = masks(base, 0)
        ahead_one = same_scr[pl.ds(base + 9, span)]
        ahead_two = same_two_scr[pl.ds(base + 10, span)]
        carry = list(carry)
        for tensor in range(2):
            zero_tap, one_tap, two_tap = taps(tensor + 1)
            own = dkv_scr[tensor, pl.ds(base, span)]
            out = zero_tap * own
            out = out + ahead_one * (one_tap * dkv_scr[tensor, pl.ds(base + 1, span)])
            out = out + ahead_two * (two_tap * dkv_scr[tensor, pl.ds(base + 2, span)])
            lanes = slice(tensor * LANES, (tensor + 1) * LANES)
            target[row : row + span, lanes] = out.astype(target.dtype)
            at = 3 * tensor
            carry[at] += fold_rows(own * kv_scr[tensor, pl.ds(base + 8, span)])
            carry[at + 1] += fold_rows(own * one * kv_scr[tensor, pl.ds(base + 7, span)])
            carry[at + 2] += fold_rows(own * two * kv_scr[tensor, pl.ds(base + 6, span)])
        return tuple(carry)

    def finish(step, carry):
        flip = step + 1
        owner = partner(me, flip)
        far_owner = partner(me, flip + group)
        near_late = blocks - 1 - owner
        places = [
            far_owner,
            jnp.where(low, blocks - 1 - far_owner, owner),
            jnp.where(low & (me > owner), owner, near_late),
        ]
        for at, place in enumerate(places):
            carry = finish_block(place, carry, sent[flip], at * span)
        return carry

    kv_sums = (zeros,) * 6
    for target, index in ((own_far_ref, partner(me, group)), (own_near_ref, me)):
        kv_sums = finish_block(index, kv_sums, target, 0)
        kv_sums = finish_block(blocks - 1 - index, kv_sums, target, span)
    kv_sums = loop(group - 1, finish, kv_sums)
    kv_sums = [jnp.sum(term, axis=0, keepdims=True) for term in kv_sums]

    padding = [jnp.zeros((2, LANES), f32)]
    left = jnp.concatenate(q_sums + kv_sums[:3] + padding, axis=0)
    right = jnp.concatenate([jnp.zeros((3, LANES), f32)] + kv_sums[3:] + padding, axis=0)
    sums_tile = jnp.concatenate([left, right], axis=1)
    sums_pair = jnp.concatenate(split_bits(sums_tile), axis=0)
    own_far_ref[2 * span :] = joined(sums_pair)
    rims = []
    for half in range(2):
        rows = [dq_scr[half, head, :2] for head in range(heads)]
        rows = [jnp.concatenate(rows[at : at + 2], axis=1) for at in range(0, heads, 2)]
        rims.append(jnp.concatenate(rows, axis=0))

    def rim_for(index):
        return jnp.concatenate(split_bits(jnp.where(index < me, rims[0], rims[1])), axis=0)

    def store_rims(step, carry):
        flip = step + 1
        owner = partner(me, flip)
        sent[flip][3 * span : 3 * span + 16] = sums_pair
        if not direct or flip & (flip + 1) == 0:
            across = (flip == group - 1) & (jnp.abs(owner - me) != 1)
            target = jnp.where(across, partner(owner, group), owner)
            sent[flip][3 * span + 16 :] = rim_for(target)
        return carry

    loop(group - 1, store_rims, 0, 16 if direct else 1)
    store.wait()


def merge_kernel(ctx_count, direct, own_near_ref, own_far_ref, *refs):
    received_refs = refs[:-6]
    near_ref, far_ref, half_sums_ref, rims_ref, sums_scr, rim_scr = refs[-6:]
    f32, bf16 = jnp.float32, jnp.bfloat16
    group = ctx_count // 2
    me = lax.axis_index("ctx")
    low = me < group
    received = Slots((own_far_ref,) + received_refs if direct else received_refs, me)
    place = lax.rem(me, jnp.int32(group))
    span = own_near_ref.shape[0] // 2
    rows = 2 * span
    sums_scr[place] = own_far_ref[rows:]
    neighbours = [jnp.minimum(me + 1, ctx_count - 1), jnp.maximum(me - 1, 0)]
    for index in neighbours:
        rim_scr[index] = jnp.zeros(rim_scr.shape[1:], f32)

    def add(step, carry):
        flip = step + 1
        source = partner(me, flip)
        message = received[flip]
        parts = [message[at * span : (at + 1) * span].astype(f32) for at in range(3)]
        near_early, near_late, far_early, far_late = carry
        sums_scr[partner(place, flip)] = joined(message[3 * span : 3 * span + 16])
        if not direct or flip & (flip + 1) == 0:
            rim_scr[source] = joined(message[3 * span + 16 :])
        to_early = low & (source > me)
        zero = jnp.zeros_like(parts[0])
        return (
            near_early + jnp.where(low, jnp.where(to_early, parts[2], zero), parts[1]),
            near_late + jnp.where(to_early, zero, parts[2]),
            far_early + parts[0],
            far_late + jnp.where(low, parts[1], zero),
        )

    init = (own_near_ref[:span], own_near_ref[span:], own_far_ref[:span], own_far_ref[span:rows])
    totals = loop(group - 1, add, init, 16 if direct else 1)
    near_ref[:span] = totals[0]
    near_ref[span:] = totals[1]
    far_ref[:span] = totals[2].astype(bf16)
    far_ref[span:rows] = totals[3].astype(bf16)
    sums = loop(group, lambda index, carry: carry + sums_scr[index], jnp.zeros((8, 2 * LANES), f32))
    pair = jnp.concatenate(split_bits(sums), axis=0)
    half_sums_ref[...] = joined(pair)
    far_ref[rows : rows + 16] = pair
    far_ref[rows + 16 :] = received[group - 1][3 * span + 16 :]
    for at, index in enumerate(neighbours):
        rims_ref[at] = rim_scr[index]


def sums_kernel(span, half_sums_ref, far_ref, out_ref):
    sums = half_sums_ref[...] + joined(far_ref[2 * span : 2 * span + 16])
    out_ref[0] = sums[0:3, :LANES]
    out_ref[1] = sums[3:6, :LANES]
    out_ref[2] = sums[3:6, LANES:]


def finish_kernel(
    ctx_count, lengths_ref, filters_ref, dq_in_hbm, tail_ref, near_ref, far_ref, rims_ref, *refs
):
    dq_hbm, dk_hbm, dv_hbm, dq_ref, dk_ref, dv_ref, sems = refs
    f32 = jnp.float32
    group = ctx_count // 2
    span = dk_ref.shape[1]
    me = lax.axis_index("ctx")
    starts = doc_starts(lengths_ref)
    blocks = 2 * ctx_count

    total = near_ref[...] + far_ref[: 2 * span].astype(f32)
    for half in range(2):
        dk_ref[half] = total[half * span : (half + 1) * span, :LANES]
        dv_ref[half] = total[half * span : (half + 1) * span, LANES:]
    stores = [
        pltpu.make_async_copy(dk_ref, dk_hbm, sems.at[0]),
        pltpu.make_async_copy(dv_ref, dv_hbm, sems.at[1]),
        pltpu.make_async_copy(dq_ref, dq_hbm.at[:, pl.ds(span - 8, 8)], sems.at[2]),
    ]
    for store in stores[:2]:
        store.start()

    def same(place):
        cut = place >= blocks * span
        for start in starts:
            cut = cut | (place == start)
        return jnp.where(cut, 0.0, 1.0).astype(f32)

    heads = dq_ref.shape[2] // LANES
    taps = [jnp.concatenate([filters_ref[0, tap : tap + 1]] * heads, axis=1) for tap in range(3)]
    row = lax.broadcasted_iota(jnp.int32, dq_ref.shape[1:], 0)
    far_rim = joined(far_ref[2 * span + 16 :])
    crosses = [me == group - 1, me == group]
    first_place = [me * span, (blocks - 1 - me) * span]
    present = [me < ctx_count - 1, me > 0]
    for half in range(2):
        rim = jnp.where(crosses[half], far_rim, rims_ref[half])
        rows = jnp.concatenate([rim[2 * at : 2 * at + 2] for at in range(rim.shape[0] // 2)], axis=1)
        end = first_place[half] + span
        zero, one, two = same(end - 1), same(end), same(end + 1)
        one = jnp.where(present[half], one, 0.0)
        last_but_one = (zero * one) * (taps[2] * rows[0:1])
        last = one * (taps[1] * rows[0:1]) + (one * two) * (taps[2] * rows[1:2])
        extra = jnp.where(row == 6, last_but_one, jnp.where(row == 7, last, 0.0))
        dq_ref[half] = tail_ref[half] + extra
    stores[2].start()
    for store in stores:
        store.wait()


def shards(q_pre, k_pre, value_before_filter, d_out, filters, doc_lengths):
    f32, bf16 = jnp.float32, jnp.bfloat16
    ctx_count = lax.axis_size("ctx")
    span, width = q_pre.shape[1:]
    length = 2 * span * ctx_count
    rim = 4 * width // (2 * LANES)
    vmem = pl.BlockSpec(memory_space=pltpu.VMEM)
    smem = pl.BlockSpec(memory_space=pltpu.SMEM)
    hbm = pl.BlockSpec(memory_space=pltpu.HBM)

    group = ctx_count // 2
    direct = group <= MAX_DIRECT
    halves = [[half * group + at for at in range(group)] for half in range(2)]
    msg_rows = 2 * span + rim

    def whole(shape):
        return pl.BlockSpec(shape, lambda i: (0,) * len(shape))

    def in_hbm(array):
        return pltpu.with_memory_space_constraint(array, pltpu.HBM)

    def flipped(array, flip):
        return lax.ppermute(array, "ctx", [(i, i ^ flip) for i in range(ctx_count)])

    def delivered(arrays):
        if direct:
            return [flipped(array, step + 1) for step, array in enumerate(arrays)]
        return [lax.all_to_all(arrays[0], "ctx", 0, 0, axis_index_groups=halves, tiled=True)]

    packed = pl.pallas_call(
        pack_kernel,
        grid=(1,),
        out_shape=jax.ShapeDtypeStruct((msg_rows, 2 * LANES), bf16),
        in_specs=[
            whole(k_pre.shape),
            whole(k_pre.shape),
            pl.BlockSpec((2, TAIL, width), lambda i: (0, span // TAIL - 1, 0)),
        ],
        out_specs=whole((msg_rows, 2 * LANES)),
        compiler_params=pltpu.CompilerParams(vmem_limit_bytes=4 * MIB),
        name="pack",
    )(*[in_hbm(array) for array in (k_pre, value_before_filter, q_pre)])
    across = flipped(packed, group)
    if direct:
        relay_shapes = [
            (3 * span + (rim if flip & (flip + 1) == 0 else 0), 2 * LANES) for flip in range(1, group)
        ]
    else:
        relay_shapes = [(group, 3 * span + rim, 2 * LANES)]
    relayed = pl.pallas_call(
        functools.partial(relay_kernel, ctx_count, direct),
        out_shape=[jax.ShapeDtypeStruct(shape, bf16) for shape in relay_shapes],
        in_specs=[vmem, vmem],
        out_specs=[vmem] * len(relay_shapes),
        compiler_params=pltpu.CompilerParams(vmem_limit_bytes=(4 if direct else 40) * MIB),
        name="relay",
    )(packed, across)
    received = [packed, across] + delivered(relayed)

    window = span * ctx_count + span
    if direct:
        sent_shapes = [
            (3 * span + (32 if flip & (flip + 1) == 0 else 16), 2 * LANES) for flip in range(1, group)
        ]
    else:
        sent_shapes = [(group, 3 * span + 32, 2 * LANES)]
    slots = 4 if direct else 1
    heads = width // LANES
    scratch = [
        pltpu.VMEM((length + 16, LANES), f32),
        pltpu.VMEM((length + 16, LANES), f32),
        pltpu.VMEM((2, length + 16, LANES), f32),
        pltpu.VMEM((2, length, LANES), bf16),
        pltpu.VMEM((2, length + 8, LANES), f32),
        pltpu.VMEM((2, heads, span + 8, LANES), f32),
        pltpu.VMEM((2, span * heads, LANES), bf16),
        pltpu.VMEM((2, span * heads, LANES), bf16),
        pltpu.VMEM((2, heads, span + 8, LANES), f32),
        pltpu.VMEM((window, LANES), f32),
        pltpu.VMEM((slots, window, 2 * LANES), f32),
        pltpu.VMEM((slots, window, 2 * LANES), f32),
        pltpu.VMEM((ctx_count, rim, 2 * LANES), f32),
        pltpu.VMEM(q_pre.shape, bf16),
        pltpu.VMEM(q_pre.shape, bf16),
        pltpu.VMEM(q_pre.shape, f32),
        pltpu.SemaphoreType.DMA((3,)),
    ]
    own_shapes = [(2 * span, 2 * LANES), (2 * span + 8, 2 * LANES)]
    d_q_main, d_q_tail, own_near, own_far, *sent = pl.pallas_call(
        functools.partial(grads_kernel, ctx_count, direct),
        out_shape=[jax.ShapeDtypeStruct(q_pre.shape, f32)]
        + [jax.ShapeDtypeStruct(shape, f32) for shape in [(2, 8, width)] + own_shapes]
        + [jax.ShapeDtypeStruct(shape, bf16) for shape in sent_shapes],
        in_specs=[smem, vmem, hbm, hbm] + [vmem] * len(received),
        out_specs=[hbm] + [vmem] * (3 + len(sent_shapes)),
        scratch_shapes=scratch,
        compiler_params=pltpu.CompilerParams(vmem_limit_bytes=(20 if direct else 62) * MIB),
        name="grads",
    )(doc_lengths, filters, in_hbm(q_pre), in_hbm(d_out), *received)
    half_terms = delivered(sent)
    merged_shapes = [
        jax.ShapeDtypeStruct((2 * span, 2 * LANES), f32),
        jax.ShapeDtypeStruct((2 * span + 32, 2 * LANES), bf16),
        jax.ShapeDtypeStruct((8, 2 * LANES), f32),
        jax.ShapeDtypeStruct((2, rim // 2, 2 * LANES), f32),
    ]
    near, far, half_sums, rims = pl.pallas_call(
        functools.partial(merge_kernel, ctx_count, direct),
        out_shape=merged_shapes,
        in_specs=[vmem] * (2 + len(half_terms)),
        out_specs=[vmem] * len(merged_shapes),
        scratch_shapes=[
            pltpu.VMEM((group, 8, 2 * LANES), f32),
            pltpu.VMEM((ctx_count, rim // 2, 2 * LANES), f32),
        ],
        compiler_params=pltpu.CompilerParams(vmem_limit_bytes=(4 if direct else 40) * MIB),
        name="merge",
    )(own_near, own_far, *half_terms)
    from_half = flipped(far, group)

    sums = pl.pallas_call(
        functools.partial(sums_kernel, span),
        out_shape=jax.ShapeDtypeStruct(filters.shape, f32),
        in_specs=[vmem, vmem],
        out_specs=vmem,
        compiler_params=pltpu.CompilerParams(vmem_limit_bytes=2 * MIB),
        name="sums",
    )(half_sums, from_half)
    count = lax.axis_size("tp")
    level = [sums] + [
        lax.ppermute(sums, "tp", [(i, i ^ flip) for i in range(count)]) for flip in range(1, count)
    ]

    d_q_pre, d_k_pre, d_v_pre = pl.pallas_call(
        functools.partial(finish_kernel, ctx_count),
        out_shape=(
            jax.ShapeDtypeStruct(q_pre.shape, f32),
            jax.ShapeDtypeStruct(k_pre.shape, f32),
            jax.ShapeDtypeStruct(k_pre.shape, f32),
        ),
        in_specs=[smem, vmem, hbm, vmem, vmem, vmem, vmem],
        out_specs=(hbm, hbm, hbm),
        scratch_shapes=[
            pltpu.VMEM((2, 8, width), f32),
            pltpu.VMEM(k_pre.shape, f32),
            pltpu.VMEM(k_pre.shape, f32),
            pltpu.SemaphoreType.DMA((3,)),
        ],
        input_output_aliases={2: 0},
        compiler_params=pltpu.CompilerParams(vmem_limit_bytes=4 * MIB),
        name="finish",
    )(doc_lengths, filters, d_q_main, d_q_tail, near, from_half, rims)

    while len(level) > 1:
        level = [level[at] + level[at + 1] for at in range(0, len(level), 2)]
    d_filters = level[0]
    return (d_q_pre, d_k_pre, d_v_pre, d_filters)


def solution(mesh):
    split = P(None, "ctx", "tp")
    return jax.shard_map(
        shards,
        mesh=mesh,
        in_specs=(split, split, split, split, P(), P()),
        out_specs=(split, split, split, P()),
        check_vma=False,
    )
```

```python
import functools

import jax
import jax.numpy as jnp
import numpy as np
from jax import lax
from jax.experimental import pallas as pl
from jax.experimental.pallas import tpu as pltpu
from jax.sharding import PartitionSpec as P

LANES = 128
NT = (((1,), (1,)), ((), ()))
NN = (((1,), (0,)), ((), ()))
TN = (((0,), (0,)), ((), ()))
TAIL = 16
MAX_CHUNK = 640
MAX_DIRECT = 4
MIB = 1 << 20


def loop(count, body, init, unrolled=16):
    if count <= unrolled:
        for step in range(count):
            init = body(step, init)
        return init
    return lax.fori_loop(0, count, body, init)


def aligned(start, multiple):
    return start if isinstance(start, int) else pl.multiple_of(start, multiple)


def doc_starts(lengths_ref):
    starts = [jnp.int32(0)]
    for index in range(lengths_ref.shape[0] - 1):
        starts.append(starts[-1] + lengths_ref[index])
    return starts


def fold_rows(terms):
    rows, lanes = terms.shape
    return jnp.sum(terms.reshape(rows // 8, 8, lanes), axis=0)


def split_bits(values):
    high = values.astype(jnp.bfloat16)
    low = (values - high.astype(jnp.float32)).astype(jnp.bfloat16)
    return high, low


def joined(pair):
    rows = pair.shape[0] // 2
    pair = pair.astype(jnp.float32)
    return pair[:rows] + pair[rows:]


class Slots:
    def __init__(self, refs, me):
        self.refs, self.me = refs, me

    def __getitem__(self, flip):
        if len(self.refs) == 1:
            place = lax.rem(self.me, jnp.int32(self.refs[0].shape[0]))
            return self.refs[0].at[partner(place, flip)]
        return self.refs[flip]


def partner(me, flip):
    return lax.bitwise_xor(me, jnp.int32(flip))


def pack_kernel(k_ref, v_ref, q_ref, out_ref):
    span = k_ref.shape[1]
    kv = jnp.concatenate([k_ref[...], v_ref[...]], axis=2).reshape(2 * span, 2 * LANES)
    tails = []
    for half in range(2):
        last = q_ref[half].astype(jnp.float32)[TAIL - 2 :]
        tails += [last[:, at : at + 2 * LANES] for at in range(0, last.shape[1], 2 * LANES)]
    out_ref[: 2 * span] = kv
    out_ref[2 * span :] = jnp.concatenate(tails, axis=0).astype(jnp.bfloat16)


def grads_kernel(ctx_count, direct, lengths_ref, filters_ref, q_hbm, d_out_hbm, *refs):
    group = ctx_count // 2
    arrays = group if direct else 1
    near_in, far_in, refs = refs[:arrays], refs[arrays : 2 * arrays], refs[2 * arrays :]
    dq_hbm, dq_tail_ref, own_near_ref, own_far_ref = refs[:4]
    arrays = group - 1 if direct else 1
    out_refs, refs = refs[4 : 4 + arrays], refs[4 + arrays :]
    same_scr, same_two_scr, kv_scr, conv_scr, dkv_scr, q_scr, qc_scr, do_scr, dq_scr = refs[:9]
    bias_scr, s_scr, dp_scr, rim_scr, q_ref, d_out_ref, dq_ref, sems = refs[9:]
    f32, bf16 = jnp.float32, jnp.bfloat16
    loads = [
        pltpu.make_async_copy(q_hbm, q_ref, sems.at[0]),
        pltpu.make_async_copy(d_out_hbm, d_out_ref, sems.at[1]),
    ]
    for load in loads:
        load.start()
    span = q_ref.shape[1]
    heads = q_ref.shape[2] // LANES
    half_rows = span * ctx_count
    length = 2 * half_rows
    blocks = 2 * ctx_count
    me = lax.axis_index("ctx")
    near_in, far_in = Slots(near_in, me), Slots(far_in, me)
    sent = Slots((own_far_ref,) + out_refs if direct else out_refs, me)
    scale = LANES**-0.5
    log2_scale = scale * 1.4426950408889634
    starts = doc_starts(lengths_ref)

    def fill(index, carry):
        rows = pl.ds(aligned(8 + index * span, 8), span)
        same_scr[rows] = jnp.ones((span, LANES), f32)
        same_two_scr[rows] = jnp.ones((span, LANES), f32)
        return carry

    loop(blocks, fill, 0)
    zeros = jnp.zeros((8, LANES), f32)
    for rows in (slice(0, 8), slice(8 + length, 16 + length)):
        same_scr[rows] = zeros
        same_two_scr[rows] = zeros
        for tensor in range(2):
            kv_scr[tensor, rows] = zeros
    for start in starts:
        same_scr[pl.ds(8 + start, 1)] = zeros[:1]
        same_two_scr[pl.ds(8 + start, 1)] = zeros[:1]
        same_two_scr[pl.ds(9 + start, 1)] = zeros[:1]

    def place_blocks(flip, carry):
        for message, index in (
            (near_in[flip], partner(me, flip)),
            (far_in[flip], partner(me, flip + group)),
        ):
            early = aligned(8 + index * span, 8)
            late = aligned(8 + (blocks - 1 - index) * span, 8)
            for tensor in range(2):
                lanes = slice(tensor * LANES, (tensor + 1) * LANES)
                kv_scr[tensor, pl.ds(early, span)] = message[:span, lanes].astype(f32)
                kv_scr[tensor, pl.ds(late, span)] = message[span : 2 * span, lanes].astype(f32)
            rim_scr[index] = message[2 * span :].astype(f32)
        return carry

    loop(group, place_blocks, 0)

    def taps(tensor):
        return [filters_ref[tensor, tap : tap + 1] for tap in range(3)]

    def masks(base, ahead):
        one = same_scr[pl.ds(base + 8 + min(ahead, 1), span)]
        return one, same_two_scr[pl.ds(base + 8 + ahead, span)]

    def convolve_kv(index, carry):
        base = index * span
        one, two = masks(base, 0)
        for tensor in range(2):
            zero_tap, one_tap, two_tap = taps(tensor + 1)
            total = zero_tap * kv_scr[tensor, pl.ds(aligned(base + 8, 8), span)]
            total = total + one * (one_tap * kv_scr[tensor, pl.ds(base + 7, span)])
            total = total + two * (two_tap * kv_scr[tensor, pl.ds(base + 6, span)])
            conv_scr[tensor, pl.ds(aligned(base, 16), span)] = total.astype(bf16)
        return carry

    loop(blocks, convolve_kv, 0)

    middle = me == ctx_count - 1
    rim_rows = rim_scr.shape[1] // 2
    rim_before = rim_scr[jnp.maximum(me - 1, 0)]
    rim_after = rim_scr[jnp.minimum(me + 1, ctx_count - 1)]
    late_rim = jnp.where(middle, rim_after[:rim_rows], rim_after[rim_rows:])
    rims = [rim_before[:rim_rows], late_rim]
    first_place = [me * span, (blocks - 1 - me) * span]

    for load in loads:
        load.wait()
    for half in range(2):
        one, two = masks(first_place[half], 0)
        zero_tap, one_tap, two_tap = taps(0)
        for head in range(heads):
            lanes = slice(head * LANES, (head + 1) * LANES)
            at = 2 * (head // 2)
            q_scr[half, head, 6:8] = rims[half][at : at + 2, (head % 2) * LANES : (head % 2 + 1) * LANES]
            q_scr[half, head, 8:] = q_ref[half, :, lanes].astype(f32)
            total = zero_tap * q_scr[half, head, 8:]
            total = total + one * (one_tap * q_scr[half, head, 7 : 7 + span])
            total = total + two * (two_tap * q_scr[half, head, 6 : 6 + span])
            qc_scr[half, head * span : (head + 1) * span] = total.astype(bf16)
            do_scr[half, head * span : (head + 1) * span] = d_out_ref[half, :, lanes]

    def attend(half, window, first_key, add):
        chunks = 1
        while window // chunks > MAX_CHUNK or window % (16 * chunks):
            chunks += 1
        size = window // chunks
        query = first_place[half] + lax.rem(
            lax.broadcasted_iota(jnp.int32, (1, LANES), 1), jnp.int32(span)
        )
        lowest = jnp.zeros((1, LANES), jnp.int32)
        for start in starts[1:]:
            lowest = jnp.where(query >= start, start, lowest)
        wide = 2 * LANES

        def fill_bias(step, carry):
            places = first_key + step * size + lax.broadcasted_iota(jnp.int32, (size, LANES), 0)
            allowed = (places >= lowest) & (places <= query)
            bias_scr[pl.ds(aligned(step * size, 16), size)] = jnp.where(allowed, 0.0, -1e30)
            return carry

        loop(chunks, fill_bias, 0, 1)
        whole_window = pl.ds(aligned(first_key, 16), window)
        keys_t = conv_scr[0, whole_window].T if chunks == 1 else None
        for at in range(heads * span // wide):
            slot = (half * (heads * span // wide) + at) % s_scr.shape[0]
            cols = slice(at * wide, (at + 1) * wide)
            queries = qc_scr[half, cols]
            grads = do_scr[half, cols]

            def key_rows(step):
                return pl.ds(aligned(first_key + step * size, 16), size)

            def score(step, top):
                keys = conv_scr[0, key_rows(step)]
                scores = lax.dot_general(keys, queries, NT, preferred_element_type=f32)
                bias = bias_scr[pl.ds(aligned(step * size, 16), size)]
                scores = scores + jnp.concatenate([bias, bias], axis=1)
                s_scr[slot, pl.ds(aligned(step * size, 16), size)] = scores
                return jnp.maximum(top, jnp.max(scores, axis=0, keepdims=True))

            top = loop(chunks, score, jnp.full((1, wide), -1e30, f32), 1)

            def weigh(step, carry):
                total, weighted = carry
                rows = pl.ds(aligned(step * size, 16), size)
                weights = jnp.exp2((s_scr[slot, rows] - top) * log2_scale)
                values = conv_scr[1, key_rows(step)]
                prob_grads = lax.dot_general(values, grads, NT, preferred_element_type=f32)
                s_scr[slot, rows] = weights
                dp_scr[slot, rows] = prob_grads
                total = total + jnp.sum(weights, axis=0, keepdims=True)
                weighted = weighted + jnp.sum(weights * prob_grads, axis=0, keepdims=True)
                return total, weighted

            zeros = jnp.zeros((1, wide), f32)
            total, weighted = loop(chunks, weigh, (zeros, zeros), 1)
            inverse = 1.0 / total
            mean = weighted * inverse
            slope = inverse * scale

            def accumulate(step, dq):
                rows = pl.ds(aligned(step * size, 16), size)
                weights = s_scr[slot, rows]
                probs = (weights * inverse).astype(bf16)
                score_grads = (weights * slope * (dp_scr[slot, rows] - mean)).astype(bf16)
                dk = lax.dot_general(score_grads, queries, NN, preferred_element_type=f32)
                dv = lax.dot_general(probs, grads, NN, preferred_element_type=f32)
                target = pl.ds(aligned(first_key + step * size, 16), size)
                for tensor, terms in enumerate((dk, dv)):
                    if add or at:
                        dkv_scr[tensor, target] += terms
                    else:
                        dkv_scr[tensor, target] = terms
                if keys_t is not None:
                    return lax.dot_general(keys_t, score_grads, NN, preferred_element_type=f32)
                keys = conv_scr[0, key_rows(step)]
                return dq + lax.dot_general(keys, score_grads, TN, preferred_element_type=f32)

            dq = loop(chunks, accumulate, jnp.zeros((LANES, wide), f32), 1)
            dq = dq.T
            for part in range(wide // span):
                head = at * (wide // span) + part
                dq_scr[half, head, :span] = dq[part * span : (part + 1) * span]

    for tensor in range(2):
        dkv_scr[tensor, half_rows:] = jnp.zeros((half_rows + 8, LANES), f32)
    attend(0, half_rows, 0, False)
    attend(1, half_rows + span, (ctx_count - 1 - me) * span, True)

    next_rows = jnp.where(middle, dq_scr[1, :, :8], 0.0)
    dq_scr[0, :, span:] = next_rows
    dq_scr[1, :, span:] = jnp.zeros_like(next_rows)
    sums = [jnp.zeros((8, LANES), f32) for _ in range(3)]
    for half in range(2):
        one, two = masks(first_place[half], 0)
        ahead_one = same_scr[pl.ds(first_place[half] + 9, span)]
        ahead_two = same_two_scr[pl.ds(first_place[half] + 10, span)]
        zero_tap, one_tap, two_tap = taps(0)
        for head in range(heads):
            lanes = slice(head * LANES, (head + 1) * LANES)
            grads = dq_scr[half, head, :span]
            out = zero_tap * grads
            out = out + ahead_one * (one_tap * dq_scr[half, head, 1 : 1 + span])
            out = out + ahead_two * (two_tap * dq_scr[half, head, 2 : 2 + span])
            dq_ref[half, :, lanes] = out
            dq_tail_ref[half, :, lanes] = out[span - 8 :]
            sums[0] += fold_rows(grads * q_scr[half, head, 8:])
            sums[1] += fold_rows(grads * one * q_scr[half, head, 7 : 7 + span])
            sums[2] += fold_rows(grads * two * q_scr[half, head, 6 : 6 + span])
    q_sums = [jnp.sum(term, axis=0, keepdims=True) for term in sums]
    store = pltpu.make_async_copy(dq_ref, dq_hbm, sems.at[2])
    store.start()

    def finish_block(index, carry, target, row):
        base = pl.multiple_of(index * span, 8)
        one, two = masks(base, 0)
        ahead_one = same_scr[pl.ds(base + 9, span)]
        ahead_two = same_two_scr[pl.ds(base + 10, span)]
        carry = list(carry)
        for tensor in range(2):
            zero_tap, one_tap, two_tap = taps(tensor + 1)
            own = dkv_scr[tensor, pl.ds(base, span)]
            out = zero_tap * own
            out = out + ahead_one * (one_tap * dkv_scr[tensor, pl.ds(base + 1, span)])
            out = out + ahead_two * (two_tap * dkv_scr[tensor, pl.ds(base + 2, span)])
            lanes = slice(tensor * LANES, (tensor + 1) * LANES)
            target[row : row + span, lanes] = out.astype(target.dtype)
            at = 3 * tensor
            carry[at] += fold_rows(own * kv_scr[tensor, pl.ds(base + 8, span)])
            carry[at + 1] += fold_rows(own * one * kv_scr[tensor, pl.ds(base + 7, span)])
            carry[at + 2] += fold_rows(own * two * kv_scr[tensor, pl.ds(base + 6, span)])
        return tuple(carry)

    low = me < group

    def finish(step, carry):
        flip = step + 1
        owner = partner(me, flip)
        far_owner = partner(me, flip + group)
        near_late = blocks - 1 - owner
        places = [
            far_owner,
            jnp.where(low, blocks - 1 - far_owner, owner),
            jnp.where(low & (me > owner), owner, near_late),
        ]
        for at, place in enumerate(places):
            carry = finish_block(place, carry, sent[flip], at * span)
        return carry

    kv_sums = (zeros,) * 6
    for target, index in ((own_far_ref, partner(me, group)), (own_near_ref, me)):
        kv_sums = finish_block(index, kv_sums, target, 0)
        kv_sums = finish_block(blocks - 1 - index, kv_sums, target, span)
    kv_sums = loop(group - 1, finish, kv_sums)
    kv_sums = [jnp.sum(term, axis=0, keepdims=True) for term in kv_sums]

    padding = [jnp.zeros((2, LANES), f32)]
    left = jnp.concatenate(q_sums + kv_sums[:3] + padding, axis=0)
    right = jnp.concatenate([jnp.zeros((3, LANES), f32)] + kv_sums[3:] + padding, axis=0)
    sums_tile = jnp.concatenate([left, right], axis=1)
    sums_pair = jnp.concatenate(split_bits(sums_tile), axis=0)
    own_far_ref[2 * span :] = joined(sums_pair)
    rims = []
    for half in range(2):
        rows = [dq_scr[half, head, :2] for head in range(heads)]
        rows = [jnp.concatenate(rows[at : at + 2], axis=1) for at in range(0, heads, 2)]
        rims.append(jnp.concatenate(rows, axis=0))

    def rim_for(index):
        return jnp.concatenate(split_bits(jnp.where(index < me, rims[0], rims[1])), axis=0)

    def store_rims(step, carry):
        flip = step + 1
        owner = partner(me, flip)
        sent[flip][3 * span : 3 * span + 16] = sums_pair
        if not direct or flip & (flip + 1) == 0:
            across = (flip == group - 1) & (jnp.abs(owner - me) != 1)
            target = jnp.where(across, partner(owner, group), owner)
            sent[flip][3 * span + 16 :] = rim_for(target)
        return carry

    loop(group - 1, store_rims, 0, 16 if direct else 1)
    store.wait()


def merge_kernel(ctx_count, direct, own_near_ref, own_far_ref, *refs):
    received_refs = refs[:-6]
    near_ref, far_ref, half_sums_ref, rims_ref, sums_scr, rim_scr = refs[-6:]
    f32, bf16 = jnp.float32, jnp.bfloat16
    group = ctx_count // 2
    me = lax.axis_index("ctx")
    low = me < group
    received = Slots((own_far_ref,) + received_refs if direct else received_refs, me)
    place = lax.rem(me, jnp.int32(group))
    span = own_near_ref.shape[0] // 2
    rows = 2 * span
    sums_scr[place] = own_far_ref[rows:]
    neighbours = [jnp.minimum(me + 1, ctx_count - 1), jnp.maximum(me - 1, 0)]
    for index in neighbours:
        rim_scr[index] = jnp.zeros(rim_scr.shape[1:], f32)

    def add(step, carry):
        flip = step + 1
        source = partner(me, flip)
        message = received[flip]
        parts = [message[at * span : (at + 1) * span].astype(f32) for at in range(3)]
        near_early, near_late, far_early, far_late = carry
        sums_scr[partner(place, flip)] = joined(message[3 * span : 3 * span + 16])
        if not direct or flip & (flip + 1) == 0:
            rim_scr[source] = joined(message[3 * span + 16 :])
        to_early = low & (source > me)
        zero = jnp.zeros_like(parts[0])
        return (
            near_early + jnp.where(low, jnp.where(to_early, parts[2], zero), parts[1]),
            near_late + jnp.where(to_early, zero, parts[2]),
            far_early + parts[0],
            far_late + jnp.where(low, parts[1], zero),
        )

    init = (own_near_ref[:span], own_near_ref[span:], own_far_ref[:span], own_far_ref[span:rows])
    totals = loop(group - 1, add, init, 16 if direct else 1)
    near_ref[:span] = totals[0]
    near_ref[span:] = totals[1]
    far_ref[:span] = totals[2].astype(bf16)
    far_ref[span:rows] = totals[3].astype(bf16)
    sums = loop(group, lambda index, carry: carry + sums_scr[index], jnp.zeros((8, 2 * LANES), f32))
    half_sums_ref[...] = sums
    far_ref[rows:] = received[group - 1][3 * span + 16 :]
    for at, index in enumerate(neighbours):
        rims_ref[at] = rim_scr[index]


def tree_sum_kernel(*refs):
    level = [ref[...] for ref in refs[:-1]]
    while len(level) > 1:
        level = [level[at] + level[at + 1] for at in range(0, len(level), 2)]
    refs[-1][...] = level[0]


def finish_kernel(
    ctx_count, lengths_ref, filters_ref, dq_in_hbm, tail_ref, near_ref, far_ref, rims_ref, *refs
):
    sums_ref, across_sums_ref, dq_hbm, dk_hbm, dv_hbm, d_filters_hbm = refs[:6]
    dq_ref, dk_ref, dv_ref, d_filters_ref, sems = refs[6:]
    f32 = jnp.float32
    group = ctx_count // 2
    span = dk_ref.shape[1]
    me = lax.axis_index("ctx")
    starts = doc_starts(lengths_ref)
    blocks = 2 * ctx_count

    total = near_ref[...] + far_ref[: 2 * span].astype(f32)
    for half in range(2):
        dk_ref[half] = total[half * span : (half + 1) * span, :LANES]
        dv_ref[half] = total[half * span : (half + 1) * span, LANES:]
    stores = [
        pltpu.make_async_copy(dk_ref, dk_hbm, sems.at[0]),
        pltpu.make_async_copy(dv_ref, dv_hbm, sems.at[1]),
        pltpu.make_async_copy(d_filters_ref, d_filters_hbm, sems.at[2]),
        pltpu.make_async_copy(dq_ref, dq_hbm.at[:, pl.ds(span - 8, 8)], sems.at[3]),
    ]
    sums = sums_ref[...] + across_sums_ref[...]
    d_filters_ref[0] = sums[0:3, :LANES]
    d_filters_ref[1] = sums[3:6, :LANES]
    d_filters_ref[2] = sums[3:6, LANES:]
    for store in stores[:3]:
        store.start()

    def same(place):
        cut = place >= blocks * span
        for start in starts:
            cut = cut | (place == start)
        return jnp.where(cut, 0.0, 1.0).astype(f32)

    heads = dq_ref.shape[2] // LANES
    taps = [jnp.concatenate([filters_ref[0, tap : tap + 1]] * heads, axis=1) for tap in range(3)]
    row = lax.broadcasted_iota(jnp.int32, dq_ref.shape[1:], 0)
    far_rim = joined(far_ref[2 * span :])
    crosses = [me == group - 1, me == group]
    first_place = [me * span, (blocks - 1 - me) * span]
    present = [me < ctx_count - 1, me > 0]
    for half in range(2):
        rim = jnp.where(crosses[half], far_rim, rims_ref[half])
        rows = jnp.concatenate([rim[2 * at : 2 * at + 2] for at in range(rim.shape[0] // 2)], axis=1)
        end = first_place[half] + span
        zero, one, two = same(end - 1), same(end), same(end + 1)
        one = jnp.where(present[half], one, 0.0)
        last_but_one = (zero * one) * (taps[2] * rows[0:1])
        last = one * (taps[1] * rows[0:1]) + (one * two) * (taps[2] * rows[1:2])
        extra = jnp.where(row == 6, last_but_one, jnp.where(row == 7, last, 0.0))
        dq_ref[half] = tail_ref[half] + extra
    stores[3].start()
    for store in stores:
        store.wait()


def shards(q_pre, k_pre, value_before_filter, d_out, filters, doc_lengths):
    f32, bf16 = jnp.float32, jnp.bfloat16
    ctx_count = lax.axis_size("ctx")
    span, width = q_pre.shape[1:]
    length = 2 * span * ctx_count
    rim = 4 * width // (2 * LANES)
    vmem = pl.BlockSpec(memory_space=pltpu.VMEM)
    smem = pl.BlockSpec(memory_space=pltpu.SMEM)
    hbm = pl.BlockSpec(memory_space=pltpu.HBM)

    group = ctx_count // 2
    direct = group <= MAX_DIRECT
    halves = [[half * group + at for at in range(group)] for half in range(2)]
    msg_rows = 2 * span + rim

    def whole(shape):
        return pl.BlockSpec(shape, lambda i: (0,) * len(shape))

    def in_hbm(array):
        return pltpu.with_memory_space_constraint(array, pltpu.HBM)

    def flipped(array, flip):
        return lax.ppermute(array, "ctx", [(i, i ^ flip) for i in range(ctx_count)])

    def gathered(array):
        if direct:
            return [array] + [flipped(array, flip) for flip in range(1, group)]
        return [lax.all_gather(array, "ctx", axis_index_groups=halves)]

    def delivered(arrays):
        if direct:
            return [flipped(array, step + 1) for step, array in enumerate(arrays)]
        return [lax.all_to_all(arrays[0], "ctx", 0, 0, axis_index_groups=halves, tiled=True)]

    packed = pl.pallas_call(
        pack_kernel,
        grid=(1,),
        out_shape=jax.ShapeDtypeStruct((msg_rows, 2 * LANES), bf16),
        in_specs=[
            whole(k_pre.shape),
            whole(k_pre.shape),
            pl.BlockSpec((2, TAIL, width), lambda i: (0, span // TAIL - 1, 0)),
        ],
        out_specs=whole((msg_rows, 2 * LANES)),
        compiler_params=pltpu.CompilerParams(vmem_limit_bytes=4 * MIB),
        name="pack",
    )(*[in_hbm(array) for array in (k_pre, value_before_filter, q_pre)])
    across = flipped(packed, group)
    received = gathered(packed) + gathered(across)

    window = span * ctx_count + span
    if direct:
        sent_shapes = [
            (3 * span + (32 if flip & (flip + 1) == 0 else 16), 2 * LANES) for flip in range(1, group)
        ]
    else:
        sent_shapes = [(group, 3 * span + 32, 2 * LANES)]
    slots = 4 if direct else 1
    heads = width // LANES
    scratch = [
        pltpu.VMEM((length + 16, LANES), f32),
        pltpu.VMEM((length + 16, LANES), f32),
        pltpu.VMEM((2, length + 16, LANES), f32),
        pltpu.VMEM((2, length, LANES), bf16),
        pltpu.VMEM((2, length + 8, LANES), f32),
        pltpu.VMEM((2, heads, span + 8, LANES), f32),
        pltpu.VMEM((2, span * heads, LANES), bf16),
        pltpu.VMEM((2, span * heads, LANES), bf16),
        pltpu.VMEM((2, heads, span + 8, LANES), f32),
        pltpu.VMEM((window, LANES), f32),
        pltpu.VMEM((slots, window, 2 * LANES), f32),
        pltpu.VMEM((slots, window, 2 * LANES), f32),
        pltpu.VMEM((ctx_count, rim, 2 * LANES), f32),
        pltpu.VMEM(q_pre.shape, bf16),
        pltpu.VMEM(q_pre.shape, bf16),
        pltpu.VMEM(q_pre.shape, f32),
        pltpu.SemaphoreType.DMA((3,)),
    ]
    own_shapes = [(2 * span, 2 * LANES), (2 * span + 8, 2 * LANES)]
    d_q_main, d_q_tail, own_near, own_far, *sent = pl.pallas_call(
        functools.partial(grads_kernel, ctx_count, direct),
        out_shape=[jax.ShapeDtypeStruct(q_pre.shape, f32)]
        + [jax.ShapeDtypeStruct(shape, f32) for shape in [(2, 8, width)] + own_shapes]
        + [jax.ShapeDtypeStruct(shape, bf16) for shape in sent_shapes],
        in_specs=[smem, vmem, hbm, hbm] + [vmem] * len(received),
        out_specs=[hbm] + [vmem] * (3 + len(sent_shapes)),
        scratch_shapes=scratch,
        compiler_params=pltpu.CompilerParams(vmem_limit_bytes=(20 if direct else 62) * MIB),
        name="grads",
    )(doc_lengths, filters, in_hbm(q_pre), in_hbm(d_out), *received)
    half_terms = delivered(sent)
    merged_shapes = [
        jax.ShapeDtypeStruct((2 * span, 2 * LANES), f32),
        jax.ShapeDtypeStruct((2 * span + 16, 2 * LANES), bf16),
        jax.ShapeDtypeStruct((8, 2 * LANES), f32),
        jax.ShapeDtypeStruct((2, rim // 2, 2 * LANES), f32),
    ]
    near, far, half_sums, rims = pl.pallas_call(
        functools.partial(merge_kernel, ctx_count, direct),
        out_shape=merged_shapes,
        in_specs=[vmem] * (2 + len(half_terms)),
        out_specs=[vmem] * len(merged_shapes),
        scratch_shapes=[
            pltpu.VMEM((group, 8, 2 * LANES), f32),
            pltpu.VMEM((ctx_count, rim // 2, 2 * LANES), f32),
        ],
        compiler_params=pltpu.CompilerParams(vmem_limit_bytes=(4 if direct else 40) * MIB),
        name="merge",
    )(own_near, own_far, *half_terms)
    from_half = flipped(far, group)

    count = lax.axis_size("tp")
    sums = pl.pallas_call(
        tree_sum_kernel,
        out_shape=jax.ShapeDtypeStruct(half_sums.shape, f32),
        in_specs=[vmem] * count,
        out_specs=vmem,
        compiler_params=pltpu.CompilerParams(vmem_limit_bytes=2 * MIB),
        name="sums",
    )(
        half_sums,
        *[
            lax.ppermute(half_sums, "tp", [(i, i ^ flip) for i in range(count)])
            for flip in range(1, count)
        ],
    )
    across_sums = flipped(sums, group)
    return pl.pallas_call(
        functools.partial(finish_kernel, ctx_count),
        out_shape=(
            jax.ShapeDtypeStruct(q_pre.shape, f32),
            jax.ShapeDtypeStruct(k_pre.shape, f32),
            jax.ShapeDtypeStruct(k_pre.shape, f32),
            jax.ShapeDtypeStruct(filters.shape, f32),
        ),
        in_specs=[smem, vmem, hbm, vmem, vmem, vmem, vmem, vmem, vmem],
        out_specs=(hbm, hbm, hbm, hbm),
        scratch_shapes=[
            pltpu.VMEM((2, 8, width), f32),
            pltpu.VMEM(k_pre.shape, f32),
            pltpu.VMEM(k_pre.shape, f32),
            pltpu.VMEM(filters.shape, f32),
            pltpu.SemaphoreType.DMA((4,)),
        ],
        input_output_aliases={2: 0},
        compiler_params=pltpu.CompilerParams(vmem_limit_bytes=4 * MIB),
        name="finish",
    )(doc_lengths, filters, d_q_main, d_q_tail, near, from_half, rims, sums, across_sums)


def solution(mesh):
    split = P(None, "ctx", "tp")
    return jax.shard_map(
        shards,
        mesh=mesh,
        in_specs=(split, split, split, split, P(), P()),
        out_specs=(split, split, split, P()),
        check_vma=False,
    )
```

```python
import functools

import jax
import jax.numpy as jnp
import numpy as np
from jax import lax
from jax.experimental import pallas as pl
from jax.experimental.pallas import tpu as pltpu
from jax.sharding import PartitionSpec as P

LANES = 128
NT = (((1,), (1,)), ((), ()))
NN = (((1,), (0,)), ((), ()))
TN = (((0,), (0,)), ((), ()))
TAIL = 16
MAX_CHUNK = 640
MAX_DIRECT = 4
MIB = 1 << 20


def loop(count, body, init, unrolled=16):
    if count <= unrolled:
        for step in range(count):
            init = body(step, init)
        return init
    return lax.fori_loop(0, count, body, init)


def aligned(start, multiple):
    return start if isinstance(start, int) else pl.multiple_of(start, multiple)


def doc_starts(lengths_ref):
    starts = [jnp.int32(0)]
    for index in range(lengths_ref.shape[0] - 1):
        starts.append(starts[-1] + lengths_ref[index])
    return starts


def fold_rows(terms):
    rows, lanes = terms.shape
    return jnp.sum(terms.reshape(rows // 8, 8, lanes), axis=0)


def split_bits(values):
    high = values.astype(jnp.bfloat16)
    low = (values - high.astype(jnp.float32)).astype(jnp.bfloat16)
    return high, low


def joined(pair):
    rows = pair.shape[0] // 2
    pair = pair.astype(jnp.float32)
    return pair[:rows] + pair[rows:]


class Slots:
    def __init__(self, refs, me):
        self.refs, self.me = refs, me

    def __getitem__(self, flip):
        if len(self.refs) == 1:
            place = lax.rem(self.me, jnp.int32(self.refs[0].shape[0]))
            return self.refs[0].at[partner(place, flip)]
        return self.refs[flip]


def partner(me, flip):
    return lax.bitwise_xor(me, jnp.int32(flip))


def pack_kernel(k_ref, v_ref, q_ref, out_ref):
    span = k_ref.shape[1]
    kv = jnp.concatenate([k_ref[...], v_ref[...]], axis=2).reshape(2 * span, 2 * LANES)
    tails = []
    for half in range(2):
        last = q_ref[half].astype(jnp.float32)[TAIL - 2 :]
        tails += [last[:, at : at + 2 * LANES] for at in range(0, last.shape[1], 2 * LANES)]
    out_ref[: 2 * span] = kv
    out_ref[2 * span :] = jnp.concatenate(tails, axis=0).astype(jnp.bfloat16)


def grads_kernel(ctx_count, direct, lengths_ref, filters_ref, q_hbm, d_out_hbm, *refs):
    group = ctx_count // 2
    arrays = group if direct else 1
    near_in, far_in, refs = refs[:arrays], refs[arrays : 2 * arrays], refs[2 * arrays :]
    dq_hbm, dq_tail_ref, own_near_ref, own_far_ref, sums_ref = refs[:5]
    arrays = group - 1 if direct else 1
    out_refs, refs = refs[5 : 5 + arrays], refs[5 + arrays :]
    same_scr, same_two_scr, kv_scr, conv_scr, dkv_scr, q_scr, qc_scr, do_scr, dq_scr = refs[:9]
    bias_scr, s_scr, dp_scr, rim_scr, q_ref, d_out_ref, dq_ref, sems = refs[9:]
    f32, bf16 = jnp.float32, jnp.bfloat16
    loads = [
        pltpu.make_async_copy(q_hbm, q_ref, sems.at[0]),
        pltpu.make_async_copy(d_out_hbm, d_out_ref, sems.at[1]),
    ]
    for load in loads:
        load.start()
    span = q_ref.shape[1]
    heads = q_ref.shape[2] // LANES
    half_rows = span * ctx_count
    length = 2 * half_rows
    blocks = 2 * ctx_count
    me = lax.axis_index("ctx")
    near_in, far_in = Slots(near_in, me), Slots(far_in, me)
    sent = Slots((own_far_ref,) + out_refs if direct else out_refs, me)
    scale = LANES**-0.5
    log2_scale = scale * 1.4426950408889634
    starts = doc_starts(lengths_ref)

    def fill(index, carry):
        rows = pl.ds(aligned(8 + index * span, 8), span)
        same_scr[rows] = jnp.ones((span, LANES), f32)
        same_two_scr[rows] = jnp.ones((span, LANES), f32)
        return carry

    loop(blocks, fill, 0)
    zeros = jnp.zeros((8, LANES), f32)
    for rows in (slice(0, 8), slice(8 + length, 16 + length)):
        same_scr[rows] = zeros
        same_two_scr[rows] = zeros
        for tensor in range(2):
            kv_scr[tensor, rows] = zeros
    for start in starts:
        same_scr[pl.ds(8 + start, 1)] = zeros[:1]
        same_two_scr[pl.ds(8 + start, 1)] = zeros[:1]
        same_two_scr[pl.ds(9 + start, 1)] = zeros[:1]

    def place_blocks(flip, carry):
        for message, index in (
            (near_in[flip], partner(me, flip)),
            (far_in[flip], partner(me, flip + group)),
        ):
            early = aligned(8 + index * span, 8)
            late = aligned(8 + (blocks - 1 - index) * span, 8)
            for tensor in range(2):
                lanes = slice(tensor * LANES, (tensor + 1) * LANES)
                kv_scr[tensor, pl.ds(early, span)] = message[:span, lanes].astype(f32)
                kv_scr[tensor, pl.ds(late, span)] = message[span : 2 * span, lanes].astype(f32)
            rim_scr[index] = message[2 * span :].astype(f32)
        return carry

    loop(group, place_blocks, 0)

    def taps(tensor):
        return [filters_ref[tensor, tap : tap + 1] for tap in range(3)]

    def masks(base, ahead):
        one = same_scr[pl.ds(base + 8 + min(ahead, 1), span)]
        return one, same_two_scr[pl.ds(base + 8 + ahead, span)]

    def convolve_kv(index, carry):
        base = index * span
        one, two = masks(base, 0)
        for tensor in range(2):
            zero_tap, one_tap, two_tap = taps(tensor + 1)
            total = zero_tap * kv_scr[tensor, pl.ds(aligned(base + 8, 8), span)]
            total = total + one * (one_tap * kv_scr[tensor, pl.ds(base + 7, span)])
            total = total + two * (two_tap * kv_scr[tensor, pl.ds(base + 6, span)])
            conv_scr[tensor, pl.ds(aligned(base, 16), span)] = total.astype(bf16)
        return carry

    loop(blocks, convolve_kv, 0)

    middle = me == ctx_count - 1
    rim_rows = rim_scr.shape[1] // 2
    rim_before = rim_scr[jnp.maximum(me - 1, 0)]
    rim_after = rim_scr[jnp.minimum(me + 1, ctx_count - 1)]
    late_rim = jnp.where(middle, rim_after[:rim_rows], rim_after[rim_rows:])
    rims = [rim_before[:rim_rows], late_rim]
    first_place = [me * span, (blocks - 1 - me) * span]

    for load in loads:
        load.wait()
    for half in range(2):
        one, two = masks(first_place[half], 0)
        zero_tap, one_tap, two_tap = taps(0)
        for head in range(heads):
            lanes = slice(head * LANES, (head + 1) * LANES)
            at = 2 * (head // 2)
            q_scr[half, head, 6:8] = rims[half][at : at + 2, (head % 2) * LANES : (head % 2 + 1) * LANES]
            q_scr[half, head, 8:] = q_ref[half, :, lanes].astype(f32)
            total = zero_tap * q_scr[half, head, 8:]
            total = total + one * (one_tap * q_scr[half, head, 7 : 7 + span])
            total = total + two * (two_tap * q_scr[half, head, 6 : 6 + span])
            qc_scr[half, head * span : (head + 1) * span] = total.astype(bf16)
            do_scr[half, head * span : (head + 1) * span] = d_out_ref[half, :, lanes]

    def attend(half, window, first_key, add):
        chunks = 1
        while window // chunks > MAX_CHUNK or window % (16 * chunks):
            chunks += 1
        size = window // chunks
        query = first_place[half] + lax.rem(
            lax.broadcasted_iota(jnp.int32, (1, LANES), 1), jnp.int32(span)
        )
        lowest = jnp.zeros((1, LANES), jnp.int32)
        for start in starts[1:]:
            lowest = jnp.where(query >= start, start, lowest)
        wide = 2 * LANES

        def fill_bias(step, carry):
            places = first_key + step * size + lax.broadcasted_iota(jnp.int32, (size, LANES), 0)
            allowed = (places >= lowest) & (places <= query)
            bias_scr[pl.ds(aligned(step * size, 16), size)] = jnp.where(allowed, 0.0, -1e30)
            return carry

        loop(chunks, fill_bias, 0, 1)
        whole_window = pl.ds(aligned(first_key, 16), window)
        keys_t = conv_scr[0, whole_window].T if chunks == 1 else None
        for at in range(heads * span // wide):
            slot = (half * (heads * span // wide) + at) % s_scr.shape[0]
            cols = slice(at * wide, (at + 1) * wide)
            queries = qc_scr[half, cols]
            grads = do_scr[half, cols]

            def key_rows(step):
                return pl.ds(aligned(first_key + step * size, 16), size)

            def score(step, top):
                keys = conv_scr[0, key_rows(step)]
                scores = lax.dot_general(keys, queries, NT, preferred_element_type=f32)
                bias = bias_scr[pl.ds(aligned(step * size, 16), size)]
                scores = scores + jnp.concatenate([bias, bias], axis=1)
                s_scr[slot, pl.ds(aligned(step * size, 16), size)] = scores
                return jnp.maximum(top, jnp.max(scores, axis=0, keepdims=True))

            top = loop(chunks, score, jnp.full((1, wide), -1e30, f32), 1)

            def weigh(step, carry):
                total, weighted = carry
                rows = pl.ds(aligned(step * size, 16), size)
                weights = jnp.exp2((s_scr[slot, rows] - top) * log2_scale)
                values = conv_scr[1, key_rows(step)]
                prob_grads = lax.dot_general(values, grads, NT, preferred_element_type=f32)
                s_scr[slot, rows] = weights
                dp_scr[slot, rows] = prob_grads
                total = total + jnp.sum(weights, axis=0, keepdims=True)
                weighted = weighted + jnp.sum(weights * prob_grads, axis=0, keepdims=True)
                return total, weighted

            zeros = jnp.zeros((1, wide), f32)
            total, weighted = loop(chunks, weigh, (zeros, zeros), 1)
            inverse = 1.0 / total
            mean = weighted * inverse
            slope = inverse * scale

            def accumulate(step, dq):
                rows = pl.ds(aligned(step * size, 16), size)
                weights = s_scr[slot, rows]
                probs = (weights * inverse).astype(bf16)
                score_grads = (weights * slope * (dp_scr[slot, rows] - mean)).astype(bf16)
                dk = lax.dot_general(score_grads, queries, NN, preferred_element_type=f32)
                dv = lax.dot_general(probs, grads, NN, preferred_element_type=f32)
                target = pl.ds(aligned(first_key + step * size, 16), size)
                for tensor, terms in enumerate((dk, dv)):
                    if add or at:
                        dkv_scr[tensor, target] += terms
                    else:
                        dkv_scr[tensor, target] = terms
                if keys_t is not None:
                    return lax.dot_general(keys_t, score_grads, NN, preferred_element_type=f32)
                keys = conv_scr[0, key_rows(step)]
                return dq + lax.dot_general(keys, score_grads, TN, preferred_element_type=f32)

            dq = loop(chunks, accumulate, jnp.zeros((LANES, wide), f32), 1)
            dq = dq.T
            for part in range(wide // span):
                head = at * (wide // span) + part
                dq_scr[half, head, :span] = dq[part * span : (part + 1) * span]

    for tensor in range(2):
        dkv_scr[tensor, half_rows:] = jnp.zeros((half_rows + 8, LANES), f32)
    attend(0, half_rows, 0, False)
    attend(1, half_rows + span, (ctx_count - 1 - me) * span, True)

    next_rows = jnp.where(middle, dq_scr[1, :, :8], 0.0)
    dq_scr[0, :, span:] = next_rows
    dq_scr[1, :, span:] = jnp.zeros_like(next_rows)
    sums = [jnp.zeros((8, LANES), f32) for _ in range(3)]
    for half in range(2):
        one, two = masks(first_place[half], 0)
        ahead_one = same_scr[pl.ds(first_place[half] + 9, span)]
        ahead_two = same_two_scr[pl.ds(first_place[half] + 10, span)]
        zero_tap, one_tap, two_tap = taps(0)
        for head in range(heads):
            lanes = slice(head * LANES, (head + 1) * LANES)
            grads = dq_scr[half, head, :span]
            out = zero_tap * grads
            out = out + ahead_one * (one_tap * dq_scr[half, head, 1 : 1 + span])
            out = out + ahead_two * (two_tap * dq_scr[half, head, 2 : 2 + span])
            dq_ref[half, :, lanes] = out
            dq_tail_ref[half, :, lanes] = out[span - 8 :]
            sums[0] += fold_rows(grads * q_scr[half, head, 8:])
            sums[1] += fold_rows(grads * one * q_scr[half, head, 7 : 7 + span])
            sums[2] += fold_rows(grads * two * q_scr[half, head, 6 : 6 + span])
    q_sums = [jnp.sum(term, axis=0, keepdims=True) for term in sums]
    store = pltpu.make_async_copy(dq_ref, dq_hbm, sems.at[2])
    store.start()

    def finish_block(index, carry, target, row):
        base = pl.multiple_of(index * span, 8)
        one, two = masks(base, 0)
        ahead_one = same_scr[pl.ds(base + 9, span)]
        ahead_two = same_two_scr[pl.ds(base + 10, span)]
        carry = list(carry)
        for tensor in range(2):
            zero_tap, one_tap, two_tap = taps(tensor + 1)
            own = dkv_scr[tensor, pl.ds(base, span)]
            out = zero_tap * own
            out = out + ahead_one * (one_tap * dkv_scr[tensor, pl.ds(base + 1, span)])
            out = out + ahead_two * (two_tap * dkv_scr[tensor, pl.ds(base + 2, span)])
            lanes = slice(tensor * LANES, (tensor + 1) * LANES)
            target[row : row + span, lanes] = out.astype(target.dtype)
            at = 3 * tensor
            carry[at] += fold_rows(own * kv_scr[tensor, pl.ds(base + 8, span)])
            carry[at + 1] += fold_rows(own * one * kv_scr[tensor, pl.ds(base + 7, span)])
            carry[at + 2] += fold_rows(own * two * kv_scr[tensor, pl.ds(base + 6, span)])
        return tuple(carry)

    low = me < group

    def finish(step, carry):
        flip = step + 1
        owner = partner(me, flip)
        far_owner = partner(me, flip + group)
        near_late = blocks - 1 - owner
        places = [
            far_owner,
            jnp.where(low, blocks - 1 - far_owner, owner),
            jnp.where(low & (me > owner), owner, near_late),
        ]
        for at, place in enumerate(places):
            carry = finish_block(place, carry, sent[flip], at * span)
        return carry

    kv_sums = (zeros,) * 6
    for target, index in ((own_far_ref, partner(me, group)), (own_near_ref, me)):
        kv_sums = finish_block(index, kv_sums, target, 0)
        kv_sums = finish_block(blocks - 1 - index, kv_sums, target, span)
    kv_sums = loop(group - 1, finish, kv_sums)
    kv_sums = [jnp.sum(term, axis=0, keepdims=True) for term in kv_sums]

    padding = [jnp.zeros((2, LANES), f32)]
    left = jnp.concatenate(q_sums + kv_sums[:3] + padding, axis=0)
    right = jnp.concatenate([jnp.zeros((3, LANES), f32)] + kv_sums[3:] + padding, axis=0)
    sums_ref[...] = jnp.concatenate([left, right], axis=1)

    rims = []
    for half in range(2):
        rows = [dq_scr[half, head, :2] for head in range(heads)]
        rows = [jnp.concatenate(rows[at : at + 2], axis=1) for at in range(0, heads, 2)]
        rims.append(jnp.concatenate(rows, axis=0))

    def rim_for(index):
        return jnp.concatenate(split_bits(jnp.where(index < me, rims[0], rims[1])), axis=0)

    def store_rims(step, carry):
        flip = step + 1
        owner = partner(me, flip)
        if not direct or flip & (flip + 1) == 0:
            across = (flip == group - 1) & (jnp.abs(owner - me) != 1)
            target = jnp.where(across, partner(owner, group), owner)
            sent[flip][3 * span :] = rim_for(target)
        return carry

    loop(group - 1, store_rims, 0, 16 if direct else 1)
    store.wait()


def merge_kernel(ctx_count, direct, own_near_ref, own_far_ref, *refs):
    received_refs, (near_ref, far_ref, rims_ref, rim_scr) = refs[:-4], refs[-4:]
    f32, bf16 = jnp.float32, jnp.bfloat16
    group = ctx_count // 2
    me = lax.axis_index("ctx")
    low = me < group
    received = Slots((own_far_ref,) + received_refs if direct else received_refs, me)
    span = own_near_ref.shape[0] // 2
    rows = 2 * span
    neighbours = [jnp.minimum(me + 1, ctx_count - 1), jnp.maximum(me - 1, 0)]
    for index in neighbours:
        rim_scr[index] = jnp.zeros(rim_scr.shape[1:], f32)

    def add(step, carry):
        flip = step + 1
        source = partner(me, flip)
        message = received[flip]
        parts = [message[at * span : (at + 1) * span].astype(f32) for at in range(3)]
        near_early, near_late, far_early, far_late = carry
        if not direct or flip & (flip + 1) == 0:
            rim_scr[source] = joined(message[3 * span :])
        to_early = low & (source > me)
        zero = jnp.zeros_like(parts[0])
        return (
            near_early + jnp.where(low, jnp.where(to_early, parts[2], zero), parts[1]),
            near_late + jnp.where(to_early, zero, parts[2]),
            far_early + parts[0],
            far_late + jnp.where(low, parts[1], zero),
        )

    init = (own_near_ref[:span], own_near_ref[span:], own_far_ref[:span], own_far_ref[span:rows])
    totals = loop(group - 1, add, init, 16 if direct else 1)
    near_ref[:span] = totals[0]
    near_ref[span:] = totals[1]
    far_ref[:span] = totals[2].astype(bf16)
    far_ref[span:rows] = totals[3].astype(bf16)
    far_ref[rows:] = received[group - 1][3 * span :]
    for at, index in enumerate(neighbours):
        rims_ref[at] = rim_scr[index]


def tree_sum(refs):
    level = [ref[...] for ref in refs]
    while len(level) > 1:
        level = [level[at] + level[at + 1] for at in range(0, len(level), 2)]
    return level[0]


def sums_kernel(*refs):
    refs[-1][...] = tree_sum(refs[:-1])


def finish_kernel(
    ctx_count, lengths_ref, filters_ref, dq_in_hbm, tail_ref, near_ref, far_ref, rims_ref, *refs
):
    sums_refs, refs = refs[:-9], refs[-9:]
    dq_hbm, dk_hbm, dv_hbm, d_filters_hbm, dq_ref, dk_ref, dv_ref, d_filters_ref, sems = refs
    f32 = jnp.float32
    group = ctx_count // 2
    span = dk_ref.shape[1]
    me = lax.axis_index("ctx")
    starts = doc_starts(lengths_ref)
    blocks = 2 * ctx_count

    total = near_ref[...] + far_ref[: 2 * span].astype(f32)
    for half in range(2):
        dk_ref[half] = total[half * span : (half + 1) * span, :LANES]
        dv_ref[half] = total[half * span : (half + 1) * span, LANES:]
    stores = [
        pltpu.make_async_copy(dk_ref, dk_hbm, sems.at[0]),
        pltpu.make_async_copy(dv_ref, dv_hbm, sems.at[1]),
        pltpu.make_async_copy(d_filters_ref, d_filters_hbm, sems.at[2]),
        pltpu.make_async_copy(dq_ref, dq_hbm.at[:, pl.ds(span - 8, 8)], sems.at[3]),
    ]
    sums = tree_sum(sums_refs)
    d_filters_ref[0] = sums[0:3, :LANES]
    d_filters_ref[1] = sums[3:6, :LANES]
    d_filters_ref[2] = sums[3:6, LANES:]
    for store in stores[:3]:
        store.start()

    def same(place):
        cut = place >= blocks * span
        for start in starts:
            cut = cut | (place == start)
        return jnp.where(cut, 0.0, 1.0).astype(f32)

    heads = dq_ref.shape[2] // LANES
    taps = [jnp.concatenate([filters_ref[0, tap : tap + 1]] * heads, axis=1) for tap in range(3)]
    row = lax.broadcasted_iota(jnp.int32, dq_ref.shape[1:], 0)
    far_rim = joined(far_ref[2 * span :])
    crosses = [me == group - 1, me == group]
    first_place = [me * span, (blocks - 1 - me) * span]
    present = [me < ctx_count - 1, me > 0]
    for half in range(2):
        rim = jnp.where(crosses[half], far_rim, rims_ref[half])
        rows = jnp.concatenate([rim[2 * at : 2 * at + 2] for at in range(rim.shape[0] // 2)], axis=1)
        end = first_place[half] + span
        zero, one, two = same(end - 1), same(end), same(end + 1)
        one = jnp.where(present[half], one, 0.0)
        last_but_one = (zero * one) * (taps[2] * rows[0:1])
        last = one * (taps[1] * rows[0:1]) + (one * two) * (taps[2] * rows[1:2])
        extra = jnp.where(row == 6, last_but_one, jnp.where(row == 7, last, 0.0))
        dq_ref[half] = tail_ref[half] + extra
    stores[3].start()
    for store in stores:
        store.wait()


def shards(q_pre, k_pre, value_before_filter, d_out, filters, doc_lengths):
    f32, bf16 = jnp.float32, jnp.bfloat16
    ctx_count = lax.axis_size("ctx")
    span, width = q_pre.shape[1:]
    length = 2 * span * ctx_count
    rim = 4 * width // (2 * LANES)
    vmem = pl.BlockSpec(memory_space=pltpu.VMEM)
    smem = pl.BlockSpec(memory_space=pltpu.SMEM)
    hbm = pl.BlockSpec(memory_space=pltpu.HBM)

    group = ctx_count // 2
    direct = group <= MAX_DIRECT
    halves = [[half * group + at for at in range(group)] for half in range(2)]
    msg_rows = 2 * span + rim

    def whole(shape):
        return pl.BlockSpec(shape, lambda i: (0,) * len(shape))

    def in_hbm(array):
        return pltpu.with_memory_space_constraint(array, pltpu.HBM)

    def flipped(array, flip):
        return lax.ppermute(array, "ctx", [(i, i ^ flip) for i in range(ctx_count)])

    def gathered(array):
        if direct:
            return [array] + [flipped(array, flip) for flip in range(1, group)]
        return [lax.all_gather(array, "ctx", axis_index_groups=halves)]

    def delivered(arrays):
        if direct:
            return [flipped(array, step + 1) for step, array in enumerate(arrays)]
        return [lax.all_to_all(arrays[0], "ctx", 0, 0, axis_index_groups=halves, tiled=True)]

    packed = pl.pallas_call(
        pack_kernel,
        grid=(1,),
        out_shape=jax.ShapeDtypeStruct((msg_rows, 2 * LANES), bf16),
        in_specs=[
            whole(k_pre.shape),
            whole(k_pre.shape),
            pl.BlockSpec((2, TAIL, width), lambda i: (0, span // TAIL - 1, 0)),
        ],
        out_specs=whole((msg_rows, 2 * LANES)),
        compiler_params=pltpu.CompilerParams(vmem_limit_bytes=4 * MIB),
        name="pack",
    )(*[in_hbm(array) for array in (k_pre, value_before_filter, q_pre)])
    across = flipped(packed, group)
    received = gathered(packed) + gathered(across)

    window = span * ctx_count + span
    if direct:
        sent_shapes = [
            (3 * span + (16 if flip & (flip + 1) == 0 else 0), 2 * LANES) for flip in range(1, group)
        ]
    else:
        sent_shapes = [(group, 3 * span + 16, 2 * LANES)]
    slots = 4 if direct else 1
    heads = width // LANES
    scratch = [
        pltpu.VMEM((length + 16, LANES), f32),
        pltpu.VMEM((length + 16, LANES), f32),
        pltpu.VMEM((2, length + 16, LANES), f32),
        pltpu.VMEM((2, length, LANES), bf16),
        pltpu.VMEM((2, length + 8, LANES), f32),
        pltpu.VMEM((2, heads, span + 8, LANES), f32),
        pltpu.VMEM((2, span * heads, LANES), bf16),
        pltpu.VMEM((2, span * heads, LANES), bf16),
        pltpu.VMEM((2, heads, span + 8, LANES), f32),
        pltpu.VMEM((window, LANES), f32),
        pltpu.VMEM((slots, window, 2 * LANES), f32),
        pltpu.VMEM((slots, window, 2 * LANES), f32),
        pltpu.VMEM((ctx_count, rim, 2 * LANES), f32),
        pltpu.VMEM(q_pre.shape, bf16),
        pltpu.VMEM(q_pre.shape, bf16),
        pltpu.VMEM(q_pre.shape, f32),
        pltpu.SemaphoreType.DMA((3,)),
    ]
    own_shapes = [(2 * span, 2 * LANES), (2 * span, 2 * LANES), (8, 2 * LANES)]
    d_q_main, d_q_tail, own_near, own_far, own_sums, *sent = pl.pallas_call(
        functools.partial(grads_kernel, ctx_count, direct),
        out_shape=[jax.ShapeDtypeStruct(q_pre.shape, f32)]
        + [jax.ShapeDtypeStruct(shape, f32) for shape in [(2, 8, width)] + own_shapes]
        + [jax.ShapeDtypeStruct(shape, bf16) for shape in sent_shapes],
        in_specs=[smem, vmem, hbm, hbm] + [vmem] * len(received),
        out_specs=[hbm] + [vmem] * (4 + len(sent_shapes)),
        scratch_shapes=scratch,
        compiler_params=pltpu.CompilerParams(vmem_limit_bytes=(20 if direct else 62) * MIB),
        name="grads",
    )(doc_lengths, filters, in_hbm(q_pre), in_hbm(d_out), *received)
    half_terms = delivered(sent)
    count = lax.axis_size("tp")

    def added(arrays):
        return pl.pallas_call(
            sums_kernel,
            out_shape=jax.ShapeDtypeStruct(own_sums.shape, f32),
            in_specs=[vmem] * len(arrays),
            out_specs=vmem,
            compiler_params=pltpu.CompilerParams(vmem_limit_bytes=2 * MIB),
            name="sums",
        )(*arrays)

    def over_tp(array, flip):
        return lax.ppermute(array, "tp", [(i, i ^ flip) for i in range(count)])

    sums = added([own_sums] + [over_tp(own_sums, flip) for flip in range(1, count)])
    sums = added([sums, flipped(sums, group)])
    sums, *half_terms = lax.optimization_barrier((sums, *half_terms))
    merged_shapes = [
        jax.ShapeDtypeStruct((2 * span, 2 * LANES), f32),
        jax.ShapeDtypeStruct((2 * span + 16, 2 * LANES), bf16),
        jax.ShapeDtypeStruct((2, rim // 2, 2 * LANES), f32),
    ]
    near, far, rims = pl.pallas_call(
        functools.partial(merge_kernel, ctx_count, direct),
        out_shape=merged_shapes,
        in_specs=[vmem] * (2 + len(half_terms)),
        out_specs=[vmem] * len(merged_shapes),
        scratch_shapes=[
            pltpu.VMEM((ctx_count, rim // 2, 2 * LANES), f32),
        ],
        compiler_params=pltpu.CompilerParams(vmem_limit_bytes=(4 if direct else 40) * MIB),
        name="merge",
    )(own_near, own_far, *half_terms)
    from_half = flipped(far, group)

    if direct:
        all_sums = [sums] + [flipped(sums, flip) for flip in range(1, group)]
    else:
        flip = 1
        while flip < group:
            sums = added([sums, flipped(sums, flip)])
            flip *= 2
        all_sums = [sums]

    return pl.pallas_call(
        functools.partial(finish_kernel, ctx_count),
        out_shape=(
            jax.ShapeDtypeStruct(q_pre.shape, f32),
            jax.ShapeDtypeStruct(k_pre.shape, f32),
            jax.ShapeDtypeStruct(k_pre.shape, f32),
            jax.ShapeDtypeStruct(filters.shape, f32),
        ),
        in_specs=[smem, vmem, hbm] + [vmem] * (4 + len(all_sums)),
        out_specs=(hbm, hbm, hbm, hbm),
        scratch_shapes=[
            pltpu.VMEM((2, 8, width), f32),
            pltpu.VMEM(k_pre.shape, f32),
            pltpu.VMEM(k_pre.shape, f32),
            pltpu.VMEM(filters.shape, f32),
            pltpu.SemaphoreType.DMA((4,)),
        ],
        input_output_aliases={2: 0},
        compiler_params=pltpu.CompilerParams(vmem_limit_bytes=4 * MIB),
        name="finish",
    )(doc_lengths, filters, d_q_main, d_q_tail, near, from_half, rims, *all_sums)


def solution(mesh):
    split = P(None, "ctx", "tp")
    return jax.shard_map(
        shards,
        mesh=mesh,
        in_specs=(split, split, split, split, P(), P()),
        out_specs=(split, split, split, P()),
        check_vma=False,
    )
```

```python
import functools

import jax
import jax.numpy as jnp
import numpy as np
from jax import lax
from jax.experimental import pallas as pl
from jax.experimental.pallas import tpu as pltpu
from jax.sharding import PartitionSpec as P

LANES = 128
NT = (((1,), (1,)), ((), ()))
NN = (((1,), (0,)), ((), ()))
TN = (((0,), (0,)), ((), ()))
TAIL = 16
MAX_CHUNK = 640
MAX_DIRECT = 4
WINDOWS = (2, 4, 6)
MIB = 1 << 20


def loop(count, body, init, unrolled=16):
    if count <= unrolled:
        for step in range(count):
            init = body(step, init)
        return init
    return lax.fori_loop(0, count, body, init)


def aligned(start, multiple):
    return start if isinstance(start, int) else pl.multiple_of(start, multiple)


def doc_starts(lengths_ref):
    starts = [jnp.int32(0)]
    for index in range(lengths_ref.shape[0] - 1):
        starts.append(starts[-1] + lengths_ref[index])
    return starts


def fold_rows(terms):
    rows, lanes = terms.shape
    return jnp.sum(terms.reshape(rows // 8, 8, lanes), axis=0)


def split_bits(values):
    high = values.astype(jnp.bfloat16)
    low = (values - high.astype(jnp.float32)).astype(jnp.bfloat16)
    return high, low


def joined(pair):
    rows = pair.shape[0] // 2
    pair = pair.astype(jnp.float32)
    return pair[:rows] + pair[rows:]


class Slots:
    def __init__(self, refs, me):
        self.refs, self.me = refs, me

    def __getitem__(self, flip):
        if len(self.refs) == 1:
            place = lax.rem(self.me, jnp.int32(self.refs[0].shape[0]))
            return self.refs[0].at[partner(place, flip)]
        return self.refs[flip]


def partner(me, flip):
    return lax.bitwise_xor(me, jnp.int32(flip))


def pack_kernel(k_ref, v_ref, q_ref, out_ref):
    span = k_ref.shape[1]
    kv = jnp.concatenate([k_ref[...], v_ref[...]], axis=2).reshape(2 * span, 2 * LANES)
    tails = []
    for half in range(2):
        last = q_ref[half].astype(jnp.float32)[TAIL - 2 :]
        tails += [last[:, at : at + 2 * LANES] for at in range(0, last.shape[1], 2 * LANES)]
    out_ref[: 2 * span] = kv
    out_ref[2 * span :] = jnp.concatenate(tails, axis=0).astype(jnp.bfloat16)


def grads_kernel(ctx_count, direct, lengths_ref, filters_ref, q_hbm, d_out_hbm, *refs):
    group = ctx_count // 2
    arrays = group if direct else 1
    near_in, far_in, refs = refs[:arrays], refs[arrays : 2 * arrays], refs[2 * arrays :]
    dq_hbm, dq_tail_ref, own_near_ref, own_far_ref = refs[:4]
    arrays = group - 1 if direct else 1
    out_refs, refs = refs[4 : 4 + arrays], refs[4 + arrays :]
    same_scr, same_two_scr, kv_scr, conv_scr, dkv_scr, q_scr, qc_scr, do_scr, dq_scr = refs[:9]
    bias_scr, s_scr, dp_scr, rim_scr, q_ref, d_out_ref, dq_ref, sems = refs[9:]
    f32, bf16 = jnp.float32, jnp.bfloat16
    loads = [
        pltpu.make_async_copy(q_hbm, q_ref, sems.at[0]),
        pltpu.make_async_copy(d_out_hbm, d_out_ref, sems.at[1]),
    ]
    for load in loads:
        load.start()
    span = q_ref.shape[1]
    heads = q_ref.shape[2] // LANES
    half_rows = span * ctx_count
    length = 2 * half_rows
    blocks = 2 * ctx_count
    me = lax.axis_index("ctx")
    near_in, far_in = Slots(near_in, me), Slots(far_in, me)
    sent = Slots((own_far_ref,) + out_refs if direct else out_refs, me)
    scale = LANES**-0.5
    log2_scale = scale * 1.4426950408889634
    starts = doc_starts(lengths_ref)

    def fill(index, carry):
        rows = pl.ds(aligned(8 + index * span, 8), span)
        same_scr[rows] = jnp.ones((span, LANES), f32)
        same_two_scr[rows] = jnp.ones((span, LANES), f32)
        return carry

    loop(blocks, fill, 0)
    zeros = jnp.zeros((8, LANES), f32)
    for rows in (slice(0, 8), slice(8 + length, 16 + length)):
        same_scr[rows] = zeros
        same_two_scr[rows] = zeros
        for tensor in range(2):
            kv_scr[tensor, rows] = zeros
    for start in starts:
        same_scr[pl.ds(8 + start, 1)] = zeros[:1]
        same_two_scr[pl.ds(8 + start, 1)] = zeros[:1]
        same_two_scr[pl.ds(9 + start, 1)] = zeros[:1]

    def place_blocks(flip, carry):
        for message, index in (
            (near_in[flip], partner(me, flip)),
            (far_in[flip], partner(me, flip + group)),
        ):
            early = aligned(8 + index * span, 8)
            late = aligned(8 + (blocks - 1 - index) * span, 8)
            for tensor in range(2):
                lanes = slice(tensor * LANES, (tensor + 1) * LANES)
                kv_scr[tensor, pl.ds(early, span)] = message[:span, lanes].astype(f32)
                kv_scr[tensor, pl.ds(late, span)] = message[span : 2 * span, lanes].astype(f32)
            rim_scr[index] = message[2 * span :].astype(f32)
        return carry

    loop(group, place_blocks, 0)

    def taps(tensor):
        return [filters_ref[tensor, tap : tap + 1] for tap in range(3)]

    def masks(base, ahead):
        one = same_scr[pl.ds(base + 8 + min(ahead, 1), span)]
        return one, same_two_scr[pl.ds(base + 8 + ahead, span)]

    def convolve_kv(index, carry):
        base = index * span
        one, two = masks(base, 0)
        for tensor in range(2):
            zero_tap, one_tap, two_tap = taps(tensor + 1)
            total = zero_tap * kv_scr[tensor, pl.ds(aligned(base + 8, 8), span)]
            total = total + one * (one_tap * kv_scr[tensor, pl.ds(base + 7, span)])
            total = total + two * (two_tap * kv_scr[tensor, pl.ds(base + 6, span)])
            conv_scr[tensor, pl.ds(aligned(base, 16), span)] = total.astype(bf16)
        return carry

    loop(blocks, convolve_kv, 0)

    middle = me == ctx_count - 1
    rim_rows = rim_scr.shape[1] // 2
    rim_before = rim_scr[jnp.maximum(me - 1, 0)]
    rim_after = rim_scr[jnp.minimum(me + 1, ctx_count - 1)]
    late_rim = jnp.where(middle, rim_after[:rim_rows], rim_after[rim_rows:])
    rims = [rim_before[:rim_rows], late_rim]
    first_place = [me * span, (blocks - 1 - me) * span]

    for load in loads:
        load.wait()
    for half in range(2):
        one, two = masks(first_place[half], 0)
        zero_tap, one_tap, two_tap = taps(0)
        for head in range(heads):
            lanes = slice(head * LANES, (head + 1) * LANES)
            at = 2 * (head // 2)
            q_scr[half, head, 6:8] = rims[half][at : at + 2, (head % 2) * LANES : (head % 2 + 1) * LANES]
            q_scr[half, head, 8:] = q_ref[half, :, lanes].astype(f32)
            total = zero_tap * q_scr[half, head, 8:]
            total = total + one * (one_tap * q_scr[half, head, 7 : 7 + span])
            total = total + two * (two_tap * q_scr[half, head, 6 : 6 + span])
            qc_scr[half, head * span : (head + 1) * span] = total.astype(bf16)
            do_scr[half, head * span : (head + 1) * span] = d_out_ref[half, :, lanes]

    def attend(half, window, first_key):
        chunks = 1
        while window // chunks > MAX_CHUNK or window % (16 * chunks):
            chunks += 1
        size = window // chunks
        query = first_place[half] + lax.rem(
            lax.broadcasted_iota(jnp.int32, (1, LANES), 1), jnp.int32(span)
        )
        lowest = jnp.zeros((1, LANES), jnp.int32)
        for start in starts[1:]:
            lowest = jnp.where(query >= start, start, lowest)
        wide = 2 * LANES

        def fill_bias(step, carry):
            places = first_key + step * size + lax.broadcasted_iota(jnp.int32, (size, LANES), 0)
            allowed = (places >= lowest) & (places <= query)
            bias_scr[pl.ds(aligned(step * size, 16), size)] = jnp.where(allowed, 0.0, -1e30)
            return carry

        loop(chunks, fill_bias, 0, 1)
        whole_window = pl.ds(aligned(first_key, 16), window)
        keys_t = conv_scr[0, whole_window].T if chunks == 1 else None
        for at in range(heads * span // wide):
            slot = (half * (heads * span // wide) + at) % s_scr.shape[0]
            cols = slice(at * wide, (at + 1) * wide)
            queries = qc_scr[half, cols]
            grads = do_scr[half, cols]

            def key_rows(step):
                return pl.ds(aligned(first_key + step * size, 16), size)

            def score(step, top):
                keys = conv_scr[0, key_rows(step)]
                scores = lax.dot_general(keys, queries, NT, preferred_element_type=f32)
                bias = bias_scr[pl.ds(aligned(step * size, 16), size)]
                scores = scores + jnp.concatenate([bias, bias], axis=1)
                s_scr[slot, pl.ds(aligned(step * size, 16), size)] = scores
                return jnp.maximum(top, jnp.max(scores, axis=0, keepdims=True))

            top = loop(chunks, score, jnp.full((1, wide), -1e30, f32), 1)

            def weigh(step, carry):
                total, weighted = carry
                rows = pl.ds(aligned(step * size, 16), size)
                weights = jnp.exp2((s_scr[slot, rows] - top) * log2_scale)
                values = conv_scr[1, key_rows(step)]
                prob_grads = lax.dot_general(values, grads, NT, preferred_element_type=f32)
                s_scr[slot, rows] = weights
                dp_scr[slot, rows] = prob_grads
                total = total + jnp.sum(weights, axis=0, keepdims=True)
                weighted = weighted + jnp.sum(weights * prob_grads, axis=0, keepdims=True)
                return total, weighted

            zeros = jnp.zeros((1, wide), f32)
            total, weighted = loop(chunks, weigh, (zeros, zeros), 1)
            inverse = 1.0 / total
            mean = weighted * inverse
            slope = inverse * scale

            def accumulate(step, dq):
                rows = pl.ds(aligned(step * size, 16), size)
                weights = s_scr[slot, rows]
                probs = (weights * inverse).astype(bf16)
                score_grads = (weights * slope * (dp_scr[slot, rows] - mean)).astype(bf16)
                dk = lax.dot_general(score_grads, queries, NN, preferred_element_type=f32)
                dv = lax.dot_general(probs, grads, NN, preferred_element_type=f32)
                target = pl.ds(aligned(first_key + step * size, 16), size)
                for tensor, terms in enumerate((dk, dv)):
                    dkv_scr[tensor, target] += terms
                if keys_t is not None:
                    return lax.dot_general(keys_t, score_grads, NN, preferred_element_type=f32)
                keys = conv_scr[0, key_rows(step)]
                return dq + lax.dot_general(keys, score_grads, TN, preferred_element_type=f32)

            dq = loop(chunks, accumulate, jnp.zeros((LANES, wide), f32), 1)
            dq = dq.T
            for part in range(wide // span):
                head = at * (wide // span) + part
                dq_scr[half, head, :span] = dq[part * span : (part + 1) * span]

    def clear(index, carry):
        for tensor in range(2):
            dkv_scr[tensor, pl.ds(aligned(index * span, 8), span)] = jnp.zeros((span, LANES), f32)
        return carry

    loop(blocks, clear, 0)
    for tensor in range(2):
        dkv_scr[tensor, length:] = zeros

    for half in range(2):
        widest = ctx_count + half
        lowest = jnp.int32(0)
        for start in starts[1:]:
            lowest = jnp.where(first_place[half] >= start, start, lowest)
        needed = first_place[half] // span - lowest // span + 1
        below = 0
        for count in [count for count in WINDOWS if direct and count < widest] + [widest]:

            @pl.when((needed > below) & (needed <= count))
            def _(half=half, count=count):
                first_key = jnp.maximum(first_place[half] + span - count * span, 0)
                attend(half, count * span, first_key)

            below = count

    next_rows = jnp.where(middle, dq_scr[1, :, :8], 0.0)
    dq_scr[0, :, span:] = next_rows
    dq_scr[1, :, span:] = jnp.zeros_like(next_rows)
    sums = [jnp.zeros((8, LANES), f32) for _ in range(3)]
    for half in range(2):
        one, two = masks(first_place[half], 0)
        ahead_one = same_scr[pl.ds(first_place[half] + 9, span)]
        ahead_two = same_two_scr[pl.ds(first_place[half] + 10, span)]
        zero_tap, one_tap, two_tap = taps(0)
        for head in range(heads):
            lanes = slice(head * LANES, (head + 1) * LANES)
            grads = dq_scr[half, head, :span]
            out = zero_tap * grads
            out = out + ahead_one * (one_tap * dq_scr[half, head, 1 : 1 + span])
            out = out + ahead_two * (two_tap * dq_scr[half, head, 2 : 2 + span])
            dq_ref[half, :, lanes] = out
            dq_tail_ref[half, :, lanes] = out[span - 8 :]
            sums[0] += fold_rows(grads * q_scr[half, head, 8:])
            sums[1] += fold_rows(grads * one * q_scr[half, head, 7 : 7 + span])
            sums[2] += fold_rows(grads * two * q_scr[half, head, 6 : 6 + span])
    q_sums = [jnp.sum(term, axis=0, keepdims=True) for term in sums]
    store = pltpu.make_async_copy(dq_ref, dq_hbm, sems.at[2])
    store.start()

    def finish_block(index, carry, target, row):
        base = pl.multiple_of(index * span, 8)
        one, two = masks(base, 0)
        ahead_one = same_scr[pl.ds(base + 9, span)]
        ahead_two = same_two_scr[pl.ds(base + 10, span)]
        carry = list(carry)
        for tensor in range(2):
            zero_tap, one_tap, two_tap = taps(tensor + 1)
            own = dkv_scr[tensor, pl.ds(base, span)]
            out = zero_tap * own
            out = out + ahead_one * (one_tap * dkv_scr[tensor, pl.ds(base + 1, span)])
            out = out + ahead_two * (two_tap * dkv_scr[tensor, pl.ds(base + 2, span)])
            lanes = slice(tensor * LANES, (tensor + 1) * LANES)
            target[row : row + span, lanes] = out.astype(target.dtype)
            at = 3 * tensor
            carry[at] += fold_rows(own * kv_scr[tensor, pl.ds(base + 8, span)])
            carry[at + 1] += fold_rows(own * one * kv_scr[tensor, pl.ds(base + 7, span)])
            carry[at + 2] += fold_rows(own * two * kv_scr[tensor, pl.ds(base + 6, span)])
        return tuple(carry)

    low = me < group

    def finish(step, carry):
        flip = step + 1
        owner = partner(me, flip)
        far_owner = partner(me, flip + group)
        near_late = blocks - 1 - owner
        places = [
            far_owner,
            jnp.where(low, blocks - 1 - far_owner, owner),
            jnp.where(low & (me > owner), owner, near_late),
        ]
        for at, place in enumerate(places):
            carry = finish_block(place, carry, sent[flip], at * span)
        return carry

    kv_sums = (zeros,) * 6
    for target, index in ((own_far_ref, partner(me, group)), (own_near_ref, me)):
        kv_sums = finish_block(index, kv_sums, target, 0)
        kv_sums = finish_block(blocks - 1 - index, kv_sums, target, span)
    kv_sums = loop(group - 1, finish, kv_sums)
    kv_sums = [jnp.sum(term, axis=0, keepdims=True) for term in kv_sums]

    padding = [jnp.zeros((2, LANES), f32)]
    left = jnp.concatenate(q_sums + kv_sums[:3] + padding, axis=0)
    right = jnp.concatenate([jnp.zeros((3, LANES), f32)] + kv_sums[3:] + padding, axis=0)
    sums_tile = jnp.concatenate([left, right], axis=1)
    sums_pair = jnp.concatenate(split_bits(sums_tile), axis=0)
    own_far_ref[2 * span :] = joined(sums_pair)
    rims = []
    for half in range(2):
        rows = [dq_scr[half, head, :2] for head in range(heads)]
        rows = [jnp.concatenate(rows[at : at + 2], axis=1) for at in range(0, heads, 2)]
        rims.append(jnp.concatenate(rows, axis=0))

    def rim_for(index):
        return jnp.concatenate(split_bits(jnp.where(index < me, rims[0], rims[1])), axis=0)

    def store_rims(step, carry):
        flip = step + 1
        owner = partner(me, flip)
        sent[flip][3 * span : 3 * span + 16] = sums_pair
        if not direct or flip & (flip + 1) == 0:
            across = (flip == group - 1) & (jnp.abs(owner - me) != 1)
            target = jnp.where(across, partner(owner, group), owner)
            sent[flip][3 * span + 16 :] = rim_for(target)
        return carry

    loop(group - 1, store_rims, 0, 16 if direct else 1)
    store.wait()


def merge_kernel(ctx_count, direct, own_near_ref, own_far_ref, *refs):
    received_refs = refs[:-6]
    near_ref, far_ref, half_sums_ref, rims_ref, sums_scr, rim_scr = refs[-6:]
    f32, bf16 = jnp.float32, jnp.bfloat16
    group = ctx_count // 2
    me = lax.axis_index("ctx")
    low = me < group
    received = Slots((own_far_ref,) + received_refs if direct else received_refs, me)
    place = lax.rem(me, jnp.int32(group))
    span = own_near_ref.shape[0] // 2
    rows = 2 * span
    sums_scr[place] = own_far_ref[rows:]
    neighbours = [jnp.minimum(me + 1, ctx_count - 1), jnp.maximum(me - 1, 0)]
    for index in neighbours:
        rim_scr[index] = jnp.zeros(rim_scr.shape[1:], f32)

    def add(step, carry):
        flip = step + 1
        source = partner(me, flip)
        message = received[flip]
        parts = [message[at * span : (at + 1) * span].astype(f32) for at in range(3)]
        near_early, near_late, far_early, far_late = carry
        sums_scr[partner(place, flip)] = joined(message[3 * span : 3 * span + 16])
        if not direct or flip & (flip + 1) == 0:
            rim_scr[source] = joined(message[3 * span + 16 :])
        to_early = low & (source > me)
        zero = jnp.zeros_like(parts[0])
        return (
            near_early + jnp.where(low, jnp.where(to_early, parts[2], zero), parts[1]),
            near_late + jnp.where(to_early, zero, parts[2]),
            far_early + parts[0],
            far_late + jnp.where(low, parts[1], zero),
        )

    init = (own_near_ref[:span], own_near_ref[span:], own_far_ref[:span], own_far_ref[span:rows])
    totals = loop(group - 1, add, init, 16 if direct else 1)
    near_ref[:span] = totals[0]
    near_ref[span:] = totals[1]
    far_ref[:span] = totals[2].astype(bf16)
    far_ref[span:rows] = totals[3].astype(bf16)
    sums = loop(group, lambda index, carry: carry + sums_scr[index], jnp.zeros((8, 2 * LANES), f32))
    pair = jnp.concatenate(split_bits(sums), axis=0)
    half_sums_ref[...] = joined(pair)
    far_ref[rows : rows + 16] = pair
    far_ref[rows + 16 :] = received[group - 1][3 * span + 16 :]
    for at, index in enumerate(neighbours):
        rims_ref[at] = rim_scr[index]


def sums_kernel(span, half_sums_ref, far_ref, out_ref):
    sums = half_sums_ref[...] + joined(far_ref[2 * span : 2 * span + 16])
    out_ref[0] = sums[0:3, :LANES]
    out_ref[1] = sums[3:6, :LANES]
    out_ref[2] = sums[3:6, LANES:]


def finish_kernel(
    ctx_count, lengths_ref, filters_ref, dq_in_hbm, tail_ref, near_ref, far_ref, rims_ref, *refs
):
    sums_refs, refs = refs[:-9], refs[-9:]
    dq_hbm, dk_hbm, dv_hbm, d_filters_hbm, dq_ref, dk_ref, dv_ref, d_filters_ref, sems = refs
    f32 = jnp.float32
    group = ctx_count // 2
    span = dk_ref.shape[1]
    me = lax.axis_index("ctx")
    starts = doc_starts(lengths_ref)
    blocks = 2 * ctx_count

    total = near_ref[...] + far_ref[: 2 * span].astype(f32)
    for half in range(2):
        dk_ref[half] = total[half * span : (half + 1) * span, :LANES]
        dv_ref[half] = total[half * span : (half + 1) * span, LANES:]
    stores = [
        pltpu.make_async_copy(dk_ref, dk_hbm, sems.at[0]),
        pltpu.make_async_copy(dv_ref, dv_hbm, sems.at[1]),
        pltpu.make_async_copy(d_filters_ref, d_filters_hbm, sems.at[2]),
        pltpu.make_async_copy(dq_ref, dq_hbm.at[:, pl.ds(span - 8, 8)], sems.at[3]),
    ]
    level = [ref[...] for ref in sums_refs]
    while len(level) > 1:
        level = [level[at] + level[at + 1] for at in range(0, len(level), 2)]
    d_filters_ref[...] = level[0]
    for store in stores[:3]:
        store.start()

    def same(place):
        cut = place >= blocks * span
        for start in starts:
            cut = cut | (place == start)
        return jnp.where(cut, 0.0, 1.0).astype(f32)

    heads = dq_ref.shape[2] // LANES
    taps = [jnp.concatenate([filters_ref[0, tap : tap + 1]] * heads, axis=1) for tap in range(3)]
    row = lax.broadcasted_iota(jnp.int32, dq_ref.shape[1:], 0)
    far_rim = joined(far_ref[2 * span + 16 :])
    crosses = [me == group - 1, me == group]
    first_place = [me * span, (blocks - 1 - me) * span]
    present = [me < ctx_count - 1, me > 0]
    for half in range(2):
        rim = jnp.where(crosses[half], far_rim, rims_ref[half])
        rows = jnp.concatenate([rim[2 * at : 2 * at + 2] for at in range(rim.shape[0] // 2)], axis=1)
        end = first_place[half] + span
        zero, one, two = same(end - 1), same(end), same(end + 1)
        one = jnp.where(present[half], one, 0.0)
        last_but_one = (zero * one) * (taps[2] * rows[0:1])
        last = one * (taps[1] * rows[0:1]) + (one * two) * (taps[2] * rows[1:2])
        extra = jnp.where(row == 6, last_but_one, jnp.where(row == 7, last, 0.0))
        dq_ref[half] = tail_ref[half] + extra
    stores[3].start()
    for store in stores:
        store.wait()


def shards(q_pre, k_pre, value_before_filter, d_out, filters, doc_lengths):
    f32, bf16 = jnp.float32, jnp.bfloat16
    ctx_count = lax.axis_size("ctx")
    span, width = q_pre.shape[1:]
    length = 2 * span * ctx_count
    rim = 4 * width // (2 * LANES)
    vmem = pl.BlockSpec(memory_space=pltpu.VMEM)
    smem = pl.BlockSpec(memory_space=pltpu.SMEM)
    hbm = pl.BlockSpec(memory_space=pltpu.HBM)

    group = ctx_count // 2
    direct = group <= MAX_DIRECT
    halves = [[half * group + at for at in range(group)] for half in range(2)]
    msg_rows = 2 * span + rim

    def whole(shape):
        return pl.BlockSpec(shape, lambda i: (0,) * len(shape))

    def in_hbm(array):
        return pltpu.with_memory_space_constraint(array, pltpu.HBM)

    def flipped(array, flip):
        return lax.ppermute(array, "ctx", [(i, i ^ flip) for i in range(ctx_count)])

    def gathered(array):
        if direct:
            return [array] + [flipped(array, flip) for flip in range(1, group)]
        return [lax.all_gather(array, "ctx", axis_index_groups=halves)]

    def delivered(arrays):
        if direct:
            return [flipped(array, step + 1) for step, array in enumerate(arrays)]
        return [lax.all_to_all(arrays[0], "ctx", 0, 0, axis_index_groups=halves, tiled=True)]

    packed = pl.pallas_call(
        pack_kernel,
        grid=(1,),
        out_shape=jax.ShapeDtypeStruct((msg_rows, 2 * LANES), bf16),
        in_specs=[
            whole(k_pre.shape),
            whole(k_pre.shape),
            pl.BlockSpec((2, TAIL, width), lambda i: (0, span // TAIL - 1, 0)),
        ],
        out_specs=whole((msg_rows, 2 * LANES)),
        compiler_params=pltpu.CompilerParams(vmem_limit_bytes=4 * MIB),
        name="pack",
    )(*[in_hbm(array) for array in (k_pre, value_before_filter, q_pre)])
    across = flipped(packed, group)
    received = gathered(packed) + gathered(across)

    window = span * ctx_count + span
    if direct:
        sent_shapes = [
            (3 * span + (32 if flip & (flip + 1) == 0 else 16), 2 * LANES) for flip in range(1, group)
        ]
    else:
        sent_shapes = [(group, 3 * span + 32, 2 * LANES)]
    slots = 4 if direct else 1
    heads = width // LANES
    scratch = [
        pltpu.VMEM((length + 16, LANES), f32),
        pltpu.VMEM((length + 16, LANES), f32),
        pltpu.VMEM((2, length + 16, LANES), f32),
        pltpu.VMEM((2, length, LANES), bf16),
        pltpu.VMEM((2, length + 8, LANES), f32),
        pltpu.VMEM((2, heads, span + 8, LANES), f32),
        pltpu.VMEM((2, span * heads, LANES), bf16),
        pltpu.VMEM((2, span * heads, LANES), bf16),
        pltpu.VMEM((2, heads, span + 8, LANES), f32),
        pltpu.VMEM((window, LANES), f32),
        pltpu.VMEM((slots, window, 2 * LANES), f32),
        pltpu.VMEM((slots, window, 2 * LANES), f32),
        pltpu.VMEM((ctx_count, rim, 2 * LANES), f32),
        pltpu.VMEM(q_pre.shape, bf16),
        pltpu.VMEM(q_pre.shape, bf16),
        pltpu.VMEM(q_pre.shape, f32),
        pltpu.SemaphoreType.DMA((3,)),
    ]
    own_shapes = [(2 * span, 2 * LANES), (2 * span + 8, 2 * LANES)]
    d_q_main, d_q_tail, own_near, own_far, *sent = pl.pallas_call(
        functools.partial(grads_kernel, ctx_count, direct),
        out_shape=[jax.ShapeDtypeStruct(q_pre.shape, f32)]
        + [jax.ShapeDtypeStruct(shape, f32) for shape in [(2, 8, width)] + own_shapes]
        + [jax.ShapeDtypeStruct(shape, bf16) for shape in sent_shapes],
        in_specs=[smem, vmem, hbm, hbm] + [vmem] * len(received),
        out_specs=[hbm] + [vmem] * (3 + len(sent_shapes)),
        scratch_shapes=scratch,
        compiler_params=pltpu.CompilerParams(vmem_limit_bytes=(20 if direct else 62) * MIB),
        name="grads",
    )(doc_lengths, filters, in_hbm(q_pre), in_hbm(d_out), *received)
    half_terms = delivered(sent)
    merged_shapes = [
        jax.ShapeDtypeStruct((2 * span, 2 * LANES), f32),
        jax.ShapeDtypeStruct((2 * span + 32, 2 * LANES), bf16),
        jax.ShapeDtypeStruct((8, 2 * LANES), f32),
        jax.ShapeDtypeStruct((2, rim // 2, 2 * LANES), f32),
    ]
    near, far, half_sums, rims = pl.pallas_call(
        functools.partial(merge_kernel, ctx_count, direct),
        out_shape=merged_shapes,
        in_specs=[vmem] * (2 + len(half_terms)),
        out_specs=[vmem] * len(merged_shapes),
        scratch_shapes=[
            pltpu.VMEM((group, 8, 2 * LANES), f32),
            pltpu.VMEM((ctx_count, rim // 2, 2 * LANES), f32),
        ],
        compiler_params=pltpu.CompilerParams(vmem_limit_bytes=(4 if direct else 40) * MIB),
        name="merge",
    )(own_near, own_far, *half_terms)
    from_half = flipped(far, group)

    sums = pl.pallas_call(
        functools.partial(sums_kernel, span),
        out_shape=jax.ShapeDtypeStruct(filters.shape, f32),
        in_specs=[vmem, vmem],
        out_specs=vmem,
        compiler_params=pltpu.CompilerParams(vmem_limit_bytes=2 * MIB),
        name="sums",
    )(half_sums, from_half)
    count = lax.axis_size("tp")
    all_sums = [sums] + [
        lax.ppermute(sums, "tp", [(i, i ^ flip) for i in range(count)]) for flip in range(1, count)
    ]
    return pl.pallas_call(
        functools.partial(finish_kernel, ctx_count),
        out_shape=(
            jax.ShapeDtypeStruct(q_pre.shape, f32),
            jax.ShapeDtypeStruct(k_pre.shape, f32),
            jax.ShapeDtypeStruct(k_pre.shape, f32),
            jax.ShapeDtypeStruct(filters.shape, f32),
        ),
        in_specs=[smem, vmem, hbm] + [vmem] * (4 + count),
        out_specs=(hbm, hbm, hbm, hbm),
        scratch_shapes=[
            pltpu.VMEM((2, 8, width), f32),
            pltpu.VMEM(k_pre.shape, f32),
            pltpu.VMEM(k_pre.shape, f32),
            pltpu.VMEM(filters.shape, f32),
            pltpu.SemaphoreType.DMA((4,)),
        ],
        input_output_aliases={2: 0},
        compiler_params=pltpu.CompilerParams(vmem_limit_bytes=4 * MIB),
        name="finish",
    )(doc_lengths, filters, d_q_main, d_q_tail, near, from_half, rims, *all_sums)


def solution(mesh):
    split = P(None, "ctx", "tp")
    return jax.shard_map(
        shards,
        mesh=mesh,
        in_specs=(split, split, split, split, P(), P()),
        out_specs=(split, split, split, P()),
        check_vma=False,
    )
```

```python
import functools

import jax
import jax.numpy as jnp
import numpy as np
from jax import lax
from jax.experimental import pallas as pl
from jax.experimental.pallas import tpu as pltpu
from jax.sharding import PartitionSpec as P

LANES = 128
NT = (((1,), (1,)), ((), ()))
NN = (((1,), (0,)), ((), ()))
TN = (((0,), (0,)), ((), ()))
TAIL = 16
MAX_CHUNK = 640
MAX_DIRECT = 4
WINDOWS = (2, 4, 6)
MIB = 1 << 20


def loop(count, body, init, unrolled=16):
    if count <= unrolled:
        for step in range(count):
            init = body(step, init)
        return init
    return lax.fori_loop(0, count, body, init)


def aligned(start, multiple):
    return start if isinstance(start, int) else pl.multiple_of(start, multiple)


def doc_starts(lengths_ref):
    starts = [jnp.int32(0)]
    for index in range(lengths_ref.shape[0] - 1):
        starts.append(starts[-1] + lengths_ref[index])
    return starts


def fold_rows(terms):
    rows, lanes = terms.shape
    return jnp.sum(terms.reshape(rows // 8, 8, lanes), axis=0)


def split_bits(values):
    high = values.astype(jnp.bfloat16)
    low = (values - high.astype(jnp.float32)).astype(jnp.bfloat16)
    return high, low


def joined(pair):
    rows = pair.shape[0] // 2
    pair = pair.astype(jnp.float32)
    return pair[:rows] + pair[rows:]


class Slots:
    def __init__(self, refs, me):
        self.refs, self.me = refs, me

    def __getitem__(self, flip):
        if len(self.refs) == 1:
            place = lax.rem(self.me, jnp.int32(self.refs[0].shape[0]))
            return self.refs[0].at[partner(place, flip)]
        return self.refs[flip]


def partner(me, flip):
    return lax.bitwise_xor(me, jnp.int32(flip))


def pack_kernel(ctx_count, direct, k_ref, v_ref, q_ref, out_ref, *near_refs):
    span = k_ref.shape[1]
    kv = jnp.concatenate([k_ref[...], v_ref[...]], axis=2).reshape(2 * span, 2 * LANES)
    tails = []
    for half in range(2):
        last = q_ref[half].astype(jnp.float32)[TAIL - 2 :]
        tails += [last[:, at : at + 2 * LANES] for at in range(0, last.shape[1], 2 * LANES)]
    out_ref[: 2 * span] = kv
    tail = jnp.concatenate(tails, axis=0).astype(jnp.bfloat16)
    out_ref[2 * span :] = tail
    me = lax.axis_index("ctx")
    near = Slots((None,) + near_refs if direct else near_refs, me)

    def send(step, carry):
        flip = step + 1
        near[flip][:span] = jnp.where(partner(me, flip) > me, kv[:span], kv[span:])
        if not direct or flip & (flip + 1) == 0:
            near[flip][span:] = tail
        return carry

    loop(ctx_count // 2 - 1, send, 0, 16 if direct else 1)


def relay_kernel(ctx_count, own_ref, across_ref, body_ref, full_ref):
    span = own_ref.shape[0] // 2 - TAIL // 2
    low = lax.axis_index("ctx") < ctx_count // 2
    second = jnp.where(low, across_ref[span : 2 * span], own_ref[:span])
    for out_ref in (body_ref, full_ref):
        out_ref[:span] = across_ref[:span]
        out_ref[span : 2 * span] = second
    full_ref[2 * span :] = across_ref[2 * span :]


def grads_kernel(ctx_count, direct, lengths_ref, filters_ref, q_hbm, d_out_hbm, *refs):
    group = ctx_count // 2
    arrays = group - 1 if direct else 1
    own_ref, across_ref, refs = refs[0], refs[1], refs[2:]
    near_in, far_in, refs = refs[:arrays], refs[arrays : 2 * arrays], refs[2 * arrays :]
    dq_hbm, dq_tail_ref, own_near_ref, own_far_ref = refs[:4]
    arrays = group - 1 if direct else 1
    out_refs, refs = refs[4 : 4 + arrays], refs[4 + arrays :]
    same_scr, same_two_scr, kv_scr, conv_scr, dkv_scr, q_scr, qc_scr, do_scr, dq_scr = refs[:9]
    bias_scr, s_scr, dp_scr, rim_scr, q_ref, d_out_ref, dq_ref, sems = refs[9:]
    f32, bf16 = jnp.float32, jnp.bfloat16
    loads = [
        pltpu.make_async_copy(q_hbm, q_ref, sems.at[0]),
        pltpu.make_async_copy(d_out_hbm, d_out_ref, sems.at[1]),
    ]
    for load in loads:
        load.start()
    span = q_ref.shape[1]
    heads = q_ref.shape[2] // LANES
    half_rows = span * ctx_count
    length = 2 * half_rows
    blocks = 2 * ctx_count
    me = lax.axis_index("ctx")
    near_in = Slots((None,) + near_in if direct else near_in, me)
    far_in = Slots((None,) + far_in if direct else far_in, me)
    sent = Slots((own_far_ref,) + out_refs if direct else out_refs, me)
    scale = LANES**-0.5
    log2_scale = scale * 1.4426950408889634
    starts = doc_starts(lengths_ref)

    def fill(index, carry):
        rows = pl.ds(aligned(8 + index * span, 8), span)
        same_scr[rows] = jnp.ones((span, LANES), f32)
        same_two_scr[rows] = jnp.ones((span, LANES), f32)
        return carry

    loop(blocks, fill, 0)
    zeros = jnp.zeros((8, LANES), f32)
    for rows in (slice(0, 8), slice(8 + length, 16 + length)):
        same_scr[rows] = zeros
        same_two_scr[rows] = zeros
        for tensor in range(2):
            kv_scr[tensor, rows] = zeros
    for start in starts:
        same_scr[pl.ds(8 + start, 1)] = zeros[:1]
        same_two_scr[pl.ds(8 + start, 1)] = zeros[:1]
        same_two_scr[pl.ds(9 + start, 1)] = zeros[:1]

    def place(index, block):
        for tensor in range(2):
            lanes = slice(tensor * LANES, (tensor + 1) * LANES)
            kv_scr[tensor, pl.ds(aligned(8 + index * span, 8), span)] = block[:, lanes].astype(f32)

    def clear_kv(index, carry):
        for tensor in range(2):
            kv_scr[tensor, pl.ds(aligned(8 + index * span, 8), span)] = jnp.zeros((span, LANES), f32)
        return carry

    low = me < group

    def place_received(step, carry):
        flip = step + 1
        source = partner(me, flip)
        across = partner(source, group)
        near, far = near_in[flip], far_in[flip]
        place(jnp.where(source < me, source, blocks - 1 - source), near[:span])
        place(across, far[:span])
        place(jnp.where(low, blocks - 1 - across, source), far[span : 2 * span])
        if not direct or flip & (flip + 1) == 0:
            rim_scr[source] = near[span:].astype(f32)
        if not direct or flip == group - 1:
            rim_scr[across] = far[2 * span :].astype(f32)
        return carry

    loop(blocks, clear_kv, 0)
    for block_ref, index in ((own_ref, me), (across_ref, partner(me, group))):
        place(index, block_ref[:span])
        place(blocks - 1 - index, block_ref[span : 2 * span])
        rim_scr[index] = block_ref[2 * span :].astype(f32)
    loop(group - 1, place_received, 0, 16 if direct else 1)

    def taps(tensor):
        return [filters_ref[tensor, tap : tap + 1] for tap in range(3)]

    def masks(base, ahead):
        one = same_scr[pl.ds(base + 8 + min(ahead, 1), span)]
        return one, same_two_scr[pl.ds(base + 8 + ahead, span)]

    def convolve_kv(index, carry):
        base = index * span
        one, two = masks(base, 0)
        for tensor in range(2):
            zero_tap, one_tap, two_tap = taps(tensor + 1)
            total = zero_tap * kv_scr[tensor, pl.ds(aligned(base + 8, 8), span)]
            total = total + one * (one_tap * kv_scr[tensor, pl.ds(base + 7, span)])
            total = total + two * (two_tap * kv_scr[tensor, pl.ds(base + 6, span)])
            conv_scr[tensor, pl.ds(aligned(base, 16), span)] = total.astype(bf16)
        return carry

    loop(blocks, convolve_kv, 0)

    middle = me == ctx_count - 1
    rim_rows = rim_scr.shape[1] // 2
    rim_before = rim_scr[jnp.maximum(me - 1, 0)]
    rim_after = rim_scr[jnp.minimum(me + 1, ctx_count - 1)]
    late_rim = jnp.where(middle, rim_after[:rim_rows], rim_after[rim_rows:])
    rims = [rim_before[:rim_rows], late_rim]
    first_place = [me * span, (blocks - 1 - me) * span]

    for load in loads:
        load.wait()
    for half in range(2):
        one, two = masks(first_place[half], 0)
        zero_tap, one_tap, two_tap = taps(0)
        for head in range(heads):
            lanes = slice(head * LANES, (head + 1) * LANES)
            at = 2 * (head // 2)
            q_scr[half, head, 6:8] = rims[half][at : at + 2, (head % 2) * LANES : (head % 2 + 1) * LANES]
            q_scr[half, head, 8:] = q_ref[half, :, lanes].astype(f32)
            total = zero_tap * q_scr[half, head, 8:]
            total = total + one * (one_tap * q_scr[half, head, 7 : 7 + span])
            total = total + two * (two_tap * q_scr[half, head, 6 : 6 + span])
            qc_scr[half, head * span : (head + 1) * span] = total.astype(bf16)
            do_scr[half, head * span : (head + 1) * span] = d_out_ref[half, :, lanes]

    def attend(half, window, first_key):
        chunks = 1
        while window // chunks > MAX_CHUNK or window % (16 * chunks):
            chunks += 1
        size = window // chunks
        query = first_place[half] + lax.rem(
            lax.broadcasted_iota(jnp.int32, (1, LANES), 1), jnp.int32(span)
        )
        lowest = jnp.zeros((1, LANES), jnp.int32)
        for start in starts[1:]:
            lowest = jnp.where(query >= start, start, lowest)
        wide = 2 * LANES

        def fill_bias(step, carry):
            places = first_key + step * size + lax.broadcasted_iota(jnp.int32, (size, LANES), 0)
            allowed = (places >= lowest) & (places <= query)
            bias_scr[pl.ds(aligned(step * size, 16), size)] = jnp.where(allowed, 0.0, -1e30)
            return carry

        loop(chunks, fill_bias, 0, 1)
        whole_window = pl.ds(aligned(first_key, 16), window)
        keys_t = conv_scr[0, whole_window].T if chunks == 1 else None
        for at in range(heads * span // wide):
            slot = (half * (heads * span // wide) + at) % s_scr.shape[0]
            cols = slice(at * wide, (at + 1) * wide)
            queries = qc_scr[half, cols]
            grads = do_scr[half, cols]

            def key_rows(step):
                return pl.ds(aligned(first_key + step * size, 16), size)

            def score(step, top):
                keys = conv_scr[0, key_rows(step)]
                scores = lax.dot_general(keys, queries, NT, preferred_element_type=f32)
                bias = bias_scr[pl.ds(aligned(step * size, 16), size)]
                scores = scores + jnp.concatenate([bias, bias], axis=1)
                s_scr[slot, pl.ds(aligned(step * size, 16), size)] = scores
                return jnp.maximum(top, jnp.max(scores, axis=0, keepdims=True))

            top = loop(chunks, score, jnp.full((1, wide), -1e30, f32), 1)

            def weigh(step, carry):
                total, weighted = carry
                rows = pl.ds(aligned(step * size, 16), size)
                weights = jnp.exp2((s_scr[slot, rows] - top) * log2_scale)
                values = conv_scr[1, key_rows(step)]
                prob_grads = lax.dot_general(values, grads, NT, preferred_element_type=f32)
                s_scr[slot, rows] = weights
                dp_scr[slot, rows] = prob_grads
                total = total + jnp.sum(weights, axis=0, keepdims=True)
                weighted = weighted + jnp.sum(weights * prob_grads, axis=0, keepdims=True)
                return total, weighted

            zeros = jnp.zeros((1, wide), f32)
            total, weighted = loop(chunks, weigh, (zeros, zeros), 1)
            inverse = 1.0 / total
            mean = weighted * inverse
            slope = inverse * scale

            def accumulate(step, dq):
                rows = pl.ds(aligned(step * size, 16), size)
                weights = s_scr[slot, rows]
                probs = (weights * inverse).astype(bf16)
                score_grads = (weights * slope * (dp_scr[slot, rows] - mean)).astype(bf16)
                dk = lax.dot_general(score_grads, queries, NN, preferred_element_type=f32)
                dv = lax.dot_general(probs, grads, NN, preferred_element_type=f32)
                target = pl.ds(aligned(first_key + step * size, 16), size)
                for tensor, terms in enumerate((dk, dv)):
                    dkv_scr[tensor, target] += terms
                if keys_t is not None:
                    return lax.dot_general(keys_t, score_grads, NN, preferred_element_type=f32)
                keys = conv_scr[0, key_rows(step)]
                return dq + lax.dot_general(keys, score_grads, TN, preferred_element_type=f32)

            dq = loop(chunks, accumulate, jnp.zeros((LANES, wide), f32), 1)
            dq = dq.T
            for part in range(wide // span):
                head = at * (wide // span) + part
                dq_scr[half, head, :span] = dq[part * span : (part + 1) * span]

    def clear(index, carry):
        for tensor in range(2):
            dkv_scr[tensor, pl.ds(aligned(index * span, 8), span)] = jnp.zeros((span, LANES), f32)
        return carry

    loop(blocks, clear, 0)
    for tensor in range(2):
        dkv_scr[tensor, length:] = zeros

    for half in range(2):
        widest = ctx_count + half
        lowest = jnp.int32(0)
        for start in starts[1:]:
            lowest = jnp.where(first_place[half] >= start, start, lowest)
        needed = first_place[half] // span - lowest // span + 1
        below = 0
        for count in [count for count in WINDOWS if direct and count < widest] + [widest]:

            @pl.when((needed > below) & (needed <= count))
            def _(half=half, count=count):
                first_key = jnp.maximum(first_place[half] + span - count * span, 0)
                attend(half, count * span, first_key)

            below = count

    next_rows = jnp.where(middle, dq_scr[1, :, :8], 0.0)
    dq_scr[0, :, span:] = next_rows
    dq_scr[1, :, span:] = jnp.zeros_like(next_rows)
    sums = [jnp.zeros((8, LANES), f32) for _ in range(3)]
    for half in range(2):
        one, two = masks(first_place[half], 0)
        ahead_one = same_scr[pl.ds(first_place[half] + 9, span)]
        ahead_two = same_two_scr[pl.ds(first_place[half] + 10, span)]
        zero_tap, one_tap, two_tap = taps(0)
        for head in range(heads):
            lanes = slice(head * LANES, (head + 1) * LANES)
            grads = dq_scr[half, head, :span]
            out = zero_tap * grads
            out = out + ahead_one * (one_tap * dq_scr[half, head, 1 : 1 + span])
            out = out + ahead_two * (two_tap * dq_scr[half, head, 2 : 2 + span])
            dq_ref[half, :, lanes] = out
            dq_tail_ref[half, :, lanes] = out[span - 8 :]
            sums[0] += fold_rows(grads * q_scr[half, head, 8:])
            sums[1] += fold_rows(grads * one * q_scr[half, head, 7 : 7 + span])
            sums[2] += fold_rows(grads * two * q_scr[half, head, 6 : 6 + span])
    q_sums = [jnp.sum(term, axis=0, keepdims=True) for term in sums]
    store = pltpu.make_async_copy(dq_ref, dq_hbm, sems.at[2])
    store.start()

    def finish_block(index, carry, target, row):
        base = pl.multiple_of(index * span, 8)
        one, two = masks(base, 0)
        ahead_one = same_scr[pl.ds(base + 9, span)]
        ahead_two = same_two_scr[pl.ds(base + 10, span)]
        carry = list(carry)
        for tensor in range(2):
            zero_tap, one_tap, two_tap = taps(tensor + 1)
            own = dkv_scr[tensor, pl.ds(base, span)]
            out = zero_tap * own
            out = out + ahead_one * (one_tap * dkv_scr[tensor, pl.ds(base + 1, span)])
            out = out + ahead_two * (two_tap * dkv_scr[tensor, pl.ds(base + 2, span)])
            lanes = slice(tensor * LANES, (tensor + 1) * LANES)
            target[row : row + span, lanes] = out.astype(target.dtype)
            at = 3 * tensor
            carry[at] += fold_rows(own * kv_scr[tensor, pl.ds(base + 8, span)])
            carry[at + 1] += fold_rows(own * one * kv_scr[tensor, pl.ds(base + 7, span)])
            carry[at + 2] += fold_rows(own * two * kv_scr[tensor, pl.ds(base + 6, span)])
        return tuple(carry)

    def finish(step, carry):
        flip = step + 1
        owner = partner(me, flip)
        far_owner = partner(me, flip + group)
        near_late = blocks - 1 - owner
        places = [
            far_owner,
            jnp.where(low, blocks - 1 - far_owner, owner),
            jnp.where(low & (me > owner), owner, near_late),
        ]
        for at, place in enumerate(places):
            carry = finish_block(place, carry, sent[flip], at * span)
        return carry

    kv_sums = (zeros,) * 6
    for target, index in ((own_far_ref, partner(me, group)), (own_near_ref, me)):
        kv_sums = finish_block(index, kv_sums, target, 0)
        kv_sums = finish_block(blocks - 1 - index, kv_sums, target, span)
    kv_sums = loop(group - 1, finish, kv_sums)
    kv_sums = [jnp.sum(term, axis=0, keepdims=True) for term in kv_sums]

    padding = [jnp.zeros((2, LANES), f32)]
    left = jnp.concatenate(q_sums + kv_sums[:3] + padding, axis=0)
    right = jnp.concatenate([jnp.zeros((3, LANES), f32)] + kv_sums[3:] + padding, axis=0)
    sums_tile = jnp.concatenate([left, right], axis=1)
    sums_pair = jnp.concatenate(split_bits(sums_tile), axis=0)
    own_far_ref[2 * span :] = joined(sums_pair)
    rims = []
    for half in range(2):
        rows = [dq_scr[half, head, :2] for head in range(heads)]
        rows = [jnp.concatenate(rows[at : at + 2], axis=1) for at in range(0, heads, 2)]
        rims.append(jnp.concatenate(rows, axis=0))

    def rim_for(index):
        return jnp.concatenate(split_bits(jnp.where(index < me, rims[0], rims[1])), axis=0)

    def store_rims(step, carry):
        flip = step + 1
        owner = partner(me, flip)
        sent[flip][3 * span : 3 * span + 16] = sums_pair
        if not direct or flip & (flip + 1) == 0:
            across = (flip == group - 1) & (jnp.abs(owner - me) != 1)
            target = jnp.where(across, partner(owner, group), owner)
            sent[flip][3 * span + 16 :] = rim_for(target)
        return carry

    loop(group - 1, store_rims, 0, 16 if direct else 1)
    store.wait()


def merge_kernel(ctx_count, direct, own_near_ref, own_far_ref, *refs):
    received_refs = refs[:-6]
    near_ref, far_ref, half_sums_ref, rims_ref, sums_scr, rim_scr = refs[-6:]
    f32, bf16 = jnp.float32, jnp.bfloat16
    group = ctx_count // 2
    me = lax.axis_index("ctx")
    low = me < group
    received = Slots((own_far_ref,) + received_refs if direct else received_refs, me)
    place = lax.rem(me, jnp.int32(group))
    span = own_near_ref.shape[0] // 2
    rows = 2 * span
    sums_scr[place] = own_far_ref[rows:]
    neighbours = [jnp.minimum(me + 1, ctx_count - 1), jnp.maximum(me - 1, 0)]
    for index in neighbours:
        rim_scr[index] = jnp.zeros(rim_scr.shape[1:], f32)

    def add(step, carry):
        flip = step + 1
        source = partner(me, flip)
        message = received[flip]
        parts = [message[at * span : (at + 1) * span].astype(f32) for at in range(3)]
        near_early, near_late, far_early, far_late = carry
        sums_scr[partner(place, flip)] = joined(message[3 * span : 3 * span + 16])
        if not direct or flip & (flip + 1) == 0:
            rim_scr[source] = joined(message[3 * span + 16 :])
        to_early = low & (source > me)
        zero = jnp.zeros_like(parts[0])
        return (
            near_early + jnp.where(low, jnp.where(to_early, parts[2], zero), parts[1]),
            near_late + jnp.where(to_early, zero, parts[2]),
            far_early + parts[0],
            far_late + jnp.where(low, parts[1], zero),
        )

    init = (own_near_ref[:span], own_near_ref[span:], own_far_ref[:span], own_far_ref[span:rows])
    totals = loop(group - 1, add, init, 16 if direct else 1)
    near_ref[:span] = totals[0]
    near_ref[span:] = totals[1]
    far_ref[:span] = totals[2].astype(bf16)
    far_ref[span:rows] = totals[3].astype(bf16)
    sums = loop(group, lambda index, carry: carry + sums_scr[index], jnp.zeros((8, 2 * LANES), f32))
    pair = jnp.concatenate(split_bits(sums), axis=0)
    half_sums_ref[...] = joined(pair)
    far_ref[rows : rows + 16] = pair
    far_ref[rows + 16 :] = received[group - 1][3 * span + 16 :]
    for at, index in enumerate(neighbours):
        rims_ref[at] = rim_scr[index]


def sums_kernel(span, half_sums_ref, far_ref, out_ref):
    sums = half_sums_ref[...] + joined(far_ref[2 * span : 2 * span + 16])
    out_ref[0] = sums[0:3, :LANES]
    out_ref[1] = sums[3:6, :LANES]
    out_ref[2] = sums[3:6, LANES:]


def finish_kernel(
    ctx_count, lengths_ref, filters_ref, dq_in_hbm, tail_ref, near_ref, far_ref, rims_ref, *refs
):
    sums_refs, refs = refs[:-9], refs[-9:]
    dq_hbm, dk_hbm, dv_hbm, d_filters_hbm, dq_ref, dk_ref, dv_ref, d_filters_ref, sems = refs
    f32 = jnp.float32
    group = ctx_count // 2
    span = dk_ref.shape[1]
    me = lax.axis_index("ctx")
    starts = doc_starts(lengths_ref)
    blocks = 2 * ctx_count

    total = near_ref[...] + far_ref[: 2 * span].astype(f32)
    for half in range(2):
        dk_ref[half] = total[half * span : (half + 1) * span, :LANES]
        dv_ref[half] = total[half * span : (half + 1) * span, LANES:]
    stores = [
        pltpu.make_async_copy(dk_ref, dk_hbm, sems.at[0]),
        pltpu.make_async_copy(dv_ref, dv_hbm, sems.at[1]),
        pltpu.make_async_copy(d_filters_ref, d_filters_hbm, sems.at[2]),
        pltpu.make_async_copy(dq_ref, dq_hbm.at[:, pl.ds(span - 8, 8)], sems.at[3]),
    ]
    level = [ref[...] for ref in sums_refs]
    while len(level) > 1:
        level = [level[at] + level[at + 1] for at in range(0, len(level), 2)]
    d_filters_ref[...] = level[0]
    for store in stores[:3]:
        store.start()

    def same(place):
        cut = place >= blocks * span
        for start in starts:
            cut = cut | (place == start)
        return jnp.where(cut, 0.0, 1.0).astype(f32)

    heads = dq_ref.shape[2] // LANES
    taps = [jnp.concatenate([filters_ref[0, tap : tap + 1]] * heads, axis=1) for tap in range(3)]
    row = lax.broadcasted_iota(jnp.int32, dq_ref.shape[1:], 0)
    far_rim = joined(far_ref[2 * span + 16 :])
    crosses = [me == group - 1, me == group]
    first_place = [me * span, (blocks - 1 - me) * span]
    present = [me < ctx_count - 1, me > 0]
    for half in range(2):
        rim = jnp.where(crosses[half], far_rim, rims_ref[half])
        rows = jnp.concatenate([rim[2 * at : 2 * at + 2] for at in range(rim.shape[0] // 2)], axis=1)
        end = first_place[half] + span
        zero, one, two = same(end - 1), same(end), same(end + 1)
        one = jnp.where(present[half], one, 0.0)
        last_but_one = (zero * one) * (taps[2] * rows[0:1])
        last = one * (taps[1] * rows[0:1]) + (one * two) * (taps[2] * rows[1:2])
        extra = jnp.where(row == 6, last_but_one, jnp.where(row == 7, last, 0.0))
        dq_ref[half] = tail_ref[half] + extra
    stores[3].start()
    for store in stores:
        store.wait()


def shards(q_pre, k_pre, value_before_filter, d_out, filters, doc_lengths):
    f32, bf16 = jnp.float32, jnp.bfloat16
    ctx_count = lax.axis_size("ctx")
    span, width = q_pre.shape[1:]
    length = 2 * span * ctx_count
    rim = 4 * width // (2 * LANES)
    vmem = pl.BlockSpec(memory_space=pltpu.VMEM)
    smem = pl.BlockSpec(memory_space=pltpu.SMEM)
    hbm = pl.BlockSpec(memory_space=pltpu.HBM)

    group = ctx_count // 2
    direct = group <= MAX_DIRECT
    halves = [[half * group + at for at in range(group)] for half in range(2)]
    msg_rows = 2 * span + rim

    def whole(shape):
        return pl.BlockSpec(shape, lambda i: (0,) * len(shape))

    def in_hbm(array):
        return pltpu.with_memory_space_constraint(array, pltpu.HBM)

    def flipped(array, flip):
        return lax.ppermute(array, "ctx", [(i, i ^ flip) for i in range(ctx_count)])

    def gathered(array):
        return [lax.all_gather(array, "ctx", axis_index_groups=halves)]

    def delivered(arrays):
        if direct:
            return [flipped(array, step + 1) for step, array in enumerate(arrays)]
        return [lax.all_to_all(arrays[0], "ctx", 0, 0, axis_index_groups=halves, tiled=True)]

    if direct:
        near_shapes = [
            (span + (rim if flip & (flip + 1) == 0 else 0), 2 * LANES) for flip in range(1, group)
        ]
    else:
        near_shapes = [(group, span + rim, 2 * LANES)]
    packed, *near = pl.pallas_call(
        functools.partial(pack_kernel, ctx_count, direct),
        grid=(1,),
        out_shape=[
            jax.ShapeDtypeStruct(shape, bf16) for shape in [(msg_rows, 2 * LANES)] + near_shapes
        ],
        in_specs=[
            whole(k_pre.shape),
            whole(k_pre.shape),
            pl.BlockSpec((2, TAIL, width), lambda i: (0, span // TAIL - 1, 0)),
        ],
        out_specs=[whole(shape) for shape in [(msg_rows, 2 * LANES)] + near_shapes],
        compiler_params=pltpu.CompilerParams(vmem_limit_bytes=(4 if direct else 16) * MIB),
        name="pack",
    )(*[in_hbm(array) for array in (k_pre, value_before_filter, q_pre)])
    across = flipped(packed, group)
    near = delivered(near)
    across, *near = lax.optimization_barrier((across, *near))
    body, full = pl.pallas_call(
        functools.partial(relay_kernel, ctx_count),
        out_shape=[jax.ShapeDtypeStruct((rows, 2 * LANES), bf16) for rows in (2 * span, msg_rows)],
        in_specs=[vmem, vmem],
        out_specs=[vmem, vmem],
        compiler_params=pltpu.CompilerParams(vmem_limit_bytes=4 * MIB),
        name="relay",
    )(packed, across)
    if direct:
        far = [flipped(full if flip == group - 1 else body, flip) for flip in range(1, group)]
    else:
        far = gathered(full)
    received = [packed, across] + near + far

    window = span * ctx_count + span
    if direct:
        sent_shapes = [
            (3 * span + (32 if flip & (flip + 1) == 0 else 16), 2 * LANES) for flip in range(1, group)
        ]
    else:
        sent_shapes = [(group, 3 * span + 32, 2 * LANES)]
    slots = 4 if direct else 1
    heads = width // LANES
    scratch = [
        pltpu.VMEM((length + 16, LANES), f32),
        pltpu.VMEM((length + 16, LANES), f32),
        pltpu.VMEM((2, length + 16, LANES), f32),
        pltpu.VMEM((2, length, LANES), bf16),
        pltpu.VMEM((2, length + 8, LANES), f32),
        pltpu.VMEM((2, heads, span + 8, LANES), f32),
        pltpu.VMEM((2, span * heads, LANES), bf16),
        pltpu.VMEM((2, span * heads, LANES), bf16),
        pltpu.VMEM((2, heads, span + 8, LANES), f32),
        pltpu.VMEM((window, LANES), f32),
        pltpu.VMEM((slots, window, 2 * LANES), f32),
        pltpu.VMEM((slots, window, 2 * LANES), f32),
        pltpu.VMEM((ctx_count, rim, 2 * LANES), f32),
        pltpu.VMEM(q_pre.shape, bf16),
        pltpu.VMEM(q_pre.shape, bf16),
        pltpu.VMEM(q_pre.shape, f32),
        pltpu.SemaphoreType.DMA((3,)),
    ]
    own_shapes = [(2 * span, 2 * LANES), (2 * span + 8, 2 * LANES)]
    d_q_main, d_q_tail, own_near, own_far, *sent = pl.pallas_call(
        functools.partial(grads_kernel, ctx_count, direct),
        out_shape=[jax.ShapeDtypeStruct(q_pre.shape, f32)]
        + [jax.ShapeDtypeStruct(shape, f32) for shape in [(2, 8, width)] + own_shapes]
        + [jax.ShapeDtypeStruct(shape, bf16) for shape in sent_shapes],
        in_specs=[smem, vmem, hbm, hbm] + [vmem] * len(received),
        out_specs=[hbm] + [vmem] * (3 + len(sent_shapes)),
        scratch_shapes=scratch,
        compiler_params=pltpu.CompilerParams(vmem_limit_bytes=(20 if direct else 62) * MIB),
        name="grads",
    )(doc_lengths, filters, in_hbm(q_pre), in_hbm(d_out), *received)
    half_terms = delivered(sent)
    merged_shapes = [
        jax.ShapeDtypeStruct((2 * span, 2 * LANES), f32),
        jax.ShapeDtypeStruct((2 * span + 32, 2 * LANES), bf16),
        jax.ShapeDtypeStruct((8, 2 * LANES), f32),
        jax.ShapeDtypeStruct((2, rim // 2, 2 * LANES), f32),
    ]
    near, far, half_sums, rims = pl.pallas_call(
        functools.partial(merge_kernel, ctx_count, direct),
        out_shape=merged_shapes,
        in_specs=[vmem] * (2 + len(half_terms)),
        out_specs=[vmem] * len(merged_shapes),
        scratch_shapes=[
            pltpu.VMEM((group, 8, 2 * LANES), f32),
            pltpu.VMEM((ctx_count, rim // 2, 2 * LANES), f32),
        ],
        compiler_params=pltpu.CompilerParams(vmem_limit_bytes=(4 if direct else 40) * MIB),
        name="merge",
    )(own_near, own_far, *half_terms)
    from_half = flipped(far, group)

    sums = pl.pallas_call(
        functools.partial(sums_kernel, span),
        out_shape=jax.ShapeDtypeStruct(filters.shape, f32),
        in_specs=[vmem, vmem],
        out_specs=vmem,
        compiler_params=pltpu.CompilerParams(vmem_limit_bytes=2 * MIB),
        name="sums",
    )(half_sums, from_half)
    count = lax.axis_size("tp")
    all_sums = [sums] + [
        lax.ppermute(sums, "tp", [(i, i ^ flip) for i in range(count)]) for flip in range(1, count)
    ]
    return pl.pallas_call(
        functools.partial(finish_kernel, ctx_count),
        out_shape=(
            jax.ShapeDtypeStruct(q_pre.shape, f32),
            jax.ShapeDtypeStruct(k_pre.shape, f32),
            jax.ShapeDtypeStruct(k_pre.shape, f32),
            jax.ShapeDtypeStruct(filters.shape, f32),
        ),
        in_specs=[smem, vmem, hbm] + [vmem] * (4 + count),
        out_specs=(hbm, hbm, hbm, hbm),
        scratch_shapes=[
            pltpu.VMEM((2, 8, width), f32),
            pltpu.VMEM(k_pre.shape, f32),
            pltpu.VMEM(k_pre.shape, f32),
            pltpu.VMEM(filters.shape, f32),
            pltpu.SemaphoreType.DMA((4,)),
        ],
        input_output_aliases={2: 0},
        compiler_params=pltpu.CompilerParams(vmem_limit_bytes=4 * MIB),
        name="finish",
    )(doc_lengths, filters, d_q_main, d_q_tail, near, from_half, rims, *all_sums)


def solution(mesh):
    split = P(None, "ctx", "tp")
    return jax.shard_map(
        shards,
        mesh=mesh,
        in_specs=(split, split, split, split, P(), P()),
        out_specs=(split, split, split, P()),
        check_vma=False,
    )
```

```python
import functools

import jax
import jax.numpy as jnp
import numpy as np
from jax import lax
from jax.experimental import pallas as pl
from jax.experimental.pallas import tpu as pltpu
from jax.sharding import PartitionSpec as P

LANES = 128
NT = (((1,), (1,)), ((), ()))
NN = (((1,), (0,)), ((), ()))
TN = (((0,), (0,)), ((), ()))
TAIL = 16
MAX_CHUNK = 640
RIM = 8
MAX_DIRECT = 4
WINDOWS = (2, 4, 6)
MIB = 1 << 20


def loop(count, body, init, unrolled=16):
    if count <= unrolled:
        for step in range(count):
            init = body(step, init)
        return init
    return lax.fori_loop(0, count, body, init)


def aligned(start, multiple):
    return start if isinstance(start, int) else pl.multiple_of(start, multiple)


def doc_starts(lengths_ref):
    starts = [jnp.int32(0)]
    for index in range(lengths_ref.shape[0] - 1):
        starts.append(starts[-1] + lengths_ref[index])
    return starts


def fold_rows(terms):
    rows, lanes = terms.shape
    return jnp.sum(terms.reshape(rows // 8, 8, lanes), axis=0)


def split_bits(values):
    high = values.astype(jnp.bfloat16)
    low = (values - high.astype(jnp.float32)).astype(jnp.bfloat16)
    return high, low


def joined(pair):
    rows = pair.shape[0] // 2
    pair = pair.astype(jnp.float32)
    return pair[:rows] + pair[rows:]


class Slots:
    def __init__(self, refs, me):
        self.refs, self.me = refs, me

    def __getitem__(self, flip):
        if len(self.refs) == 1:
            place = lax.rem(self.me, jnp.int32(self.refs[0].shape[0]))
            return self.refs[0].at[partner(place, flip)]
        return self.refs[flip]


def partner(me, flip):
    return lax.bitwise_xor(me, jnp.int32(flip))


def pack_kernel(k_ref, v_ref, q_ref, out_ref):
    span = k_ref.shape[1]
    kv = jnp.concatenate([k_ref[...], v_ref[...]], axis=2).reshape(2 * span, 2 * LANES)
    tails = []
    for half in range(2):
        last = q_ref[half].astype(jnp.float32)[TAIL - 2 :]
        tails += [last[:, at : at + 2 * LANES] for at in range(0, last.shape[1], 2 * LANES)]
    out_ref[: 2 * span] = kv
    out_ref[2 * span :] = jnp.concatenate(tails, axis=0).astype(jnp.bfloat16)


def prep_kernel(ctx_count, direct, lengths_ref, filters_ref, q_hbm, d_out_hbm, own_ref, *refs):
    near_refs, refs = refs[:-9], refs[-9:]
    same_ref, same_two_ref, q_scr, qc_ref, do_ref, rim_scr, q_ref, d_out_ref, sems = refs
    f32, bf16 = jnp.float32, jnp.bfloat16
    loads = [
        pltpu.make_async_copy(q_hbm, q_ref, sems.at[0]),
        pltpu.make_async_copy(d_out_hbm, d_out_ref, sems.at[1]),
    ]
    for load in loads:
        load.start()
    group = ctx_count // 2
    span = q_ref.shape[1]
    heads = q_ref.shape[2] // LANES
    blocks = 2 * ctx_count
    length = span * blocks
    me = lax.axis_index("ctx")
    near = Slots((None,) + near_refs if direct else near_refs, me)
    starts = doc_starts(lengths_ref)

    def fill(index, carry):
        rows = pl.ds(aligned(8 + index * span, 8), span)
        same_ref[rows] = jnp.ones((span, LANES), f32)
        same_two_ref[rows] = jnp.ones((span, LANES), f32)
        return carry

    loop(blocks, fill, 0)
    zeros = jnp.zeros((8, LANES), f32)
    for rows in (slice(0, 8), slice(8 + length, 16 + length)):
        same_ref[rows] = zeros
        same_two_ref[rows] = zeros
    for start in starts:
        same_ref[pl.ds(8 + start, 1)] = zeros[:1]
        same_two_ref[pl.ds(8 + start, 1)] = zeros[:1]
        same_two_ref[pl.ds(9 + start, 1)] = zeros[:1]

    before, after = jnp.maximum(me - 1, 0), jnp.minimum(me + 1, ctx_count - 1)
    for index in (before, after):
        rim_scr[index] = jnp.zeros(rim_scr.shape[1:], f32)
    rim_scr[me] = own_ref[2 * span :].astype(f32)

    def place_rims(step, carry):
        flip = step + 1
        if not direct or flip & (flip + 1) == 0:
            rim_scr[partner(me, flip)] = near[flip][2 * span :].astype(f32)
        return carry

    loop(group - 1, place_rims, 0, 16 if direct else 1)
    rim_before, rim_after = rim_scr[before], rim_scr[after]
    late_rim = jnp.where(me == ctx_count - 1, rim_after[:RIM], rim_after[RIM:])
    rims = [rim_before[:RIM], late_rim]
    first_place = [me * span, (blocks - 1 - me) * span]
    taps = [filters_ref[0, tap : tap + 1] for tap in range(3)]

    for load in loads:
        load.wait()
    for half in range(2):
        rows = pl.ds(aligned(first_place[half] + 8, 8), span)
        one, two = same_ref[rows], same_two_ref[rows]
        for head in range(heads):
            lanes = slice(head * LANES, (head + 1) * LANES)
            at = 2 * (head // 2)
            q_scr[half, head, 6:8] = rims[half][at : at + 2, (head % 2) * LANES : (head % 2 + 1) * LANES]
            q_scr[half, head, 8:] = q_ref[half, :, lanes].astype(f32)
            total = taps[0] * q_scr[half, head, 8:]
            total = total + one * (taps[1] * q_scr[half, head, 7 : 7 + span])
            total = total + two * (taps[2] * q_scr[half, head, 6 : 6 + span])
            qc_ref[half, head * span : (head + 1) * span] = total.astype(bf16)
            do_ref[half, head * span : (head + 1) * span] = d_out_ref[half, :, lanes]


def grads_kernel(ctx_count, direct, lengths_ref, filters_ref, *refs):
    group = ctx_count // 2
    arrays = group - 1 if direct else 1
    same_scr, same_two_scr, q_in_ref, qc_in_ref, do_scr, own_ref, across_ref = refs[:7]
    refs = refs[7:]
    near_in, far_in, refs = refs[:arrays], refs[arrays : 2 * arrays], refs[2 * arrays :]
    dq_hbm, dq_tail_ref, own_near_ref, own_far_ref = refs[:4]
    arrays = group - 1 if direct else 1
    out_refs, refs = refs[4 : 4 + arrays], refs[4 + arrays :]
    kv_scr, conv_scr, dkv_scr, q_scr, qc_scr, dq_scr = refs[:6]
    bias_scr, s_scr, dp_scr, dq_ref, sems = refs[6:]
    f32, bf16 = jnp.float32, jnp.bfloat16
    span = own_ref.shape[0] // 2 - TAIL // 2
    heads = q_in_ref.shape[1]
    half_rows = span * ctx_count
    length = 2 * half_rows
    blocks = 2 * ctx_count
    me = lax.axis_index("ctx")
    near_in = Slots((None,) + near_in if direct else near_in, me)
    far_in = Slots((None,) + far_in if direct else far_in, me)
    sent = Slots((own_far_ref,) + out_refs if direct else out_refs, me)
    scale = LANES**-0.5
    log2_scale = scale * 1.4426950408889634
    starts = doc_starts(lengths_ref)

    def place(index, block):
        for tensor in range(2):
            lanes = slice(tensor * LANES, (tensor + 1) * LANES)
            kv_scr[tensor, pl.ds(aligned(8 + index * span, 8), span)] = block[:, lanes].astype(f32)

    def place_both(message, index):
        place(index, message[:span])
        place(blocks - 1 - index, message[span : 2 * span])

    def place_received(step, carry):
        flip = step + 1
        source = partner(me, flip)
        place_both(near_in[flip], source)
        place_both(far_in[flip], partner(source, group))
        return carry

    zeros = jnp.zeros((8, LANES), f32)
    for tensor in range(2):
        kv_scr[tensor, :8] = zeros
    for block_ref, index in ((own_ref, me), (across_ref, partner(me, group))):
        place_both(block_ref, index)
    loop(group - 1, place_received, 0, 16 if direct else 1)

    def taps(tensor):
        return [filters_ref[tensor, tap : tap + 1] for tap in range(3)]

    def masks(base, ahead):
        one = same_scr[pl.ds(base + 8 + min(ahead, 1), span)]
        return one, same_two_scr[pl.ds(base + 8 + ahead, span)]

    def convolve_kv(index, carry):
        base = index * span
        one, two = masks(base, 0)
        for tensor in range(2):
            zero_tap, one_tap, two_tap = taps(tensor + 1)
            total = zero_tap * kv_scr[tensor, pl.ds(aligned(base + 8, 8), span)]
            total = total + one * (one_tap * kv_scr[tensor, pl.ds(base + 7, span)])
            total = total + two * (two_tap * kv_scr[tensor, pl.ds(base + 6, span)])
            conv_scr[tensor, pl.ds(aligned(base, 16), span)] = total.astype(bf16)
        return carry

    loop(blocks, convolve_kv, 0)

    first_place = [me * span, (blocks - 1 - me) * span]
    middle = me == ctx_count - 1
    q_scr[...] = q_in_ref[...]
    qc_scr[...] = qc_in_ref[...]
    tails = far_in[group - 1][2 * span :].astype(f32)
    tails = [tails[:RIM], tails[RIM:]]
    for half, crossing in ((0, me == group), (1, me == group - 1)):

        @pl.when(crossing)
        def _(half=half):
            rows = pl.ds(aligned(first_place[half] + 8, 8), TAIL)
            one, two = same_scr[rows], same_two_scr[rows]
            zero_tap, one_tap, two_tap = taps(0)
            for head in range(heads):
                at = 2 * (head // 2)
                q_scr[half, head, 6:8] = tails[half][
                    at : at + 2, (head % 2) * LANES : (head % 2 + 1) * LANES
                ]
                total = zero_tap * q_scr[half, head, 8 : 8 + TAIL]
                total = total + one * (one_tap * q_scr[half, head, 7 : 7 + TAIL])
                total = total + two * (two_tap * q_scr[half, head, 6 : 6 + TAIL])
                qc_scr[half, head * span : head * span + TAIL] = total.astype(bf16)

    def attend(half, window, first_key):
        chunks = 1
        while window // chunks > MAX_CHUNK or window % (16 * chunks):
            chunks += 1
        size = window // chunks
        query = first_place[half] + lax.rem(
            lax.broadcasted_iota(jnp.int32, (1, LANES), 1), jnp.int32(span)
        )
        lowest = jnp.zeros((1, LANES), jnp.int32)
        for start in starts[1:]:
            lowest = jnp.where(query >= start, start, lowest)
        wide = 2 * LANES

        def fill_bias(step, carry):
            places = first_key + step * size + lax.broadcasted_iota(jnp.int32, (size, LANES), 0)
            allowed = (places >= lowest) & (places <= query)
            bias_scr[pl.ds(aligned(step * size, 16), size)] = jnp.where(allowed, 0.0, -1e30)
            return carry

        loop(chunks, fill_bias, 0, 1)
        whole_window = pl.ds(aligned(first_key, 16), window)
        keys_t = conv_scr[0, whole_window].T if chunks == 1 else None
        for at in range(heads * span // wide):
            slot = (half * (heads * span // wide) + at) % s_scr.shape[0]
            cols = slice(at * wide, (at + 1) * wide)
            queries = qc_scr[half, cols]
            grads = do_scr[half, cols]

            def key_rows(step):
                return pl.ds(aligned(first_key + step * size, 16), size)

            def score(step, top):
                keys = conv_scr[0, key_rows(step)]
                scores = lax.dot_general(keys, queries, NT, preferred_element_type=f32)
                bias = bias_scr[pl.ds(aligned(step * size, 16), size)]
                scores = scores + jnp.concatenate([bias, bias], axis=1)
                s_scr[slot, pl.ds(aligned(step * size, 16), size)] = scores
                return jnp.maximum(top, jnp.max(scores, axis=0, keepdims=True))

            top = loop(chunks, score, jnp.full((1, wide), -1e30, f32), 1)

            def weigh(step, carry):
                total, weighted = carry
                rows = pl.ds(aligned(step * size, 16), size)
                weights = jnp.exp2((s_scr[slot, rows] - top) * log2_scale)
                values = conv_scr[1, key_rows(step)]
                prob_grads = lax.dot_general(values, grads, NT, preferred_element_type=f32)
                s_scr[slot, rows] = weights
                dp_scr[slot, rows] = prob_grads
                total = total + jnp.sum(weights, axis=0, keepdims=True)
                weighted = weighted + jnp.sum(weights * prob_grads, axis=0, keepdims=True)
                return total, weighted

            zeros = jnp.zeros((1, wide), f32)
            total, weighted = loop(chunks, weigh, (zeros, zeros), 1)
            inverse = 1.0 / total
            mean = weighted * inverse
            slope = inverse * scale

            def accumulate(step, dq):
                rows = pl.ds(aligned(step * size, 16), size)
                weights = s_scr[slot, rows]
                probs = (weights * inverse).astype(bf16)
                score_grads = (weights * slope * (dp_scr[slot, rows] - mean)).astype(bf16)
                dk = lax.dot_general(score_grads, queries, NN, preferred_element_type=f32)
                dv = lax.dot_general(probs, grads, NN, preferred_element_type=f32)
                target = pl.ds(aligned(first_key + step * size, 16), size)
                for tensor, terms in enumerate((dk, dv)):
                    dkv_scr[tensor, target] += terms
                if keys_t is not None:
                    return lax.dot_general(keys_t, score_grads, NN, preferred_element_type=f32)
                keys = conv_scr[0, key_rows(step)]
                return dq + lax.dot_general(keys, score_grads, TN, preferred_element_type=f32)

            dq = loop(chunks, accumulate, jnp.zeros((LANES, wide), f32), 1)
            dq = dq.T
            for part in range(wide // span):
                head = at * (wide // span) + part
                dq_scr[half, head, :span] = dq[part * span : (part + 1) * span]

    def clear(index, carry):
        for tensor in range(2):
            dkv_scr[tensor, pl.ds(aligned(index * span, 8), span)] = jnp.zeros((span, LANES), f32)
        return carry

    loop(blocks, clear, 0)
    for tensor in range(2):
        dkv_scr[tensor, length:] = zeros

    for half in range(2):
        widest = ctx_count + half
        lowest = jnp.int32(0)
        for start in starts[1:]:
            lowest = jnp.where(first_place[half] >= start, start, lowest)
        needed = first_place[half] // span - lowest // span + 1
        below = 0
        for count in [count for count in WINDOWS if direct and count < widest] + [widest]:

            @pl.when((needed > below) & (needed <= count))
            def _(half=half, count=count):
                first_key = jnp.maximum(first_place[half] + span - count * span, 0)
                attend(half, count * span, first_key)

            below = count

    next_rows = jnp.where(middle, dq_scr[1, :, :8], 0.0)
    dq_scr[0, :, span:] = next_rows
    dq_scr[1, :, span:] = jnp.zeros_like(next_rows)
    sums = [jnp.zeros((8, LANES), f32) for _ in range(3)]
    for half in range(2):
        one, two = masks(first_place[half], 0)
        ahead_one = same_scr[pl.ds(first_place[half] + 9, span)]
        ahead_two = same_two_scr[pl.ds(first_place[half] + 10, span)]
        zero_tap, one_tap, two_tap = taps(0)
        for head in range(heads):
            lanes = slice(head * LANES, (head + 1) * LANES)
            grads = dq_scr[half, head, :span]
            out = zero_tap * grads
            out = out + ahead_one * (one_tap * dq_scr[half, head, 1 : 1 + span])
            out = out + ahead_two * (two_tap * dq_scr[half, head, 2 : 2 + span])
            dq_ref[half, :, lanes] = out
            dq_tail_ref[half, :, lanes] = out[span - 8 :]
            sums[0] += fold_rows(grads * q_scr[half, head, 8:])
            sums[1] += fold_rows(grads * one * q_scr[half, head, 7 : 7 + span])
            sums[2] += fold_rows(grads * two * q_scr[half, head, 6 : 6 + span])
    q_sums = [jnp.sum(term, axis=0, keepdims=True) for term in sums]
    store = pltpu.make_async_copy(dq_ref, dq_hbm, sems.at[0])
    store.start()

    def finish_block(index, carry, target, row):
        base = pl.multiple_of(index * span, 8)
        one, two = masks(base, 0)
        ahead_one = same_scr[pl.ds(base + 9, span)]
        ahead_two = same_two_scr[pl.ds(base + 10, span)]
        carry = list(carry)
        for tensor in range(2):
            zero_tap, one_tap, two_tap = taps(tensor + 1)
            own = dkv_scr[tensor, pl.ds(base, span)]
            out = zero_tap * own
            out = out + ahead_one * (one_tap * dkv_scr[tensor, pl.ds(base + 1, span)])
            out = out + ahead_two * (two_tap * dkv_scr[tensor, pl.ds(base + 2, span)])
            lanes = slice(tensor * LANES, (tensor + 1) * LANES)
            target[row : row + span, lanes] = out.astype(target.dtype)
            at = 3 * tensor
            carry[at] += fold_rows(own * kv_scr[tensor, pl.ds(base + 8, span)])
            carry[at + 1] += fold_rows(own * one * kv_scr[tensor, pl.ds(base + 7, span)])
            carry[at + 2] += fold_rows(own * two * kv_scr[tensor, pl.ds(base + 6, span)])
        return tuple(carry)

    low = me < group

    def finish(step, carry):
        flip = step + 1
        owner = partner(me, flip)
        far_owner = partner(me, flip + group)
        near_late = blocks - 1 - owner
        places = [
            far_owner,
            jnp.where(low, blocks - 1 - far_owner, owner),
            jnp.where(low & (me > owner), owner, near_late),
        ]
        for at, place in enumerate(places):
            carry = finish_block(place, carry, sent[flip], at * span)
        return carry

    kv_sums = (zeros,) * 6
    for target, index in ((own_far_ref, partner(me, group)), (own_near_ref, me)):
        kv_sums = finish_block(index, kv_sums, target, 0)
        kv_sums = finish_block(blocks - 1 - index, kv_sums, target, span)
    kv_sums = loop(group - 1, finish, kv_sums)
    kv_sums = [jnp.sum(term, axis=0, keepdims=True) for term in kv_sums]

    padding = [jnp.zeros((2, LANES), f32)]
    left = jnp.concatenate(q_sums + kv_sums[:3] + padding, axis=0)
    right = jnp.concatenate([jnp.zeros((3, LANES), f32)] + kv_sums[3:] + padding, axis=0)
    sums_tile = jnp.concatenate([left, right], axis=1)
    sums_pair = jnp.concatenate(split_bits(sums_tile), axis=0)
    own_far_ref[2 * span :] = joined(sums_pair)
    rims = []
    for half in range(2):
        rows = [dq_scr[half, head, :2] for head in range(heads)]
        rows = [jnp.concatenate(rows[at : at + 2], axis=1) for at in range(0, heads, 2)]
        rims.append(jnp.concatenate(rows, axis=0))

    def rim_for(index):
        return jnp.concatenate(split_bits(jnp.where(index < me, rims[0], rims[1])), axis=0)

    def store_rims(step, carry):
        flip = step + 1
        owner = partner(me, flip)
        sent[flip][3 * span : 3 * span + 16] = sums_pair
        if not direct or flip & (flip + 1) == 0:
            across = (flip == group - 1) & (jnp.abs(owner - me) != 1)
            target = jnp.where(across, partner(owner, group), owner)
            sent[flip][3 * span + 16 :] = rim_for(target)
        return carry

    loop(group - 1, store_rims, 0, 16 if direct else 1)
    store.wait()


def merge_kernel(ctx_count, direct, own_near_ref, own_far_ref, *refs):
    received_refs = refs[:-6]
    near_ref, far_ref, half_sums_ref, rims_ref, sums_scr, rim_scr = refs[-6:]
    f32, bf16 = jnp.float32, jnp.bfloat16
    group = ctx_count // 2
    me = lax.axis_index("ctx")
    low = me < group
    received = Slots((own_far_ref,) + received_refs if direct else received_refs, me)
    place = lax.rem(me, jnp.int32(group))
    span = own_near_ref.shape[0] // 2
    rows = 2 * span
    sums_scr[place] = own_far_ref[rows:]
    neighbours = [jnp.minimum(me + 1, ctx_count - 1), jnp.maximum(me - 1, 0)]
    for index in neighbours:
        rim_scr[index] = jnp.zeros(rim_scr.shape[1:], f32)

    def add(step, carry):
        flip = step + 1
        source = partner(me, flip)
        message = received[flip]
        parts = [message[at * span : (at + 1) * span].astype(f32) for at in range(3)]
        near_early, near_late, far_early, far_late = carry
        sums_scr[partner(place, flip)] = joined(message[3 * span : 3 * span + 16])
        if not direct or flip & (flip + 1) == 0:
            rim_scr[source] = joined(message[3 * span + 16 :])
        to_early = low & (source > me)
        zero = jnp.zeros_like(parts[0])
        return (
            near_early + jnp.where(low, jnp.where(to_early, parts[2], zero), parts[1]),
            near_late + jnp.where(to_early, zero, parts[2]),
            far_early + parts[0],
            far_late + jnp.where(low, parts[1], zero),
        )

    init = (own_near_ref[:span], own_near_ref[span:], own_far_ref[:span], own_far_ref[span:rows])
    totals = loop(group - 1, add, init, 16 if direct else 1)
    near_ref[:span] = totals[0]
    near_ref[span:] = totals[1]
    far_ref[:span] = totals[2].astype(bf16)
    far_ref[span:rows] = totals[3].astype(bf16)
    sums = loop(group, lambda index, carry: carry + sums_scr[index], jnp.zeros((8, 2 * LANES), f32))
    pair = jnp.concatenate(split_bits(sums), axis=0)
    half_sums_ref[...] = joined(pair)
    far_ref[rows : rows + 16] = pair
    far_ref[rows + 16 :] = received[group - 1][3 * span + 16 :]
    for at, index in enumerate(neighbours):
        rims_ref[at] = rim_scr[index]


def sums_kernel(span, half_sums_ref, far_ref, out_ref):
    sums = half_sums_ref[...] + joined(far_ref[2 * span : 2 * span + 16])
    out_ref[0] = sums[0:3, :LANES]
    out_ref[1] = sums[3:6, :LANES]
    out_ref[2] = sums[3:6, LANES:]


def finish_kernel(
    ctx_count, lengths_ref, filters_ref, dq_in_hbm, tail_ref, near_ref, far_ref, rims_ref, *refs
):
    sums_refs, refs = refs[:-9], refs[-9:]
    dq_hbm, dk_hbm, dv_hbm, d_filters_hbm, dq_ref, dk_ref, dv_ref, d_filters_ref, sems = refs
    f32 = jnp.float32
    group = ctx_count // 2
    span = dk_ref.shape[1]
    me = lax.axis_index("ctx")
    starts = doc_starts(lengths_ref)
    blocks = 2 * ctx_count

    total = near_ref[...] + far_ref[: 2 * span].astype(f32)
    for half in range(2):
        dk_ref[half] = total[half * span : (half + 1) * span, :LANES]
        dv_ref[half] = total[half * span : (half + 1) * span, LANES:]
    stores = [
        pltpu.make_async_copy(dk_ref, dk_hbm, sems.at[0]),
        pltpu.make_async_copy(dv_ref, dv_hbm, sems.at[1]),
        pltpu.make_async_copy(d_filters_ref, d_filters_hbm, sems.at[2]),
        pltpu.make_async_copy(dq_ref, dq_hbm.at[:, pl.ds(span - 8, 8)], sems.at[3]),
    ]
    level = [ref[...] for ref in sums_refs]
    while len(level) > 1:
        level = [level[at] + level[at + 1] for at in range(0, len(level), 2)]
    d_filters_ref[...] = level[0]
    for store in stores[:3]:
        store.start()

    def same(place):
        cut = place >= blocks * span
        for start in starts:
            cut = cut | (place == start)
        return jnp.where(cut, 0.0, 1.0).astype(f32)

    heads = dq_ref.shape[2] // LANES
    taps = [jnp.concatenate([filters_ref[0, tap : tap + 1]] * heads, axis=1) for tap in range(3)]
    row = lax.broadcasted_iota(jnp.int32, dq_ref.shape[1:], 0)
    far_rim = joined(far_ref[2 * span + 16 :])
    crosses = [me == group - 1, me == group]
    first_place = [me * span, (blocks - 1 - me) * span]
    present = [me < ctx_count - 1, me > 0]
    for half in range(2):
        rim = jnp.where(crosses[half], far_rim, rims_ref[half])
        rows = jnp.concatenate([rim[2 * at : 2 * at + 2] for at in range(rim.shape[0] // 2)], axis=1)
        end = first_place[half] + span
        zero, one, two = same(end - 1), same(end), same(end + 1)
        one = jnp.where(present[half], one, 0.0)
        last_but_one = (zero * one) * (taps[2] * rows[0:1])
        last = one * (taps[1] * rows[0:1]) + (one * two) * (taps[2] * rows[1:2])
        extra = jnp.where(row == 6, last_but_one, jnp.where(row == 7, last, 0.0))
        dq_ref[half] = tail_ref[half] + extra
    stores[3].start()
    for store in stores:
        store.wait()


def shards(q_pre, k_pre, value_before_filter, d_out, filters, doc_lengths):
    f32, bf16 = jnp.float32, jnp.bfloat16
    ctx_count = lax.axis_size("ctx")
    span, width = q_pre.shape[1:]
    length = 2 * span * ctx_count
    rim = 4 * width // (2 * LANES)
    vmem = pl.BlockSpec(memory_space=pltpu.VMEM)
    smem = pl.BlockSpec(memory_space=pltpu.SMEM)
    hbm = pl.BlockSpec(memory_space=pltpu.HBM)

    group = ctx_count // 2
    direct = group <= MAX_DIRECT
    halves = [[half * group + at for at in range(group)] for half in range(2)]
    msg_rows = 2 * span + rim

    def whole(shape):
        return pl.BlockSpec(shape, lambda i: (0,) * len(shape))

    def in_hbm(array):
        return pltpu.with_memory_space_constraint(array, pltpu.HBM)

    def flipped(array, flip):
        return lax.ppermute(array, "ctx", [(i, i ^ flip) for i in range(ctx_count)])

    def gathered(array):
        if direct:
            return [flipped(array, flip) for flip in range(1, group)]
        return [lax.all_gather(array, "ctx", axis_index_groups=halves)]

    def delivered(arrays):
        if direct:
            return [flipped(array, step + 1) for step, array in enumerate(arrays)]
        return [lax.all_to_all(arrays[0], "ctx", 0, 0, axis_index_groups=halves, tiled=True)]

    packed = pl.pallas_call(
        pack_kernel,
        grid=(1,),
        out_shape=jax.ShapeDtypeStruct((msg_rows, 2 * LANES), bf16),
        in_specs=[
            whole(k_pre.shape),
            whole(k_pre.shape),
            pl.BlockSpec((2, TAIL, width), lambda i: (0, span // TAIL - 1, 0)),
        ],
        out_specs=whole((msg_rows, 2 * LANES)),
        compiler_params=pltpu.CompilerParams(vmem_limit_bytes=4 * MIB),
        name="pack",
    )(*[in_hbm(array) for array in (k_pre, value_before_filter, q_pre)])
    across = flipped(packed, group)
    near = gathered(packed)
    far = gathered(across)
    received = [packed, across] + near + far

    window = span * ctx_count + span
    if direct:
        sent_shapes = [
            (3 * span + (32 if flip & (flip + 1) == 0 else 16), 2 * LANES) for flip in range(1, group)
        ]
    else:
        sent_shapes = [(group, 3 * span + 32, 2 * LANES)]
    slots = 4 if direct else 1
    heads = width // LANES
    by_head = (2, span * heads, LANES)
    padded = (2, heads, span + 8, LANES)
    prepared = pl.pallas_call(
        functools.partial(prep_kernel, ctx_count, direct),
        out_shape=[
            jax.ShapeDtypeStruct((length + 16, LANES), f32),
            jax.ShapeDtypeStruct((length + 16, LANES), f32),
            jax.ShapeDtypeStruct(padded, f32),
            jax.ShapeDtypeStruct(by_head, bf16),
            jax.ShapeDtypeStruct(by_head, bf16),
        ],
        in_specs=[smem, vmem, hbm, hbm] + [vmem] * (1 + len(near)),
        out_specs=[vmem] * 5,
        scratch_shapes=[
            pltpu.VMEM((ctx_count, rim, 2 * LANES), f32),
            pltpu.VMEM(q_pre.shape, bf16),
            pltpu.VMEM(q_pre.shape, bf16),
            pltpu.SemaphoreType.DMA((2,)),
        ],
        compiler_params=pltpu.CompilerParams(vmem_limit_bytes=(8 if direct else 32) * MIB),
        name="prep",
    )(doc_lengths, filters, in_hbm(q_pre), in_hbm(d_out), packed, *near)
    scratch = [
        pltpu.VMEM((2, length + 16, LANES), f32),
        pltpu.VMEM((2, length, LANES), bf16),
        pltpu.VMEM((2, length + 8, LANES), f32),
        pltpu.VMEM(padded, f32),
        pltpu.VMEM(by_head, bf16),
        pltpu.VMEM(padded, f32),
        pltpu.VMEM((window, LANES), f32),
        pltpu.VMEM((slots, window, 2 * LANES), f32),
        pltpu.VMEM((slots, window, 2 * LANES), f32),
        pltpu.VMEM(q_pre.shape, f32),
        pltpu.SemaphoreType.DMA((1,)),
    ]
    own_shapes = [(2 * span, 2 * LANES), (2 * span + 8, 2 * LANES)]
    d_q_main, d_q_tail, own_near, own_far, *sent = pl.pallas_call(
        functools.partial(grads_kernel, ctx_count, direct),
        out_shape=[jax.ShapeDtypeStruct(q_pre.shape, f32)]
        + [jax.ShapeDtypeStruct(shape, f32) for shape in [(2, 8, width)] + own_shapes]
        + [jax.ShapeDtypeStruct(shape, bf16) for shape in sent_shapes],
        in_specs=[smem, vmem] + [vmem] * (len(prepared) + len(received)),
        out_specs=[hbm] + [vmem] * (3 + len(sent_shapes)),
        scratch_shapes=scratch,
        compiler_params=pltpu.CompilerParams(vmem_limit_bytes=(20 if direct else 62) * MIB),
        name="grads",
    )(doc_lengths, filters, *prepared, *received)
    half_terms = delivered(sent)
    merged_shapes = [
        jax.ShapeDtypeStruct((2 * span, 2 * LANES), f32),
        jax.ShapeDtypeStruct((2 * span + 32, 2 * LANES), bf16),
        jax.ShapeDtypeStruct((8, 2 * LANES), f32),
        jax.ShapeDtypeStruct((2, rim // 2, 2 * LANES), f32),
    ]
    near, far, half_sums, rims = pl.pallas_call(
        functools.partial(merge_kernel, ctx_count, direct),
        out_shape=merged_shapes,
        in_specs=[vmem] * (2 + len(half_terms)),
        out_specs=[vmem] * len(merged_shapes),
        scratch_shapes=[
            pltpu.VMEM((group, 8, 2 * LANES), f32),
            pltpu.VMEM((ctx_count, rim // 2, 2 * LANES), f32),
        ],
        compiler_params=pltpu.CompilerParams(vmem_limit_bytes=(4 if direct else 40) * MIB),
        name="merge",
    )(own_near, own_far, *half_terms)
    from_half = flipped(far, group)

    sums = pl.pallas_call(
        functools.partial(sums_kernel, span),
        out_shape=jax.ShapeDtypeStruct(filters.shape, f32),
        in_specs=[vmem, vmem],
        out_specs=vmem,
        compiler_params=pltpu.CompilerParams(vmem_limit_bytes=2 * MIB),
        name="sums",
    )(half_sums, from_half)
    count = lax.axis_size("tp")
    all_sums = [sums] + [
        lax.ppermute(sums, "tp", [(i, i ^ flip) for i in range(count)]) for flip in range(1, count)
    ]
    return pl.pallas_call(
        functools.partial(finish_kernel, ctx_count),
        out_shape=(
            jax.ShapeDtypeStruct(q_pre.shape, f32),
            jax.ShapeDtypeStruct(k_pre.shape, f32),
            jax.ShapeDtypeStruct(k_pre.shape, f32),
            jax.ShapeDtypeStruct(filters.shape, f32),
        ),
        in_specs=[smem, vmem, hbm] + [vmem] * (4 + count),
        out_specs=(hbm, hbm, hbm, hbm),
        scratch_shapes=[
            pltpu.VMEM((2, 8, width), f32),
            pltpu.VMEM(k_pre.shape, f32),
            pltpu.VMEM(k_pre.shape, f32),
            pltpu.VMEM(filters.shape, f32),
            pltpu.SemaphoreType.DMA((4,)),
        ],
        input_output_aliases={2: 0},
        compiler_params=pltpu.CompilerParams(vmem_limit_bytes=4 * MIB),
        name="finish",
    )(doc_lengths, filters, d_q_main, d_q_tail, near, from_half, rims, *all_sums)


def solution(mesh):
    split = P(None, "ctx", "tp")
    return jax.shard_map(
        shards,
        mesh=mesh,
        in_specs=(split, split, split, split, P(), P()),
        out_specs=(split, split, split, P()),
        check_vma=False,
    )
```

```python
import functools

import jax
import jax.numpy as jnp
import numpy as np
from jax import lax
from jax.experimental import pallas as pl
from jax.experimental.pallas import tpu as pltpu
from jax.sharding import PartitionSpec as P

LANES = 128
NT = (((1,), (1,)), ((), ()))
NN = (((1,), (0,)), ((), ()))
TN = (((0,), (0,)), ((), ()))
TAIL = 16
MAX_CHUNK = 640
RIM = 8
MAX_DIRECT = 4
WINDOWS = (2, 4, 6)
MIB = 1 << 20


def loop(count, body, init, unrolled=16):
    if count <= unrolled:
        for step in range(count):
            init = body(step, init)
        return init
    return lax.fori_loop(0, count, body, init)


def aligned(start, multiple):
    return start if isinstance(start, int) else pl.multiple_of(start, multiple)


def doc_starts(lengths_ref):
    starts = [jnp.int32(0)]
    for index in range(lengths_ref.shape[0] - 1):
        starts.append(starts[-1] + lengths_ref[index])
    return starts


def fold_rows(terms):
    rows, lanes = terms.shape
    return jnp.sum(terms.reshape(rows // 8, 8, lanes), axis=0)


def split_bits(values):
    high = values.astype(jnp.bfloat16)
    low = (values - high.astype(jnp.float32)).astype(jnp.bfloat16)
    return high, low


def joined(pair):
    rows = pair.shape[0] // 2
    pair = pair.astype(jnp.float32)
    return pair[:rows] + pair[rows:]


class Slots:
    def __init__(self, refs, me):
        self.refs, self.me = refs, me

    def __getitem__(self, flip):
        if len(self.refs) == 1:
            place = lax.rem(self.me, jnp.int32(self.refs[0].shape[0]))
            return self.refs[0].at[partner(place, flip)]
        return self.refs[flip]


def partner(me, flip):
    return lax.bitwise_xor(me, jnp.int32(flip))


def pack_kernel(k_ref, v_ref, q_ref, out_ref):
    span = k_ref.shape[1]
    kv = jnp.concatenate([k_ref[...], v_ref[...]], axis=2).reshape(2 * span, 2 * LANES)
    tails = []
    for half in range(2):
        last = q_ref[half].astype(jnp.float32)[TAIL - 2 :]
        tails += [last[:, at : at + 2 * LANES] for at in range(0, last.shape[1], 2 * LANES)]
    out_ref[: 2 * span] = kv
    out_ref[2 * span :] = jnp.concatenate(tails, axis=0).astype(jnp.bfloat16)


def prep_kernel(ctx_count, direct, lengths_ref, filters_ref, q_hbm, d_out_hbm, own_ref, *refs):
    near_refs, refs = refs[:-9], refs[-9:]
    same_ref, same_two_ref, q_scr, qc_ref, do_ref, rim_scr, q_ref, d_out_ref, sems = refs
    f32, bf16 = jnp.float32, jnp.bfloat16
    loads = [
        pltpu.make_async_copy(q_hbm, q_ref, sems.at[0]),
        pltpu.make_async_copy(d_out_hbm, d_out_ref, sems.at[1]),
    ]
    for load in loads:
        load.start()
    group = ctx_count // 2
    span = q_ref.shape[1]
    heads = q_ref.shape[2] // LANES
    blocks = 2 * ctx_count
    length = span * blocks
    me = lax.axis_index("ctx")
    near = Slots((None,) + near_refs if direct else near_refs, me)
    starts = doc_starts(lengths_ref)

    def fill(index, carry):
        rows = pl.ds(aligned(8 + index * span, 8), span)
        same_ref[rows] = jnp.ones((span, LANES), f32)
        same_two_ref[rows] = jnp.ones((span, LANES), f32)
        return carry

    loop(blocks, fill, 0)
    zeros = jnp.zeros((8, LANES), f32)
    for rows in (slice(0, 8), slice(8 + length, 16 + length)):
        same_ref[rows] = zeros
        same_two_ref[rows] = zeros
    for start in starts:
        same_ref[pl.ds(8 + start, 1)] = zeros[:1]
        same_two_ref[pl.ds(8 + start, 1)] = zeros[:1]
        same_two_ref[pl.ds(9 + start, 1)] = zeros[:1]

    before, after = jnp.maximum(me - 1, 0), jnp.minimum(me + 1, ctx_count - 1)
    for index in (before, after):
        rim_scr[index] = jnp.zeros(rim_scr.shape[1:], f32)
    rim_scr[me] = own_ref[2 * span :].astype(f32)

    def place_rims(step, carry):
        flip = step + 1
        if not direct or flip & (flip + 1) == 0:
            rim_scr[partner(me, flip)] = near[flip][2 * span :].astype(f32)
        return carry

    loop(group - 1, place_rims, 0, 16 if direct else 1)
    rim_before, rim_after = rim_scr[before], rim_scr[after]
    late_rim = jnp.where(me == ctx_count - 1, rim_after[:RIM], rim_after[RIM:])
    rims = [rim_before[:RIM], late_rim]
    first_place = [me * span, (blocks - 1 - me) * span]
    taps = [filters_ref[0, tap : tap + 1] for tap in range(3)]

    for load in loads:
        load.wait()
    for half in range(2):
        rows = pl.ds(aligned(first_place[half] + 8, 8), span)
        one, two = same_ref[rows], same_two_ref[rows]
        for head in range(heads):
            lanes = slice(head * LANES, (head + 1) * LANES)
            at = 2 * (head // 2)
            q_scr[half, head, 6:8] = rims[half][at : at + 2, (head % 2) * LANES : (head % 2 + 1) * LANES]
            q_scr[half, head, 8:] = q_ref[half, :, lanes].astype(f32)
            total = taps[0] * q_scr[half, head, 8:]
            total = total + one * (taps[1] * q_scr[half, head, 7 : 7 + span])
            total = total + two * (taps[2] * q_scr[half, head, 6 : 6 + span])
            qc_ref[half, head * span : (head + 1) * span] = total.astype(bf16)
            do_ref[half, head * span : (head + 1) * span] = d_out_ref[half, :, lanes]


def grads_kernel(ctx_count, direct, lengths_ref, filters_ref, *refs):
    group = ctx_count // 2
    arrays = group - 1 if direct else 1
    same_scr, same_two_scr, q_in_ref, qc_in_ref, do_scr, own_ref, across_ref = refs[:7]
    refs = refs[7:]
    near_in, far_in, refs = refs[:arrays], refs[arrays : 2 * arrays], refs[2 * arrays :]
    dq_hbm, dq_tail_ref, own_near_ref, own_far_ref = refs[:4]
    arrays = group - 1 if direct else 1
    first_out, late_out, refs = refs[4 : 4 + arrays], refs[4 + arrays : 4 + 2 * arrays], refs[4 + 2 * arrays :]
    kv_scr, conv_scr, dkv_scr, q_scr, qc_scr, dq_scr = refs[:6]
    bias_scr, s_scr, dp_scr, dq_ref, sems = refs[6:]
    f32, bf16 = jnp.float32, jnp.bfloat16
    span = own_ref.shape[0] // 2 - TAIL // 2
    heads = q_in_ref.shape[1]
    half_rows = span * ctx_count
    length = 2 * half_rows
    blocks = 2 * ctx_count
    me = lax.axis_index("ctx")
    near_in = Slots((None,) + near_in if direct else near_in, me)
    far_in = Slots((None,) + far_in if direct else far_in, me)
    first_out = Slots((None,) + first_out if direct else first_out, me)
    late_out = Slots((None,) + late_out if direct else late_out, me)
    scale = LANES**-0.5
    log2_scale = scale * 1.4426950408889634
    starts = doc_starts(lengths_ref)

    def place(index, block):
        for tensor in range(2):
            lanes = slice(tensor * LANES, (tensor + 1) * LANES)
            kv_scr[tensor, pl.ds(aligned(8 + index * span, 8), span)] = block[:, lanes].astype(f32)

    def place_both(message, index):
        place(index, message[:span])
        place(blocks - 1 - index, message[span : 2 * span])

    def place_received(step, carry):
        flip = step + 1
        source = partner(me, flip)
        place_both(near_in[flip], source)
        place_both(far_in[flip], partner(source, group))
        return carry

    zeros = jnp.zeros((8, LANES), f32)
    for tensor in range(2):
        kv_scr[tensor, :8] = zeros
    for block_ref, index in ((own_ref, me), (across_ref, partner(me, group))):
        place_both(block_ref, index)
    loop(group - 1, place_received, 0, 16 if direct else 1)

    def taps(tensor):
        return [filters_ref[tensor, tap : tap + 1] for tap in range(3)]

    def masks(base, ahead):
        one = same_scr[pl.ds(base + 8 + min(ahead, 1), span)]
        return one, same_two_scr[pl.ds(base + 8 + ahead, span)]

    def convolve_kv(index, carry):
        base = index * span
        one, two = masks(base, 0)
        for tensor in range(2):
            zero_tap, one_tap, two_tap = taps(tensor + 1)
            total = zero_tap * kv_scr[tensor, pl.ds(aligned(base + 8, 8), span)]
            total = total + one * (one_tap * kv_scr[tensor, pl.ds(base + 7, span)])
            total = total + two * (two_tap * kv_scr[tensor, pl.ds(base + 6, span)])
            conv_scr[tensor, pl.ds(aligned(base, 16), span)] = total.astype(bf16)
        return carry

    loop(blocks, convolve_kv, 0)

    first_place = [me * span, (blocks - 1 - me) * span]
    middle = me == ctx_count - 1
    q_scr[...] = q_in_ref[...]
    qc_scr[...] = qc_in_ref[...]
    tails = far_in[group - 1][2 * span :].astype(f32)
    tails = [tails[:RIM], tails[RIM:]]
    for half, crossing in ((0, me == group), (1, me == group - 1)):

        @pl.when(crossing)
        def _(half=half):
            rows = pl.ds(aligned(first_place[half] + 8, 8), TAIL)
            one, two = same_scr[rows], same_two_scr[rows]
            zero_tap, one_tap, two_tap = taps(0)
            for head in range(heads):
                at = 2 * (head // 2)
                q_scr[half, head, 6:8] = tails[half][
                    at : at + 2, (head % 2) * LANES : (head % 2 + 1) * LANES
                ]
                total = zero_tap * q_scr[half, head, 8 : 8 + TAIL]
                total = total + one * (one_tap * q_scr[half, head, 7 : 7 + TAIL])
                total = total + two * (two_tap * q_scr[half, head, 6 : 6 + TAIL])
                qc_scr[half, head * span : head * span + TAIL] = total.astype(bf16)

    def attend(half, window, first_key):
        chunks = 1
        while window // chunks > MAX_CHUNK or window % (16 * chunks):
            chunks += 1
        size = window // chunks
        query = first_place[half] + lax.rem(
            lax.broadcasted_iota(jnp.int32, (1, LANES), 1), jnp.int32(span)
        )
        lowest = jnp.zeros((1, LANES), jnp.int32)
        for start in starts[1:]:
            lowest = jnp.where(query >= start, start, lowest)
        wide = 2 * LANES

        def fill_bias(step, carry):
            places = first_key + step * size + lax.broadcasted_iota(jnp.int32, (size, LANES), 0)
            allowed = (places >= lowest) & (places <= query)
            bias_scr[pl.ds(aligned(step * size, 16), size)] = jnp.where(allowed, 0.0, -1e30)
            return carry

        loop(chunks, fill_bias, 0, 1)
        whole_window = pl.ds(aligned(first_key, 16), window)
        keys_t = conv_scr[0, whole_window].T if chunks == 1 else None
        for at in range(heads * span // wide):
            slot = (half * (heads * span // wide) + at) % s_scr.shape[0]
            cols = slice(at * wide, (at + 1) * wide)
            queries = qc_scr[half, cols]
            grads = do_scr[half, cols]

            def key_rows(step):
                return pl.ds(aligned(first_key + step * size, 16), size)

            def score(step, top):
                keys = conv_scr[0, key_rows(step)]
                scores = lax.dot_general(keys, queries, NT, preferred_element_type=f32)
                bias = bias_scr[pl.ds(aligned(step * size, 16), size)]
                scores = scores + jnp.concatenate([bias, bias], axis=1)
                s_scr[slot, pl.ds(aligned(step * size, 16), size)] = scores
                return jnp.maximum(top, jnp.max(scores, axis=0, keepdims=True))

            top = loop(chunks, score, jnp.full((1, wide), -1e30, f32), 1)

            def weigh(step, carry):
                total, weighted = carry
                rows = pl.ds(aligned(step * size, 16), size)
                weights = jnp.exp2((s_scr[slot, rows] - top) * log2_scale)
                values = conv_scr[1, key_rows(step)]
                prob_grads = lax.dot_general(values, grads, NT, preferred_element_type=f32)
                s_scr[slot, rows] = weights
                dp_scr[slot, rows] = prob_grads
                total = total + jnp.sum(weights, axis=0, keepdims=True)
                weighted = weighted + jnp.sum(weights * prob_grads, axis=0, keepdims=True)
                return total, weighted

            zeros = jnp.zeros((1, wide), f32)
            total, weighted = loop(chunks, weigh, (zeros, zeros), 1)
            inverse = 1.0 / total
            mean = weighted * inverse
            slope = inverse * scale

            def accumulate(step, dq):
                rows = pl.ds(aligned(step * size, 16), size)
                weights = s_scr[slot, rows]
                probs = (weights * inverse).astype(bf16)
                score_grads = (weights * slope * (dp_scr[slot, rows] - mean)).astype(bf16)
                dk = lax.dot_general(score_grads, queries, NN, preferred_element_type=f32)
                dv = lax.dot_general(probs, grads, NN, preferred_element_type=f32)
                target = pl.ds(aligned(first_key + step * size, 16), size)
                for tensor, terms in enumerate((dk, dv)):
                    dkv_scr[tensor, target] += terms
                if keys_t is not None:
                    return lax.dot_general(keys_t, score_grads, NN, preferred_element_type=f32)
                keys = conv_scr[0, key_rows(step)]
                return dq + lax.dot_general(keys, score_grads, TN, preferred_element_type=f32)

            dq = loop(chunks, accumulate, jnp.zeros((LANES, wide), f32), 1)
            dq = dq.T
            for part in range(wide // span):
                head = at * (wide // span) + part
                dq_scr[half, head, :span] = dq[part * span : (part + 1) * span]

    def clear(index, carry):
        for tensor in range(2):
            dkv_scr[tensor, pl.ds(aligned(index * span, 8), span)] = jnp.zeros((span, LANES), f32)
        return carry

    loop(blocks, clear, 0)
    for tensor in range(2):
        dkv_scr[tensor, length:] = zeros

    for half in range(2):
        widest = ctx_count + half
        lowest = jnp.int32(0)
        for start in starts[1:]:
            lowest = jnp.where(first_place[half] >= start, start, lowest)
        needed = first_place[half] // span - lowest // span + 1
        below = 0
        for count in [count for count in WINDOWS if direct and count < widest] + [widest]:

            @pl.when((needed > below) & (needed <= count))
            def _(half=half, count=count):
                first_key = jnp.maximum(first_place[half] + span - count * span, 0)
                attend(half, count * span, first_key)

            below = count

    next_rows = jnp.where(middle, dq_scr[1, :, :8], 0.0)
    dq_scr[0, :, span:] = next_rows
    dq_scr[1, :, span:] = jnp.zeros_like(next_rows)
    sums = [jnp.zeros((8, LANES), f32) for _ in range(3)]
    for half in range(2):
        one, two = masks(first_place[half], 0)
        ahead_one = same_scr[pl.ds(first_place[half] + 9, span)]
        ahead_two = same_two_scr[pl.ds(first_place[half] + 10, span)]
        zero_tap, one_tap, two_tap = taps(0)
        for head in range(heads):
            lanes = slice(head * LANES, (head + 1) * LANES)
            grads = dq_scr[half, head, :span]
            out = zero_tap * grads
            out = out + ahead_one * (one_tap * dq_scr[half, head, 1 : 1 + span])
            out = out + ahead_two * (two_tap * dq_scr[half, head, 2 : 2 + span])
            dq_ref[half, :, lanes] = out
            dq_tail_ref[half, :, lanes] = out[span - 8 :]
            sums[0] += fold_rows(grads * q_scr[half, head, 8:])
            sums[1] += fold_rows(grads * one * q_scr[half, head, 7 : 7 + span])
            sums[2] += fold_rows(grads * two * q_scr[half, head, 6 : 6 + span])
    q_sums = [jnp.sum(term, axis=0, keepdims=True) for term in sums]
    store = pltpu.make_async_copy(dq_ref, dq_hbm, sems.at[0])
    store.start()

    def finish_block(index, carry, target, row):
        base = pl.multiple_of(index * span, 8)
        one, two = masks(base, 0)
        ahead_one = same_scr[pl.ds(base + 9, span)]
        ahead_two = same_two_scr[pl.ds(base + 10, span)]
        carry = list(carry)
        for tensor in range(2):
            zero_tap, one_tap, two_tap = taps(tensor + 1)
            own = dkv_scr[tensor, pl.ds(base, span)]
            out = zero_tap * own
            out = out + ahead_one * (one_tap * dkv_scr[tensor, pl.ds(base + 1, span)])
            out = out + ahead_two * (two_tap * dkv_scr[tensor, pl.ds(base + 2, span)])
            lanes = slice(tensor * LANES, (tensor + 1) * LANES)
            target[row : row + span, lanes] = out.astype(target.dtype)
            at = 3 * tensor
            carry[at] += fold_rows(own * kv_scr[tensor, pl.ds(base + 8, span)])
            carry[at + 1] += fold_rows(own * one * kv_scr[tensor, pl.ds(base + 7, span)])
            carry[at + 2] += fold_rows(own * two * kv_scr[tensor, pl.ds(base + 6, span)])
        return tuple(carry)

    low = me < group

    def finish(step, carry):
        flip = step + 1
        owner = partner(me, flip)
        far_owner = partner(me, flip + group)
        near_late = blocks - 1 - owner
        second = jnp.where(low, blocks - 1 - far_owner, owner)
        third = jnp.where(low & (me > owner), owner, near_late)
        carry = finish_block(far_owner, carry, first_out[flip], 0)
        carry = finish_block(second, carry, first_out[flip], span)
        carry = finish_block(third, carry, late_out[flip], 0)
        return carry

    kv_sums = (zeros,) * 6
    for target, index in ((own_far_ref, partner(me, group)), (own_near_ref, me)):
        kv_sums = finish_block(index, kv_sums, target, 0)
        kv_sums = finish_block(blocks - 1 - index, kv_sums, target, span)
    kv_sums = loop(group - 1, finish, kv_sums)
    kv_sums = [jnp.sum(term, axis=0, keepdims=True) for term in kv_sums]

    padding = [jnp.zeros((2, LANES), f32)]
    left = jnp.concatenate(q_sums + kv_sums[:3] + padding, axis=0)
    right = jnp.concatenate([jnp.zeros((3, LANES), f32)] + kv_sums[3:] + padding, axis=0)
    sums_tile = jnp.concatenate([left, right], axis=1)
    sums_pair = jnp.concatenate(split_bits(sums_tile), axis=0)
    own_far_ref[2 * span :] = joined(sums_pair)
    rims = []
    for half in range(2):
        rows = [dq_scr[half, head, :2] for head in range(heads)]
        rows = [jnp.concatenate(rows[at : at + 2], axis=1) for at in range(0, heads, 2)]
        rims.append(jnp.concatenate(rows, axis=0))

    def rim_for(index):
        return jnp.concatenate(split_bits(jnp.where(index < me, rims[0], rims[1])), axis=0)

    def store_rims(step, carry):
        flip = step + 1
        owner = partner(me, flip)
        first_out[flip][2 * span : 2 * span + 16] = sums_pair
        if not direct or flip == group - 1:
            first_out[flip][2 * span + 16 :] = rim_for(partner(owner, group))
        if not direct or flip & (flip + 1) == 0:
            late_out[flip][span:] = rim_for(owner)
        return carry

    loop(group - 1, store_rims, 0, 16 if direct else 1)
    store.wait()


def merge_kernel(ctx_count, direct, own_near_ref, own_far_ref, *refs):
    received_refs, (near_ref, far_ref, half_sums_ref, sums_scr) = refs[:-4], refs[-4:]
    f32, bf16 = jnp.float32, jnp.bfloat16
    group = ctx_count // 2
    me = lax.axis_index("ctx")
    low = me < group
    received = Slots((own_far_ref,) + received_refs if direct else received_refs, me)
    place = lax.rem(me, jnp.int32(group))
    span = own_near_ref.shape[0] // 2
    rows = 2 * span
    sums_scr[place] = own_far_ref[rows:]
    def add(step, carry):
        flip = step + 1
        message = received[flip]
        early, second = [message[at * span : (at + 1) * span].astype(f32) for at in range(2)]
        near_early, far_early, far_late = carry
        sums_scr[partner(place, flip)] = joined(message[rows : rows + 16])
        zero = jnp.zeros_like(second)
        return (
            near_early + jnp.where(low, zero, second),
            far_early + early,
            far_late + jnp.where(low, second, zero),
        )

    init = (own_near_ref[:span], own_far_ref[:span], own_far_ref[span:rows])
    totals = loop(group - 1, add, init, 16 if direct else 1)
    near_ref[:span] = totals[0]
    near_ref[span:] = own_near_ref[span:]
    far_ref[:span] = totals[1].astype(bf16)
    far_ref[span:rows] = totals[2].astype(bf16)
    sums = loop(group, lambda index, carry: carry + sums_scr[index], jnp.zeros((8, 2 * LANES), f32))
    pair = jnp.concatenate(split_bits(sums), axis=0)
    half_sums_ref[...] = joined(pair)
    far_ref[rows : rows + 16] = pair
    far_ref[rows + 16 :] = received[group - 1][rows + 16 :]


def sums_kernel(span, half_sums_ref, far_ref, out_ref):
    sums = half_sums_ref[...] + joined(far_ref[2 * span : 2 * span + 16])
    out_ref[0] = sums[0:3, :LANES]
    out_ref[1] = sums[3:6, :LANES]
    out_ref[2] = sums[3:6, LANES:]


def finish_kernel(
    ctx_count, direct, lengths_ref, filters_ref, dq_in_hbm, tail_ref, near_ref, far_ref, *refs
):
    received_refs, refs = refs[:-8], refs[-8:]
    dq_hbm, dk_hbm, dv_hbm, dq_ref, dk_ref, dv_ref, rim_scr, sems = refs
    f32 = jnp.float32
    group = ctx_count // 2
    span = dk_ref.shape[1]
    me = lax.axis_index("ctx")
    low = me < group
    received = Slots((None,) + received_refs if direct else received_refs, me)
    starts = doc_starts(lengths_ref)
    blocks = 2 * ctx_count
    neighbours = [jnp.minimum(me + 1, ctx_count - 1), jnp.maximum(me - 1, 0)]
    for index in neighbours:
        rim_scr[index] = jnp.zeros(rim_scr.shape[1:], f32)

    def add(step, carry):
        flip = step + 1
        source = partner(me, flip)
        message = received[flip]
        terms = message[:span].astype(f32)
        if not direct or flip & (flip + 1) == 0:
            rim_scr[source] = joined(message[span:])
        to_early = low & (source > me)
        zero = jnp.zeros_like(terms)
        return carry[0] + jnp.where(to_early, terms, zero), carry[1] + jnp.where(to_early, zero, terms)

    total = near_ref[...] + far_ref[: 2 * span].astype(f32)
    total = loop(group - 1, add, (total[:span], total[span:]), 16 if direct else 1)
    for half in range(2):
        dk_ref[half] = total[half][:, :LANES]
        dv_ref[half] = total[half][:, LANES:]
    stores = [
        pltpu.make_async_copy(dk_ref, dk_hbm, sems.at[0]),
        pltpu.make_async_copy(dv_ref, dv_hbm, sems.at[1]),
        pltpu.make_async_copy(dq_ref, dq_hbm.at[:, pl.ds(span - 8, 8)], sems.at[2]),
    ]
    for store in stores[:2]:
        store.start()

    def same(place):
        cut = place >= blocks * span
        for start in starts:
            cut = cut | (place == start)
        return jnp.where(cut, 0.0, 1.0).astype(f32)

    heads = dq_ref.shape[2] // LANES
    taps = [jnp.concatenate([filters_ref[0, tap : tap + 1]] * heads, axis=1) for tap in range(3)]
    row = lax.broadcasted_iota(jnp.int32, dq_ref.shape[1:], 0)
    far_rim = joined(far_ref[2 * span + 16 :])
    crosses = [me == group - 1, me == group]
    first_place = [me * span, (blocks - 1 - me) * span]
    present = [me < ctx_count - 1, me > 0]
    for half in range(2):
        rim = jnp.where(crosses[half], far_rim, rim_scr[neighbours[half]])
        rows = jnp.concatenate([rim[2 * at : 2 * at + 2] for at in range(rim.shape[0] // 2)], axis=1)
        end = first_place[half] + span
        zero, one, two = same(end - 1), same(end), same(end + 1)
        one = jnp.where(present[half], one, 0.0)
        last_but_one = (zero * one) * (taps[2] * rows[0:1])
        last = one * (taps[1] * rows[0:1]) + (one * two) * (taps[2] * rows[1:2])
        extra = jnp.where(row == 6, last_but_one, jnp.where(row == 7, last, 0.0))
        dq_ref[half] = tail_ref[half] + extra
    stores[2].start()
    for store in stores:
        store.wait()


def shards(q_pre, k_pre, value_before_filter, d_out, filters, doc_lengths):
    f32, bf16 = jnp.float32, jnp.bfloat16
    ctx_count = lax.axis_size("ctx")
    span, width = q_pre.shape[1:]
    length = 2 * span * ctx_count
    rim = 4 * width // (2 * LANES)
    vmem = pl.BlockSpec(memory_space=pltpu.VMEM)
    smem = pl.BlockSpec(memory_space=pltpu.SMEM)
    hbm = pl.BlockSpec(memory_space=pltpu.HBM)

    group = ctx_count // 2
    direct = group <= MAX_DIRECT
    halves = [[half * group + at for at in range(group)] for half in range(2)]
    msg_rows = 2 * span + rim

    def whole(shape):
        return pl.BlockSpec(shape, lambda i: (0,) * len(shape))

    def in_hbm(array):
        return pltpu.with_memory_space_constraint(array, pltpu.HBM)

    def flipped(array, flip):
        return lax.ppermute(array, "ctx", [(i, i ^ flip) for i in range(ctx_count)])

    def gathered(array):
        if direct:
            return [flipped(array, flip) for flip in range(1, group)]
        return [lax.all_gather(array, "ctx", axis_index_groups=halves)]

    def delivered(arrays):
        if direct:
            return [flipped(array, step + 1) for step, array in enumerate(arrays)]
        return [lax.all_to_all(arrays[0], "ctx", 0, 0, axis_index_groups=halves, tiled=True)]

    packed = pl.pallas_call(
        pack_kernel,
        grid=(1,),
        out_shape=jax.ShapeDtypeStruct((msg_rows, 2 * LANES), bf16),
        in_specs=[
            whole(k_pre.shape),
            whole(k_pre.shape),
            pl.BlockSpec((2, TAIL, width), lambda i: (0, span // TAIL - 1, 0)),
        ],
        out_specs=whole((msg_rows, 2 * LANES)),
        compiler_params=pltpu.CompilerParams(vmem_limit_bytes=4 * MIB),
        name="pack",
    )(*[in_hbm(array) for array in (k_pre, value_before_filter, q_pre)])
    across = flipped(packed, group)
    near = gathered(packed)
    far = gathered(across)
    received = [packed, across] + near + far

    window = span * ctx_count + span
    if direct:
        flips = range(1, group)
        first_shapes = [(2 * span + (32 if flip == group - 1 else 16), 2 * LANES) for flip in flips]
        late_shapes = [(span + (16 if flip & (flip + 1) == 0 else 0), 2 * LANES) for flip in flips]
    else:
        first_shapes = [(group, 2 * span + 32, 2 * LANES)]
        late_shapes = [(group, span + 16, 2 * LANES)]
    slots = 4 if direct else 1
    heads = width // LANES
    by_head = (2, span * heads, LANES)
    padded = (2, heads, span + 8, LANES)
    prepared = pl.pallas_call(
        functools.partial(prep_kernel, ctx_count, direct),
        out_shape=[
            jax.ShapeDtypeStruct((length + 16, LANES), f32),
            jax.ShapeDtypeStruct((length + 16, LANES), f32),
            jax.ShapeDtypeStruct(padded, f32),
            jax.ShapeDtypeStruct(by_head, bf16),
            jax.ShapeDtypeStruct(by_head, bf16),
        ],
        in_specs=[smem, vmem, hbm, hbm] + [vmem] * (1 + len(near)),
        out_specs=[vmem] * 5,
        scratch_shapes=[
            pltpu.VMEM((ctx_count, rim, 2 * LANES), f32),
            pltpu.VMEM(q_pre.shape, bf16),
            pltpu.VMEM(q_pre.shape, bf16),
            pltpu.SemaphoreType.DMA((2,)),
        ],
        compiler_params=pltpu.CompilerParams(vmem_limit_bytes=(8 if direct else 32) * MIB),
        name="prep",
    )(doc_lengths, filters, in_hbm(q_pre), in_hbm(d_out), packed, *near)
    scratch = [
        pltpu.VMEM((2, length + 16, LANES), f32),
        pltpu.VMEM((2, length, LANES), bf16),
        pltpu.VMEM((2, length + 8, LANES), f32),
        pltpu.VMEM(padded, f32),
        pltpu.VMEM(by_head, bf16),
        pltpu.VMEM(padded, f32),
        pltpu.VMEM((window, LANES), f32),
        pltpu.VMEM((slots, window, 2 * LANES), f32),
        pltpu.VMEM((slots, window, 2 * LANES), f32),
        pltpu.VMEM(q_pre.shape, f32),
        pltpu.SemaphoreType.DMA((1,)),
    ]
    own_shapes = [(2 * span, 2 * LANES), (2 * span + 8, 2 * LANES)]
    d_q_main, d_q_tail, own_near, own_far, *sent = pl.pallas_call(
        functools.partial(grads_kernel, ctx_count, direct),
        out_shape=[jax.ShapeDtypeStruct(q_pre.shape, f32)]
        + [jax.ShapeDtypeStruct(shape, f32) for shape in [(2, 8, width)] + own_shapes]
        + [jax.ShapeDtypeStruct(shape, bf16) for shape in first_shapes + late_shapes],
        in_specs=[smem, vmem] + [vmem] * (len(prepared) + len(received)),
        out_specs=[hbm] + [vmem] * (3 + len(first_shapes + late_shapes)),
        scratch_shapes=scratch,
        compiler_params=pltpu.CompilerParams(vmem_limit_bytes=(20 if direct else 62) * MIB),
        name="grads",
    )(doc_lengths, filters, *prepared, *received)
    half_terms = delivered(sent[: len(first_shapes)])
    merged_shapes = [
        jax.ShapeDtypeStruct((2 * span, 2 * LANES), f32),
        jax.ShapeDtypeStruct((2 * span + 32, 2 * LANES), bf16),
        jax.ShapeDtypeStruct((8, 2 * LANES), f32),
    ]
    near, far, half_sums = pl.pallas_call(
        functools.partial(merge_kernel, ctx_count, direct),
        out_shape=merged_shapes,
        in_specs=[vmem] * (2 + len(half_terms)),
        out_specs=[vmem] * len(merged_shapes),
        scratch_shapes=[pltpu.VMEM((group, 8, 2 * LANES), f32)],
        compiler_params=pltpu.CompilerParams(vmem_limit_bytes=(4 if direct else 40) * MIB),
        name="merge",
    )(own_near, own_far, *half_terms)
    from_half = flipped(far, group)
    late_terms = delivered(sent[len(first_shapes) :])

    sums = pl.pallas_call(
        functools.partial(sums_kernel, span),
        out_shape=jax.ShapeDtypeStruct(filters.shape, f32),
        in_specs=[vmem, vmem],
        out_specs=vmem,
        compiler_params=pltpu.CompilerParams(vmem_limit_bytes=2 * MIB),
        name="sums",
    )(half_sums, from_half)
    count = lax.axis_size("tp")
    all_sums = [sums] + [
        lax.ppermute(sums, "tp", [(i, i ^ flip) for i in range(count)]) for flip in range(1, count)
    ]
    d_q_pre, d_k_pre, d_v_pre = pl.pallas_call(
        functools.partial(finish_kernel, ctx_count, direct),
        out_shape=(
            jax.ShapeDtypeStruct(q_pre.shape, f32),
            jax.ShapeDtypeStruct(k_pre.shape, f32),
            jax.ShapeDtypeStruct(k_pre.shape, f32),
        ),
        in_specs=[smem, vmem, hbm] + [vmem] * (3 + len(late_terms)),
        out_specs=(hbm, hbm, hbm),
        scratch_shapes=[
            pltpu.VMEM((2, 8, width), f32),
            pltpu.VMEM(k_pre.shape, f32),
            pltpu.VMEM(k_pre.shape, f32),
            pltpu.VMEM((ctx_count, rim // 2, 2 * LANES), f32),
            pltpu.SemaphoreType.DMA((3,)),
        ],
        input_output_aliases={2: 0},
        compiler_params=pltpu.CompilerParams(vmem_limit_bytes=(4 if direct else 16) * MIB),
        name="finish",
    )(doc_lengths, filters, d_q_main, d_q_tail, near, from_half, *late_terms)
    while len(all_sums) > 1:
        all_sums = [all_sums[at] + all_sums[at + 1] for at in range(0, len(all_sums), 2)]
    return (d_q_pre, d_k_pre, d_v_pre, all_sums[0])


def solution(mesh):
    split = P(None, "ctx", "tp")
    return jax.shard_map(
        shards,
        mesh=mesh,
        in_specs=(split, split, split, split, P(), P()),
        out_specs=(split, split, split, P()),
        check_vma=False,
    )
```

```python
import functools

import jax
import jax.numpy as jnp
import numpy as np
from jax import lax
from jax.experimental import pallas as pl
from jax.experimental.pallas import tpu as pltpu
from jax.sharding import PartitionSpec as P

LANES = 128
NT = (((1,), (1,)), ((), ()))
NN = (((1,), (0,)), ((), ()))
TN = (((0,), (0,)), ((), ()))
TAIL = 16
MAX_CHUNK = 640
RIM = 8
MAX_DIRECT = 4
WINDOWS = (2, 4, 6)
MIB = 1 << 20


def loop(count, body, init, unrolled=16):
    if count <= unrolled:
        for step in range(count):
            init = body(step, init)
        return init
    return lax.fori_loop(0, count, body, init)


def aligned(start, multiple):
    return start if isinstance(start, int) else pl.multiple_of(start, multiple)


def doc_starts(lengths_ref):
    starts = [jnp.int32(0)]
    for index in range(lengths_ref.shape[0] - 1):
        starts.append(starts[-1] + lengths_ref[index])
    return starts


def fold_rows(terms):
    rows, lanes = terms.shape
    return jnp.sum(terms.reshape(rows // 8, 8, lanes), axis=0)


def split_bits(values):
    high = values.astype(jnp.bfloat16)
    low = (values - high.astype(jnp.float32)).astype(jnp.bfloat16)
    return high, low


def joined(pair):
    rows = pair.shape[0] // 2
    pair = pair.astype(jnp.float32)
    return pair[:rows] + pair[rows:]


class Slots:
    def __init__(self, refs, me):
        self.refs, self.me = refs, me

    def __getitem__(self, flip):
        if len(self.refs) == 1:
            place = lax.rem(self.me, jnp.int32(self.refs[0].shape[0]))
            return self.refs[0].at[partner(place, flip)]
        return self.refs[flip]


def partner(me, flip):
    return lax.bitwise_xor(me, jnp.int32(flip))


def pack_kernel(k_ref, v_ref, q_ref, out_ref):
    span = k_ref.shape[1]
    kv = jnp.concatenate([k_ref[...], v_ref[...]], axis=2).reshape(2 * span, 2 * LANES)
    tails = []
    for half in range(2):
        last = q_ref[half].astype(jnp.float32)[TAIL - 2 :]
        tails += [last[:, at : at + 2 * LANES] for at in range(0, last.shape[1], 2 * LANES)]
    out_ref[: 2 * span] = kv
    out_ref[2 * span :] = jnp.concatenate(tails, axis=0).astype(jnp.bfloat16)


def relay_kernel(across_ref, early_ref, late_ref):
    span = late_ref.shape[0]
    early_ref[:span] = across_ref[:span]
    early_ref[span:] = across_ref[2 * span :]
    late_ref[...] = across_ref[span : 2 * span]


def prep_kernel(ctx_count, direct, lengths_ref, filters_ref, q_hbm, d_out_hbm, own_ref, *refs):
    near_refs, refs = refs[:-9], refs[-9:]
    same_ref, same_two_ref, q_scr, qc_ref, do_ref, rim_scr, q_ref, d_out_ref, sems = refs
    f32, bf16 = jnp.float32, jnp.bfloat16
    loads = [
        pltpu.make_async_copy(q_hbm, q_ref, sems.at[0]),
        pltpu.make_async_copy(d_out_hbm, d_out_ref, sems.at[1]),
    ]
    for load in loads:
        load.start()
    group = ctx_count // 2
    span = q_ref.shape[1]
    heads = q_ref.shape[2] // LANES
    blocks = 2 * ctx_count
    length = span * blocks
    me = lax.axis_index("ctx")
    near = Slots((None,) + near_refs if direct else near_refs, me)
    starts = doc_starts(lengths_ref)

    def fill(index, carry):
        rows = pl.ds(aligned(8 + index * span, 8), span)
        same_ref[rows] = jnp.ones((span, LANES), f32)
        same_two_ref[rows] = jnp.ones((span, LANES), f32)
        return carry

    loop(blocks, fill, 0)
    zeros = jnp.zeros((8, LANES), f32)
    for rows in (slice(0, 8), slice(8 + length, 16 + length)):
        same_ref[rows] = zeros
        same_two_ref[rows] = zeros
    for start in starts:
        same_ref[pl.ds(8 + start, 1)] = zeros[:1]
        same_two_ref[pl.ds(8 + start, 1)] = zeros[:1]
        same_two_ref[pl.ds(9 + start, 1)] = zeros[:1]

    before, after = jnp.maximum(me - 1, 0), jnp.minimum(me + 1, ctx_count - 1)
    for index in (before, after):
        rim_scr[index] = jnp.zeros(rim_scr.shape[1:], f32)
    rim_scr[me] = own_ref[2 * span :].astype(f32)

    def place_rims(step, carry):
        flip = step + 1
        if not direct or flip & (flip + 1) == 0:
            rim_scr[partner(me, flip)] = near[flip][2 * span :].astype(f32)
        return carry

    loop(group - 1, place_rims, 0, 16 if direct else 1)
    rim_before, rim_after = rim_scr[before], rim_scr[after]
    late_rim = jnp.where(me == ctx_count - 1, rim_after[:RIM], rim_after[RIM:])
    rims = [rim_before[:RIM], late_rim]
    first_place = [me * span, (blocks - 1 - me) * span]
    taps = [filters_ref[0, tap : tap + 1] for tap in range(3)]

    for load in loads:
        load.wait()
    for half in range(2):
        rows = pl.ds(aligned(first_place[half] + 8, 8), span)
        one, two = same_ref[rows], same_two_ref[rows]
        for head in range(heads):
            lanes = slice(head * LANES, (head + 1) * LANES)
            at = 2 * (head // 2)
            q_scr[half, head, 6:8] = rims[half][at : at + 2, (head % 2) * LANES : (head % 2 + 1) * LANES]
            q_scr[half, head, 8:] = q_ref[half, :, lanes].astype(f32)
            total = taps[0] * q_scr[half, head, 8:]
            total = total + one * (taps[1] * q_scr[half, head, 7 : 7 + span])
            total = total + two * (taps[2] * q_scr[half, head, 6 : 6 + span])
            qc_ref[half, head * span : (head + 1) * span] = total.astype(bf16)
            do_ref[half, head * span : (head + 1) * span] = d_out_ref[half, :, lanes]


def grads_kernel(ctx_count, direct, lengths_ref, filters_ref, *refs):
    group = ctx_count // 2
    arrays = group - 1 if direct else 1
    same_scr, same_two_scr, q_in_ref, qc_in_ref, do_scr, own_ref, early_ref, late_ref = refs[:8]
    refs = refs[8:]
    near_in, early_in, late_in = [refs[at * arrays : (at + 1) * arrays] for at in range(3)]
    refs = refs[3 * arrays :]
    dq_hbm, dq_tail_ref, own_near_ref, own_far_ref = refs[:4]
    arrays = group - 1 if direct else 1
    first_out, late_out, refs = refs[4 : 4 + arrays], refs[4 + arrays : 4 + 2 * arrays], refs[4 + 2 * arrays :]
    kv_scr, conv_scr, dkv_scr, q_scr, qc_scr, dq_scr = refs[:6]
    bias_scr, s_scr, dp_scr, dq_ref, sems = refs[6:]
    f32, bf16 = jnp.float32, jnp.bfloat16
    span = own_ref.shape[0] // 2 - TAIL // 2
    heads = q_in_ref.shape[1]
    half_rows = span * ctx_count
    length = 2 * half_rows
    blocks = 2 * ctx_count
    me = lax.axis_index("ctx")
    near_in = Slots((None,) + near_in if direct else near_in, me)
    early_in = Slots((early_ref,) + early_in if direct else early_in, me)
    late_in = Slots((late_ref,) + late_in if direct else late_in, me)
    first_out = Slots((None,) + first_out if direct else first_out, me)
    late_out = Slots((None,) + late_out if direct else late_out, me)
    scale = LANES**-0.5
    log2_scale = scale * 1.4426950408889634
    starts = doc_starts(lengths_ref)

    def place(index, block):
        for tensor in range(2):
            lanes = slice(tensor * LANES, (tensor + 1) * LANES)
            kv_scr[tensor, pl.ds(aligned(8 + index * span, 8), span)] = block[:, lanes].astype(f32)

    def place_received(flip, carry):
        source = partner(me, flip)
        across = partner(source, group)
        place(across, early_in[flip][:span])
        place(blocks - 1 - across, late_in[flip])
        return carry

    def place_near(step, carry):
        source = partner(me, step + 1)
        message = near_in[step + 1]
        place(source, message[:span])
        place(blocks - 1 - source, message[span : 2 * span])
        return carry

    zeros = jnp.zeros((8, LANES), f32)
    for tensor in range(2):
        kv_scr[tensor, :8] = zeros
    place(me, own_ref[:span])
    place(blocks - 1 - me, own_ref[span : 2 * span])
    loop(group - 1, place_near, 0)
    loop(group, place_received, 0)

    def taps(tensor):
        return [filters_ref[tensor, tap : tap + 1] for tap in range(3)]

    def masks(base, ahead):
        one = same_scr[pl.ds(base + 8 + min(ahead, 1), span)]
        return one, same_two_scr[pl.ds(base + 8 + ahead, span)]

    def convolve_kv(index, carry):
        base = index * span
        one, two = masks(base, 0)
        for tensor in range(2):
            zero_tap, one_tap, two_tap = taps(tensor + 1)
            total = zero_tap * kv_scr[tensor, pl.ds(aligned(base + 8, 8), span)]
            total = total + one * (one_tap * kv_scr[tensor, pl.ds(base + 7, span)])
            total = total + two * (two_tap * kv_scr[tensor, pl.ds(base + 6, span)])
            conv_scr[tensor, pl.ds(aligned(base, 16), span)] = total.astype(bf16)
        return carry

    loop(blocks, convolve_kv, 0)

    first_place = [me * span, (blocks - 1 - me) * span]
    middle = me == ctx_count - 1
    q_scr[...] = q_in_ref[...]
    qc_scr[...] = qc_in_ref[...]
    tails = early_in[group - 1][span:].astype(f32)
    tails = [tails[:RIM], tails[RIM:]]
    for half, crossing in ((0, me == group), (1, me == group - 1)):

        @pl.when(crossing)
        def _(half=half):
            rows = pl.ds(aligned(first_place[half] + 8, 8), TAIL)
            one, two = same_scr[rows], same_two_scr[rows]
            zero_tap, one_tap, two_tap = taps(0)
            for head in range(heads):
                at = 2 * (head // 2)
                q_scr[half, head, 6:8] = tails[half][
                    at : at + 2, (head % 2) * LANES : (head % 2 + 1) * LANES
                ]
                total = zero_tap * q_scr[half, head, 8 : 8 + TAIL]
                total = total + one * (one_tap * q_scr[half, head, 7 : 7 + TAIL])
                total = total + two * (two_tap * q_scr[half, head, 6 : 6 + TAIL])
                qc_scr[half, head * span : head * span + TAIL] = total.astype(bf16)

    def attend(half, window, first_key):
        chunks = 1
        while window // chunks > MAX_CHUNK or window % (16 * chunks):
            chunks += 1
        size = window // chunks
        query = first_place[half] + lax.rem(
            lax.broadcasted_iota(jnp.int32, (1, LANES), 1), jnp.int32(span)
        )
        lowest = jnp.zeros((1, LANES), jnp.int32)
        for start in starts[1:]:
            lowest = jnp.where(query >= start, start, lowest)
        wide = 2 * LANES

        def fill_bias(step, carry):
            places = first_key + step * size + lax.broadcasted_iota(jnp.int32, (size, LANES), 0)
            allowed = (places >= lowest) & (places <= query)
            bias_scr[pl.ds(aligned(step * size, 16), size)] = jnp.where(allowed, 0.0, -1e30)
            return carry

        loop(chunks, fill_bias, 0, 1)
        whole_window = pl.ds(aligned(first_key, 16), window)
        keys_t = conv_scr[0, whole_window].T if chunks == 1 else None
        for at in range(heads * span // wide):
            slot = (half * (heads * span // wide) + at) % s_scr.shape[0]
            cols = slice(at * wide, (at + 1) * wide)
            queries = qc_scr[half, cols]
            grads = do_scr[half, cols]

            def key_rows(step):
                return pl.ds(aligned(first_key + step * size, 16), size)

            def score(step, top):
                keys = conv_scr[0, key_rows(step)]
                scores = lax.dot_general(keys, queries, NT, preferred_element_type=f32)
                bias = bias_scr[pl.ds(aligned(step * size, 16), size)]
                scores = scores + jnp.concatenate([bias, bias], axis=1)
                s_scr[slot, pl.ds(aligned(step * size, 16), size)] = scores
                return jnp.maximum(top, jnp.max(scores, axis=0, keepdims=True))

            top = loop(chunks, score, jnp.full((1, wide), -1e30, f32), 1)

            def weigh(step, carry):
                total, weighted = carry
                rows = pl.ds(aligned(step * size, 16), size)
                weights = jnp.exp2((s_scr[slot, rows] - top) * log2_scale)
                values = conv_scr[1, key_rows(step)]
                prob_grads = lax.dot_general(values, grads, NT, preferred_element_type=f32)
                s_scr[slot, rows] = weights
                dp_scr[slot, rows] = prob_grads
                total = total + jnp.sum(weights, axis=0, keepdims=True)
                weighted = weighted + jnp.sum(weights * prob_grads, axis=0, keepdims=True)
                return total, weighted

            zeros = jnp.zeros((1, wide), f32)
            total, weighted = loop(chunks, weigh, (zeros, zeros), 1)
            inverse = 1.0 / total
            mean = weighted * inverse
            slope = inverse * scale

            def accumulate(step, dq):
                rows = pl.ds(aligned(step * size, 16), size)
                weights = s_scr[slot, rows]
                probs = (weights * inverse).astype(bf16)
                score_grads = (weights * slope * (dp_scr[slot, rows] - mean)).astype(bf16)
                dk = lax.dot_general(score_grads, queries, NN, preferred_element_type=f32)
                dv = lax.dot_general(probs, grads, NN, preferred_element_type=f32)
                target = pl.ds(aligned(first_key + step * size, 16), size)
                for tensor, terms in enumerate((dk, dv)):
                    dkv_scr[tensor, target] += terms
                if keys_t is not None:
                    return lax.dot_general(keys_t, score_grads, NN, preferred_element_type=f32)
                keys = conv_scr[0, key_rows(step)]
                return dq + lax.dot_general(keys, score_grads, TN, preferred_element_type=f32)

            dq = loop(chunks, accumulate, jnp.zeros((LANES, wide), f32), 1)
            dq = dq.T
            for part in range(wide // span):
                head = at * (wide // span) + part
                dq_scr[half, head, :span] = dq[part * span : (part + 1) * span]

    def clear(index, carry):
        for tensor in range(2):
            dkv_scr[tensor, pl.ds(aligned(index * span, 8), span)] = jnp.zeros((span, LANES), f32)
        return carry

    loop(blocks, clear, 0)
    for tensor in range(2):
        dkv_scr[tensor, length:] = zeros

    for half in range(2):
        widest = ctx_count + half
        lowest = jnp.int32(0)
        for start in starts[1:]:
            lowest = jnp.where(first_place[half] >= start, start, lowest)
        needed = first_place[half] // span - lowest // span + 1
        below = 0
        for count in [count for count in WINDOWS if direct and count < widest] + [widest]:

            @pl.when((needed > below) & (needed <= count))
            def _(half=half, count=count):
                first_key = jnp.maximum(first_place[half] + span - count * span, 0)
                attend(half, count * span, first_key)

            below = count

    next_rows = jnp.where(middle, dq_scr[1, :, :8], 0.0)
    dq_scr[0, :, span:] = next_rows
    dq_scr[1, :, span:] = jnp.zeros_like(next_rows)
    sums = [jnp.zeros((8, LANES), f32) for _ in range(3)]
    for half in range(2):
        one, two = masks(first_place[half], 0)
        ahead_one = same_scr[pl.ds(first_place[half] + 9, span)]
        ahead_two = same_two_scr[pl.ds(first_place[half] + 10, span)]
        zero_tap, one_tap, two_tap = taps(0)
        for head in range(heads):
            lanes = slice(head * LANES, (head + 1) * LANES)
            grads = dq_scr[half, head, :span]
            out = zero_tap * grads
            out = out + ahead_one * (one_tap * dq_scr[half, head, 1 : 1 + span])
            out = out + ahead_two * (two_tap * dq_scr[half, head, 2 : 2 + span])
            dq_ref[half, :, lanes] = out
            dq_tail_ref[half, :, lanes] = out[span - 8 :]
            sums[0] += fold_rows(grads * q_scr[half, head, 8:])
            sums[1] += fold_rows(grads * one * q_scr[half, head, 7 : 7 + span])
            sums[2] += fold_rows(grads * two * q_scr[half, head, 6 : 6 + span])
    q_sums = [jnp.sum(term, axis=0, keepdims=True) for term in sums]
    store = pltpu.make_async_copy(dq_ref, dq_hbm, sems.at[0])
    store.start()

    def finish_block(index, carry, target, row):
        base = pl.multiple_of(index * span, 8)
        one, two = masks(base, 0)
        ahead_one = same_scr[pl.ds(base + 9, span)]
        ahead_two = same_two_scr[pl.ds(base + 10, span)]
        carry = list(carry)
        for tensor in range(2):
            zero_tap, one_tap, two_tap = taps(tensor + 1)
            own = dkv_scr[tensor, pl.ds(base, span)]
            out = zero_tap * own
            out = out + ahead_one * (one_tap * dkv_scr[tensor, pl.ds(base + 1, span)])
            out = out + ahead_two * (two_tap * dkv_scr[tensor, pl.ds(base + 2, span)])
            lanes = slice(tensor * LANES, (tensor + 1) * LANES)
            target[row : row + span, lanes] = out.astype(target.dtype)
            at = 3 * tensor
            carry[at] += fold_rows(own * kv_scr[tensor, pl.ds(base + 8, span)])
            carry[at + 1] += fold_rows(own * one * kv_scr[tensor, pl.ds(base + 7, span)])
            carry[at + 2] += fold_rows(own * two * kv_scr[tensor, pl.ds(base + 6, span)])
        return tuple(carry)

    low = me < group

    def finish(step, carry):
        flip = step + 1
        owner = partner(me, flip)
        far_owner = partner(me, flip + group)
        near_late = blocks - 1 - owner
        second = jnp.where(low, blocks - 1 - far_owner, owner)
        third = jnp.where(low & (me > owner), owner, near_late)
        carry = finish_block(far_owner, carry, first_out[flip], 0)
        carry = finish_block(second, carry, first_out[flip], span)
        carry = finish_block(third, carry, late_out[flip], 0)
        return carry

    kv_sums = (zeros,) * 6
    for target, index in ((own_far_ref, partner(me, group)), (own_near_ref, me)):
        kv_sums = finish_block(index, kv_sums, target, 0)
        kv_sums = finish_block(blocks - 1 - index, kv_sums, target, span)
    kv_sums = loop(group - 1, finish, kv_sums)
    kv_sums = [jnp.sum(term, axis=0, keepdims=True) for term in kv_sums]

    padding = [jnp.zeros((2, LANES), f32)]
    left = jnp.concatenate(q_sums + kv_sums[:3] + padding, axis=0)
    right = jnp.concatenate([jnp.zeros((3, LANES), f32)] + kv_sums[3:] + padding, axis=0)
    sums_tile = jnp.concatenate([left, right], axis=1)
    sums_pair = jnp.concatenate(split_bits(sums_tile), axis=0)
    own_far_ref[2 * span :] = joined(sums_pair)
    rims = []
    for half in range(2):
        rows = [dq_scr[half, head, :2] for head in range(heads)]
        rows = [jnp.concatenate(rows[at : at + 2], axis=1) for at in range(0, heads, 2)]
        rims.append(jnp.concatenate(rows, axis=0))

    def rim_for(index):
        return jnp.concatenate(split_bits(jnp.where(index < me, rims[0], rims[1])), axis=0)

    def store_rims(step, carry):
        flip = step + 1
        owner = partner(me, flip)
        first_out[flip][2 * span : 2 * span + 16] = sums_pair
        if not direct or flip == group - 1:
            first_out[flip][2 * span + 16 :] = rim_for(partner(owner, group))
        if not direct or flip & (flip + 1) == 0:
            late_out[flip][span:] = rim_for(owner)
        return carry

    loop(group - 1, store_rims, 0, 16 if direct else 1)
    store.wait()


def merge_kernel(ctx_count, direct, own_near_ref, own_far_ref, *refs):
    received_refs, (near_ref, far_ref, half_sums_ref, sums_scr) = refs[:-4], refs[-4:]
    f32, bf16 = jnp.float32, jnp.bfloat16
    group = ctx_count // 2
    me = lax.axis_index("ctx")
    low = me < group
    received = Slots((own_far_ref,) + received_refs if direct else received_refs, me)
    place = lax.rem(me, jnp.int32(group))
    span = own_near_ref.shape[0] // 2
    rows = 2 * span
    sums_scr[place] = own_far_ref[rows:]
    def add(step, carry):
        flip = step + 1
        message = received[flip]
        early, second = [message[at * span : (at + 1) * span].astype(f32) for at in range(2)]
        near_early, far_early, far_late = carry
        sums_scr[partner(place, flip)] = joined(message[rows : rows + 16])
        zero = jnp.zeros_like(second)
        return (
            near_early + jnp.where(low, zero, second),
            far_early + early,
            far_late + jnp.where(low, second, zero),
        )

    init = (own_near_ref[:span], own_far_ref[:span], own_far_ref[span:rows])
    totals = loop(group - 1, add, init, 16 if direct else 1)
    near_ref[:span] = totals[0]
    near_ref[span:] = own_near_ref[span:]
    far_ref[:span] = totals[1].astype(bf16)
    far_ref[span:rows] = totals[2].astype(bf16)
    sums = loop(group, lambda index, carry: carry + sums_scr[index], jnp.zeros((8, 2 * LANES), f32))
    pair = jnp.concatenate(split_bits(sums), axis=0)
    half_sums_ref[...] = joined(pair)
    far_ref[rows : rows + 16] = pair
    far_ref[rows + 16 :] = received[group - 1][rows + 16 :]


def sums_kernel(span, half_sums_ref, far_ref, out_ref):
    sums = half_sums_ref[...] + joined(far_ref[2 * span : 2 * span + 16])
    out_ref[0] = sums[0:3, :LANES]
    out_ref[1] = sums[3:6, :LANES]
    out_ref[2] = sums[3:6, LANES:]


def finish_kernel(
    ctx_count, direct, lengths_ref, filters_ref, dq_in_hbm, tail_ref, near_ref, far_ref, *refs
):
    received_refs, refs = refs[:-8], refs[-8:]
    dq_hbm, dk_hbm, dv_hbm, dq_ref, dk_ref, dv_ref, rim_scr, sems = refs
    f32 = jnp.float32
    group = ctx_count // 2
    span = dk_ref.shape[1]
    me = lax.axis_index("ctx")
    low = me < group
    received = Slots((None,) + received_refs if direct else received_refs, me)
    starts = doc_starts(lengths_ref)
    blocks = 2 * ctx_count
    neighbours = [jnp.minimum(me + 1, ctx_count - 1), jnp.maximum(me - 1, 0)]
    for index in neighbours:
        rim_scr[index] = jnp.zeros(rim_scr.shape[1:], f32)

    def add(step, carry):
        flip = step + 1
        source = partner(me, flip)
        message = received[flip]
        terms = message[:span].astype(f32)
        if not direct or flip & (flip + 1) == 0:
            rim_scr[source] = joined(message[span:])
        to_early = low & (source > me)
        zero = jnp.zeros_like(terms)
        return carry[0] + jnp.where(to_early, terms, zero), carry[1] + jnp.where(to_early, zero, terms)

    total = near_ref[...] + far_ref[: 2 * span].astype(f32)
    total = loop(group - 1, add, (total[:span], total[span:]), 16 if direct else 1)
    for half in range(2):
        dk_ref[half] = total[half][:, :LANES]
        dv_ref[half] = total[half][:, LANES:]
    stores = [
        pltpu.make_async_copy(dk_ref, dk_hbm, sems.at[0]),
        pltpu.make_async_copy(dv_ref, dv_hbm, sems.at[1]),
        pltpu.make_async_copy(dq_ref, dq_hbm.at[:, pl.ds(span - 8, 8)], sems.at[2]),
    ]
    for store in stores[:2]:
        store.start()

    def same(place):
        cut = place >= blocks * span
        for start in starts:
            cut = cut | (place == start)
        return jnp.where(cut, 0.0, 1.0).astype(f32)

    heads = dq_ref.shape[2] // LANES
    taps = [jnp.concatenate([filters_ref[0, tap : tap + 1]] * heads, axis=1) for tap in range(3)]
    row = lax.broadcasted_iota(jnp.int32, dq_ref.shape[1:], 0)
    far_rim = joined(far_ref[2 * span + 16 :])
    crosses = [me == group - 1, me == group]
    first_place = [me * span, (blocks - 1 - me) * span]
    present = [me < ctx_count - 1, me > 0]
    for half in range(2):
        rim = jnp.where(crosses[half], far_rim, rim_scr[neighbours[half]])
        rows = jnp.concatenate([rim[2 * at : 2 * at + 2] for at in range(rim.shape[0] // 2)], axis=1)
        end = first_place[half] + span
        zero, one, two = same(end - 1), same(end), same(end + 1)
        one = jnp.where(present[half], one, 0.0)
        last_but_one = (zero * one) * (taps[2] * rows[0:1])
        last = one * (taps[1] * rows[0:1]) + (one * two) * (taps[2] * rows[1:2])
        extra = jnp.where(row == 6, last_but_one, jnp.where(row == 7, last, 0.0))
        dq_ref[half] = tail_ref[half] + extra
    stores[2].start()
    for store in stores:
        store.wait()


def shards(q_pre, k_pre, value_before_filter, d_out, filters, doc_lengths):
    f32, bf16 = jnp.float32, jnp.bfloat16
    ctx_count = lax.axis_size("ctx")
    span, width = q_pre.shape[1:]
    length = 2 * span * ctx_count
    rim = 4 * width // (2 * LANES)
    vmem = pl.BlockSpec(memory_space=pltpu.VMEM)
    smem = pl.BlockSpec(memory_space=pltpu.SMEM)
    hbm = pl.BlockSpec(memory_space=pltpu.HBM)

    group = ctx_count // 2
    direct = group <= MAX_DIRECT
    halves = [[half * group + at for at in range(group)] for half in range(2)]
    msg_rows = 2 * span + rim

    def whole(shape):
        return pl.BlockSpec(shape, lambda i: (0,) * len(shape))

    def in_hbm(array):
        return pltpu.with_memory_space_constraint(array, pltpu.HBM)

    def flipped(array, flip):
        return lax.ppermute(array, "ctx", [(i, i ^ flip) for i in range(ctx_count)])

    def gathered(array):
        if direct:
            return [flipped(array, flip) for flip in range(1, group)]
        return [lax.all_gather(array, "ctx", axis_index_groups=halves)]

    def delivered(arrays):
        if direct:
            return [flipped(array, step + 1) for step, array in enumerate(arrays)]
        return [lax.all_to_all(arrays[0], "ctx", 0, 0, axis_index_groups=halves, tiled=True)]

    packed = pl.pallas_call(
        pack_kernel,
        grid=(1,),
        out_shape=jax.ShapeDtypeStruct((msg_rows, 2 * LANES), bf16),
        in_specs=[
            whole(k_pre.shape),
            whole(k_pre.shape),
            pl.BlockSpec((2, TAIL, width), lambda i: (0, span // TAIL - 1, 0)),
        ],
        out_specs=whole((msg_rows, 2 * LANES)),
        compiler_params=pltpu.CompilerParams(vmem_limit_bytes=4 * MIB),
        name="pack",
    )(*[in_hbm(array) for array in (k_pre, value_before_filter, q_pre)])
    across = flipped(packed, group)
    early, late = pl.pallas_call(
        relay_kernel,
        out_shape=[jax.ShapeDtypeStruct((rows, 2 * LANES), bf16) for rows in (span + rim, span)],
        in_specs=[vmem],
        out_specs=[vmem, vmem],
        compiler_params=pltpu.CompilerParams(vmem_limit_bytes=2 * MIB),
        name="relay",
    )(across)
    near = gathered(packed)
    if direct:
        late_near = [
            lax.ppermute(late, "ctx", [(i, i ^ flip) for i in range(group)]) for flip in range(1, group)
        ]
    else:
        late_near = gathered(late)
    received = [packed, early, late] + near + gathered(early) + late_near

    window = span * ctx_count + span
    if direct:
        flips = range(1, group)
        first_shapes = [(2 * span + (32 if flip == group - 1 else 16), 2 * LANES) for flip in flips]
        late_shapes = [(span + (16 if flip & (flip + 1) == 0 else 0), 2 * LANES) for flip in flips]
    else:
        first_shapes = [(group, 2 * span + 32, 2 * LANES)]
        late_shapes = [(group, span + 16, 2 * LANES)]
    slots = 4 if direct else 1
    heads = width // LANES
    by_head = (2, span * heads, LANES)
    padded = (2, heads, span + 8, LANES)
    prepared = pl.pallas_call(
        functools.partial(prep_kernel, ctx_count, direct),
        out_shape=[
            jax.ShapeDtypeStruct((length + 16, LANES), f32),
            jax.ShapeDtypeStruct((length + 16, LANES), f32),
            jax.ShapeDtypeStruct(padded, f32),
            jax.ShapeDtypeStruct(by_head, bf16),
            jax.ShapeDtypeStruct(by_head, bf16),
        ],
        in_specs=[smem, vmem, hbm, hbm] + [vmem] * (1 + len(near)),
        out_specs=[vmem] * 5,
        scratch_shapes=[
            pltpu.VMEM((ctx_count, rim, 2 * LANES), f32),
            pltpu.VMEM(q_pre.shape, bf16),
            pltpu.VMEM(q_pre.shape, bf16),
            pltpu.SemaphoreType.DMA((2,)),
        ],
        compiler_params=pltpu.CompilerParams(vmem_limit_bytes=(8 if direct else 32) * MIB),
        name="prep",
    )(doc_lengths, filters, in_hbm(q_pre), in_hbm(d_out), packed, *near)
    scratch = [
        pltpu.VMEM((2, length + 16, LANES), f32),
        pltpu.VMEM((2, length, LANES), bf16),
        pltpu.VMEM((2, length + 8, LANES), f32),
        pltpu.VMEM(padded, f32),
        pltpu.VMEM(by_head, bf16),
        pltpu.VMEM(padded, f32),
        pltpu.VMEM((window, LANES), f32),
        pltpu.VMEM((slots, window, 2 * LANES), f32),
        pltpu.VMEM((slots, window, 2 * LANES), f32),
        pltpu.VMEM(q_pre.shape, f32),
        pltpu.SemaphoreType.DMA((1,)),
    ]
    own_shapes = [(2 * span, 2 * LANES), (2 * span + 8, 2 * LANES)]
    d_q_main, d_q_tail, own_near, own_far, *sent = pl.pallas_call(
        functools.partial(grads_kernel, ctx_count, direct),
        out_shape=[jax.ShapeDtypeStruct(q_pre.shape, f32)]
        + [jax.ShapeDtypeStruct(shape, f32) for shape in [(2, 8, width)] + own_shapes]
        + [jax.ShapeDtypeStruct(shape, bf16) for shape in first_shapes + late_shapes],
        in_specs=[smem, vmem] + [vmem] * (len(prepared) + len(received)),
        out_specs=[hbm] + [vmem] * (3 + len(first_shapes + late_shapes)),
        scratch_shapes=scratch,
        compiler_params=pltpu.CompilerParams(vmem_limit_bytes=(20 if direct else 62) * MIB),
        name="grads",
    )(doc_lengths, filters, *prepared, *received)
    half_terms = delivered(sent[: len(first_shapes)])
    merged_shapes = [
        jax.ShapeDtypeStruct((2 * span, 2 * LANES), f32),
        jax.ShapeDtypeStruct((2 * span + 32, 2 * LANES), bf16),
        jax.ShapeDtypeStruct((8, 2 * LANES), f32),
    ]
    near, far, half_sums = pl.pallas_call(
        functools.partial(merge_kernel, ctx_count, direct),
        out_shape=merged_shapes,
        in_specs=[vmem] * (2 + len(half_terms)),
        out_specs=[vmem] * len(merged_shapes),
        scratch_shapes=[pltpu.VMEM((group, 8, 2 * LANES), f32)],
        compiler_params=pltpu.CompilerParams(vmem_limit_bytes=(4 if direct else 40) * MIB),
        name="merge",
    )(own_near, own_far, *half_terms)
    from_half = flipped(far, group)
    late_terms = delivered(sent[len(first_shapes) :])

    sums = pl.pallas_call(
        functools.partial(sums_kernel, span),
        out_shape=jax.ShapeDtypeStruct(filters.shape, f32),
        in_specs=[vmem, vmem],
        out_specs=vmem,
        compiler_params=pltpu.CompilerParams(vmem_limit_bytes=2 * MIB),
        name="sums",
    )(half_sums, from_half)
    count = lax.axis_size("tp")
    all_sums = [sums] + [
        lax.ppermute(sums, "tp", [(i, i ^ flip) for i in range(count)]) for flip in range(1, count)
    ]
    d_q_pre, d_k_pre, d_v_pre = pl.pallas_call(
        functools.partial(finish_kernel, ctx_count, direct),
        out_shape=(
            jax.ShapeDtypeStruct(q_pre.shape, f32),
            jax.ShapeDtypeStruct(k_pre.shape, f32),
            jax.ShapeDtypeStruct(k_pre.shape, f32),
        ),
        in_specs=[smem, vmem, hbm] + [vmem] * (3 + len(late_terms)),
        out_specs=(hbm, hbm, hbm),
        scratch_shapes=[
            pltpu.VMEM((2, 8, width), f32),
            pltpu.VMEM(k_pre.shape, f32),
            pltpu.VMEM(k_pre.shape, f32),
            pltpu.VMEM((ctx_count, rim // 2, 2 * LANES), f32),
            pltpu.SemaphoreType.DMA((3,)),
        ],
        input_output_aliases={2: 0},
        compiler_params=pltpu.CompilerParams(vmem_limit_bytes=(4 if direct else 16) * MIB),
        name="finish",
    )(doc_lengths, filters, d_q_main, d_q_tail, near, from_half, *late_terms)
    while len(all_sums) > 1:
        all_sums = [all_sums[at] + all_sums[at + 1] for at in range(0, len(all_sums), 2)]
    return (d_q_pre, d_k_pre, d_v_pre, all_sums[0])


def solution(mesh):
    split = P(None, "ctx", "tp")
    return jax.shard_map(
        shards,
        mesh=mesh,
        in_specs=(split, split, split, split, P(), P()),
        out_specs=(split, split, split, P()),
        check_vma=False,
    )
```

```python
import functools

import jax
import jax.numpy as jnp
import numpy as np
from jax import lax
from jax.experimental import pallas as pl
from jax.experimental.pallas import tpu as pltpu
from jax.sharding import PartitionSpec as P

LANES = 128
NT = (((1,), (1,)), ((), ()))
NN = (((1,), (0,)), ((), ()))
TN = (((0,), (0,)), ((), ()))
TAIL = 16
MAX_CHUNK = 640
RIM = 8
MAX_DIRECT = 4
WINDOWS = (2, 4, 6)
MIB = 1 << 20


def loop(count, body, init, unrolled=16):
    if count <= unrolled:
        for step in range(count):
            init = body(step, init)
        return init
    return lax.fori_loop(0, count, body, init)


def aligned(start, multiple):
    return start if isinstance(start, int) else pl.multiple_of(start, multiple)


def doc_starts(lengths_ref):
    starts = [jnp.int32(0)]
    for index in range(lengths_ref.shape[0] - 1):
        starts.append(starts[-1] + lengths_ref[index])
    return starts


def fold_rows(terms):
    rows, lanes = terms.shape
    return jnp.sum(terms.reshape(rows // 8, 8, lanes), axis=0)


def split_bits(values):
    high = values.astype(jnp.bfloat16)
    low = (values - high.astype(jnp.float32)).astype(jnp.bfloat16)
    return high, low


def joined(pair):
    rows = pair.shape[0] // 2
    pair = pair.astype(jnp.float32)
    return pair[:rows] + pair[rows:]


class Slots:
    def __init__(self, refs, me):
        self.refs, self.me = refs, me

    def __getitem__(self, flip):
        if len(self.refs) == 1:
            place = lax.rem(self.me, jnp.int32(self.refs[0].shape[0]))
            return self.refs[0].at[partner(place, flip)]
        return self.refs[flip]


def splits(direct, flip, group):
    return not direct or flip == group - 1


def partner(me, flip):
    return lax.bitwise_xor(me, jnp.int32(flip))


def pack_kernel(k_ref, v_ref, q_ref, out_ref):
    span = k_ref.shape[1]
    kv = jnp.concatenate([k_ref[...], v_ref[...]], axis=2).reshape(2 * span, 2 * LANES)
    tails = []
    for half in range(2):
        last = q_ref[half].astype(jnp.float32)[TAIL - 2 :]
        tails += [last[:, at : at + 2 * LANES] for at in range(0, last.shape[1], 2 * LANES)]
    out_ref[: 2 * span] = kv
    out_ref[2 * span :] = jnp.concatenate(tails, axis=0).astype(jnp.bfloat16)


def prep_kernel(ctx_count, direct, lengths_ref, filters_ref, q_hbm, d_out_hbm, own_ref, *refs):
    near_refs, refs = refs[:-9], refs[-9:]
    same_ref, same_two_ref, q_scr, qc_ref, do_ref, rim_scr, q_ref, d_out_ref, sems = refs
    f32, bf16 = jnp.float32, jnp.bfloat16
    loads = [
        pltpu.make_async_copy(q_hbm, q_ref, sems.at[0]),
        pltpu.make_async_copy(d_out_hbm, d_out_ref, sems.at[1]),
    ]
    for load in loads:
        load.start()
    group = ctx_count // 2
    span = q_ref.shape[1]
    heads = q_ref.shape[2] // LANES
    blocks = 2 * ctx_count
    length = span * blocks
    me = lax.axis_index("ctx")
    near = Slots((None,) + near_refs if direct else near_refs, me)
    starts = doc_starts(lengths_ref)

    def fill(index, carry):
        rows = pl.ds(aligned(8 + index * span, 8), span)
        same_ref[rows] = jnp.ones((span, LANES), f32)
        same_two_ref[rows] = jnp.ones((span, LANES), f32)
        return carry

    lax.fori_loop(0, blocks, fill, 0, unroll=2)
    zeros = jnp.zeros((8, LANES), f32)
    for rows in (slice(0, 8), slice(8 + length, 16 + length)):
        same_ref[rows] = zeros
        same_two_ref[rows] = zeros
    for start in starts:
        same_ref[pl.ds(8 + start, 1)] = zeros[:1]
        same_two_ref[pl.ds(8 + start, 1)] = zeros[:1]
        same_two_ref[pl.ds(9 + start, 1)] = zeros[:1]

    before, after = jnp.maximum(me - 1, 0), jnp.minimum(me + 1, ctx_count - 1)
    for index in (before, after):
        rim_scr[index] = jnp.zeros(rim_scr.shape[1:], f32)
    rim_scr[me] = own_ref[2 * span :].astype(f32)

    def place_rims(step, carry):
        flip = step + 1
        if not direct or flip & (flip + 1) == 0:
            rim_scr[partner(me, flip)] = near[flip][2 * span :].astype(f32)
        return carry

    loop(group - 1, place_rims, 0, 16 if direct else 1)
    rim_before, rim_after = rim_scr[before], rim_scr[after]
    late_rim = jnp.where(me == ctx_count - 1, rim_after[:RIM], rim_after[RIM:])
    rims = [rim_before[:RIM], late_rim]
    first_place = [me * span, (blocks - 1 - me) * span]
    taps = [filters_ref[0, tap : tap + 1] for tap in range(3)]

    for load in loads:
        load.wait()
    for half in range(2):
        rows = pl.ds(aligned(first_place[half] + 8, 8), span)
        one, two = same_ref[rows], same_two_ref[rows]
        for head in range(heads):
            at = 2 * (head // 2)
            q_scr[half, head, 6:8] = rims[half][at : at + 2, (head % 2) * LANES : (head % 2 + 1) * LANES]

        def convolve_head(head, carry, half=half, one=one, two=two):
            lanes = pl.ds(pl.multiple_of(head * LANES, LANES), LANES)
            target = pl.ds(pl.multiple_of(head * span, 16), span)
            q_scr[half, head, 8:] = q_ref[half, :, lanes].astype(f32)
            total = taps[0] * q_scr[half, head, 8:]
            total = total + one * (taps[1] * q_scr[half, head, 7 : 7 + span])
            total = total + two * (taps[2] * q_scr[half, head, 6 : 6 + span])
            qc_ref[half, target] = total.astype(bf16)
            do_ref[half, target] = d_out_ref[half, :, lanes]
            return carry

        lax.fori_loop(0, heads, convolve_head, 0)


def grads_kernel(ctx_count, direct, lengths_ref, filters_ref, *refs):
    group = ctx_count // 2
    arrays = group - 1 if direct else 1
    same_scr, same_two_scr, q_in_ref, qc_in_ref, do_scr, own_ref, across_ref = refs[:7]
    refs = refs[7:]
    near_in, far_in, refs = refs[:arrays], refs[arrays : 2 * arrays], refs[2 * arrays :]
    dq_hbm, dq_tail_ref, own_near_ref, own_far_ref = refs[:4]
    arrays = group - 1 if direct else 1
    first_out, late_out, refs = refs[4 : 4 + arrays], refs[4 + arrays : 5 + arrays], refs[5 + arrays :]
    kv_scr, conv_scr, dkv_scr, q_scr, qc_scr, dq_scr = refs[:6]
    bias_scr, s_scr, dp_scr, dq_ref, terms_scr, sems = refs[6:]
    f32, bf16 = jnp.float32, jnp.bfloat16
    span = own_ref.shape[0] // 2 - TAIL // 2
    heads = q_in_ref.shape[1]
    half_rows = span * ctx_count
    length = 2 * half_rows
    blocks = 2 * ctx_count
    me = lax.axis_index("ctx")
    near_in = Slots((None,) + near_in if direct else near_in, me)
    far_in = Slots((None,) + far_in if direct else far_in, me)
    first_out = Slots((None,) + first_out if direct else first_out, me)
    late_out = Slots((None,) * (group - 1) + late_out if direct else late_out, me)
    scale = LANES**-0.5
    log2_scale = scale * 1.4426950408889634
    starts = doc_starts(lengths_ref)

    def place(index, block):
        for tensor in range(2):
            lanes = slice(tensor * LANES, (tensor + 1) * LANES)
            kv_scr[tensor, pl.ds(aligned(8 + index * span, 8), span)] = block[:, lanes].astype(f32)

    def place_both(message, index):
        place(index, message[:span])
        place(blocks - 1 - index, message[span : 2 * span])

    def place_received(step, carry):
        flip = step + 1
        source = partner(me, flip)
        place_both(near_in[flip], source)
        place_both(far_in[flip], partner(source, group))
        return carry

    zeros = jnp.zeros((8, LANES), f32)
    for tensor in range(2):
        kv_scr[tensor, :8] = zeros
    for block_ref, index in ((own_ref, me), (across_ref, partner(me, group))):
        place_both(block_ref, index)
    loop(group - 1, place_received, 0, 16 if direct else 1)

    def taps(tensor):
        return [filters_ref[tensor, tap : tap + 1] for tap in range(3)]

    def masks(base, ahead):
        one = same_scr[pl.ds(base + 8 + min(ahead, 1), span)]
        return one, same_two_scr[pl.ds(base + 8 + ahead, span)]

    def convolve_kv(index, carry):
        base = index * span
        one, two = masks(base, 0)
        for tensor in range(2):
            zero_tap, one_tap, two_tap = taps(tensor + 1)
            total = zero_tap * kv_scr[tensor, pl.ds(aligned(base + 8, 8), span)]
            total = total + one * (one_tap * kv_scr[tensor, pl.ds(base + 7, span)])
            total = total + two * (two_tap * kv_scr[tensor, pl.ds(base + 6, span)])
            conv_scr[tensor, pl.ds(aligned(base, 16), span)] = total.astype(bf16)
        return carry

    first_place = [me * span, (blocks - 1 - me) * span]
    firsts = []
    for half in range(2):
        lowest = jnp.int32(0)
        for start in starts[1:]:
            lowest = jnp.where(first_place[half] >= start, start, lowest)
        firsts.append(lowest // span)

    def over_needed(body, init):
        carry = lax.fori_loop(firsts[0], me + 1, body, init)
        return lax.fori_loop(jnp.maximum(firsts[1], me + 1), blocks - me, body, carry)

    def clear(index, carry):
        for tensor in range(2):
            rows = pl.ds(pl.multiple_of(index * span, 16), span)
            conv_scr[tensor, rows] = jnp.zeros((span, LANES), bf16)
            dkv_scr[tensor, rows] = jnp.zeros((span, LANES), f32)
        terms_scr[index] = jnp.zeros((span, 2 * LANES), f32)
        return carry

    lax.fori_loop(0, blocks, clear, 0, unroll=2)
    for tensor in range(2):
        dkv_scr[tensor, length:] = zeros
    over_needed(convolve_kv, 0)

    middle = me == ctx_count - 1
    q_scr[...] = q_in_ref[...]
    qc_scr[...] = qc_in_ref[...]
    tails = far_in[group - 1][2 * span :].astype(f32)
    tails = [tails[:RIM], tails[RIM:]]
    for half, crossing in ((0, me == group), (1, me == group - 1)):

        @pl.when(crossing)
        def _(half=half):
            rows = pl.ds(aligned(first_place[half] + 8, 8), TAIL)
            one, two = same_scr[rows], same_two_scr[rows]
            zero_tap, one_tap, two_tap = taps(0)
            for head in range(heads):
                at = 2 * (head // 2)
                q_scr[half, head, 6:8] = tails[half][
                    at : at + 2, (head % 2) * LANES : (head % 2 + 1) * LANES
                ]
                total = zero_tap * q_scr[half, head, 8 : 8 + TAIL]
                total = total + one * (one_tap * q_scr[half, head, 7 : 7 + TAIL])
                total = total + two * (two_tap * q_scr[half, head, 6 : 6 + TAIL])
                qc_scr[half, head * span : head * span + TAIL] = total.astype(bf16)

    def attend(half, window, first_key):
        chunks = 1
        while window // chunks > MAX_CHUNK or window % (16 * chunks):
            chunks += 1
        size = window // chunks
        query = first_place[half] + lax.rem(
            lax.broadcasted_iota(jnp.int32, (1, LANES), 1), jnp.int32(span)
        )
        lowest = jnp.zeros((1, LANES), jnp.int32)
        for start in starts[1:]:
            lowest = jnp.where(query >= start, start, lowest)
        wide = 2 * LANES

        def fill_bias(step, carry):
            places = first_key + step * size + lax.broadcasted_iota(jnp.int32, (size, LANES), 0)
            allowed = (places >= lowest) & (places <= query)
            bias_scr[pl.ds(aligned(step * size, 16), size)] = jnp.where(allowed, 0.0, -1e30)
            return carry

        loop(chunks, fill_bias, 0, 1)
        whole_window = pl.ds(aligned(first_key, 16), window)
        keys_t = conv_scr[0, whole_window].T if chunks == 1 else None
        for at in range(heads * span // wide):
            slot = (half * (heads * span // wide) + at) % s_scr.shape[0]
            cols = slice(at * wide, (at + 1) * wide)
            queries = qc_scr[half, cols]
            grads = do_scr[half, cols]

            def key_rows(step):
                return pl.ds(aligned(first_key + step * size, 16), size)

            def score(step, top):
                keys = conv_scr[0, key_rows(step)]
                scores = lax.dot_general(keys, queries, NT, preferred_element_type=f32)
                bias = bias_scr[pl.ds(aligned(step * size, 16), size)]
                scores = scores + jnp.concatenate([bias, bias], axis=1)
                s_scr[slot, pl.ds(aligned(step * size, 16), size)] = scores
                return jnp.maximum(top, jnp.max(scores, axis=0, keepdims=True))

            top = loop(chunks, score, jnp.full((1, wide), -1e30, f32), 1)

            def weigh(step, carry):
                total, weighted = carry
                rows = pl.ds(aligned(step * size, 16), size)
                weights = jnp.exp2((s_scr[slot, rows] - top) * log2_scale)
                values = conv_scr[1, key_rows(step)]
                prob_grads = lax.dot_general(values, grads, NT, preferred_element_type=f32)
                s_scr[slot, rows] = weights
                dp_scr[slot, rows] = prob_grads
                total = total + jnp.sum(weights, axis=0, keepdims=True)
                weighted = weighted + jnp.sum(weights * prob_grads, axis=0, keepdims=True)
                return total, weighted

            zeros = jnp.zeros((1, wide), f32)
            total, weighted = loop(chunks, weigh, (zeros, zeros), 1)
            inverse = 1.0 / total
            mean = weighted * inverse
            slope = inverse * scale

            def accumulate(step, dq):
                rows = pl.ds(aligned(step * size, 16), size)
                weights = s_scr[slot, rows]
                probs = (weights * inverse).astype(bf16)
                score_grads = (weights * slope * (dp_scr[slot, rows] - mean)).astype(bf16)
                dk = lax.dot_general(score_grads, queries, NN, preferred_element_type=f32)
                dv = lax.dot_general(probs, grads, NN, preferred_element_type=f32)
                target = pl.ds(aligned(first_key + step * size, 16), size)
                for tensor, terms in enumerate((dk, dv)):
                    dkv_scr[tensor, target] += terms
                if keys_t is not None:
                    return lax.dot_general(keys_t, score_grads, NN, preferred_element_type=f32)
                keys = conv_scr[0, key_rows(step)]
                return dq + lax.dot_general(keys, score_grads, TN, preferred_element_type=f32)

            dq = loop(chunks, accumulate, jnp.zeros((LANES, wide), f32), 1)
            dq = dq.T
            for part in range(wide // span):
                head = at * (wide // span) + part
                dq_scr[half, head, :span] = dq[part * span : (part + 1) * span]

    for half in range(2):
        widest = ctx_count + half
        needed = first_place[half] // span - firsts[half] + 1
        below = 0
        for count in [count for count in WINDOWS if direct and count < widest] + [widest]:

            @pl.when((needed > below) & (needed <= count))
            def _(half=half, count=count):
                first_key = jnp.maximum(first_place[half] + span - count * span, 0)
                attend(half, count * span, first_key)

            below = count

    next_rows = jnp.where(middle, dq_scr[1, :, :8], 0.0)
    dq_scr[0, :, span:] = next_rows
    dq_scr[1, :, span:] = jnp.zeros_like(next_rows)
    sums = [jnp.zeros((8, LANES), f32) for _ in range(3)]
    for half in range(2):
        one, two = masks(first_place[half], 0)
        ahead_one = same_scr[pl.ds(first_place[half] + 9, span)]
        ahead_two = same_two_scr[pl.ds(first_place[half] + 10, span)]
        zero_tap, one_tap, two_tap = taps(0)

        def finish_head(head, carry, half=half, one=one, two=two, ahead_one=ahead_one, ahead_two=ahead_two):
            lanes = pl.ds(pl.multiple_of(head * LANES, LANES), LANES)
            grads = dq_scr[half, head, :span]
            out = zero_tap * grads
            out = out + ahead_one * (one_tap * dq_scr[half, head, 1 : 1 + span])
            out = out + ahead_two * (two_tap * dq_scr[half, head, 2 : 2 + span])
            dq_ref[half, :, lanes] = out
            dq_tail_ref[half, :, lanes] = out[span - 8 :]
            return (
                carry[0] + fold_rows(grads * q_scr[half, head, 8:]),
                carry[1] + fold_rows(grads * one * q_scr[half, head, 7 : 7 + span]),
                carry[2] + fold_rows(grads * two * q_scr[half, head, 6 : 6 + span]),
            )

        sums = lax.fori_loop(0, heads, finish_head, tuple(sums))
    q_sums = [jnp.sum(term, axis=0, keepdims=True) for term in sums]
    store = pltpu.make_async_copy(dq_ref, dq_hbm, sems.at[0])
    store.start()

    def finish_block(index, carry):
        base = pl.multiple_of(index * span, 8)
        one, two = masks(base, 0)
        ahead_one = same_scr[pl.ds(base + 9, span)]
        ahead_two = same_two_scr[pl.ds(base + 10, span)]
        carry = list(carry)
        for tensor in range(2):
            zero_tap, one_tap, two_tap = taps(tensor + 1)
            own = dkv_scr[tensor, pl.ds(base, span)]
            out = zero_tap * own
            out = out + ahead_one * (one_tap * dkv_scr[tensor, pl.ds(base + 1, span)])
            out = out + ahead_two * (two_tap * dkv_scr[tensor, pl.ds(base + 2, span)])
            lanes = slice(tensor * LANES, (tensor + 1) * LANES)
            terms_scr[index, :, lanes] = out
            at = 3 * tensor
            carry[at] += fold_rows(own * kv_scr[tensor, pl.ds(base + 8, span)])
            carry[at + 1] += fold_rows(own * one * kv_scr[tensor, pl.ds(base + 7, span)])
            carry[at + 2] += fold_rows(own * two * kv_scr[tensor, pl.ds(base + 6, span)])
        return tuple(carry)

    low = me < group

    kv_sums = over_needed(finish_block, (zeros,) * 6)
    for target, index in ((own_far_ref, partner(me, group)), (own_near_ref, me)):
        target[:span] = terms_scr[index]
        target[span : 2 * span] = terms_scr[blocks - 1 - index]

    def send(step, carry):
        flip = step + 1
        owner = partner(me, flip)
        far_owner = partner(me, flip + group)
        near_late = blocks - 1 - owner
        second = jnp.where(low, blocks - 1 - far_owner, owner)
        third = jnp.where(low & (me > owner), owner, near_late)
        first_out[flip][:span] = terms_scr[far_owner].astype(bf16)
        first_out[flip][span : 2 * span] = terms_scr[second].astype(bf16)
        if splits(direct, flip, group):
            late_out[flip][:span] = terms_scr[third].astype(bf16)
        else:
            first_out[flip][2 * span : 3 * span] = terms_scr[third].astype(bf16)
        return carry

    loop(group - 1, send, 0, 16 if direct else 1)
    kv_sums = [jnp.sum(term, axis=0, keepdims=True) for term in kv_sums]

    padding = [jnp.zeros((2, LANES), f32)]
    left = jnp.concatenate(q_sums + kv_sums[:3] + padding, axis=0)
    right = jnp.concatenate([jnp.zeros((3, LANES), f32)] + kv_sums[3:] + padding, axis=0)
    sums_tile = jnp.concatenate([left, right], axis=1)
    sums_pair = jnp.concatenate(split_bits(sums_tile), axis=0)
    own_far_ref[2 * span :] = joined(sums_pair)
    rims = []
    for half in range(2):
        rows = [dq_scr[half, head, :2] for head in range(heads)]
        rows = [jnp.concatenate(rows[at : at + 2], axis=1) for at in range(0, heads, 2)]
        rims.append(jnp.concatenate(rows, axis=0))

    def rim_for(index):
        return jnp.concatenate(split_bits(jnp.where(index < me, rims[0], rims[1])), axis=0)

    def store_rims(step, carry):
        flip = step + 1
        owner = partner(me, flip)
        after = (2 if splits(direct, flip, group) else 3) * span
        first_out[flip][after : after + 16] = sums_pair
        if not direct or flip == group - 1:
            first_out[flip][after + 16 :] = rim_for(partner(owner, group))
        if not direct or flip & (flip + 1) == 0:
            if splits(direct, flip, group):
                late_out[flip][span:] = rim_for(owner)
            else:
                first_out[flip][after + 16 :] = rim_for(owner)
        return carry

    loop(group - 1, store_rims, 0, 16 if direct else 1)
    store.wait()


def merge_kernel(ctx_count, direct, own_near_ref, own_far_ref, *refs):
    received_refs, refs = refs[:-6], refs[-6:]
    near_ref, far_ref, half_sums_ref, rims_ref, sums_scr, rim_scr = refs
    f32, bf16 = jnp.float32, jnp.bfloat16
    group = ctx_count // 2
    me = lax.axis_index("ctx")
    low = me < group
    received = Slots((own_far_ref,) + received_refs if direct else received_refs, me)
    place = lax.rem(me, jnp.int32(group))
    span = own_near_ref.shape[0] // 2
    rows = 2 * span
    sums_scr[place] = own_far_ref[rows:]
    def add(step, carry):
        flip = step + 1
        source = partner(me, flip)
        message = received[flip]
        early, second = [message[at * span : (at + 1) * span].astype(f32) for at in range(2)]
        near_early, near_late, far_early, far_late = carry
        zero = jnp.zeros_like(second)
        after = (2 if splits(direct, flip, group) else 3) * span
        sums_scr[partner(place, flip)] = joined(message[after : after + 16])
        near_early = near_early + jnp.where(low, zero, second)
        if not splits(direct, flip, group):
            third = message[2 * span : 3 * span].astype(f32)
            to_early = low & (source > me)
            near_early = near_early + jnp.where(to_early, third, zero)
            near_late = near_late + jnp.where(to_early, zero, third)
            if flip & (flip + 1) == 0:
                rim_scr[source] = joined(message[after + 16 :])
        return near_early, near_late, far_early + early, far_late + jnp.where(low, second, zero)

    neighbours = [jnp.minimum(me + 1, ctx_count - 1), jnp.maximum(me - 1, 0)]
    for index in neighbours:
        rim_scr[index] = jnp.zeros(rim_scr.shape[1:], f32)
    init = (own_near_ref[:span], own_near_ref[span:], own_far_ref[:span], own_far_ref[span:rows])
    totals = loop(group - 1, add, init, 16 if direct else 1)
    near_ref[:span] = totals[0]
    near_ref[span:] = totals[1]
    far_ref[:span] = totals[2].astype(bf16)
    far_ref[span:rows] = totals[3].astype(bf16)
    for at, index in enumerate(neighbours):
        rims_ref[at] = rim_scr[index]
    sums = loop(group, lambda index, carry: carry + sums_scr[index], jnp.zeros((8, 2 * LANES), f32))
    pair = jnp.concatenate(split_bits(sums), axis=0)
    half_sums_ref[...] = joined(pair)
    far_ref[rows : rows + 16] = pair
    far_ref[rows + 16 :] = received[group - 1][rows + 16 :]


def sums_kernel(span, half_sums_ref, far_ref, out_ref):
    sums = half_sums_ref[...] + joined(far_ref[2 * span : 2 * span + 16])
    out_ref[0] = sums[0:3, :LANES]
    out_ref[1] = sums[3:6, :LANES]
    out_ref[2] = sums[3:6, LANES:]


def finish_kernel(
    ctx_count, direct, lengths_ref, filters_ref, dq_in_hbm, tail_ref, near_ref, far_ref, rims_ref, *refs
):
    received_refs, refs = refs[:-8], refs[-8:]
    dq_hbm, dk_hbm, dv_hbm, dq_ref, dk_ref, dv_ref, rim_scr, sems = refs
    f32 = jnp.float32
    group = ctx_count // 2
    span = dk_ref.shape[1]
    me = lax.axis_index("ctx")
    low = me < group
    received = Slots((None,) * (group - 1) + received_refs if direct else received_refs, me)
    starts = doc_starts(lengths_ref)
    blocks = 2 * ctx_count
    neighbours = [jnp.minimum(me + 1, ctx_count - 1), jnp.maximum(me - 1, 0)]
    for at, index in enumerate(neighbours):
        rim_scr[index] = rims_ref[at]

    def add(step, carry):
        flip = step + 1
        source = partner(me, flip)
        message = received[flip]
        terms = message[:span].astype(f32)
        if not direct or flip & (flip + 1) == 0:
            rim_scr[source] = joined(message[span:])
        to_early = low & (source > me)
        zero = jnp.zeros_like(terms)
        return carry[0] + jnp.where(to_early, terms, zero), carry[1] + jnp.where(to_early, zero, terms)

    total = near_ref[...] + far_ref[: 2 * span].astype(f32)
    total = (total[:span], total[span:])
    total = add(group - 2, total) if direct else loop(group - 1, add, total, 1)
    for half in range(2):
        dk_ref[half] = total[half][:, :LANES]
        dv_ref[half] = total[half][:, LANES:]
    stores = [
        pltpu.make_async_copy(dk_ref, dk_hbm, sems.at[0]),
        pltpu.make_async_copy(dv_ref, dv_hbm, sems.at[1]),
        pltpu.make_async_copy(dq_ref, dq_hbm.at[:, pl.ds(span - 8, 8)], sems.at[2]),
    ]
    for store in stores[:2]:
        store.start()

    def same(place):
        cut = place >= blocks * span
        for start in starts:
            cut = cut | (place == start)
        return jnp.where(cut, 0.0, 1.0).astype(f32)

    heads = dq_ref.shape[2] // LANES
    taps = [jnp.concatenate([filters_ref[0, tap : tap + 1]] * heads, axis=1) for tap in range(3)]
    row = lax.broadcasted_iota(jnp.int32, dq_ref.shape[1:], 0)
    far_rim = joined(far_ref[2 * span + 16 :])
    crosses = [me == group - 1, me == group]
    first_place = [me * span, (blocks - 1 - me) * span]
    present = [me < ctx_count - 1, me > 0]
    for half in range(2):
        rim = jnp.where(crosses[half], far_rim, rim_scr[neighbours[half]])
        rows = jnp.concatenate([rim[2 * at : 2 * at + 2] for at in range(rim.shape[0] // 2)], axis=1)
        end = first_place[half] + span
        zero, one, two = same(end - 1), same(end), same(end + 1)
        one = jnp.where(present[half], one, 0.0)
        last_but_one = (zero * one) * (taps[2] * rows[0:1])
        last = one * (taps[1] * rows[0:1]) + (one * two) * (taps[2] * rows[1:2])
        extra = jnp.where(row == 6, last_but_one, jnp.where(row == 7, last, 0.0))
        dq_ref[half] = tail_ref[half] + extra
    stores[2].start()
    for store in stores:
        store.wait()


def shards(q_pre, k_pre, value_before_filter, d_out, filters, doc_lengths):
    f32, bf16 = jnp.float32, jnp.bfloat16
    ctx_count = lax.axis_size("ctx")
    span, width = q_pre.shape[1:]
    length = 2 * span * ctx_count
    rim = 4 * width // (2 * LANES)
    vmem = pl.BlockSpec(memory_space=pltpu.VMEM)
    smem = pl.BlockSpec(memory_space=pltpu.SMEM)
    hbm = pl.BlockSpec(memory_space=pltpu.HBM)

    group = ctx_count // 2
    direct = group <= MAX_DIRECT
    halves = [[half * group + at for at in range(group)] for half in range(2)]
    msg_rows = 2 * span + rim

    def whole(shape):
        return pl.BlockSpec(shape, lambda i: (0,) * len(shape))

    def in_hbm(array):
        return pltpu.with_memory_space_constraint(array, pltpu.HBM)

    def flipped(array, flip):
        return lax.ppermute(array, "ctx", [(i, i ^ flip) for i in range(ctx_count)])

    def gathered(array):
        if direct:
            return [flipped(array, flip) for flip in range(1, group)]
        return [lax.all_gather(array, "ctx", axis_index_groups=halves)]

    def delivered(arrays):
        if direct:
            return [flipped(array, step + 1) for step, array in enumerate(arrays)]
        return [lax.all_to_all(arrays[0], "ctx", 0, 0, axis_index_groups=halves, tiled=True)]

    packed = pl.pallas_call(
        pack_kernel,
        grid=(1,),
        out_shape=jax.ShapeDtypeStruct((msg_rows, 2 * LANES), bf16),
        in_specs=[
            whole(k_pre.shape),
            whole(k_pre.shape),
            pl.BlockSpec((2, TAIL, width), lambda i: (0, span // TAIL - 1, 0)),
        ],
        out_specs=whole((msg_rows, 2 * LANES)),
        compiler_params=pltpu.CompilerParams(vmem_limit_bytes=4 * MIB),
        name="pack",
    )(*[in_hbm(array) for array in (k_pre, value_before_filter, q_pre)])
    across = flipped(packed, group)
    near = gathered(packed)
    far = gathered(across)
    received = [packed, across] + near + far

    window = span * ctx_count + span
    if direct:
        flips = range(1, group)
        first_shapes = []
        for flip in flips:
            rows = (2 if splits(direct, flip, group) else 3) * span + 16
            rows += 16 if flip == group - 1 or flip & (flip + 1) == 0 else 0
            first_shapes.append((rows, 2 * LANES))
        late_shapes = [(span + 16, 2 * LANES)]
    else:
        first_shapes = [(group, 2 * span + 32, 2 * LANES)]
        late_shapes = [(group, span + 16, 2 * LANES)]
    slots = 4 if direct else 1
    heads = width // LANES
    by_head = (2, span * heads, LANES)
    padded = (2, heads, span + 8, LANES)
    prepared = pl.pallas_call(
        functools.partial(prep_kernel, ctx_count, direct),
        out_shape=[
            jax.ShapeDtypeStruct((length + 16, LANES), f32),
            jax.ShapeDtypeStruct((length + 16, LANES), f32),
            jax.ShapeDtypeStruct(padded, f32),
            jax.ShapeDtypeStruct(by_head, bf16),
            jax.ShapeDtypeStruct(by_head, bf16),
        ],
        in_specs=[smem, vmem, hbm, hbm] + [vmem] * (1 + len(near)),
        out_specs=[vmem] * 5,
        scratch_shapes=[
            pltpu.VMEM((ctx_count, rim, 2 * LANES), f32),
            pltpu.VMEM(q_pre.shape, bf16),
            pltpu.VMEM(q_pre.shape, bf16),
            pltpu.SemaphoreType.DMA((2,)),
        ],
        compiler_params=pltpu.CompilerParams(vmem_limit_bytes=(8 if direct else 32) * MIB),
        name="prep",
    )(doc_lengths, filters, in_hbm(q_pre), in_hbm(d_out), packed, *near)
    scratch = [
        pltpu.VMEM((2, length + 16, LANES), f32),
        pltpu.VMEM((2, length, LANES), bf16),
        pltpu.VMEM((2, length + 8, LANES), f32),
        pltpu.VMEM(padded, f32),
        pltpu.VMEM(by_head, bf16),
        pltpu.VMEM(padded, f32),
        pltpu.VMEM((window, LANES), f32),
        pltpu.VMEM((slots, window, 2 * LANES), f32),
        pltpu.VMEM((slots, window, 2 * LANES), f32),
        pltpu.VMEM(q_pre.shape, f32),
        pltpu.VMEM((2 * ctx_count, span, 2 * LANES), f32),
        pltpu.SemaphoreType.DMA((1,)),
    ]
    own_shapes = [(2 * span, 2 * LANES), (2 * span + 8, 2 * LANES)]
    d_q_main, d_q_tail, own_near, own_far, *sent = pl.pallas_call(
        functools.partial(grads_kernel, ctx_count, direct),
        out_shape=[jax.ShapeDtypeStruct(q_pre.shape, f32)]
        + [jax.ShapeDtypeStruct(shape, f32) for shape in [(2, 8, width)] + own_shapes]
        + [jax.ShapeDtypeStruct(shape, bf16) for shape in first_shapes + late_shapes],
        in_specs=[smem, vmem] + [vmem] * (len(prepared) + len(received)),
        out_specs=[hbm] + [vmem] * (3 + len(first_shapes + late_shapes)),
        scratch_shapes=scratch,
        compiler_params=pltpu.CompilerParams(vmem_limit_bytes=(20 if direct else 62) * MIB),
        name="grads",
    )(doc_lengths, filters, *prepared, *received)
    half_terms = delivered(sent[: len(first_shapes)])
    merged_shapes = [
        jax.ShapeDtypeStruct((2 * span, 2 * LANES), f32),
        jax.ShapeDtypeStruct((2 * span + 32, 2 * LANES), bf16),
        jax.ShapeDtypeStruct((8, 2 * LANES), f32),
        jax.ShapeDtypeStruct((2, rim // 2, 2 * LANES), f32),
    ]
    near, far, half_sums, rims = pl.pallas_call(
        functools.partial(merge_kernel, ctx_count, direct),
        out_shape=merged_shapes,
        in_specs=[vmem] * (2 + len(half_terms)),
        out_specs=[vmem] * len(merged_shapes),
        scratch_shapes=[
            pltpu.VMEM((group, 8, 2 * LANES), f32),
            pltpu.VMEM((ctx_count, rim // 2, 2 * LANES), f32),
        ],
        compiler_params=pltpu.CompilerParams(vmem_limit_bytes=(4 if direct else 40) * MIB),
        name="merge",
    )(own_near, own_far, *half_terms)
    from_half = flipped(far, group)
    late_terms = sent[len(first_shapes) :]
    late_terms = [flipped(late_terms[0], group - 1)] if direct else delivered(late_terms)

    sums = pl.pallas_call(
        functools.partial(sums_kernel, span),
        out_shape=jax.ShapeDtypeStruct(filters.shape, f32),
        in_specs=[vmem, vmem],
        out_specs=vmem,
        compiler_params=pltpu.CompilerParams(vmem_limit_bytes=2 * MIB),
        name="sums",
    )(half_sums, from_half)
    count = lax.axis_size("tp")
    all_sums = [sums] + [
        lax.ppermute(sums, "tp", [(i, i ^ flip) for i in range(count)]) for flip in range(1, count)
    ]
    d_q_pre, d_k_pre, d_v_pre = pl.pallas_call(
        functools.partial(finish_kernel, ctx_count, direct),
        out_shape=(
            jax.ShapeDtypeStruct(q_pre.shape, f32),
            jax.ShapeDtypeStruct(k_pre.shape, f32),
            jax.ShapeDtypeStruct(k_pre.shape, f32),
        ),
        in_specs=[smem, vmem, hbm] + [vmem] * (4 + len(late_terms)),
        out_specs=(hbm, hbm, hbm),
        scratch_shapes=[
            pltpu.VMEM((2, 8, width), f32),
            pltpu.VMEM(k_pre.shape, f32),
            pltpu.VMEM(k_pre.shape, f32),
            pltpu.VMEM((ctx_count, rim // 2, 2 * LANES), f32),
            pltpu.SemaphoreType.DMA((3,)),
        ],
        input_output_aliases={2: 0},
        compiler_params=pltpu.CompilerParams(vmem_limit_bytes=(4 if direct else 16) * MIB),
        name="finish",
    )(doc_lengths, filters, d_q_main, d_q_tail, near, from_half, rims, *late_terms)
    while len(all_sums) > 1:
        all_sums = [all_sums[at] + all_sums[at + 1] for at in range(0, len(all_sums), 2)]
    return (d_q_pre, d_k_pre, d_v_pre, all_sums[0])


def solution(mesh):
    split = P(None, "ctx", "tp")
    return jax.shard_map(
        shards,
        mesh=mesh,
        in_specs=(split, split, split, split, P(), P()),
        out_specs=(split, split, split, P()),
        check_vma=False,
    )
```

```python
import functools

import jax
import jax.numpy as jnp
import numpy as np
from jax import lax
from jax.experimental import pallas as pl
from jax.experimental.pallas import tpu as pltpu
from jax.sharding import PartitionSpec as P

LANES = 128
NT = (((1,), (1,)), ((), ()))
NN = (((1,), (0,)), ((), ()))
TN = (((0,), (0,)), ((), ()))
TAIL = 16
MAX_CHUNK = 640
RIM = 8
MAX_DIRECT = 4
WINDOWS = (2, 4, 6)
MIB = 1 << 20


def loop(count, body, init, unrolled=16):
    if count <= unrolled:
        for step in range(count):
            init = body(step, init)
        return init
    return lax.fori_loop(0, count, body, init)


def aligned(start, multiple):
    return start if isinstance(start, int) else pl.multiple_of(start, multiple)


def doc_starts(lengths_ref):
    starts = [jnp.int32(0)]
    for index in range(lengths_ref.shape[0] - 1):
        starts.append(starts[-1] + lengths_ref[index])
    return starts


def fold_rows(terms):
    rows, lanes = terms.shape
    return jnp.sum(terms.reshape(rows // 8, 8, lanes), axis=0)


def split_bits(values):
    high = values.astype(jnp.bfloat16)
    low = (values - high.astype(jnp.float32)).astype(jnp.bfloat16)
    return high, low


def joined(pair):
    rows = pair.shape[0] // 2
    pair = pair.astype(jnp.float32)
    return pair[:rows] + pair[rows:]


class Slots:
    def __init__(self, refs, me):
        self.refs, self.me = refs, me

    def __getitem__(self, flip):
        if len(self.refs) == 1:
            place = lax.rem(self.me, jnp.int32(self.refs[0].shape[0]))
            return self.refs[0].at[partner(place, flip)]
        return self.refs[flip]


def splits(direct, flip, group):
    return not direct or flip == group - 1


def partner(me, flip):
    return lax.bitwise_xor(me, jnp.int32(flip))


def pack_kernel(k_ref, v_ref, q_ref, out_ref):
    span = k_ref.shape[1]
    kv = jnp.concatenate([k_ref[...], v_ref[...]], axis=2).reshape(2 * span, 2 * LANES)
    tails = []
    for half in range(2):
        last = q_ref[half].astype(jnp.float32)[TAIL - 2 :]
        tails += [last[:, at : at + 2 * LANES] for at in range(0, last.shape[1], 2 * LANES)]
    out_ref[: 2 * span] = kv
    out_ref[2 * span :] = jnp.concatenate(tails, axis=0).astype(jnp.bfloat16)


def prep_kernel(ctx_count, direct, lengths_ref, filters_ref, q_hbm, d_out_hbm, own_ref, *refs):
    near_refs, refs = refs[:-9], refs[-9:]
    same_ref, same_two_ref, q_scr, qc_ref, do_ref, rim_scr, q_ref, d_out_ref, sems = refs
    f32, bf16 = jnp.float32, jnp.bfloat16
    loads = [
        pltpu.make_async_copy(q_hbm, q_ref, sems.at[0]),
        pltpu.make_async_copy(d_out_hbm, d_out_ref, sems.at[1]),
    ]
    for load in loads:
        load.start()
    group = ctx_count // 2
    span = q_ref.shape[1]
    heads = q_ref.shape[2] // LANES
    blocks = 2 * ctx_count
    length = span * blocks
    me = lax.axis_index("ctx")
    near = Slots((None,) + near_refs if direct else near_refs, me)
    starts = doc_starts(lengths_ref)

    def fill(index, carry):
        rows = pl.ds(aligned(8 + index * span, 8), span)
        same_ref[rows] = jnp.ones((span, LANES), f32)
        same_two_ref[rows] = jnp.ones((span, LANES), f32)
        return carry

    lax.fori_loop(0, blocks, fill, 0, unroll=2)
    zeros = jnp.zeros((8, LANES), f32)
    for rows in (slice(0, 8), slice(8 + length, 16 + length)):
        same_ref[rows] = zeros
        same_two_ref[rows] = zeros
    for start in starts:
        same_ref[pl.ds(8 + start, 1)] = zeros[:1]
        same_two_ref[pl.ds(8 + start, 1)] = zeros[:1]
        same_two_ref[pl.ds(9 + start, 1)] = zeros[:1]

    before, after = jnp.maximum(me - 1, 0), jnp.minimum(me + 1, ctx_count - 1)
    for index in (before, after):
        rim_scr[index] = jnp.zeros(rim_scr.shape[1:], f32)
    rim_scr[me] = own_ref[2 * span :].astype(f32)

    def place_rims(step, carry):
        flip = step + 1
        if not direct or flip & (flip + 1) == 0:
            rim_scr[partner(me, flip)] = near[flip][2 * span :].astype(f32)
        return carry

    loop(group - 1, place_rims, 0, 16 if direct else 1)
    rim_before, rim_after = rim_scr[before], rim_scr[after]
    late_rim = jnp.where(me == ctx_count - 1, rim_after[:RIM], rim_after[RIM:])
    rims = [rim_before[:RIM], late_rim]
    first_place = [me * span, (blocks - 1 - me) * span]
    taps = [filters_ref[0, tap : tap + 1] for tap in range(3)]

    for load in loads:
        load.wait()
    for half in range(2):
        rows = pl.ds(aligned(first_place[half] + 8, 8), span)
        one, two = same_ref[rows], same_two_ref[rows]
        for head in range(heads):
            at = 2 * (head // 2)
            q_scr[half, head, 6:8] = rims[half][at : at + 2, (head % 2) * LANES : (head % 2 + 1) * LANES]

        def convolve_head(head, carry, half=half, one=one, two=two):
            lanes = pl.ds(pl.multiple_of(head * LANES, LANES), LANES)
            target = pl.ds(pl.multiple_of(head * span, 16), span)
            q_scr[half, head, 8:] = q_ref[half, :, lanes].astype(f32)
            total = taps[0] * q_scr[half, head, 8:]
            total = total + one * (taps[1] * q_scr[half, head, 7 : 7 + span])
            total = total + two * (taps[2] * q_scr[half, head, 6 : 6 + span])
            qc_ref[half, target] = total.astype(bf16)
            do_ref[half, target] = d_out_ref[half, :, lanes]
            return carry

        lax.fori_loop(0, heads, convolve_head, 0, unroll=4)


def grads_kernel(ctx_count, direct, lengths_ref, filters_ref, *refs):
    group = ctx_count // 2
    arrays = group - 1 if direct else 1
    same_scr, same_two_scr, q_in_ref, qc_in_ref, do_scr, own_ref, across_ref = refs[:7]
    refs = refs[7:]
    near_in, far_in, refs = refs[:arrays], refs[arrays : 2 * arrays], refs[2 * arrays :]
    dq_ref, dq_tail_ref, own_near_ref, own_far_ref = refs[:4]
    arrays = group - 1 if direct else 1
    first_out, late_out, refs = refs[4 : 4 + arrays], refs[4 + arrays : 5 + arrays], refs[5 + arrays :]
    kv_scr, conv_scr, dkv_scr, q_scr, qc_scr, dq_scr = refs[:6]
    bias_scr, s_scr, dp_scr, terms_scr = refs[6:]
    f32, bf16 = jnp.float32, jnp.bfloat16
    span = own_ref.shape[0] // 2 - TAIL // 2
    heads = q_in_ref.shape[1]
    half_rows = span * ctx_count
    length = 2 * half_rows
    blocks = 2 * ctx_count
    me = lax.axis_index("ctx")
    near_in = Slots((None,) + near_in if direct else near_in, me)
    far_in = Slots((None,) + far_in if direct else far_in, me)
    first_out = Slots((None,) + first_out if direct else first_out, me)
    late_out = Slots((None,) * (group - 1) + late_out if direct else late_out, me)
    scale = LANES**-0.5
    log2_scale = scale * 1.4426950408889634
    starts = doc_starts(lengths_ref)

    def place(index, block):
        for tensor in range(2):
            lanes = slice(tensor * LANES, (tensor + 1) * LANES)
            kv_scr[tensor, pl.ds(aligned(8 + index * span, 8), span)] = block[:, lanes].astype(f32)

    def place_both(message, index):
        place(index, message[:span])
        place(blocks - 1 - index, message[span : 2 * span])

    def place_received(step, carry):
        flip = step + 1
        source = partner(me, flip)
        place_both(near_in[flip], source)
        place_both(far_in[flip], partner(source, group))
        return carry

    zeros = jnp.zeros((8, LANES), f32)
    for tensor in range(2):
        kv_scr[tensor, :8] = zeros
    for block_ref, index in ((own_ref, me), (across_ref, partner(me, group))):
        place_both(block_ref, index)
    loop(group - 1, place_received, 0, 16 if direct else 1)

    def taps(tensor):
        return [filters_ref[tensor, tap : tap + 1] for tap in range(3)]

    def masks(base, ahead):
        one = same_scr[pl.ds(base + 8 + min(ahead, 1), span)]
        return one, same_two_scr[pl.ds(base + 8 + ahead, span)]

    def convolve_kv(index, carry):
        base = index * span
        one, two = masks(base, 0)
        for tensor in range(2):
            zero_tap, one_tap, two_tap = taps(tensor + 1)
            total = zero_tap * kv_scr[tensor, pl.ds(aligned(base + 8, 8), span)]
            total = total + one * (one_tap * kv_scr[tensor, pl.ds(base + 7, span)])
            total = total + two * (two_tap * kv_scr[tensor, pl.ds(base + 6, span)])
            conv_scr[tensor, pl.ds(aligned(base, 16), span)] = total.astype(bf16)
        return carry

    first_place = [me * span, (blocks - 1 - me) * span]
    firsts = []
    for half in range(2):
        lowest = jnp.int32(0)
        for start in starts[1:]:
            lowest = jnp.where(first_place[half] >= start, start, lowest)
        firsts.append(lowest // span)

    def over_needed(body, init):
        carry = lax.fori_loop(firsts[0], me + 1, body, init)
        return lax.fori_loop(jnp.maximum(firsts[1], me + 1), blocks - me, body, carry)

    def clear(index, carry):
        for tensor in range(2):
            rows = pl.ds(pl.multiple_of(index * span, 16), span)
            conv_scr[tensor, rows] = jnp.zeros((span, LANES), bf16)
            dkv_scr[tensor, rows] = jnp.zeros((span, LANES), f32)
        terms_scr[index] = jnp.zeros((span, 2 * LANES), f32)
        return carry

    lax.fori_loop(0, blocks, clear, 0, unroll=2)
    for tensor in range(2):
        dkv_scr[tensor, length:] = zeros
    over_needed(convolve_kv, 0)

    middle = me == ctx_count - 1
    q_scr[...] = q_in_ref[...]
    qc_scr[...] = qc_in_ref[...]
    tails = far_in[group - 1][2 * span :].astype(f32)
    tails = [tails[:RIM], tails[RIM:]]
    for half, crossing in ((0, me == group), (1, me == group - 1)):

        @pl.when(crossing)
        def _(half=half):
            rows = pl.ds(aligned(first_place[half] + 8, 8), TAIL)
            one, two = same_scr[rows], same_two_scr[rows]
            zero_tap, one_tap, two_tap = taps(0)
            for head in range(heads):
                at = 2 * (head // 2)
                q_scr[half, head, 6:8] = tails[half][
                    at : at + 2, (head % 2) * LANES : (head % 2 + 1) * LANES
                ]
                total = zero_tap * q_scr[half, head, 8 : 8 + TAIL]
                total = total + one * (one_tap * q_scr[half, head, 7 : 7 + TAIL])
                total = total + two * (two_tap * q_scr[half, head, 6 : 6 + TAIL])
                qc_scr[half, head * span : head * span + TAIL] = total.astype(bf16)

    def attend(half, window, first_key):
        chunks = 1
        while window // chunks > MAX_CHUNK or window % (16 * chunks):
            chunks += 1
        size = window // chunks
        query = first_place[half] + lax.rem(
            lax.broadcasted_iota(jnp.int32, (1, LANES), 1), jnp.int32(span)
        )
        lowest = jnp.zeros((1, LANES), jnp.int32)
        for start in starts[1:]:
            lowest = jnp.where(query >= start, start, lowest)
        wide = 2 * LANES

        def fill_bias(step, carry):
            places = first_key + step * size + lax.broadcasted_iota(jnp.int32, (size, LANES), 0)
            allowed = (places >= lowest) & (places <= query)
            bias_scr[pl.ds(aligned(step * size, 16), size)] = jnp.where(allowed, 0.0, -1e30)
            return carry

        loop(chunks, fill_bias, 0, 1)
        whole_window = pl.ds(aligned(first_key, 16), window)
        keys_t = conv_scr[0, whole_window].T if chunks == 1 else None
        for at in range(heads * span // wide):
            slot = (half * (heads * span // wide) + at) % s_scr.shape[0]
            cols = slice(at * wide, (at + 1) * wide)
            queries = qc_scr[half, cols]
            grads = do_scr[half, cols]

            def key_rows(step):
                return pl.ds(aligned(first_key + step * size, 16), size)

            def score(step, top):
                keys = conv_scr[0, key_rows(step)]
                scores = lax.dot_general(keys, queries, NT, preferred_element_type=f32)
                bias = bias_scr[pl.ds(aligned(step * size, 16), size)]
                scores = scores + jnp.concatenate([bias, bias], axis=1)
                s_scr[slot, pl.ds(aligned(step * size, 16), size)] = scores
                return jnp.maximum(top, jnp.max(scores, axis=0, keepdims=True))

            top = loop(chunks, score, jnp.full((1, wide), -1e30, f32), 1)

            def weigh(step, carry):
                total, weighted = carry
                rows = pl.ds(aligned(step * size, 16), size)
                weights = jnp.exp2((s_scr[slot, rows] - top) * log2_scale)
                values = conv_scr[1, key_rows(step)]
                prob_grads = lax.dot_general(values, grads, NT, preferred_element_type=f32)
                s_scr[slot, rows] = weights
                dp_scr[slot, rows] = prob_grads
                total = total + jnp.sum(weights, axis=0, keepdims=True)
                weighted = weighted + jnp.sum(weights * prob_grads, axis=0, keepdims=True)
                return total, weighted

            zeros = jnp.zeros((1, wide), f32)
            total, weighted = loop(chunks, weigh, (zeros, zeros), 1)
            inverse = 1.0 / total
            mean = weighted * inverse
            slope = inverse * scale

            def accumulate(step, dq):
                rows = pl.ds(aligned(step * size, 16), size)
                weights = s_scr[slot, rows]
                probs = (weights * inverse).astype(bf16)
                score_grads = (weights * slope * (dp_scr[slot, rows] - mean)).astype(bf16)
                dk = lax.dot_general(score_grads, queries, NN, preferred_element_type=f32)
                dv = lax.dot_general(probs, grads, NN, preferred_element_type=f32)
                target = pl.ds(aligned(first_key + step * size, 16), size)
                for tensor, terms in enumerate((dk, dv)):
                    dkv_scr[tensor, target] += terms
                if keys_t is not None:
                    return lax.dot_general(keys_t, score_grads, NN, preferred_element_type=f32)
                keys = conv_scr[0, key_rows(step)]
                return dq + lax.dot_general(keys, score_grads, TN, preferred_element_type=f32)

            dq = loop(chunks, accumulate, jnp.zeros((LANES, wide), f32), 1)
            dq = dq.T
            for part in range(wide // span):
                head = at * (wide // span) + part
                dq_scr[half, head, :span] = dq[part * span : (part + 1) * span]

    for half in range(2):
        widest = ctx_count + half
        needed = first_place[half] // span - firsts[half] + 1
        below = 0
        for count in [count for count in WINDOWS if direct and count < widest] + [widest]:

            @pl.when((needed > below) & (needed <= count))
            def _(half=half, count=count):
                first_key = jnp.maximum(first_place[half] + span - count * span, 0)
                attend(half, count * span, first_key)

            below = count

    next_rows = jnp.where(middle, dq_scr[1, :, :8], 0.0)
    dq_scr[0, :, span:] = next_rows
    dq_scr[1, :, span:] = jnp.zeros_like(next_rows)
    sums = [jnp.zeros((8, LANES), f32) for _ in range(3)]
    for half in range(2):
        one, two = masks(first_place[half], 0)
        ahead_one = same_scr[pl.ds(first_place[half] + 9, span)]
        ahead_two = same_two_scr[pl.ds(first_place[half] + 10, span)]
        zero_tap, one_tap, two_tap = taps(0)

        def finish_head(head, carry, half=half, one=one, two=two, ahead_one=ahead_one, ahead_two=ahead_two):
            lanes = pl.ds(pl.multiple_of(head * LANES, LANES), LANES)
            grads = dq_scr[half, head, :span]
            out = zero_tap * grads
            out = out + ahead_one * (one_tap * dq_scr[half, head, 1 : 1 + span])
            out = out + ahead_two * (two_tap * dq_scr[half, head, 2 : 2 + span])
            dq_ref[half, :, lanes] = out
            dq_tail_ref[half, :, lanes] = out[span - 8 :]
            return (
                carry[0] + fold_rows(grads * q_scr[half, head, 8:]),
                carry[1] + fold_rows(grads * one * q_scr[half, head, 7 : 7 + span]),
                carry[2] + fold_rows(grads * two * q_scr[half, head, 6 : 6 + span]),
            )

        sums = lax.fori_loop(0, heads, finish_head, tuple(sums), unroll=4)
    q_sums = [jnp.sum(term, axis=0, keepdims=True) for term in sums]

    def finish_block(index, carry):
        base = pl.multiple_of(index * span, 8)
        one, two = masks(base, 0)
        ahead_one = same_scr[pl.ds(base + 9, span)]
        ahead_two = same_two_scr[pl.ds(base + 10, span)]
        carry = list(carry)
        for tensor in range(2):
            zero_tap, one_tap, two_tap = taps(tensor + 1)
            own = dkv_scr[tensor, pl.ds(base, span)]
            out = zero_tap * own
            out = out + ahead_one * (one_tap * dkv_scr[tensor, pl.ds(base + 1, span)])
            out = out + ahead_two * (two_tap * dkv_scr[tensor, pl.ds(base + 2, span)])
            lanes = slice(tensor * LANES, (tensor + 1) * LANES)
            terms_scr[index, :, lanes] = out
            at = 3 * tensor
            carry[at] += fold_rows(own * kv_scr[tensor, pl.ds(base + 8, span)])
            carry[at + 1] += fold_rows(own * one * kv_scr[tensor, pl.ds(base + 7, span)])
            carry[at + 2] += fold_rows(own * two * kv_scr[tensor, pl.ds(base + 6, span)])
        return tuple(carry)

    low = me < group

    kv_sums = over_needed(finish_block, (zeros,) * 6)
    for target, index in ((own_far_ref, partner(me, group)), (own_near_ref, me)):
        target[:span] = terms_scr[index]
        target[span : 2 * span] = terms_scr[blocks - 1 - index]

    def send(step, carry):
        flip = step + 1
        owner = partner(me, flip)
        far_owner = partner(me, flip + group)
        near_late = blocks - 1 - owner
        second = jnp.where(low, blocks - 1 - far_owner, owner)
        third = jnp.where(low & (me > owner), owner, near_late)
        first_out[flip][:span] = terms_scr[far_owner].astype(bf16)
        first_out[flip][span : 2 * span] = terms_scr[second].astype(bf16)
        if splits(direct, flip, group):
            late_out[flip][:span] = terms_scr[third].astype(bf16)
        else:
            first_out[flip][2 * span : 3 * span] = terms_scr[third].astype(bf16)
        return carry

    loop(group - 1, send, 0, 16 if direct else 1)
    kv_sums = [jnp.sum(term, axis=0, keepdims=True) for term in kv_sums]

    padding = [jnp.zeros((2, LANES), f32)]
    left = jnp.concatenate(q_sums + kv_sums[:3] + padding, axis=0)
    right = jnp.concatenate([jnp.zeros((3, LANES), f32)] + kv_sums[3:] + padding, axis=0)
    sums_tile = jnp.concatenate([left, right], axis=1)
    sums_pair = jnp.concatenate(split_bits(sums_tile), axis=0)
    own_far_ref[2 * span :] = joined(sums_pair)
    rims = []
    for half in range(2):
        rows = [dq_scr[half, head, :2] for head in range(heads)]
        rows = [jnp.concatenate(rows[at : at + 2], axis=1) for at in range(0, heads, 2)]
        rims.append(jnp.concatenate(rows, axis=0))

    def rim_for(index):
        return jnp.concatenate(split_bits(jnp.where(index < me, rims[0], rims[1])), axis=0)

    def store_rims(step, carry):
        flip = step + 1
        owner = partner(me, flip)
        after = (2 if splits(direct, flip, group) else 3) * span
        first_out[flip][after : after + 16] = sums_pair
        if not direct or flip == group - 1:
            first_out[flip][after + 16 :] = rim_for(partner(owner, group))
        if not direct or flip & (flip + 1) == 0:
            if splits(direct, flip, group):
                late_out[flip][span:] = rim_for(owner)
            else:
                first_out[flip][after + 16 :] = rim_for(owner)
        return carry

    loop(group - 1, store_rims, 0, 16 if direct else 1)


def merge_kernel(ctx_count, direct, own_near_ref, own_far_ref, *refs):
    received_refs, refs = refs[:-6], refs[-6:]
    near_ref, far_ref, half_sums_ref, rims_ref, sums_scr, rim_scr = refs
    f32, bf16 = jnp.float32, jnp.bfloat16
    group = ctx_count // 2
    me = lax.axis_index("ctx")
    low = me < group
    received = Slots((own_far_ref,) + received_refs if direct else received_refs, me)
    place = lax.rem(me, jnp.int32(group))
    span = own_near_ref.shape[0] // 2
    rows = 2 * span
    sums_scr[place] = own_far_ref[rows:]
    def add(step, carry):
        flip = step + 1
        source = partner(me, flip)
        message = received[flip]
        early, second = [message[at * span : (at + 1) * span].astype(f32) for at in range(2)]
        near_early, near_late, far_early, far_late = carry
        zero = jnp.zeros_like(second)
        after = (2 if splits(direct, flip, group) else 3) * span
        sums_scr[partner(place, flip)] = joined(message[after : after + 16])
        near_early = near_early + jnp.where(low, zero, second)
        if not splits(direct, flip, group):
            third = message[2 * span : 3 * span].astype(f32)
            to_early = low & (source > me)
            near_early = near_early + jnp.where(to_early, third, zero)
            near_late = near_late + jnp.where(to_early, zero, third)
            if flip & (flip + 1) == 0:
                rim_scr[source] = joined(message[after + 16 :])
        return near_early, near_late, far_early + early, far_late + jnp.where(low, second, zero)

    neighbours = [jnp.minimum(me + 1, ctx_count - 1), jnp.maximum(me - 1, 0)]
    for index in neighbours:
        rim_scr[index] = jnp.zeros(rim_scr.shape[1:], f32)
    init = (own_near_ref[:span], own_near_ref[span:], own_far_ref[:span], own_far_ref[span:rows])
    totals = loop(group - 1, add, init, 16 if direct else 1)
    near_ref[:span] = totals[0]
    near_ref[span:] = totals[1]
    far_ref[:span] = totals[2].astype(bf16)
    far_ref[span:rows] = totals[3].astype(bf16)
    for at, index in enumerate(neighbours):
        rims_ref[at] = rim_scr[index]
    sums = loop(group, lambda index, carry: carry + sums_scr[index], jnp.zeros((8, 2 * LANES), f32))
    pair = jnp.concatenate(split_bits(sums), axis=0)
    half_sums_ref[...] = joined(pair)
    far_ref[rows : rows + 16] = pair
    far_ref[rows + 16 :] = received[group - 1][rows + 16 :]


def save_kernel(source_ref, target_hbm, sem):
    copy = pltpu.make_async_copy(source_ref, target_hbm, sem)
    copy.start()
    copy.wait()


def sums_kernel(span, half_sums_ref, far_ref, out_ref):
    sums = half_sums_ref[...] + joined(far_ref[2 * span : 2 * span + 16])
    out_ref[0] = sums[0:3, :LANES]
    out_ref[1] = sums[3:6, :LANES]
    out_ref[2] = sums[3:6, LANES:]


def finish_kernel(
    ctx_count, direct, lengths_ref, filters_ref, dq_in_hbm, tail_ref, near_ref, far_ref, rims_ref, *refs
):
    received_refs, refs = refs[:-8], refs[-8:]
    dq_hbm, dk_hbm, dv_hbm, dq_ref, dk_ref, dv_ref, rim_scr, sems = refs
    f32 = jnp.float32
    group = ctx_count // 2
    span = dk_ref.shape[1]
    me = lax.axis_index("ctx")
    low = me < group
    received = Slots((None,) * (group - 1) + received_refs if direct else received_refs, me)
    starts = doc_starts(lengths_ref)
    blocks = 2 * ctx_count
    neighbours = [jnp.minimum(me + 1, ctx_count - 1), jnp.maximum(me - 1, 0)]
    for at, index in enumerate(neighbours):
        rim_scr[index] = rims_ref[at]

    def add(step, carry):
        flip = step + 1
        source = partner(me, flip)
        message = received[flip]
        terms = message[:span].astype(f32)
        if not direct or flip & (flip + 1) == 0:
            rim_scr[source] = joined(message[span:])
        to_early = low & (source > me)
        zero = jnp.zeros_like(terms)
        return carry[0] + jnp.where(to_early, terms, zero), carry[1] + jnp.where(to_early, zero, terms)

    total = near_ref[...] + far_ref[: 2 * span].astype(f32)
    total = (total[:span], total[span:])
    total = add(group - 2, total) if direct else loop(group - 1, add, total, 1)
    for half in range(2):
        dk_ref[half] = total[half][:, :LANES]
        dv_ref[half] = total[half][:, LANES:]
    stores = [
        pltpu.make_async_copy(dk_ref, dk_hbm, sems.at[0]),
        pltpu.make_async_copy(dv_ref, dv_hbm, sems.at[1]),
        pltpu.make_async_copy(dq_ref, dq_hbm.at[:, pl.ds(span - 8, 8)], sems.at[2]),
    ]
    for store in stores[:2]:
        store.start()

    def same(place):
        cut = place >= blocks * span
        for start in starts:
            cut = cut | (place == start)
        return jnp.where(cut, 0.0, 1.0).astype(f32)

    heads = dq_ref.shape[2] // LANES
    taps = [jnp.concatenate([filters_ref[0, tap : tap + 1]] * heads, axis=1) for tap in range(3)]
    row = lax.broadcasted_iota(jnp.int32, dq_ref.shape[1:], 0)
    far_rim = joined(far_ref[2 * span + 16 :])
    crosses = [me == group - 1, me == group]
    first_place = [me * span, (blocks - 1 - me) * span]
    present = [me < ctx_count - 1, me > 0]
    for half in range(2):
        rim = jnp.where(crosses[half], far_rim, rim_scr[neighbours[half]])
        rows = jnp.concatenate([rim[2 * at : 2 * at + 2] for at in range(rim.shape[0] // 2)], axis=1)
        end = first_place[half] + span
        zero, one, two = same(end - 1), same(end), same(end + 1)
        one = jnp.where(present[half], one, 0.0)
        last_but_one = (zero * one) * (taps[2] * rows[0:1])
        last = one * (taps[1] * rows[0:1]) + (one * two) * (taps[2] * rows[1:2])
        extra = jnp.where(row == 6, last_but_one, jnp.where(row == 7, last, 0.0))
        dq_ref[half] = tail_ref[half] + extra
    stores[2].start()
    for store in stores:
        store.wait()


def shards(q_pre, k_pre, value_before_filter, d_out, filters, doc_lengths):
    f32, bf16 = jnp.float32, jnp.bfloat16
    ctx_count = lax.axis_size("ctx")
    span, width = q_pre.shape[1:]
    length = 2 * span * ctx_count
    rim = 4 * width // (2 * LANES)
    vmem = pl.BlockSpec(memory_space=pltpu.VMEM)
    smem = pl.BlockSpec(memory_space=pltpu.SMEM)
    hbm = pl.BlockSpec(memory_space=pltpu.HBM)

    group = ctx_count // 2
    direct = group <= MAX_DIRECT
    halves = [[half * group + at for at in range(group)] for half in range(2)]
    msg_rows = 2 * span + rim

    def whole(shape):
        return pl.BlockSpec(shape, lambda i: (0,) * len(shape))

    def in_hbm(array):
        return pltpu.with_memory_space_constraint(array, pltpu.HBM)

    def flipped(array, flip):
        return lax.ppermute(array, "ctx", [(i, i ^ flip) for i in range(ctx_count)])

    def gathered(array):
        if direct:
            return [flipped(array, flip) for flip in range(1, group)]
        return [lax.all_gather(array, "ctx", axis_index_groups=halves)]

    def delivered(arrays):
        if direct:
            return [flipped(array, step + 1) for step, array in enumerate(arrays)]
        return [lax.all_to_all(arrays[0], "ctx", 0, 0, axis_index_groups=halves, tiled=True)]

    packed = pl.pallas_call(
        pack_kernel,
        grid=(1,),
        out_shape=jax.ShapeDtypeStruct((msg_rows, 2 * LANES), bf16),
        in_specs=[
            whole(k_pre.shape),
            whole(k_pre.shape),
            pl.BlockSpec((2, TAIL, width), lambda i: (0, span // TAIL - 1, 0)),
        ],
        out_specs=whole((msg_rows, 2 * LANES)),
        compiler_params=pltpu.CompilerParams(vmem_limit_bytes=4 * MIB),
        name="pack",
    )(*[in_hbm(array) for array in (k_pre, value_before_filter, q_pre)])
    across = flipped(packed, group)
    near = gathered(packed)
    far = gathered(across)
    received = [packed, across] + near + far

    window = span * ctx_count + span
    if direct:
        flips = range(1, group)
        first_shapes = []
        for flip in flips:
            rows = (2 if splits(direct, flip, group) else 3) * span + 16
            rows += 16 if flip == group - 1 or flip & (flip + 1) == 0 else 0
            first_shapes.append((rows, 2 * LANES))
        late_shapes = [(span + 16, 2 * LANES)]
    else:
        first_shapes = [(group, 2 * span + 32, 2 * LANES)]
        late_shapes = [(group, span + 16, 2 * LANES)]
    slots = 4 if direct else 1
    heads = width // LANES
    by_head = (2, span * heads, LANES)
    padded = (2, heads, span + 8, LANES)
    prepared = pl.pallas_call(
        functools.partial(prep_kernel, ctx_count, direct),
        out_shape=[
            jax.ShapeDtypeStruct((length + 16, LANES), f32),
            jax.ShapeDtypeStruct((length + 16, LANES), f32),
            jax.ShapeDtypeStruct(padded, f32),
            jax.ShapeDtypeStruct(by_head, bf16),
            jax.ShapeDtypeStruct(by_head, bf16),
        ],
        in_specs=[smem, vmem, hbm, hbm] + [vmem] * (1 + len(near)),
        out_specs=[vmem] * 5,
        scratch_shapes=[
            pltpu.VMEM((ctx_count, rim, 2 * LANES), f32),
            pltpu.VMEM(q_pre.shape, bf16),
            pltpu.VMEM(q_pre.shape, bf16),
            pltpu.SemaphoreType.DMA((2,)),
        ],
        compiler_params=pltpu.CompilerParams(vmem_limit_bytes=(8 if direct else 32) * MIB),
        name="prep",
    )(doc_lengths, filters, in_hbm(q_pre), in_hbm(d_out), packed, *near)
    scratch = [
        pltpu.VMEM((2, length + 16, LANES), f32),
        pltpu.VMEM((2, length, LANES), bf16),
        pltpu.VMEM((2, length + 8, LANES), f32),
        pltpu.VMEM(padded, f32),
        pltpu.VMEM(by_head, bf16),
        pltpu.VMEM(padded, f32),
        pltpu.VMEM((window, LANES), f32),
        pltpu.VMEM((slots, window, 2 * LANES), f32),
        pltpu.VMEM((slots, window, 2 * LANES), f32),
        pltpu.VMEM((2 * ctx_count, span, 2 * LANES), f32),
    ]
    own_shapes = [(2 * span, 2 * LANES), (2 * span + 8, 2 * LANES)]
    d_q_main, d_q_tail, own_near, own_far, *sent = pl.pallas_call(
        functools.partial(grads_kernel, ctx_count, direct),
        out_shape=[jax.ShapeDtypeStruct(q_pre.shape, f32)]
        + [jax.ShapeDtypeStruct(shape, f32) for shape in [(2, 8, width)] + own_shapes]
        + [jax.ShapeDtypeStruct(shape, bf16) for shape in first_shapes + late_shapes],
        in_specs=[smem, vmem] + [vmem] * (len(prepared) + len(received)),
        out_specs=[vmem] * (4 + len(first_shapes + late_shapes)),
        scratch_shapes=scratch,
        compiler_params=pltpu.CompilerParams(vmem_limit_bytes=(20 if direct else 62) * MIB),
        name="grads",
    )(doc_lengths, filters, *prepared, *received)
    d_q_main = pl.pallas_call(
        save_kernel,
        out_shape=jax.ShapeDtypeStruct(q_pre.shape, f32),
        in_specs=[vmem],
        out_specs=hbm,
        scratch_shapes=[pltpu.SemaphoreType.DMA(())],
        compiler_params=pltpu.CompilerParams(vmem_limit_bytes=2 * MIB),
        name="save",
    )(d_q_main)
    half_terms = delivered(sent[: len(first_shapes)])
    merged_shapes = [
        jax.ShapeDtypeStruct((2 * span, 2 * LANES), f32),
        jax.ShapeDtypeStruct((2 * span + 32, 2 * LANES), bf16),
        jax.ShapeDtypeStruct((8, 2 * LANES), f32),
        jax.ShapeDtypeStruct((2, rim // 2, 2 * LANES), f32),
    ]
    near, far, half_sums, rims = pl.pallas_call(
        functools.partial(merge_kernel, ctx_count, direct),
        out_shape=merged_shapes,
        in_specs=[vmem] * (2 + len(half_terms)),
        out_specs=[vmem] * len(merged_shapes),
        scratch_shapes=[
            pltpu.VMEM((group, 8, 2 * LANES), f32),
            pltpu.VMEM((ctx_count, rim // 2, 2 * LANES), f32),
        ],
        compiler_params=pltpu.CompilerParams(vmem_limit_bytes=(4 if direct else 40) * MIB),
        name="merge",
    )(own_near, own_far, *half_terms)
    from_half = flipped(far, group)
    late_terms = sent[len(first_shapes) :]
    late_terms = [flipped(late_terms[0], group - 1)] if direct else delivered(late_terms)

    sums = pl.pallas_call(
        functools.partial(sums_kernel, span),
        out_shape=jax.ShapeDtypeStruct(filters.shape, f32),
        in_specs=[vmem, vmem],
        out_specs=vmem,
        compiler_params=pltpu.CompilerParams(vmem_limit_bytes=2 * MIB),
        name="sums",
    )(half_sums, from_half)
    count = lax.axis_size("tp")
    all_sums = [sums] + [
        lax.ppermute(sums, "tp", [(i, i ^ flip) for i in range(count)]) for flip in range(1, count)
    ]
    d_q_pre, d_k_pre, d_v_pre = pl.pallas_call(
        functools.partial(finish_kernel, ctx_count, direct),
        out_shape=(
            jax.ShapeDtypeStruct(q_pre.shape, f32),
            jax.ShapeDtypeStruct(k_pre.shape, f32),
            jax.ShapeDtypeStruct(k_pre.shape, f32),
        ),
        in_specs=[smem, vmem, hbm] + [vmem] * (4 + len(late_terms)),
        out_specs=(hbm, hbm, hbm),
        scratch_shapes=[
            pltpu.VMEM((2, 8, width), f32),
            pltpu.VMEM(k_pre.shape, f32),
            pltpu.VMEM(k_pre.shape, f32),
            pltpu.VMEM((ctx_count, rim // 2, 2 * LANES), f32),
            pltpu.SemaphoreType.DMA((3,)),
        ],
        input_output_aliases={2: 0},
        compiler_params=pltpu.CompilerParams(vmem_limit_bytes=(4 if direct else 16) * MIB),
        name="finish",
    )(doc_lengths, filters, d_q_main, d_q_tail, near, from_half, rims, *late_terms)
    while len(all_sums) > 1:
        all_sums = [all_sums[at] + all_sums[at + 1] for at in range(0, len(all_sums), 2)]
    return (d_q_pre, d_k_pre, d_v_pre, all_sums[0])


def solution(mesh):
    split = P(None, "ctx", "tp")
    return jax.shard_map(
        shards,
        mesh=mesh,
        in_specs=(split, split, split, split, P(), P()),
        out_specs=(split, split, split, P()),
        check_vma=False,
    )
```

```python
import functools

import jax
import jax.numpy as jnp
import numpy as np
from jax import lax
from jax.experimental import pallas as pl
from jax.experimental.pallas import tpu as pltpu
from jax.sharding import PartitionSpec as P

LANES = 128
NT = (((1,), (1,)), ((), ()))
NN = (((1,), (0,)), ((), ()))
TN = (((0,), (0,)), ((), ()))
TAIL = 16
MAX_CHUNK = 640
RIM = 8
MAX_DIRECT = 4
WINDOWS = (2, 4, 6)
MIB = 1 << 20


def loop(count, body, init, unrolled=16):
    if count <= unrolled:
        for step in range(count):
            init = body(step, init)
        return init
    return lax.fori_loop(0, count, body, init)


def aligned(start, multiple):
    return start if isinstance(start, int) else pl.multiple_of(start, multiple)


def doc_starts(lengths_ref):
    starts = [jnp.int32(0)]
    for index in range(lengths_ref.shape[0] - 1):
        starts.append(starts[-1] + lengths_ref[index])
    return starts


def fold_rows(terms):
    rows, lanes = terms.shape
    return jnp.sum(terms.reshape(rows // 8, 8, lanes), axis=0)


def split_bits(values):
    high = values.astype(jnp.bfloat16)
    low = (values - high.astype(jnp.float32)).astype(jnp.bfloat16)
    return high, low


def joined(pair):
    rows = pair.shape[0] // 2
    pair = pair.astype(jnp.float32)
    return pair[:rows] + pair[rows:]


class Slots:
    def __init__(self, refs, me):
        self.refs, self.me = refs, me

    def __getitem__(self, flip):
        if len(self.refs) == 1:
            place = lax.rem(self.me, jnp.int32(self.refs[0].shape[0]))
            return self.refs[0].at[partner(place, flip)]
        return self.refs[flip]


def splits(direct, flip, group):
    return not direct or flip == group - 1


def partner(me, flip):
    return lax.bitwise_xor(me, jnp.int32(flip))


def pack_kernel(k_ref, v_ref, q_ref, out_ref):
    span = k_ref.shape[1]
    kv = jnp.concatenate([k_ref[...], v_ref[...]], axis=2).reshape(2 * span, 2 * LANES)
    tails = []
    for half in range(2):
        last = q_ref[half].astype(jnp.float32)[TAIL - 2 :]
        tails += [last[:, at : at + 2 * LANES] for at in range(0, last.shape[1], 2 * LANES)]
    out_ref[: 2 * span] = kv
    out_ref[2 * span :] = jnp.concatenate(tails, axis=0).astype(jnp.bfloat16)


def prep_kernel(ctx_count, direct, lengths_ref, filters_ref, q_hbm, d_out_hbm, own_ref, *refs):
    near_refs, refs = refs[:-9], refs[-9:]
    same_ref, same_two_ref, q_scr, qc_ref, do_ref, rim_scr, q_ref, d_out_ref, sems = refs
    f32, bf16 = jnp.float32, jnp.bfloat16
    loads = [
        pltpu.make_async_copy(q_hbm, q_ref, sems.at[0]),
        pltpu.make_async_copy(d_out_hbm, d_out_ref, sems.at[1]),
    ]
    for load in loads:
        load.start()
    group = ctx_count // 2
    span = q_ref.shape[1]
    heads = q_ref.shape[2] // LANES
    blocks = 2 * ctx_count
    length = span * blocks
    me = lax.axis_index("ctx")
    near = Slots((None,) + near_refs if direct else near_refs, me)
    starts = doc_starts(lengths_ref)

    def fill(index, carry):
        rows = pl.ds(aligned(8 + index * span, 8), span)
        same_ref[rows] = jnp.ones((span, LANES), f32)
        same_two_ref[rows] = jnp.ones((span, LANES), f32)
        return carry

    lax.fori_loop(0, blocks, fill, 0, unroll=2)
    zeros = jnp.zeros((8, LANES), f32)
    for rows in (slice(0, 8), slice(8 + length, 16 + length)):
        same_ref[rows] = zeros
        same_two_ref[rows] = zeros
    for start in starts:
        same_ref[pl.ds(8 + start, 1)] = zeros[:1]
        same_two_ref[pl.ds(8 + start, 1)] = zeros[:1]
        same_two_ref[pl.ds(9 + start, 1)] = zeros[:1]

    before, after = jnp.maximum(me - 1, 0), jnp.minimum(me + 1, ctx_count - 1)
    for index in (before, after):
        rim_scr[index] = jnp.zeros(rim_scr.shape[1:], f32)
    rim_scr[me] = own_ref[2 * span :].astype(f32)

    def place_rims(step, carry):
        flip = step + 1
        if not direct or flip & (flip + 1) == 0:
            rim_scr[partner(me, flip)] = near[flip][2 * span :].astype(f32)
        return carry

    loop(group - 1, place_rims, 0, 16 if direct else 1)
    rim_before, rim_after = rim_scr[before], rim_scr[after]
    late_rim = jnp.where(me == ctx_count - 1, rim_after[:RIM], rim_after[RIM:])
    rims = [rim_before[:RIM], late_rim]
    first_place = [me * span, (blocks - 1 - me) * span]
    taps = [filters_ref[0, tap : tap + 1] for tap in range(3)]

    for load in loads:
        load.wait()
    for half in range(2):
        rows = pl.ds(aligned(first_place[half] + 8, 8), span)
        one, two = same_ref[rows], same_two_ref[rows]
        for head in range(heads):
            at = 2 * (head // 2)
            q_scr[half, head, 6:8] = rims[half][at : at + 2, (head % 2) * LANES : (head % 2 + 1) * LANES]

        def convolve_head(head, carry, half=half, one=one, two=two):
            lanes = pl.ds(pl.multiple_of(head * LANES, LANES), LANES)
            target = pl.ds(pl.multiple_of(head * span, 16), span)
            q_scr[half, head, 8:] = q_ref[half, :, lanes].astype(f32)
            total = taps[0] * q_scr[half, head, 8:]
            total = total + one * (taps[1] * q_scr[half, head, 7 : 7 + span])
            total = total + two * (taps[2] * q_scr[half, head, 6 : 6 + span])
            qc_ref[half, target] = total.astype(bf16)
            do_ref[half, target] = d_out_ref[half, :, lanes]
            return carry

        lax.fori_loop(0, heads, convolve_head, 0, unroll=4)


def grads_kernel(ctx_count, direct, lengths_ref, filters_ref, *refs):
    group = ctx_count // 2
    arrays = group - 1 if direct else 1
    same_scr, same_two_scr, q_in_ref, qc_in_ref, do_scr, own_ref, across_ref = refs[:7]
    refs = refs[7:]
    near_in, far_in, refs = refs[:arrays], refs[arrays : 2 * arrays], refs[2 * arrays :]
    dq_ref, dq_tail_ref, own_near_ref, own_far_ref = refs[:4]
    arrays = group - 1 if direct else 1
    first_out, late_out, refs = refs[4 : 4 + arrays], refs[4 + arrays : 5 + arrays], refs[5 + arrays :]
    kv_scr, conv_scr, dkv_scr, q_scr, qc_scr, dq_scr = refs[:6]
    bias_scr, s_scr, dp_scr, terms_scr, p_scr, ds_scr = refs[6:]
    f32, bf16 = jnp.float32, jnp.bfloat16
    span = own_ref.shape[0] // 2 - TAIL // 2
    heads = q_in_ref.shape[1]
    half_rows = span * ctx_count
    length = 2 * half_rows
    blocks = 2 * ctx_count
    me = lax.axis_index("ctx")
    near_in = Slots((None,) + near_in if direct else near_in, me)
    far_in = Slots((None,) + far_in if direct else far_in, me)
    first_out = Slots((None,) + first_out if direct else first_out, me)
    late_out = Slots((None,) * (group - 1) + late_out if direct else late_out, me)
    scale = LANES**-0.5
    log2_scale = scale * 1.4426950408889634
    starts = doc_starts(lengths_ref)

    def place(index, block):
        for tensor in range(2):
            lanes = slice(tensor * LANES, (tensor + 1) * LANES)
            kv_scr[tensor, pl.ds(aligned(8 + index * span, 8), span)] = block[:, lanes].astype(f32)

    def place_both(message, index):
        place(index, message[:span])
        place(blocks - 1 - index, message[span : 2 * span])

    def place_received(step, carry):
        flip = step + 1
        source = partner(me, flip)
        place_both(near_in[flip], source)
        place_both(far_in[flip], partner(source, group))
        return carry

    zeros = jnp.zeros((8, LANES), f32)
    for tensor in range(2):
        kv_scr[tensor, :8] = zeros
    for block_ref, index in ((own_ref, me), (across_ref, partner(me, group))):
        place_both(block_ref, index)
    loop(group - 1, place_received, 0, 16 if direct else 1)

    def taps(tensor):
        return [filters_ref[tensor, tap : tap + 1] for tap in range(3)]

    def masks(base, ahead):
        one = same_scr[pl.ds(base + 8 + min(ahead, 1), span)]
        return one, same_two_scr[pl.ds(base + 8 + ahead, span)]

    def convolve_kv(index, carry):
        base = index * span
        one, two = masks(base, 0)
        for tensor in range(2):
            zero_tap, one_tap, two_tap = taps(tensor + 1)
            total = zero_tap * kv_scr[tensor, pl.ds(aligned(base + 8, 8), span)]
            total = total + one * (one_tap * kv_scr[tensor, pl.ds(base + 7, span)])
            total = total + two * (two_tap * kv_scr[tensor, pl.ds(base + 6, span)])
            conv_scr[tensor, pl.ds(aligned(base, 16), span)] = total.astype(bf16)
        return carry

    first_place = [me * span, (blocks - 1 - me) * span]
    firsts = []
    for half in range(2):
        lowest = jnp.int32(0)
        for start in starts[1:]:
            lowest = jnp.where(first_place[half] >= start, start, lowest)
        firsts.append(lowest // span)

    def over_needed(body, init):
        carry = lax.fori_loop(firsts[0], me + 1, body, init)
        return lax.fori_loop(jnp.maximum(firsts[1], me + 1), blocks - me, body, carry)

    def clear(index, carry):
        for tensor in range(2):
            rows = pl.ds(pl.multiple_of(index * span, 16), span)
            conv_scr[tensor, rows] = jnp.zeros((span, LANES), bf16)
            dkv_scr[tensor, rows] = jnp.zeros((span, LANES), f32)
        terms_scr[index] = jnp.zeros((span, 2 * LANES), f32)
        return carry

    lax.fori_loop(0, blocks, clear, 0, unroll=2)
    for tensor in range(2):
        dkv_scr[tensor, length:] = zeros
    over_needed(convolve_kv, 0)

    middle = me == ctx_count - 1
    q_scr[...] = q_in_ref[...]
    qc_scr[...] = qc_in_ref[...]
    tails = far_in[group - 1][2 * span :].astype(f32)
    tails = [tails[:RIM], tails[RIM:]]
    for half, crossing in ((0, me == group), (1, me == group - 1)):

        @pl.when(crossing)
        def _(half=half):
            rows = pl.ds(aligned(first_place[half] + 8, 8), TAIL)
            one, two = same_scr[rows], same_two_scr[rows]
            zero_tap, one_tap, two_tap = taps(0)
            for head in range(heads):
                at = 2 * (head // 2)
                q_scr[half, head, 6:8] = tails[half][
                    at : at + 2, (head % 2) * LANES : (head % 2 + 1) * LANES
                ]
                total = zero_tap * q_scr[half, head, 8 : 8 + TAIL]
                total = total + one * (one_tap * q_scr[half, head, 7 : 7 + TAIL])
                total = total + two * (two_tap * q_scr[half, head, 6 : 6 + TAIL])
                qc_scr[half, head * span : head * span + TAIL] = total.astype(bf16)

    wide = 2 * LANES
    parts = heads * span // wide

    def reach(half):
        lane = lax.broadcasted_iota(jnp.int32, (1, LANES), 1)
        query = first_place[half] + lax.rem(lane, jnp.int32(span))
        lowest = jnp.zeros((1, LANES), jnp.int32)
        for start in starts[1:]:
            lowest = jnp.where(query >= start, start, lowest)
        return query, lowest

    def attend_at_once(window):
        units = [(half, at) for half in range(2) for at in range(parts)]
        keys_rows, tops, scaled = [], [], []
        for half in range(2):
            first_key = pl.multiple_of(jnp.maximum(first_place[half] + span - window, 0), 16)
            keys_rows.append(pl.ds(first_key, window))
            query, lowest = reach(half)
            places = first_key + lax.broadcasted_iota(jnp.int32, (window, LANES), 0)
            allowed = (places >= lowest) & (places <= query)
            bias_scr[half, :window] = jnp.where(allowed, 0.0, -1e30)
        for slot, (half, at) in enumerate(units):
            queries = qc_scr[half, at * wide : (at + 1) * wide]
            scores = lax.dot_general(
                conv_scr[0, keys_rows[half]], queries, NT, preferred_element_type=f32
            )
            bias = bias_scr[half, :window]
            scores = scores + jnp.concatenate([bias, bias], axis=1)
            s_scr[slot, :window] = scores
            tops.append(jnp.max(scores, axis=0, keepdims=True))
        for slot, (half, at) in enumerate(units):
            grads = do_scr[half, at * wide : (at + 1) * wide]
            prob_grads = lax.dot_general(
                conv_scr[1, keys_rows[half]], grads, NT, preferred_element_type=f32
            )
            weights = jnp.exp2((s_scr[slot, :window] - tops[slot]) * log2_scale)
            s_scr[slot, :window] = weights
            dp_scr[slot, :window] = prob_grads
            total = jnp.sum(weights, axis=0, keepdims=True)
            weighted = jnp.sum(weights * prob_grads, axis=0, keepdims=True)
            inverse = 1.0 / total
            scaled.append((inverse, weighted * inverse, inverse * scale))
        for slot, (half, at) in enumerate(units):
            inverse, mean, slope = scaled[slot]
            weights = s_scr[slot, :window]
            cols = slice(at * wide, (at + 1) * wide)
            p_scr[half, :window, cols] = (weights * inverse).astype(bf16)
            ds_scr[half, :window, cols] = (weights * slope * (dp_scr[slot, :window] - mean)).astype(bf16)
        for half in range(2):
            score_grads = ds_scr[half, :window]
            keys_t = conv_scr[0, keys_rows[half]].T
            dq = lax.dot_general(keys_t, score_grads, NN, preferred_element_type=f32).T
            for head in range(heads):
                dq_scr[half, head, :span] = dq[head * span : (head + 1) * span]
            dkv_scr[0, keys_rows[half]] += lax.dot_general(
                score_grads, qc_scr[half], NN, preferred_element_type=f32
            )
            dkv_scr[1, keys_rows[half]] += lax.dot_general(
                p_scr[half, :window], do_scr[half], NN, preferred_element_type=f32
            )

    def attend(half, window, first_key):
        chunks = 1
        while window // chunks > MAX_CHUNK or window % (16 * chunks):
            chunks += 1
        size = window // chunks
        query, lowest = reach(half)

        def fill_bias(step, carry):
            places = first_key + step * size + lax.broadcasted_iota(jnp.int32, (size, LANES), 0)
            allowed = (places >= lowest) & (places <= query)
            bias_scr[0, pl.ds(aligned(step * size, 16), size)] = jnp.where(allowed, 0.0, -1e30)
            return carry

        loop(chunks, fill_bias, 0, 1)
        whole_window = pl.ds(aligned(first_key, 16), window)
        keys_t = conv_scr[0, whole_window].T if chunks == 1 else None
        for at in range(parts):
            slot = 0
            cols = slice(at * wide, (at + 1) * wide)
            queries = qc_scr[half, cols]
            grads = do_scr[half, cols]

            def key_rows(step):
                return pl.ds(aligned(first_key + step * size, 16), size)

            def score(step, top):
                keys = conv_scr[0, key_rows(step)]
                scores = lax.dot_general(keys, queries, NT, preferred_element_type=f32)
                bias = bias_scr[0, pl.ds(aligned(step * size, 16), size)]
                scores = scores + jnp.concatenate([bias, bias], axis=1)
                s_scr[slot, pl.ds(aligned(step * size, 16), size)] = scores
                return jnp.maximum(top, jnp.max(scores, axis=0, keepdims=True))

            top = loop(chunks, score, jnp.full((1, wide), -1e30, f32), 1)

            def weigh(step, carry):
                total, weighted = carry
                rows = pl.ds(aligned(step * size, 16), size)
                weights = jnp.exp2((s_scr[slot, rows] - top) * log2_scale)
                values = conv_scr[1, key_rows(step)]
                prob_grads = lax.dot_general(values, grads, NT, preferred_element_type=f32)
                s_scr[slot, rows] = weights
                dp_scr[slot, rows] = prob_grads
                total = total + jnp.sum(weights, axis=0, keepdims=True)
                weighted = weighted + jnp.sum(weights * prob_grads, axis=0, keepdims=True)
                return total, weighted

            zeros = jnp.zeros((1, wide), f32)
            total, weighted = loop(chunks, weigh, (zeros, zeros), 1)
            inverse = 1.0 / total
            mean = weighted * inverse
            slope = inverse * scale

            def accumulate(step, dq):
                rows = pl.ds(aligned(step * size, 16), size)
                weights = s_scr[slot, rows]
                probs = (weights * inverse).astype(bf16)
                score_grads = (weights * slope * (dp_scr[slot, rows] - mean)).astype(bf16)
                dk = lax.dot_general(score_grads, queries, NN, preferred_element_type=f32)
                dv = lax.dot_general(probs, grads, NN, preferred_element_type=f32)
                target = pl.ds(aligned(first_key + step * size, 16), size)
                for tensor, terms in enumerate((dk, dv)):
                    dkv_scr[tensor, target] += terms
                if keys_t is not None:
                    return lax.dot_general(keys_t, score_grads, NN, preferred_element_type=f32)
                keys = conv_scr[0, key_rows(step)]
                return dq + lax.dot_general(keys, score_grads, TN, preferred_element_type=f32)

            dq = loop(chunks, accumulate, jnp.zeros((LANES, wide), f32), 1)
            dq = dq.T
            for part in range(wide // span):
                head = at * (wide // span) + part
                dq_scr[half, head, :span] = dq[part * span : (part + 1) * span]

    needed = [first_place[half] // span - firsts[half] + 1 for half in range(2)]
    if direct:
        below, both = 0, jnp.maximum(needed[0], needed[1])
        for count in [count for count in WINDOWS if count <= ctx_count] + [ctx_count + 1]:

            @pl.when((both > below) & (both <= count))
            def _(count=count):
                attend_at_once(count * span)

            below = count
    else:
        for half in range(2):
            attend(half, half_rows + half * span, half * (ctx_count - 1 - me) * span)

    next_rows = jnp.where(middle, dq_scr[1, :, :8], 0.0)
    dq_scr[0, :, span:] = next_rows
    dq_scr[1, :, span:] = jnp.zeros_like(next_rows)
    sums = [jnp.zeros((8, LANES), f32) for _ in range(3)]
    for half in range(2):
        one, two = masks(first_place[half], 0)
        ahead_one = same_scr[pl.ds(first_place[half] + 9, span)]
        ahead_two = same_two_scr[pl.ds(first_place[half] + 10, span)]
        zero_tap, one_tap, two_tap = taps(0)

        def finish_head(head, carry, half=half, one=one, two=two, ahead_one=ahead_one, ahead_two=ahead_two):
            lanes = pl.ds(pl.multiple_of(head * LANES, LANES), LANES)
            grads = dq_scr[half, head, :span]
            out = zero_tap * grads
            out = out + ahead_one * (one_tap * dq_scr[half, head, 1 : 1 + span])
            out = out + ahead_two * (two_tap * dq_scr[half, head, 2 : 2 + span])
            dq_ref[half, :, lanes] = out
            dq_tail_ref[half, :, lanes] = out[span - 8 :]
            return (
                carry[0] + fold_rows(grads * q_scr[half, head, 8:]),
                carry[1] + fold_rows(grads * one * q_scr[half, head, 7 : 7 + span]),
                carry[2] + fold_rows(grads * two * q_scr[half, head, 6 : 6 + span]),
            )

        sums = lax.fori_loop(0, heads, finish_head, tuple(sums), unroll=4)
    q_sums = [jnp.sum(term, axis=0, keepdims=True) for term in sums]

    def finish_block(index, carry):
        base = pl.multiple_of(index * span, 8)
        one, two = masks(base, 0)
        ahead_one = same_scr[pl.ds(base + 9, span)]
        ahead_two = same_two_scr[pl.ds(base + 10, span)]
        carry = list(carry)
        for tensor in range(2):
            zero_tap, one_tap, two_tap = taps(tensor + 1)
            own = dkv_scr[tensor, pl.ds(base, span)]
            out = zero_tap * own
            out = out + ahead_one * (one_tap * dkv_scr[tensor, pl.ds(base + 1, span)])
            out = out + ahead_two * (two_tap * dkv_scr[tensor, pl.ds(base + 2, span)])
            lanes = slice(tensor * LANES, (tensor + 1) * LANES)
            terms_scr[index, :, lanes] = out
            at = 3 * tensor
            carry[at] += fold_rows(own * kv_scr[tensor, pl.ds(base + 8, span)])
            carry[at + 1] += fold_rows(own * one * kv_scr[tensor, pl.ds(base + 7, span)])
            carry[at + 2] += fold_rows(own * two * kv_scr[tensor, pl.ds(base + 6, span)])
        return tuple(carry)

    low = me < group

    kv_sums = over_needed(finish_block, (zeros,) * 6)
    for target, index in ((own_far_ref, partner(me, group)), (own_near_ref, me)):
        target[:span] = terms_scr[index]
        target[span : 2 * span] = terms_scr[blocks - 1 - index]

    def send(step, carry):
        flip = step + 1
        owner = partner(me, flip)
        far_owner = partner(me, flip + group)
        near_late = blocks - 1 - owner
        second = jnp.where(low, blocks - 1 - far_owner, owner)
        third = jnp.where(low & (me > owner), owner, near_late)
        first_out[flip][:span] = terms_scr[far_owner].astype(bf16)
        first_out[flip][span : 2 * span] = terms_scr[second].astype(bf16)
        if splits(direct, flip, group):
            late_out[flip][:span] = terms_scr[third].astype(bf16)
        else:
            first_out[flip][2 * span : 3 * span] = terms_scr[third].astype(bf16)
        return carry

    loop(group - 1, send, 0, 16 if direct else 1)
    kv_sums = [jnp.sum(term, axis=0, keepdims=True) for term in kv_sums]

    padding = [jnp.zeros((2, LANES), f32)]
    left = jnp.concatenate(q_sums + kv_sums[:3] + padding, axis=0)
    right = jnp.concatenate([jnp.zeros((3, LANES), f32)] + kv_sums[3:] + padding, axis=0)
    sums_tile = jnp.concatenate([left, right], axis=1)
    sums_pair = jnp.concatenate(split_bits(sums_tile), axis=0)
    own_far_ref[2 * span :] = joined(sums_pair)
    rims = []
    for half in range(2):
        rows = [dq_scr[half, head, :2] for head in range(heads)]
        rows = [jnp.concatenate(rows[at : at + 2], axis=1) for at in range(0, heads, 2)]
        rims.append(jnp.concatenate(rows, axis=0))

    def rim_for(index):
        return jnp.concatenate(split_bits(jnp.where(index < me, rims[0], rims[1])), axis=0)

    def store_rims(step, carry):
        flip = step + 1
        owner = partner(me, flip)
        after = (2 if splits(direct, flip, group) else 3) * span
        first_out[flip][after : after + 16] = sums_pair
        if not direct or flip == group - 1:
            first_out[flip][after + 16 :] = rim_for(partner(owner, group))
        if not direct or flip & (flip + 1) == 0:
            if splits(direct, flip, group):
                late_out[flip][span:] = rim_for(owner)
            else:
                first_out[flip][after + 16 :] = rim_for(owner)
        return carry

    loop(group - 1, store_rims, 0, 16 if direct else 1)


def merge_kernel(ctx_count, direct, own_near_ref, own_far_ref, *refs):
    received_refs, refs = refs[:-6], refs[-6:]
    near_ref, far_ref, half_sums_ref, rims_ref, sums_scr, rim_scr = refs
    f32, bf16 = jnp.float32, jnp.bfloat16
    group = ctx_count // 2
    me = lax.axis_index("ctx")
    low = me < group
    received = Slots((own_far_ref,) + received_refs if direct else received_refs, me)
    place = lax.rem(me, jnp.int32(group))
    span = own_near_ref.shape[0] // 2
    rows = 2 * span
    sums_scr[place] = own_far_ref[rows:]
    def add(step, carry):
        flip = step + 1
        source = partner(me, flip)
        message = received[flip]
        early, second = [message[at * span : (at + 1) * span].astype(f32) for at in range(2)]
        near_early, near_late, far_early, far_late = carry
        zero = jnp.zeros_like(second)
        after = (2 if splits(direct, flip, group) else 3) * span
        sums_scr[partner(place, flip)] = joined(message[after : after + 16])
        near_early = near_early + jnp.where(low, zero, second)
        if not splits(direct, flip, group):
            third = message[2 * span : 3 * span].astype(f32)
            to_early = low & (source > me)
            near_early = near_early + jnp.where(to_early, third, zero)
            near_late = near_late + jnp.where(to_early, zero, third)
            if flip & (flip + 1) == 0:
                rim_scr[source] = joined(message[after + 16 :])
        return near_early, near_late, far_early + early, far_late + jnp.where(low, second, zero)

    neighbours = [jnp.minimum(me + 1, ctx_count - 1), jnp.maximum(me - 1, 0)]
    for index in neighbours:
        rim_scr[index] = jnp.zeros(rim_scr.shape[1:], f32)
    init = (own_near_ref[:span], own_near_ref[span:], own_far_ref[:span], own_far_ref[span:rows])
    totals = loop(group - 1, add, init, 16 if direct else 1)
    near_ref[:span] = totals[0]
    near_ref[span:] = totals[1]
    far_ref[:span] = totals[2].astype(bf16)
    far_ref[span:rows] = totals[3].astype(bf16)
    for at, index in enumerate(neighbours):
        rims_ref[at] = rim_scr[index]
    sums = loop(group, lambda index, carry: carry + sums_scr[index], jnp.zeros((8, 2 * LANES), f32))
    pair = jnp.concatenate(split_bits(sums), axis=0)
    half_sums_ref[...] = joined(pair)
    far_ref[rows : rows + 16] = pair
    far_ref[rows + 16 :] = received[group - 1][rows + 16 :]


def save_kernel(source_ref, target_hbm, sem):
    copy = pltpu.make_async_copy(source_ref, target_hbm, sem)
    copy.start()
    copy.wait()


def sums_kernel(span, half_sums_ref, far_ref, out_ref):
    sums = half_sums_ref[...] + joined(far_ref[2 * span : 2 * span + 16])
    out_ref[0] = sums[0:3, :LANES]
    out_ref[1] = sums[3:6, :LANES]
    out_ref[2] = sums[3:6, LANES:]


def finish_kernel(
    ctx_count, direct, lengths_ref, filters_ref, dq_in_hbm, tail_ref, near_ref, far_ref, rims_ref, *refs
):
    received_refs, refs = refs[:-8], refs[-8:]
    dq_hbm, dk_hbm, dv_hbm, dq_ref, dk_ref, dv_ref, rim_scr, sems = refs
    f32 = jnp.float32
    group = ctx_count // 2
    span = dk_ref.shape[1]
    me = lax.axis_index("ctx")
    low = me < group
    received = Slots((None,) * (group - 1) + received_refs if direct else received_refs, me)
    starts = doc_starts(lengths_ref)
    blocks = 2 * ctx_count
    neighbours = [jnp.minimum(me + 1, ctx_count - 1), jnp.maximum(me - 1, 0)]
    for at, index in enumerate(neighbours):
        rim_scr[index] = rims_ref[at]

    def add(step, carry):
        flip = step + 1
        source = partner(me, flip)
        message = received[flip]
        terms = message[:span].astype(f32)
        if not direct or flip & (flip + 1) == 0:
            rim_scr[source] = joined(message[span:])
        to_early = low & (source > me)
        zero = jnp.zeros_like(terms)
        return carry[0] + jnp.where(to_early, terms, zero), carry[1] + jnp.where(to_early, zero, terms)

    total = near_ref[...] + far_ref[: 2 * span].astype(f32)
    total = (total[:span], total[span:])
    total = add(group - 2, total) if direct else loop(group - 1, add, total, 1)
    for half in range(2):
        dk_ref[half] = total[half][:, :LANES]
        dv_ref[half] = total[half][:, LANES:]
    stores = [
        pltpu.make_async_copy(dk_ref, dk_hbm, sems.at[0]),
        pltpu.make_async_copy(dv_ref, dv_hbm, sems.at[1]),
        pltpu.make_async_copy(dq_ref, dq_hbm.at[:, pl.ds(span - 8, 8)], sems.at[2]),
    ]
    for store in stores[:2]:
        store.start()

    def same(place):
        cut = place >= blocks * span
        for start in starts:
            cut = cut | (place == start)
        return jnp.where(cut, 0.0, 1.0).astype(f32)

    heads = dq_ref.shape[2] // LANES
    taps = [jnp.concatenate([filters_ref[0, tap : tap + 1]] * heads, axis=1) for tap in range(3)]
    row = lax.broadcasted_iota(jnp.int32, dq_ref.shape[1:], 0)
    far_rim = joined(far_ref[2 * span + 16 :])
    crosses = [me == group - 1, me == group]
    first_place = [me * span, (blocks - 1 - me) * span]
    present = [me < ctx_count - 1, me > 0]
    for half in range(2):
        rim = jnp.where(crosses[half], far_rim, rim_scr[neighbours[half]])
        rows = jnp.concatenate([rim[2 * at : 2 * at + 2] for at in range(rim.shape[0] // 2)], axis=1)
        end = first_place[half] + span
        zero, one, two = same(end - 1), same(end), same(end + 1)
        one = jnp.where(present[half], one, 0.0)
        last_but_one = (zero * one) * (taps[2] * rows[0:1])
        last = one * (taps[1] * rows[0:1]) + (one * two) * (taps[2] * rows[1:2])
        extra = jnp.where(row == 6, last_but_one, jnp.where(row == 7, last, 0.0))
        dq_ref[half] = tail_ref[half] + extra
    stores[2].start()
    for store in stores:
        store.wait()


def shards(q_pre, k_pre, value_before_filter, d_out, filters, doc_lengths):
    f32, bf16 = jnp.float32, jnp.bfloat16
    ctx_count = lax.axis_size("ctx")
    span, width = q_pre.shape[1:]
    length = 2 * span * ctx_count
    rim = 4 * width // (2 * LANES)
    vmem = pl.BlockSpec(memory_space=pltpu.VMEM)
    smem = pl.BlockSpec(memory_space=pltpu.SMEM)
    hbm = pl.BlockSpec(memory_space=pltpu.HBM)

    group = ctx_count // 2
    direct = group <= MAX_DIRECT
    halves = [[half * group + at for at in range(group)] for half in range(2)]
    msg_rows = 2 * span + rim

    def whole(shape):
        return pl.BlockSpec(shape, lambda i: (0,) * len(shape))

    def in_hbm(array):
        return pltpu.with_memory_space_constraint(array, pltpu.HBM)

    def flipped(array, flip):
        return lax.ppermute(array, "ctx", [(i, i ^ flip) for i in range(ctx_count)])

    def gathered(array):
        if direct:
            return [flipped(array, flip) for flip in range(1, group)]
        return [lax.all_gather(array, "ctx", axis_index_groups=halves)]

    def delivered(arrays):
        if direct:
            return [flipped(array, step + 1) for step, array in enumerate(arrays)]
        return [lax.all_to_all(arrays[0], "ctx", 0, 0, axis_index_groups=halves, tiled=True)]

    packed = pl.pallas_call(
        pack_kernel,
        grid=(1,),
        out_shape=jax.ShapeDtypeStruct((msg_rows, 2 * LANES), bf16),
        in_specs=[
            whole(k_pre.shape),
            whole(k_pre.shape),
            pl.BlockSpec((2, TAIL, width), lambda i: (0, span // TAIL - 1, 0)),
        ],
        out_specs=whole((msg_rows, 2 * LANES)),
        compiler_params=pltpu.CompilerParams(vmem_limit_bytes=4 * MIB),
        name="pack",
    )(*[in_hbm(array) for array in (k_pre, value_before_filter, q_pre)])
    across = flipped(packed, group)
    near = gathered(packed)
    far = gathered(across)
    received = [packed, across] + near + far

    window = span * ctx_count + span
    if direct:
        flips = range(1, group)
        first_shapes = []
        for flip in flips:
            rows = (2 if splits(direct, flip, group) else 3) * span + 16
            rows += 16 if flip == group - 1 or flip & (flip + 1) == 0 else 0
            first_shapes.append((rows, 2 * LANES))
        late_shapes = [(span + 16, 2 * LANES)]
    else:
        first_shapes = [(group, 2 * span + 32, 2 * LANES)]
        late_shapes = [(group, span + 16, 2 * LANES)]
    slots = 4 if direct else 1
    heads = width // LANES
    by_head = (2, span * heads, LANES)
    padded = (2, heads, span + 8, LANES)
    prepared = pl.pallas_call(
        functools.partial(prep_kernel, ctx_count, direct),
        out_shape=[
            jax.ShapeDtypeStruct((length + 16, LANES), f32),
            jax.ShapeDtypeStruct((length + 16, LANES), f32),
            jax.ShapeDtypeStruct(padded, f32),
            jax.ShapeDtypeStruct(by_head, bf16),
            jax.ShapeDtypeStruct(by_head, bf16),
        ],
        in_specs=[smem, vmem, hbm, hbm] + [vmem] * (1 + len(near)),
        out_specs=[vmem] * 5,
        scratch_shapes=[
            pltpu.VMEM((ctx_count, rim, 2 * LANES), f32),
            pltpu.VMEM(q_pre.shape, bf16),
            pltpu.VMEM(q_pre.shape, bf16),
            pltpu.SemaphoreType.DMA((2,)),
        ],
        compiler_params=pltpu.CompilerParams(vmem_limit_bytes=(8 if direct else 32) * MIB),
        name="prep",
    )(doc_lengths, filters, in_hbm(q_pre), in_hbm(d_out), packed, *near)
    scratch = [
        pltpu.VMEM((2, length + 16, LANES), f32),
        pltpu.VMEM((2, length, LANES), bf16),
        pltpu.VMEM((2, length + 8, LANES), f32),
        pltpu.VMEM(padded, f32),
        pltpu.VMEM(by_head, bf16),
        pltpu.VMEM(padded, f32),
        pltpu.VMEM((2, window, LANES), f32),
        pltpu.VMEM((slots, window, 2 * LANES), f32),
        pltpu.VMEM((slots, window, 2 * LANES), f32),
        pltpu.VMEM((2 * ctx_count, span, 2 * LANES), f32),
        pltpu.VMEM((2, window, heads * span) if direct else (2, 16, LANES), bf16),
        pltpu.VMEM((2, window, heads * span) if direct else (2, 16, LANES), bf16),
    ]
    own_shapes = [(2 * span, 2 * LANES), (2 * span + 8, 2 * LANES)]
    d_q_main, d_q_tail, own_near, own_far, *sent = pl.pallas_call(
        functools.partial(grads_kernel, ctx_count, direct),
        out_shape=[jax.ShapeDtypeStruct(q_pre.shape, f32)]
        + [jax.ShapeDtypeStruct(shape, f32) for shape in [(2, 8, width)] + own_shapes]
        + [jax.ShapeDtypeStruct(shape, bf16) for shape in first_shapes + late_shapes],
        in_specs=[smem, vmem] + [vmem] * (len(prepared) + len(received)),
        out_specs=[vmem] * (4 + len(first_shapes + late_shapes)),
        scratch_shapes=scratch,
        compiler_params=pltpu.CompilerParams(vmem_limit_bytes=(20 if direct else 62) * MIB),
        name="grads",
    )(doc_lengths, filters, *prepared, *received)
    d_q_main = pl.pallas_call(
        save_kernel,
        out_shape=jax.ShapeDtypeStruct(q_pre.shape, f32),
        in_specs=[vmem],
        out_specs=hbm,
        scratch_shapes=[pltpu.SemaphoreType.DMA(())],
        compiler_params=pltpu.CompilerParams(vmem_limit_bytes=2 * MIB),
        name="save",
    )(d_q_main)
    half_terms = delivered(sent[: len(first_shapes)])
    d_q_main, *half_terms = lax.optimization_barrier((d_q_main, *half_terms))
    merged_shapes = [
        jax.ShapeDtypeStruct((2 * span, 2 * LANES), f32),
        jax.ShapeDtypeStruct((2 * span + 32, 2 * LANES), bf16),
        jax.ShapeDtypeStruct((8, 2 * LANES), f32),
        jax.ShapeDtypeStruct((2, rim // 2, 2 * LANES), f32),
    ]
    near, far, half_sums, rims = pl.pallas_call(
        functools.partial(merge_kernel, ctx_count, direct),
        out_shape=merged_shapes,
        in_specs=[vmem] * (2 + len(half_terms)),
        out_specs=[vmem] * len(merged_shapes),
        scratch_shapes=[
            pltpu.VMEM((group, 8, 2 * LANES), f32),
            pltpu.VMEM((ctx_count, rim // 2, 2 * LANES), f32),
        ],
        compiler_params=pltpu.CompilerParams(vmem_limit_bytes=(4 if direct else 40) * MIB),
        name="merge",
    )(own_near, own_far, *half_terms)
    from_half = flipped(far, group)
    late_terms = sent[len(first_shapes) :]
    late_terms = [flipped(late_terms[0], group - 1)] if direct else delivered(late_terms)

    sums = pl.pallas_call(
        functools.partial(sums_kernel, span),
        out_shape=jax.ShapeDtypeStruct(filters.shape, f32),
        in_specs=[vmem, vmem],
        out_specs=vmem,
        compiler_params=pltpu.CompilerParams(vmem_limit_bytes=2 * MIB),
        name="sums",
    )(half_sums, from_half)
    count = lax.axis_size("tp")
    all_sums = [sums] + [
        lax.ppermute(sums, "tp", [(i, i ^ flip) for i in range(count)]) for flip in range(1, count)
    ]
    d_q_pre, d_k_pre, d_v_pre = pl.pallas_call(
        functools.partial(finish_kernel, ctx_count, direct),
        out_shape=(
            jax.ShapeDtypeStruct(q_pre.shape, f32),
            jax.ShapeDtypeStruct(k_pre.shape, f32),
            jax.ShapeDtypeStruct(k_pre.shape, f32),
        ),
        in_specs=[smem, vmem, hbm] + [vmem] * (4 + len(late_terms)),
        out_specs=(hbm, hbm, hbm),
        scratch_shapes=[
            pltpu.VMEM((2, 8, width), f32),
            pltpu.VMEM(k_pre.shape, f32),
            pltpu.VMEM(k_pre.shape, f32),
            pltpu.VMEM((ctx_count, rim // 2, 2 * LANES), f32),
            pltpu.SemaphoreType.DMA((3,)),
        ],
        input_output_aliases={2: 0},
        compiler_params=pltpu.CompilerParams(vmem_limit_bytes=(4 if direct else 16) * MIB),
        name="finish",
    )(doc_lengths, filters, d_q_main, d_q_tail, near, from_half, rims, *late_terms)
    while len(all_sums) > 1:
        all_sums = [all_sums[at] + all_sums[at + 1] for at in range(0, len(all_sums), 2)]
    return (d_q_pre, d_k_pre, d_v_pre, all_sums[0])


def solution(mesh):
    split = P(None, "ctx", "tp")
    return jax.shard_map(
        shards,
        mesh=mesh,
        in_specs=(split, split, split, split, P(), P()),
        out_specs=(split, split, split, P()),
        check_vma=False,
    )
```

```python
import functools

import jax
import jax.numpy as jnp
import numpy as np
from jax import lax
from jax.experimental import pallas as pl
from jax.experimental.pallas import tpu as pltpu
from jax.sharding import PartitionSpec as P

LANES = 128
NT = (((1,), (1,)), ((), ()))
NN = (((1,), (0,)), ((), ()))
TN = (((0,), (0,)), ((), ()))
TAIL = 16
MAX_CHUNK = 640
RIM = 8
MAX_DIRECT = 4
WINDOWS = ((2, 2), (4, 4), (6, 6), (4, 9), (9, 4), (9, 9))
MIB = 1 << 20


def loop(count, body, init, unrolled=16):
    if count <= unrolled:
        for step in range(count):
            init = body(step, init)
        return init
    return lax.fori_loop(0, count, body, init)


def aligned(start, multiple):
    return start if isinstance(start, int) else pl.multiple_of(start, multiple)


def doc_starts(lengths_ref):
    starts = [jnp.int32(0)]
    for index in range(lengths_ref.shape[0] - 1):
        starts.append(starts[-1] + lengths_ref[index])
    return starts


def fold_rows(terms):
    rows, lanes = terms.shape
    return jnp.sum(terms.reshape(rows // 8, 8, lanes), axis=0)


def split_bits(values):
    high = values.astype(jnp.bfloat16)
    low = (values - high.astype(jnp.float32)).astype(jnp.bfloat16)
    return high, low


def joined(pair):
    rows = pair.shape[0] // 2
    pair = pair.astype(jnp.float32)
    return pair[:rows] + pair[rows:]


class Slots:
    def __init__(self, refs, me):
        self.refs, self.me = refs, me

    def __getitem__(self, flip):
        if len(self.refs) == 1:
            place = lax.rem(self.me, jnp.int32(self.refs[0].shape[0]))
            return self.refs[0].at[partner(place, flip)]
        return self.refs[flip]


def splits(direct, flip, group):
    return not direct or flip == group - 1


def partner(me, flip):
    return lax.bitwise_xor(me, jnp.int32(flip))


def pack_kernel(k_ref, v_ref, q_ref, out_ref):
    span = k_ref.shape[1]
    kv = jnp.concatenate([k_ref[...], v_ref[...]], axis=2).reshape(2 * span, 2 * LANES)
    tails = []
    for half in range(2):
        last = q_ref[half].astype(jnp.float32)[TAIL - 2 :]
        tails += [last[:, at : at + 2 * LANES] for at in range(0, last.shape[1], 2 * LANES)]
    out_ref[: 2 * span] = kv
    out_ref[2 * span :] = jnp.concatenate(tails, axis=0).astype(jnp.bfloat16)


def prep_kernel(ctx_count, direct, lengths_ref, filters_ref, q_hbm, d_out_hbm, own_ref, *refs):
    near_refs, refs = refs[:-9], refs[-9:]
    same_ref, same_two_ref, q_scr, qc_ref, do_ref, rim_scr, q_ref, d_out_ref, sems = refs
    f32, bf16 = jnp.float32, jnp.bfloat16
    loads = [
        pltpu.make_async_copy(q_hbm, q_ref, sems.at[0]),
        pltpu.make_async_copy(d_out_hbm, d_out_ref, sems.at[1]),
    ]
    for load in loads:
        load.start()
    group = ctx_count // 2
    span = q_ref.shape[1]
    heads = q_ref.shape[2] // LANES
    blocks = 2 * ctx_count
    length = span * blocks
    me = lax.axis_index("ctx")
    near = Slots((None,) + near_refs if direct else near_refs, me)
    starts = doc_starts(lengths_ref)

    def fill(index, carry):
        rows = pl.ds(aligned(8 + index * span, 8), span)
        same_ref[rows] = jnp.ones((span, LANES), f32)
        same_two_ref[rows] = jnp.ones((span, LANES), f32)
        return carry

    lax.fori_loop(0, blocks, fill, 0, unroll=2)
    zeros = jnp.zeros((8, LANES), f32)
    for rows in (slice(0, 8), slice(8 + length, 16 + length)):
        same_ref[rows] = zeros
        same_two_ref[rows] = zeros
    for start in starts:
        same_ref[pl.ds(8 + start, 1)] = zeros[:1]
        same_two_ref[pl.ds(8 + start, 1)] = zeros[:1]
        same_two_ref[pl.ds(9 + start, 1)] = zeros[:1]

    before, after = jnp.maximum(me - 1, 0), jnp.minimum(me + 1, ctx_count - 1)
    for index in (before, after):
        rim_scr[index] = jnp.zeros(rim_scr.shape[1:], f32)
    rim_scr[me] = own_ref[2 * span :].astype(f32)

    def place_rims(step, carry):
        flip = step + 1
        if not direct or flip & (flip + 1) == 0:
            rim_scr[partner(me, flip)] = near[flip][2 * span :].astype(f32)
        return carry

    loop(group - 1, place_rims, 0, 16 if direct else 1)
    rim_before, rim_after = rim_scr[before], rim_scr[after]
    late_rim = jnp.where(me == ctx_count - 1, rim_after[:RIM], rim_after[RIM:])
    rims = [rim_before[:RIM], late_rim]
    first_place = [me * span, (blocks - 1 - me) * span]
    taps = [filters_ref[0, tap : tap + 1] for tap in range(3)]

    for load in loads:
        load.wait()
    for half in range(2):
        rows = pl.ds(aligned(first_place[half] + 8, 8), span)
        one, two = same_ref[rows], same_two_ref[rows]
        for head in range(heads):
            at = 2 * (head // 2)
            q_scr[half, head, 6:8] = rims[half][at : at + 2, (head % 2) * LANES : (head % 2 + 1) * LANES]

        def convolve_head(head, carry, half=half, one=one, two=two):
            lanes = pl.ds(pl.multiple_of(head * LANES, LANES), LANES)
            target = pl.ds(pl.multiple_of(head * span, 16), span)
            q_scr[half, head, 8:] = q_ref[half, :, lanes].astype(f32)
            total = taps[0] * q_scr[half, head, 8:]
            total = total + one * (taps[1] * q_scr[half, head, 7 : 7 + span])
            total = total + two * (taps[2] * q_scr[half, head, 6 : 6 + span])
            qc_ref[half, target] = total.astype(bf16)
            do_ref[half, target] = d_out_ref[half, :, lanes]
            return carry

        lax.fori_loop(0, heads, convolve_head, 0, unroll=4)


def grads_kernel(ctx_count, direct, lengths_ref, filters_ref, *refs):
    group = ctx_count // 2
    arrays = group - 1 if direct else 1
    same_scr, same_two_scr, q_in_ref, qc_in_ref, do_scr, own_ref, across_ref = refs[:7]
    refs = refs[7:]
    near_in, far_in, refs = refs[:arrays], refs[arrays : 2 * arrays], refs[2 * arrays :]
    dq_ref, dq_tail_ref, own_near_ref, own_far_ref = refs[:4]
    arrays = group - 1 if direct else 1
    first_out, late_out, refs = refs[4 : 4 + arrays], refs[4 + arrays : 5 + arrays], refs[5 + arrays :]
    kv_scr, conv_scr, dkv_scr, q_scr, qc_scr, dq_scr = refs[:6]
    bias_scr, s_scr, dp_scr, terms_scr, p_scr, ds_scr = refs[6:]
    f32, bf16 = jnp.float32, jnp.bfloat16
    span = own_ref.shape[0] // 2 - TAIL // 2
    heads = q_in_ref.shape[1]
    half_rows = span * ctx_count
    length = 2 * half_rows
    blocks = 2 * ctx_count
    me = lax.axis_index("ctx")
    near_in = Slots((None,) + near_in if direct else near_in, me)
    far_in = Slots((None,) + far_in if direct else far_in, me)
    first_out = Slots((None,) + first_out if direct else first_out, me)
    late_out = Slots((None,) * (group - 1) + late_out if direct else late_out, me)
    scale = LANES**-0.5
    log2_scale = scale * 1.4426950408889634
    starts = doc_starts(lengths_ref)

    def place(index, block):
        for tensor in range(2):
            lanes = slice(tensor * LANES, (tensor + 1) * LANES)
            kv_scr[tensor, pl.ds(aligned(8 + index * span, 8), span)] = block[:, lanes].astype(f32)

    def place_both(message, index):
        place(index, message[:span])
        place(blocks - 1 - index, message[span : 2 * span])

    def place_received(step, carry):
        flip = step + 1
        source = partner(me, flip)
        place_both(near_in[flip], source)
        place_both(far_in[flip], partner(source, group))
        return carry

    zeros = jnp.zeros((8, LANES), f32)
    for tensor in range(2):
        kv_scr[tensor, :8] = zeros
    for block_ref, index in ((own_ref, me), (across_ref, partner(me, group))):
        place_both(block_ref, index)
    loop(group - 1, place_received, 0, 16 if direct else 1)

    def taps(tensor):
        return [filters_ref[tensor, tap : tap + 1] for tap in range(3)]

    def masks(base, ahead):
        one = same_scr[pl.ds(base + 8 + min(ahead, 1), span)]
        return one, same_two_scr[pl.ds(base + 8 + ahead, span)]

    def convolve_kv(index, carry):
        base = index * span
        one, two = masks(base, 0)
        for tensor in range(2):
            zero_tap, one_tap, two_tap = taps(tensor + 1)
            total = zero_tap * kv_scr[tensor, pl.ds(aligned(base + 8, 8), span)]
            total = total + one * (one_tap * kv_scr[tensor, pl.ds(base + 7, span)])
            total = total + two * (two_tap * kv_scr[tensor, pl.ds(base + 6, span)])
            conv_scr[tensor, pl.ds(aligned(base, 16), span)] = total.astype(bf16)
        return carry

    first_place = [me * span, (blocks - 1 - me) * span]
    firsts = []
    for half in range(2):
        lowest = jnp.int32(0)
        for start in starts[1:]:
            lowest = jnp.where(first_place[half] >= start, start, lowest)
        firsts.append(lowest // span)

    def over_needed(body, init):
        carry = lax.fori_loop(firsts[0], me + 1, body, init)
        return lax.fori_loop(jnp.maximum(firsts[1], me + 1), blocks - me, body, carry)

    def clear(index, carry):
        for tensor in range(2):
            rows = pl.ds(pl.multiple_of(index * span, 16), span)
            conv_scr[tensor, rows] = jnp.zeros((span, LANES), bf16)
            dkv_scr[tensor, rows] = jnp.zeros((span, LANES), f32)
        terms_scr[index] = jnp.zeros((span, 2 * LANES), f32)
        return carry

    lax.fori_loop(0, blocks, clear, 0, unroll=2)
    for tensor in range(2):
        dkv_scr[tensor, length:] = zeros
    over_needed(convolve_kv, 0)

    middle = me == ctx_count - 1
    q_scr[...] = q_in_ref[...]
    qc_scr[...] = qc_in_ref[...]
    tails = far_in[group - 1][2 * span :].astype(f32)
    tails = [tails[:RIM], tails[RIM:]]
    for half, crossing in ((0, me == group), (1, me == group - 1)):

        @pl.when(crossing)
        def _(half=half):
            rows = pl.ds(aligned(first_place[half] + 8, 8), TAIL)
            one, two = same_scr[rows], same_two_scr[rows]
            zero_tap, one_tap, two_tap = taps(0)
            for head in range(heads):
                at = 2 * (head // 2)
                q_scr[half, head, 6:8] = tails[half][
                    at : at + 2, (head % 2) * LANES : (head % 2 + 1) * LANES
                ]
                total = zero_tap * q_scr[half, head, 8 : 8 + TAIL]
                total = total + one * (one_tap * q_scr[half, head, 7 : 7 + TAIL])
                total = total + two * (two_tap * q_scr[half, head, 6 : 6 + TAIL])
                qc_scr[half, head * span : head * span + TAIL] = total.astype(bf16)

    wide = 2 * LANES
    parts = heads * span // wide

    def reach(half):
        lane = lax.broadcasted_iota(jnp.int32, (1, LANES), 1)
        query = first_place[half] + lax.rem(lane, jnp.int32(span))
        lowest = jnp.zeros((1, LANES), jnp.int32)
        for start in starts[1:]:
            lowest = jnp.where(query >= start, start, lowest)
        return query, lowest

    def attend_at_once(windows):
        units = [(half, at) for half in range(2) for at in range(parts)]
        keys_rows, tops, scaled = [], [], []
        for half, window in enumerate(windows):
            first_key = pl.multiple_of(jnp.maximum(first_place[half] + span - window, 0), 16)
            keys_rows.append(pl.ds(first_key, window))
            query, lowest = reach(half)
            places = first_key + lax.broadcasted_iota(jnp.int32, (window, LANES), 0)
            allowed = (places >= lowest) & (places <= query)
            bias_scr[half, :window] = jnp.where(allowed, 0.0, -1e30)
        for slot, (half, at) in enumerate(units):
            window = windows[half]
            queries = qc_scr[half, at * wide : (at + 1) * wide]
            scores = lax.dot_general(
                conv_scr[0, keys_rows[half]], queries, NT, preferred_element_type=f32
            )
            bias = bias_scr[half, :window]
            scores = scores + jnp.concatenate([bias, bias], axis=1)
            s_scr[slot, :window] = scores
            tops.append(jnp.max(scores, axis=0, keepdims=True))
        for slot, (half, at) in enumerate(units):
            window = windows[half]
            grads = do_scr[half, at * wide : (at + 1) * wide]
            prob_grads = lax.dot_general(
                conv_scr[1, keys_rows[half]], grads, NT, preferred_element_type=f32
            )
            weights = jnp.exp2((s_scr[slot, :window] - tops[slot]) * log2_scale)
            s_scr[slot, :window] = weights
            dp_scr[slot, :window] = prob_grads
            total = jnp.sum(weights, axis=0, keepdims=True)
            weighted = jnp.sum(weights * prob_grads, axis=0, keepdims=True)
            inverse = 1.0 / total
            scaled.append((inverse, weighted * inverse, inverse * scale))
        for slot, (half, at) in enumerate(units):
            window = windows[half]
            inverse, mean, slope = scaled[slot]
            weights = s_scr[slot, :window]
            cols = slice(at * wide, (at + 1) * wide)
            p_scr[half, :window, cols] = (weights * inverse).astype(bf16)
            ds_scr[half, :window, cols] = (weights * slope * (dp_scr[slot, :window] - mean)).astype(bf16)
        for half, window in enumerate(windows):
            score_grads = ds_scr[half, :window]
            keys_t = conv_scr[0, keys_rows[half]].T
            dq = lax.dot_general(keys_t, score_grads, NN, preferred_element_type=f32).T
            for head in range(heads):
                dq_scr[half, head, :span] = dq[head * span : (head + 1) * span]
            dkv_scr[0, keys_rows[half]] += lax.dot_general(
                score_grads, qc_scr[half], NN, preferred_element_type=f32
            )
            dkv_scr[1, keys_rows[half]] += lax.dot_general(
                p_scr[half, :window], do_scr[half], NN, preferred_element_type=f32
            )

    def attend(half, window, first_key):
        chunks = 1
        while window // chunks > MAX_CHUNK or window % (16 * chunks):
            chunks += 1
        size = window // chunks
        query, lowest = reach(half)

        def fill_bias(step, carry):
            places = first_key + step * size + lax.broadcasted_iota(jnp.int32, (size, LANES), 0)
            allowed = (places >= lowest) & (places <= query)
            bias_scr[0, pl.ds(aligned(step * size, 16), size)] = jnp.where(allowed, 0.0, -1e30)
            return carry

        loop(chunks, fill_bias, 0, 1)
        whole_window = pl.ds(aligned(first_key, 16), window)
        keys_t = conv_scr[0, whole_window].T if chunks == 1 else None
        for at in range(parts):
            slot = 0
            cols = slice(at * wide, (at + 1) * wide)
            queries = qc_scr[half, cols]
            grads = do_scr[half, cols]

            def key_rows(step):
                return pl.ds(aligned(first_key + step * size, 16), size)

            def score(step, top):
                keys = conv_scr[0, key_rows(step)]
                scores = lax.dot_general(keys, queries, NT, preferred_element_type=f32)
                bias = bias_scr[0, pl.ds(aligned(step * size, 16), size)]
                scores = scores + jnp.concatenate([bias, bias], axis=1)
                s_scr[slot, pl.ds(aligned(step * size, 16), size)] = scores
                return jnp.maximum(top, jnp.max(scores, axis=0, keepdims=True))

            top = loop(chunks, score, jnp.full((1, wide), -1e30, f32), 1)

            def weigh(step, carry):
                total, weighted = carry
                rows = pl.ds(aligned(step * size, 16), size)
                weights = jnp.exp2((s_scr[slot, rows] - top) * log2_scale)
                values = conv_scr[1, key_rows(step)]
                prob_grads = lax.dot_general(values, grads, NT, preferred_element_type=f32)
                s_scr[slot, rows] = weights
                dp_scr[slot, rows] = prob_grads
                total = total + jnp.sum(weights, axis=0, keepdims=True)
                weighted = weighted + jnp.sum(weights * prob_grads, axis=0, keepdims=True)
                return total, weighted

            zeros = jnp.zeros((1, wide), f32)
            total, weighted = loop(chunks, weigh, (zeros, zeros), 1)
            inverse = 1.0 / total
            mean = weighted * inverse
            slope = inverse * scale

            def accumulate(step, dq):
                rows = pl.ds(aligned(step * size, 16), size)
                weights = s_scr[slot, rows]
                probs = (weights * inverse).astype(bf16)
                score_grads = (weights * slope * (dp_scr[slot, rows] - mean)).astype(bf16)
                dk = lax.dot_general(score_grads, queries, NN, preferred_element_type=f32)
                dv = lax.dot_general(probs, grads, NN, preferred_element_type=f32)
                target = pl.ds(aligned(first_key + step * size, 16), size)
                for tensor, terms in enumerate((dk, dv)):
                    dkv_scr[tensor, target] += terms
                if keys_t is not None:
                    return lax.dot_general(keys_t, score_grads, NN, preferred_element_type=f32)
                keys = conv_scr[0, key_rows(step)]
                return dq + lax.dot_general(keys, score_grads, TN, preferred_element_type=f32)

            dq = loop(chunks, accumulate, jnp.zeros((LANES, wide), f32), 1)
            dq = dq.T
            for part in range(wide // span):
                head = at * (wide // span) + part
                dq_scr[half, head, :span] = dq[part * span : (part + 1) * span]

    needed = [first_place[half] // span - firsts[half] + 1 for half in range(2)]
    if direct:
        done = jnp.bool_(False)
        for sizes in WINDOWS:
            sizes = [min(size, ctx_count + 1) for size in sizes]
            fits = (needed[0] <= sizes[0]) & (needed[1] <= sizes[1])

            @pl.when(fits & jnp.logical_not(done))
            def _(sizes=sizes):
                attend_at_once([size * span for size in sizes])

            done = done | fits
    else:
        for half in range(2):
            attend(half, half_rows + half * span, half * (ctx_count - 1 - me) * span)

    next_rows = jnp.where(middle, dq_scr[1, :, :8], 0.0)
    dq_scr[0, :, span:] = next_rows
    dq_scr[1, :, span:] = jnp.zeros_like(next_rows)
    sums = [jnp.zeros((8, LANES), f32) for _ in range(3)]
    for half in range(2):
        one, two = masks(first_place[half], 0)
        ahead_one = same_scr[pl.ds(first_place[half] + 9, span)]
        ahead_two = same_two_scr[pl.ds(first_place[half] + 10, span)]
        zero_tap, one_tap, two_tap = taps(0)

        def finish_head(head, carry, half=half, one=one, two=two, ahead_one=ahead_one, ahead_two=ahead_two):
            lanes = pl.ds(pl.multiple_of(head * LANES, LANES), LANES)
            grads = dq_scr[half, head, :span]
            out = zero_tap * grads
            out = out + ahead_one * (one_tap * dq_scr[half, head, 1 : 1 + span])
            out = out + ahead_two * (two_tap * dq_scr[half, head, 2 : 2 + span])
            dq_ref[half, :, lanes] = out
            dq_tail_ref[half, :, lanes] = out[span - 8 :]
            return (
                carry[0] + fold_rows(grads * q_scr[half, head, 8:]),
                carry[1] + fold_rows(grads * one * q_scr[half, head, 7 : 7 + span]),
                carry[2] + fold_rows(grads * two * q_scr[half, head, 6 : 6 + span]),
            )

        sums = lax.fori_loop(0, heads, finish_head, tuple(sums), unroll=4)
    q_sums = [jnp.sum(term, axis=0, keepdims=True) for term in sums]

    def finish_block(index, carry):
        base = pl.multiple_of(index * span, 8)
        one, two = masks(base, 0)
        ahead_one = same_scr[pl.ds(base + 9, span)]
        ahead_two = same_two_scr[pl.ds(base + 10, span)]
        carry = list(carry)
        for tensor in range(2):
            zero_tap, one_tap, two_tap = taps(tensor + 1)
            own = dkv_scr[tensor, pl.ds(base, span)]
            out = zero_tap * own
            out = out + ahead_one * (one_tap * dkv_scr[tensor, pl.ds(base + 1, span)])
            out = out + ahead_two * (two_tap * dkv_scr[tensor, pl.ds(base + 2, span)])
            lanes = slice(tensor * LANES, (tensor + 1) * LANES)
            terms_scr[index, :, lanes] = out
            at = 3 * tensor
            carry[at] += fold_rows(own * kv_scr[tensor, pl.ds(base + 8, span)])
            carry[at + 1] += fold_rows(own * one * kv_scr[tensor, pl.ds(base + 7, span)])
            carry[at + 2] += fold_rows(own * two * kv_scr[tensor, pl.ds(base + 6, span)])
        return tuple(carry)

    low = me < group

    kv_sums = over_needed(finish_block, (zeros,) * 6)
    for target, index in ((own_far_ref, partner(me, group)), (own_near_ref, me)):
        target[:span] = terms_scr[index]
        target[span : 2 * span] = terms_scr[blocks - 1 - index]

    def send(step, carry):
        flip = step + 1
        owner = partner(me, flip)
        far_owner = partner(me, flip + group)
        near_late = blocks - 1 - owner
        second = jnp.where(low, blocks - 1 - far_owner, owner)
        third = jnp.where(low & (me > owner), owner, near_late)
        first_out[flip][:span] = terms_scr[far_owner].astype(bf16)
        first_out[flip][span : 2 * span] = terms_scr[second].astype(bf16)
        if splits(direct, flip, group):
            late_out[flip][:span] = terms_scr[third].astype(bf16)
        else:
            first_out[flip][2 * span : 3 * span] = terms_scr[third].astype(bf16)
        return carry

    loop(group - 1, send, 0, 16 if direct else 1)
    kv_sums = [jnp.sum(term, axis=0, keepdims=True) for term in kv_sums]

    padding = [jnp.zeros((2, LANES), f32)]
    left = jnp.concatenate(q_sums + kv_sums[:3] + padding, axis=0)
    right = jnp.concatenate([jnp.zeros((3, LANES), f32)] + kv_sums[3:] + padding, axis=0)
    sums_tile = jnp.concatenate([left, right], axis=1)
    sums_pair = jnp.concatenate(split_bits(sums_tile), axis=0)
    own_far_ref[2 * span :] = joined(sums_pair)
    rims = []
    for half in range(2):
        rows = [dq_scr[half, head, :2] for head in range(heads)]
        rows = [jnp.concatenate(rows[at : at + 2], axis=1) for at in range(0, heads, 2)]
        rims.append(jnp.concatenate(rows, axis=0))

    def rim_for(index):
        return jnp.concatenate(split_bits(jnp.where(index < me, rims[0], rims[1])), axis=0)

    def store_rims(step, carry):
        flip = step + 1
        owner = partner(me, flip)
        after = (2 if splits(direct, flip, group) else 3) * span
        first_out[flip][after : after + 16] = sums_pair
        if not direct or flip == group - 1:
            first_out[flip][after + 16 :] = rim_for(partner(owner, group))
        if not direct or flip & (flip + 1) == 0:
            if splits(direct, flip, group):
                late_out[flip][span:] = rim_for(owner)
            else:
                first_out[flip][after + 16 :] = rim_for(owner)
        return carry

    loop(group - 1, store_rims, 0, 16 if direct else 1)


def merge_kernel(ctx_count, direct, own_near_ref, own_far_ref, *refs):
    received_refs, refs = refs[:-6], refs[-6:]
    near_ref, far_ref, half_sums_ref, rims_ref, sums_scr, rim_scr = refs
    f32, bf16 = jnp.float32, jnp.bfloat16
    group = ctx_count // 2
    me = lax.axis_index("ctx")
    low = me < group
    received = Slots((own_far_ref,) + received_refs if direct else received_refs, me)
    place = lax.rem(me, jnp.int32(group))
    span = own_near_ref.shape[0] // 2
    rows = 2 * span
    sums_scr[place] = own_far_ref[rows:]
    def add(step, carry):
        flip = step + 1
        source = partner(me, flip)
        message = received[flip]
        early, second = [message[at * span : (at + 1) * span].astype(f32) for at in range(2)]
        near_early, near_late, far_early, far_late = carry
        zero = jnp.zeros_like(second)
        after = (2 if splits(direct, flip, group) else 3) * span
        sums_scr[partner(place, flip)] = joined(message[after : after + 16])
        near_early = near_early + jnp.where(low, zero, second)
        if not splits(direct, flip, group):
            third = message[2 * span : 3 * span].astype(f32)
            to_early = low & (source > me)
            near_early = near_early + jnp.where(to_early, third, zero)
            near_late = near_late + jnp.where(to_early, zero, third)
            if flip & (flip + 1) == 0:
                rim_scr[source] = joined(message[after + 16 :])
        return near_early, near_late, far_early + early, far_late + jnp.where(low, second, zero)

    neighbours = [jnp.minimum(me + 1, ctx_count - 1), jnp.maximum(me - 1, 0)]
    for index in neighbours:
        rim_scr[index] = jnp.zeros(rim_scr.shape[1:], f32)
    init = (own_near_ref[:span], own_near_ref[span:], own_far_ref[:span], own_far_ref[span:rows])
    totals = loop(group - 1, add, init, 16 if direct else 1)
    near_ref[:span] = totals[0]
    near_ref[span:] = totals[1]
    far_ref[:span] = totals[2].astype(bf16)
    far_ref[span:rows] = totals[3].astype(bf16)
    for at, index in enumerate(neighbours):
        rims_ref[at] = rim_scr[index]
    sums = loop(group, lambda index, carry: carry + sums_scr[index], jnp.zeros((8, 2 * LANES), f32))
    pair = jnp.concatenate(split_bits(sums), axis=0)
    half_sums_ref[...] = joined(pair)
    far_ref[rows : rows + 16] = pair
    far_ref[rows + 16 :] = received[group - 1][rows + 16 :]


def save_kernel(source_ref, target_hbm, sem):
    copy = pltpu.make_async_copy(source_ref, target_hbm, sem)
    copy.start()
    copy.wait()


def sums_kernel(span, half_sums_ref, far_ref, out_ref):
    sums = half_sums_ref[...] + joined(far_ref[2 * span : 2 * span + 16])
    out_ref[0] = sums[0:3, :LANES]
    out_ref[1] = sums[3:6, :LANES]
    out_ref[2] = sums[3:6, LANES:]


def finish_kernel(
    ctx_count, direct, lengths_ref, filters_ref, dq_in_hbm, tail_ref, near_ref, far_ref, rims_ref, *refs
):
    received_refs, refs = refs[:-8], refs[-8:]
    dq_hbm, dk_hbm, dv_hbm, dq_ref, dk_ref, dv_ref, rim_scr, sems = refs
    f32 = jnp.float32
    group = ctx_count // 2
    span = dk_ref.shape[1]
    me = lax.axis_index("ctx")
    low = me < group
    received = Slots((None,) * (group - 1) + received_refs if direct else received_refs, me)
    starts = doc_starts(lengths_ref)
    blocks = 2 * ctx_count
    neighbours = [jnp.minimum(me + 1, ctx_count - 1), jnp.maximum(me - 1, 0)]
    for at, index in enumerate(neighbours):
        rim_scr[index] = rims_ref[at]

    def add(step, carry):
        flip = step + 1
        source = partner(me, flip)
        message = received[flip]
        terms = message[:span].astype(f32)
        if not direct or flip & (flip + 1) == 0:
            rim_scr[source] = joined(message[span:])
        to_early = low & (source > me)
        zero = jnp.zeros_like(terms)
        return carry[0] + jnp.where(to_early, terms, zero), carry[1] + jnp.where(to_early, zero, terms)

    total = near_ref[...] + far_ref[: 2 * span].astype(f32)
    total = (total[:span], total[span:])
    total = add(group - 2, total) if direct else loop(group - 1, add, total, 1)
    for half in range(2):
        dk_ref[half] = total[half][:, :LANES]
        dv_ref[half] = total[half][:, LANES:]
    stores = [
        pltpu.make_async_copy(dk_ref, dk_hbm, sems.at[0]),
        pltpu.make_async_copy(dv_ref, dv_hbm, sems.at[1]),
        pltpu.make_async_copy(dq_ref, dq_hbm.at[:, pl.ds(span - 8, 8)], sems.at[2]),
    ]
    for store in stores[:2]:
        store.start()

    def same(place):
        cut = place >= blocks * span
        for start in starts:
            cut = cut | (place == start)
        return jnp.where(cut, 0.0, 1.0).astype(f32)

    heads = dq_ref.shape[2] // LANES
    taps = [jnp.concatenate([filters_ref[0, tap : tap + 1]] * heads, axis=1) for tap in range(3)]
    row = lax.broadcasted_iota(jnp.int32, dq_ref.shape[1:], 0)
    far_rim = joined(far_ref[2 * span + 16 :])
    crosses = [me == group - 1, me == group]
    first_place = [me * span, (blocks - 1 - me) * span]
    present = [me < ctx_count - 1, me > 0]
    for half in range(2):
        rim = jnp.where(crosses[half], far_rim, rim_scr[neighbours[half]])
        rows = jnp.concatenate([rim[2 * at : 2 * at + 2] for at in range(rim.shape[0] // 2)], axis=1)
        end = first_place[half] + span
        zero, one, two = same(end - 1), same(end), same(end + 1)
        one = jnp.where(present[half], one, 0.0)
        last_but_one = (zero * one) * (taps[2] * rows[0:1])
        last = one * (taps[1] * rows[0:1]) + (one * two) * (taps[2] * rows[1:2])
        extra = jnp.where(row == 6, last_but_one, jnp.where(row == 7, last, 0.0))
        dq_ref[half] = tail_ref[half] + extra
    stores[2].start()
    for store in stores:
        store.wait()


def shards(q_pre, k_pre, value_before_filter, d_out, filters, doc_lengths):
    f32, bf16 = jnp.float32, jnp.bfloat16
    ctx_count = lax.axis_size("ctx")
    span, width = q_pre.shape[1:]
    length = 2 * span * ctx_count
    rim = 4 * width // (2 * LANES)
    vmem = pl.BlockSpec(memory_space=pltpu.VMEM)
    smem = pl.BlockSpec(memory_space=pltpu.SMEM)
    hbm = pl.BlockSpec(memory_space=pltpu.HBM)

    group = ctx_count // 2
    direct = group <= MAX_DIRECT
    halves = [[half * group + at for at in range(group)] for half in range(2)]
    msg_rows = 2 * span + rim

    def whole(shape):
        return pl.BlockSpec(shape, lambda i: (0,) * len(shape))

    def in_hbm(array):
        return pltpu.with_memory_space_constraint(array, pltpu.HBM)

    def flipped(array, flip):
        return lax.ppermute(array, "ctx", [(i, i ^ flip) for i in range(ctx_count)])

    def gathered(array):
        if direct:
            return [flipped(array, flip) for flip in range(1, group)]
        return [lax.all_gather(array, "ctx", axis_index_groups=halves)]

    def delivered(arrays):
        if direct:
            return [flipped(array, step + 1) for step, array in enumerate(arrays)]
        return [lax.all_to_all(arrays[0], "ctx", 0, 0, axis_index_groups=halves, tiled=True)]

    packed = pl.pallas_call(
        pack_kernel,
        grid=(1,),
        out_shape=jax.ShapeDtypeStruct((msg_rows, 2 * LANES), bf16),
        in_specs=[
            whole(k_pre.shape),
            whole(k_pre.shape),
            pl.BlockSpec((2, TAIL, width), lambda i: (0, span // TAIL - 1, 0)),
        ],
        out_specs=whole((msg_rows, 2 * LANES)),
        compiler_params=pltpu.CompilerParams(vmem_limit_bytes=4 * MIB),
        name="pack",
    )(*[in_hbm(array) for array in (k_pre, value_before_filter, q_pre)])
    across = flipped(packed, group)
    near = gathered(packed)
    far = gathered(across)
    received = [packed, across] + near + far

    window = span * ctx_count + span
    if direct:
        flips = range(1, group)
        first_shapes = []
        for flip in flips:
            rows = (2 if splits(direct, flip, group) else 3) * span + 16
            rows += 16 if flip == group - 1 or flip & (flip + 1) == 0 else 0
            first_shapes.append((rows, 2 * LANES))
        late_shapes = [(span + 16, 2 * LANES)]
    else:
        first_shapes = [(group, 2 * span + 32, 2 * LANES)]
        late_shapes = [(group, span + 16, 2 * LANES)]
    slots = 4 if direct else 1
    heads = width // LANES
    by_head = (2, span * heads, LANES)
    padded = (2, heads, span + 8, LANES)
    prepared = pl.pallas_call(
        functools.partial(prep_kernel, ctx_count, direct),
        out_shape=[
            jax.ShapeDtypeStruct((length + 16, LANES), f32),
            jax.ShapeDtypeStruct((length + 16, LANES), f32),
            jax.ShapeDtypeStruct(padded, f32),
            jax.ShapeDtypeStruct(by_head, bf16),
            jax.ShapeDtypeStruct(by_head, bf16),
        ],
        in_specs=[smem, vmem, hbm, hbm] + [vmem] * (1 + len(near)),
        out_specs=[vmem] * 5,
        scratch_shapes=[
            pltpu.VMEM((ctx_count, rim, 2 * LANES), f32),
            pltpu.VMEM(q_pre.shape, bf16),
            pltpu.VMEM(q_pre.shape, bf16),
            pltpu.SemaphoreType.DMA((2,)),
        ],
        compiler_params=pltpu.CompilerParams(vmem_limit_bytes=(8 if direct else 32) * MIB),
        name="prep",
    )(doc_lengths, filters, in_hbm(q_pre), in_hbm(d_out), packed, *near)
    scratch = [
        pltpu.VMEM((2, length + 16, LANES), f32),
        pltpu.VMEM((2, length, LANES), bf16),
        pltpu.VMEM((2, length + 8, LANES), f32),
        pltpu.VMEM(padded, f32),
        pltpu.VMEM(by_head, bf16),
        pltpu.VMEM(padded, f32),
        pltpu.VMEM((2, window, LANES), f32),
        pltpu.VMEM((slots, window, 2 * LANES), f32),
        pltpu.VMEM((slots, window, 2 * LANES), f32),
        pltpu.VMEM((2 * ctx_count, span, 2 * LANES), f32),
        pltpu.VMEM((2, window, heads * span) if direct else (2, 16, LANES), bf16),
        pltpu.VMEM((2, window, heads * span) if direct else (2, 16, LANES), bf16),
    ]
    own_shapes = [(2 * span, 2 * LANES), (2 * span + 8, 2 * LANES)]
    d_q_main, d_q_tail, own_near, own_far, *sent = pl.pallas_call(
        functools.partial(grads_kernel, ctx_count, direct),
        out_shape=[jax.ShapeDtypeStruct(q_pre.shape, f32)]
        + [jax.ShapeDtypeStruct(shape, f32) for shape in [(2, 8, width)] + own_shapes]
        + [jax.ShapeDtypeStruct(shape, bf16) for shape in first_shapes + late_shapes],
        in_specs=[smem, vmem] + [vmem] * (len(prepared) + len(received)),
        out_specs=[vmem] * (4 + len(first_shapes + late_shapes)),
        scratch_shapes=scratch,
        compiler_params=pltpu.CompilerParams(vmem_limit_bytes=(20 if direct else 62) * MIB),
        name="grads",
    )(doc_lengths, filters, *prepared, *received)
    d_q_main = pl.pallas_call(
        save_kernel,
        out_shape=jax.ShapeDtypeStruct(q_pre.shape, f32),
        in_specs=[vmem],
        out_specs=hbm,
        scratch_shapes=[pltpu.SemaphoreType.DMA(())],
        compiler_params=pltpu.CompilerParams(vmem_limit_bytes=2 * MIB),
        name="save",
    )(d_q_main)
    half_terms = delivered(sent[: len(first_shapes)])
    d_q_main, *half_terms = lax.optimization_barrier((d_q_main, *half_terms))
    merged_shapes = [
        jax.ShapeDtypeStruct((2 * span, 2 * LANES), f32),
        jax.ShapeDtypeStruct((2 * span + 32, 2 * LANES), bf16),
        jax.ShapeDtypeStruct((8, 2 * LANES), f32),
        jax.ShapeDtypeStruct((2, rim // 2, 2 * LANES), f32),
    ]
    near, far, half_sums, rims = pl.pallas_call(
        functools.partial(merge_kernel, ctx_count, direct),
        out_shape=merged_shapes,
        in_specs=[vmem] * (2 + len(half_terms)),
        out_specs=[vmem] * len(merged_shapes),
        scratch_shapes=[
            pltpu.VMEM((group, 8, 2 * LANES), f32),
            pltpu.VMEM((ctx_count, rim // 2, 2 * LANES), f32),
        ],
        compiler_params=pltpu.CompilerParams(vmem_limit_bytes=(4 if direct else 40) * MIB),
        name="merge",
    )(own_near, own_far, *half_terms)
    from_half = flipped(far, group)
    late_terms = sent[len(first_shapes) :]
    late_terms = [flipped(late_terms[0], group - 1)] if direct else delivered(late_terms)

    sums = pl.pallas_call(
        functools.partial(sums_kernel, span),
        out_shape=jax.ShapeDtypeStruct(filters.shape, f32),
        in_specs=[vmem, vmem],
        out_specs=vmem,
        compiler_params=pltpu.CompilerParams(vmem_limit_bytes=2 * MIB),
        name="sums",
    )(half_sums, from_half)
    count = lax.axis_size("tp")
    all_sums = [sums] + [
        lax.ppermute(sums, "tp", [(i, i ^ flip) for i in range(count)]) for flip in range(1, count)
    ]
    d_q_pre, d_k_pre, d_v_pre = pl.pallas_call(
        functools.partial(finish_kernel, ctx_count, direct),
        out_shape=(
            jax.ShapeDtypeStruct(q_pre.shape, f32),
            jax.ShapeDtypeStruct(k_pre.shape, f32),
            jax.ShapeDtypeStruct(k_pre.shape, f32),
        ),
        in_specs=[smem, vmem, hbm] + [vmem] * (4 + len(late_terms)),
        out_specs=(hbm, hbm, hbm),
        scratch_shapes=[
            pltpu.VMEM((2, 8, width), f32),
            pltpu.VMEM(k_pre.shape, f32),
            pltpu.VMEM(k_pre.shape, f32),
            pltpu.VMEM((ctx_count, rim // 2, 2 * LANES), f32),
            pltpu.SemaphoreType.DMA((3,)),
        ],
        input_output_aliases={2: 0},
        compiler_params=pltpu.CompilerParams(vmem_limit_bytes=(4 if direct else 16) * MIB),
        name="finish",
    )(doc_lengths, filters, d_q_main, d_q_tail, near, from_half, rims, *late_terms)
    while len(all_sums) > 1:
        all_sums = [all_sums[at] + all_sums[at + 1] for at in range(0, len(all_sums), 2)]
    return (d_q_pre, d_k_pre, d_v_pre, all_sums[0])


def solution(mesh):
    split = P(None, "ctx", "tp")
    return jax.shard_map(
        shards,
        mesh=mesh,
        in_specs=(split, split, split, split, P(), P()),
        out_specs=(split, split, split, P()),
        check_vma=False,
    )
```

```python
import functools

import jax
import jax.numpy as jnp
import numpy as np
from jax import lax
from jax.experimental import pallas as pl
from jax.experimental.pallas import tpu as pltpu
from jax.sharding import PartitionSpec as P

LANES = 128
NT = (((1,), (1,)), ((), ()))
NN = (((1,), (0,)), ((), ()))
TN = (((0,), (0,)), ((), ()))
TAIL = 16
MAX_CHUNK = 640
RIM = 8
MAX_DIRECT = 4
WINDOWS = ((2, 2), (4, 4), (2, 9), (6, 6), (4, 9), (9, 4), (6, 9), (9, 9))
MIB = 1 << 20


def loop(count, body, init, unrolled=16):
    if count <= unrolled:
        for step in range(count):
            init = body(step, init)
        return init
    return lax.fori_loop(0, count, body, init)


def aligned(start, multiple):
    return start if isinstance(start, int) else pl.multiple_of(start, multiple)


def doc_starts(lengths_ref):
    starts = [jnp.int32(0)]
    for index in range(lengths_ref.shape[0] - 1):
        starts.append(starts[-1] + lengths_ref[index])
    return starts


def fold_rows(terms):
    rows, lanes = terms.shape
    return jnp.sum(terms.reshape(rows // 8, 8, lanes), axis=0)


def split_bits(values):
    high = values.astype(jnp.bfloat16)
    low = (values - high.astype(jnp.float32)).astype(jnp.bfloat16)
    return high, low


def joined(pair):
    rows = pair.shape[0] // 2
    pair = pair.astype(jnp.float32)
    return pair[:rows] + pair[rows:]


class Slots:
    def __init__(self, refs, me):
        self.refs, self.me = refs, me

    def __getitem__(self, flip):
        if len(self.refs) == 1:
            place = lax.rem(self.me, jnp.int32(self.refs[0].shape[0]))
            return self.refs[0].at[partner(place, flip)]
        return self.refs[flip]


def splits(direct, flip, group):
    return not direct or flip == group - 1


def partner(me, flip):
    return lax.bitwise_xor(me, jnp.int32(flip))


def pack_kernel(k_hbm, v_hbm, q_hbm, out_ref, k_ref, v_ref, q_ref, sems):
    span = k_ref.shape[1]
    loads = [
        pltpu.make_async_copy(k_hbm, k_ref, sems.at[0]),
        pltpu.make_async_copy(v_hbm, v_ref, sems.at[1]),
        pltpu.make_async_copy(q_hbm.at[:, pl.ds(span - TAIL, TAIL)], q_ref, sems.at[2]),
    ]
    for load in loads:
        load.start()
    for load in loads:
        load.wait()
    kv = jnp.concatenate([k_ref[...], v_ref[...]], axis=2).reshape(2 * span, 2 * LANES)
    tails = []
    for half in range(2):
        last = q_ref[half].astype(jnp.float32)[TAIL - 2 :]
        tails += [last[:, at : at + 2 * LANES] for at in range(0, last.shape[1], 2 * LANES)]
    out_ref[: 2 * span] = kv
    out_ref[2 * span :] = jnp.concatenate(tails, axis=0).astype(jnp.bfloat16)


def prep_kernel(ctx_count, direct, lengths_ref, filters_ref, q_hbm, d_out_hbm, own_ref, *refs):
    near_refs, refs = refs[:-9], refs[-9:]
    same_ref, same_two_ref, q_scr, qc_ref, do_ref, rim_scr, q_ref, d_out_ref, sems = refs
    f32, bf16 = jnp.float32, jnp.bfloat16
    loads = [
        pltpu.make_async_copy(q_hbm, q_ref, sems.at[0]),
        pltpu.make_async_copy(d_out_hbm, d_out_ref, sems.at[1]),
    ]
    for load in loads:
        load.start()
    group = ctx_count // 2
    span = q_ref.shape[1]
    heads = q_ref.shape[2] // LANES
    blocks = 2 * ctx_count
    length = span * blocks
    me = lax.axis_index("ctx")
    near = Slots((None,) + near_refs if direct else near_refs, me)
    starts = doc_starts(lengths_ref)

    def fill(index, carry):
        rows = pl.ds(aligned(8 + index * span, 8), span)
        same_ref[rows] = jnp.ones((span, LANES), f32)
        same_two_ref[rows] = jnp.ones((span, LANES), f32)
        return carry

    lax.fori_loop(0, blocks, fill, 0, unroll=2)
    zeros = jnp.zeros((8, LANES), f32)
    for rows in (slice(0, 8), slice(8 + length, 16 + length)):
        same_ref[rows] = zeros
        same_two_ref[rows] = zeros
    for start in starts:
        same_ref[pl.ds(8 + start, 1)] = zeros[:1]
        same_two_ref[pl.ds(8 + start, 1)] = zeros[:1]
        same_two_ref[pl.ds(9 + start, 1)] = zeros[:1]

    before, after = jnp.maximum(me - 1, 0), jnp.minimum(me + 1, ctx_count - 1)
    for index in (before, after):
        rim_scr[index] = jnp.zeros(rim_scr.shape[1:], f32)
    rim_scr[me] = own_ref[2 * span :].astype(f32)

    def place_rims(step, carry):
        flip = step + 1
        if not direct or flip & (flip + 1) == 0:
            rim_scr[partner(me, flip)] = near[flip][2 * span :].astype(f32)
        return carry

    loop(group - 1, place_rims, 0, 16 if direct else 1)
    rim_before, rim_after = rim_scr[before], rim_scr[after]
    late_rim = jnp.where(me == ctx_count - 1, rim_after[:RIM], rim_after[RIM:])
    rims = [rim_before[:RIM], late_rim]
    first_place = [me * span, (blocks - 1 - me) * span]
    taps = [filters_ref[0, tap : tap + 1] for tap in range(3)]

    for load in loads:
        load.wait()
    for half in range(2):
        rows = pl.ds(aligned(first_place[half] + 8, 8), span)
        one, two = same_ref[rows], same_two_ref[rows]
        for head in range(heads):
            at = 2 * (head // 2)
            q_scr[half, head, 6:8] = rims[half][at : at + 2, (head % 2) * LANES : (head % 2 + 1) * LANES]

        def convolve_head(head, carry, half=half, one=one, two=two):
            lanes = pl.ds(pl.multiple_of(head * LANES, LANES), LANES)
            target = pl.ds(pl.multiple_of(head * span, 16), span)
            q_scr[half, head, 8:] = q_ref[half, :, lanes].astype(f32)
            total = taps[0] * q_scr[half, head, 8:]
            total = total + one * (taps[1] * q_scr[half, head, 7 : 7 + span])
            total = total + two * (taps[2] * q_scr[half, head, 6 : 6 + span])
            qc_ref[half, target] = total.astype(bf16)
            do_ref[half, target] = d_out_ref[half, :, lanes]
            return carry

        lax.fori_loop(0, heads, convolve_head, 0, unroll=4)


def grads_kernel(ctx_count, direct, lengths_ref, filters_ref, *refs):
    group = ctx_count // 2
    arrays = group - 1 if direct else 1
    same_scr, same_two_scr, q_in_ref, qc_in_ref, do_scr, own_ref, across_ref = refs[:7]
    refs = refs[7:]
    near_in, far_in, refs = refs[:arrays], refs[arrays : 2 * arrays], refs[2 * arrays :]
    dq_ref, dq_tail_ref, own_near_ref, own_far_ref = refs[:4]
    arrays = group - 1 if direct else 1
    first_out, late_out, refs = refs[4 : 4 + arrays], refs[4 + arrays : 5 + arrays], refs[5 + arrays :]
    kv_scr, conv_scr, dkv_scr, q_scr, qc_scr, dq_scr = refs[:6]
    bias_scr, s_scr, dp_scr, terms_scr, p_scr, ds_scr = refs[6:]
    f32, bf16 = jnp.float32, jnp.bfloat16
    span = own_ref.shape[0] // 2 - TAIL // 2
    heads = q_in_ref.shape[1]
    half_rows = span * ctx_count
    length = 2 * half_rows
    blocks = 2 * ctx_count
    me = lax.axis_index("ctx")
    near_in = Slots((None,) + near_in if direct else near_in, me)
    far_in = Slots((None,) + far_in if direct else far_in, me)
    first_out = Slots((None,) + first_out if direct else first_out, me)
    late_out = Slots((None,) * (group - 1) + late_out if direct else late_out, me)
    scale = LANES**-0.5
    log2_scale = scale * 1.4426950408889634
    starts = doc_starts(lengths_ref)

    def place(index, block):
        for tensor in range(2):
            lanes = slice(tensor * LANES, (tensor + 1) * LANES)
            kv_scr[tensor, pl.ds(aligned(8 + index * span, 8), span)] = block[:, lanes].astype(f32)

    def place_both(message, index):
        place(index, message[:span])
        place(blocks - 1 - index, message[span : 2 * span])

    def place_received(step, carry):
        flip = step + 1
        source = partner(me, flip)
        place_both(near_in[flip], source)
        place_both(far_in[flip], partner(source, group))
        return carry

    zeros = jnp.zeros((8, LANES), f32)
    for tensor in range(2):
        kv_scr[tensor, :8] = zeros
    for block_ref, index in ((own_ref, me), (across_ref, partner(me, group))):
        place_both(block_ref, index)
    loop(group - 1, place_received, 0, 16 if direct else 1)

    def taps(tensor):
        return [filters_ref[tensor, tap : tap + 1] for tap in range(3)]

    def masks(base, ahead):
        one = same_scr[pl.ds(base + 8 + min(ahead, 1), span)]
        return one, same_two_scr[pl.ds(base + 8 + ahead, span)]

    def convolve_kv(index, carry):
        base = index * span
        one, two = masks(base, 0)
        for tensor in range(2):
            zero_tap, one_tap, two_tap = taps(tensor + 1)
            total = zero_tap * kv_scr[tensor, pl.ds(aligned(base + 8, 8), span)]
            total = total + one * (one_tap * kv_scr[tensor, pl.ds(base + 7, span)])
            total = total + two * (two_tap * kv_scr[tensor, pl.ds(base + 6, span)])
            conv_scr[tensor, pl.ds(aligned(base, 16), span)] = total.astype(bf16)
        return carry

    first_place = [me * span, (blocks - 1 - me) * span]
    firsts = []
    for half in range(2):
        lowest = jnp.int32(0)
        for start in starts[1:]:
            lowest = jnp.where(first_place[half] >= start, start, lowest)
        firsts.append(lowest // span)

    def over_needed(body, init):
        carry = lax.fori_loop(firsts[0], me + 1, body, init)
        return lax.fori_loop(jnp.maximum(firsts[1], me + 1), blocks - me, body, carry)

    def clear(index, carry):
        for tensor in range(2):
            rows = pl.ds(pl.multiple_of(index * span, 16), span)
            conv_scr[tensor, rows] = jnp.zeros((span, LANES), bf16)
            dkv_scr[tensor, rows] = jnp.zeros((span, LANES), f32)
        terms_scr[index] = jnp.zeros((span, 2 * LANES), f32)
        return carry

    lax.fori_loop(0, blocks, clear, 0, unroll=2)
    for tensor in range(2):
        dkv_scr[tensor, length:] = zeros
    over_needed(convolve_kv, 0)

    middle = me == ctx_count - 1
    q_scr[...] = q_in_ref[...]
    qc_scr[...] = qc_in_ref[...]
    tails = far_in[group - 1][2 * span :].astype(f32)
    tails = [tails[:RIM], tails[RIM:]]
    for half, crossing in ((0, me == group), (1, me == group - 1)):

        @pl.when(crossing)
        def _(half=half):
            rows = pl.ds(aligned(first_place[half] + 8, 8), TAIL)
            one, two = same_scr[rows], same_two_scr[rows]
            zero_tap, one_tap, two_tap = taps(0)
            for head in range(heads):
                at = 2 * (head // 2)
                q_scr[half, head, 6:8] = tails[half][
                    at : at + 2, (head % 2) * LANES : (head % 2 + 1) * LANES
                ]
                total = zero_tap * q_scr[half, head, 8 : 8 + TAIL]
                total = total + one * (one_tap * q_scr[half, head, 7 : 7 + TAIL])
                total = total + two * (two_tap * q_scr[half, head, 6 : 6 + TAIL])
                qc_scr[half, head * span : head * span + TAIL] = total.astype(bf16)

    wide = 2 * LANES
    parts = heads * span // wide

    def reach(half):
        lane = lax.broadcasted_iota(jnp.int32, (1, LANES), 1)
        query = first_place[half] + lax.rem(lane, jnp.int32(span))
        lowest = jnp.zeros((1, LANES), jnp.int32)
        for start in starts[1:]:
            lowest = jnp.where(query >= start, start, lowest)
        return query, lowest

    def attend_at_once(windows):
        units = [(half, at) for half in range(2) for at in range(parts)]
        keys_rows, tops, scaled = [], [], []
        for half, window in enumerate(windows):
            first_key = pl.multiple_of(jnp.maximum(first_place[half] + span - window, 0), 16)
            keys_rows.append(pl.ds(first_key, window))
            query, lowest = reach(half)
            places = first_key + lax.broadcasted_iota(jnp.int32, (window, LANES), 0)
            allowed = (places >= lowest) & (places <= query)
            bias_scr[half, :window] = jnp.where(allowed, 0.0, -1e30)
        for slot, (half, at) in enumerate(units):
            window = windows[half]
            queries = qc_scr[half, at * wide : (at + 1) * wide]
            scores = lax.dot_general(
                conv_scr[0, keys_rows[half]], queries, NT, preferred_element_type=f32
            )
            bias = bias_scr[half, :window]
            scores = scores + jnp.concatenate([bias, bias], axis=1)
            s_scr[slot, :window] = scores
            tops.append(jnp.max(scores, axis=0, keepdims=True))
        for slot, (half, at) in enumerate(units):
            window = windows[half]
            grads = do_scr[half, at * wide : (at + 1) * wide]
            prob_grads = lax.dot_general(
                conv_scr[1, keys_rows[half]], grads, NT, preferred_element_type=f32
            )
            weights = jnp.exp2((s_scr[slot, :window] - tops[slot]) * log2_scale)
            s_scr[slot, :window] = weights
            dp_scr[slot, :window] = prob_grads
            total = jnp.sum(weights, axis=0, keepdims=True)
            weighted = jnp.sum(weights * prob_grads, axis=0, keepdims=True)
            inverse = 1.0 / total
            scaled.append((inverse, weighted * inverse, inverse * scale))
        for slot, (half, at) in enumerate(units):
            window = windows[half]
            inverse, mean, slope = scaled[slot]
            weights = s_scr[slot, :window]
            cols = slice(at * wide, (at + 1) * wide)
            p_scr[half, :window, cols] = (weights * inverse).astype(bf16)
            ds_scr[half, :window, cols] = (weights * slope * (dp_scr[slot, :window] - mean)).astype(bf16)
        for half, window in enumerate(windows):
            score_grads = ds_scr[half, :window]
            keys_t = conv_scr[0, keys_rows[half]].T
            dq = lax.dot_general(keys_t, score_grads, NN, preferred_element_type=f32).T
            for head in range(heads):
                dq_scr[half, head, :span] = dq[head * span : (head + 1) * span]
            dkv_scr[0, keys_rows[half]] += lax.dot_general(
                score_grads, qc_scr[half], NN, preferred_element_type=f32
            )
            dkv_scr[1, keys_rows[half]] += lax.dot_general(
                p_scr[half, :window], do_scr[half], NN, preferred_element_type=f32
            )

    def attend(half, window, first_key):
        chunks = 1
        while window // chunks > MAX_CHUNK or window % (16 * chunks):
            chunks += 1
        size = window // chunks
        query, lowest = reach(half)

        def fill_bias(step, carry):
            places = first_key + step * size + lax.broadcasted_iota(jnp.int32, (size, LANES), 0)
            allowed = (places >= lowest) & (places <= query)
            bias_scr[0, pl.ds(aligned(step * size, 16), size)] = jnp.where(allowed, 0.0, -1e30)
            return carry

        loop(chunks, fill_bias, 0, 1)
        whole_window = pl.ds(aligned(first_key, 16), window)
        keys_t = conv_scr[0, whole_window].T if chunks == 1 else None
        for at in range(parts):
            slot = 0
            cols = slice(at * wide, (at + 1) * wide)
            queries = qc_scr[half, cols]
            grads = do_scr[half, cols]

            def key_rows(step):
                return pl.ds(aligned(first_key + step * size, 16), size)

            def score(step, top):
                keys = conv_scr[0, key_rows(step)]
                scores = lax.dot_general(keys, queries, NT, preferred_element_type=f32)
                bias = bias_scr[0, pl.ds(aligned(step * size, 16), size)]
                scores = scores + jnp.concatenate([bias, bias], axis=1)
                s_scr[slot, pl.ds(aligned(step * size, 16), size)] = scores
                return jnp.maximum(top, jnp.max(scores, axis=0, keepdims=True))

            top = loop(chunks, score, jnp.full((1, wide), -1e30, f32), 1)

            def weigh(step, carry):
                total, weighted = carry
                rows = pl.ds(aligned(step * size, 16), size)
                weights = jnp.exp2((s_scr[slot, rows] - top) * log2_scale)
                values = conv_scr[1, key_rows(step)]
                prob_grads = lax.dot_general(values, grads, NT, preferred_element_type=f32)
                s_scr[slot, rows] = weights
                dp_scr[slot, rows] = prob_grads
                total = total + jnp.sum(weights, axis=0, keepdims=True)
                weighted = weighted + jnp.sum(weights * prob_grads, axis=0, keepdims=True)
                return total, weighted

            zeros = jnp.zeros((1, wide), f32)
            total, weighted = loop(chunks, weigh, (zeros, zeros), 1)
            inverse = 1.0 / total
            mean = weighted * inverse
            slope = inverse * scale

            def accumulate(step, dq):
                rows = pl.ds(aligned(step * size, 16), size)
                weights = s_scr[slot, rows]
                probs = (weights * inverse).astype(bf16)
                score_grads = (weights * slope * (dp_scr[slot, rows] - mean)).astype(bf16)
                dk = lax.dot_general(score_grads, queries, NN, preferred_element_type=f32)
                dv = lax.dot_general(probs, grads, NN, preferred_element_type=f32)
                target = pl.ds(aligned(first_key + step * size, 16), size)
                for tensor, terms in enumerate((dk, dv)):
                    dkv_scr[tensor, target] += terms
                if keys_t is not None:
                    return lax.dot_general(keys_t, score_grads, NN, preferred_element_type=f32)
                keys = conv_scr[0, key_rows(step)]
                return dq + lax.dot_general(keys, score_grads, TN, preferred_element_type=f32)

            dq = loop(chunks, accumulate, jnp.zeros((LANES, wide), f32), 1)
            dq = dq.T
            for part in range(wide // span):
                head = at * (wide // span) + part
                dq_scr[half, head, :span] = dq[part * span : (part + 1) * span]

    needed = [first_place[half] // span - firsts[half] + 1 for half in range(2)]
    if direct:
        done = jnp.bool_(False)
        for sizes in WINDOWS:
            sizes = [min(size, ctx_count + 1) for size in sizes]
            fits = (needed[0] <= sizes[0]) & (needed[1] <= sizes[1])

            @pl.when(fits & jnp.logical_not(done))
            def _(sizes=sizes):
                attend_at_once([size * span for size in sizes])

            done = done | fits
    else:
        for half in range(2):
            attend(half, half_rows + half * span, half * (ctx_count - 1 - me) * span)

    next_rows = jnp.where(middle, dq_scr[1, :, :8], 0.0)
    dq_scr[0, :, span:] = next_rows
    dq_scr[1, :, span:] = jnp.zeros_like(next_rows)
    sums = [jnp.zeros((8, LANES), f32) for _ in range(3)]
    for half in range(2):
        one, two = masks(first_place[half], 0)
        ahead_one = same_scr[pl.ds(first_place[half] + 9, span)]
        ahead_two = same_two_scr[pl.ds(first_place[half] + 10, span)]
        zero_tap, one_tap, two_tap = taps(0)

        def finish_head(head, carry, half=half, one=one, two=two, ahead_one=ahead_one, ahead_two=ahead_two):
            lanes = pl.ds(pl.multiple_of(head * LANES, LANES), LANES)
            grads = dq_scr[half, head, :span]
            out = zero_tap * grads
            out = out + ahead_one * (one_tap * dq_scr[half, head, 1 : 1 + span])
            out = out + ahead_two * (two_tap * dq_scr[half, head, 2 : 2 + span])
            dq_ref[half, :, lanes] = out
            dq_tail_ref[half, :, lanes] = out[span - 8 :]
            return (
                carry[0] + fold_rows(grads * q_scr[half, head, 8:]),
                carry[1] + fold_rows(grads * one * q_scr[half, head, 7 : 7 + span]),
                carry[2] + fold_rows(grads * two * q_scr[half, head, 6 : 6 + span]),
            )

        sums = lax.fori_loop(0, heads, finish_head, tuple(sums), unroll=4)
    q_sums = [jnp.sum(term, axis=0, keepdims=True) for term in sums]

    def finish_block(index, carry):
        base = pl.multiple_of(index * span, 8)
        one, two = masks(base, 0)
        ahead_one = same_scr[pl.ds(base + 9, span)]
        ahead_two = same_two_scr[pl.ds(base + 10, span)]
        carry = list(carry)
        for tensor in range(2):
            zero_tap, one_tap, two_tap = taps(tensor + 1)
            own = dkv_scr[tensor, pl.ds(base, span)]
            out = zero_tap * own
            out = out + ahead_one * (one_tap * dkv_scr[tensor, pl.ds(base + 1, span)])
            out = out + ahead_two * (two_tap * dkv_scr[tensor, pl.ds(base + 2, span)])
            lanes = slice(tensor * LANES, (tensor + 1) * LANES)
            terms_scr[index, :, lanes] = out
            at = 3 * tensor
            carry[at] += fold_rows(own * kv_scr[tensor, pl.ds(base + 8, span)])
            carry[at + 1] += fold_rows(own * one * kv_scr[tensor, pl.ds(base + 7, span)])
            carry[at + 2] += fold_rows(own * two * kv_scr[tensor, pl.ds(base + 6, span)])
        return tuple(carry)

    low = me < group

    kv_sums = over_needed(finish_block, (zeros,) * 6)
    for target, index in ((own_far_ref, partner(me, group)), (own_near_ref, me)):
        target[:span] = terms_scr[index]
        target[span : 2 * span] = terms_scr[blocks - 1 - index]

    def send(step, carry):
        flip = step + 1
        owner = partner(me, flip)
        far_owner = partner(me, flip + group)
        near_late = blocks - 1 - owner
        second = jnp.where(low, blocks - 1 - far_owner, owner)
        third = jnp.where(low & (me > owner), owner, near_late)
        first_out[flip][:span] = terms_scr[far_owner].astype(bf16)
        first_out[flip][span : 2 * span] = terms_scr[second].astype(bf16)
        if splits(direct, flip, group):
            late_out[flip][:span] = terms_scr[third].astype(bf16)
        else:
            first_out[flip][2 * span : 3 * span] = terms_scr[third].astype(bf16)
        return carry

    loop(group - 1, send, 0, 16 if direct else 1)
    kv_sums = [jnp.sum(term, axis=0, keepdims=True) for term in kv_sums]

    padding = [jnp.zeros((2, LANES), f32)]
    left = jnp.concatenate(q_sums + kv_sums[:3] + padding, axis=0)
    right = jnp.concatenate([jnp.zeros((3, LANES), f32)] + kv_sums[3:] + padding, axis=0)
    sums_tile = jnp.concatenate([left, right], axis=1)
    sums_pair = jnp.concatenate(split_bits(sums_tile), axis=0)
    own_far_ref[2 * span :] = joined(sums_pair)
    rims = []
    for half in range(2):
        rows = [dq_scr[half, head, :2] for head in range(heads)]
        rows = [jnp.concatenate(rows[at : at + 2], axis=1) for at in range(0, heads, 2)]
        rims.append(jnp.concatenate(rows, axis=0))

    def rim_for(index):
        return jnp.concatenate(split_bits(jnp.where(index < me, rims[0], rims[1])), axis=0)

    def store_rims(step, carry):
        flip = step + 1
        owner = partner(me, flip)
        after = (2 if splits(direct, flip, group) else 3) * span
        first_out[flip][after : after + 16] = sums_pair
        if not direct or flip == group - 1:
            first_out[flip][after + 16 :] = rim_for(partner(owner, group))
        if not direct or flip & (flip + 1) == 0:
            if splits(direct, flip, group):
                late_out[flip][span:] = rim_for(owner)
            else:
                first_out[flip][after + 16 :] = rim_for(owner)
        return carry

    loop(group - 1, store_rims, 0, 16 if direct else 1)


def merge_kernel(ctx_count, direct, own_near_ref, own_far_ref, *refs):
    received_refs, refs = refs[:-6], refs[-6:]
    near_ref, far_ref, half_sums_ref, rims_ref, sums_scr, rim_scr = refs
    f32, bf16 = jnp.float32, jnp.bfloat16
    group = ctx_count // 2
    me = lax.axis_index("ctx")
    low = me < group
    received = Slots((own_far_ref,) + received_refs if direct else received_refs, me)
    place = lax.rem(me, jnp.int32(group))
    span = own_near_ref.shape[0] // 2
    rows = 2 * span
    sums_scr[place] = own_far_ref[rows:]
    def add(step, carry):
        flip = step + 1
        source = partner(me, flip)
        message = received[flip]
        early, second = [message[at * span : (at + 1) * span].astype(f32) for at in range(2)]
        near_early, near_late, far_early, far_late = carry
        zero = jnp.zeros_like(second)
        after = (2 if splits(direct, flip, group) else 3) * span
        sums_scr[partner(place, flip)] = joined(message[after : after + 16])
        near_early = near_early + jnp.where(low, zero, second)
        if not splits(direct, flip, group):
            third = message[2 * span : 3 * span].astype(f32)
            to_early = low & (source > me)
            near_early = near_early + jnp.where(to_early, third, zero)
            near_late = near_late + jnp.where(to_early, zero, third)
            if flip & (flip + 1) == 0:
                rim_scr[source] = joined(message[after + 16 :])
        return near_early, near_late, far_early + early, far_late + jnp.where(low, second, zero)

    neighbours = [jnp.minimum(me + 1, ctx_count - 1), jnp.maximum(me - 1, 0)]
    for index in neighbours:
        rim_scr[index] = jnp.zeros(rim_scr.shape[1:], f32)
    init = (own_near_ref[:span], own_near_ref[span:], own_far_ref[:span], own_far_ref[span:rows])
    totals = loop(group - 1, add, init, 16 if direct else 1)
    near_ref[:span] = totals[0]
    near_ref[span:] = totals[1]
    far_ref[:span] = totals[2].astype(bf16)
    far_ref[span:rows] = totals[3].astype(bf16)
    for at, index in enumerate(neighbours):
        rims_ref[at] = rim_scr[index]
    sums = loop(group, lambda index, carry: carry + sums_scr[index], jnp.zeros((8, 2 * LANES), f32))
    pair = jnp.concatenate(split_bits(sums), axis=0)
    half_sums_ref[...] = joined(pair)
    far_ref[rows : rows + 16] = pair
    far_ref[rows + 16 :] = received[group - 1][rows + 16 :]


def save_kernel(source_ref, target_hbm, sem):
    copy = pltpu.make_async_copy(source_ref, target_hbm, sem)
    copy.start()
    copy.wait()


def sums_kernel(span, half_sums_ref, far_ref, out_ref):
    sums = half_sums_ref[...] + joined(far_ref[2 * span : 2 * span + 16])
    out_ref[0] = sums[0:3, :LANES]
    out_ref[1] = sums[3:6, :LANES]
    out_ref[2] = sums[3:6, LANES:]


def finish_kernel(
    ctx_count, direct, lengths_ref, filters_ref, dq_in_hbm, tail_ref, near_ref, far_ref, rims_ref, *refs
):
    received_refs, refs = refs[:-8], refs[-8:]
    dq_hbm, dk_hbm, dv_hbm, dq_ref, dk_ref, dv_ref, rim_scr, sems = refs
    f32 = jnp.float32
    group = ctx_count // 2
    span = dk_ref.shape[1]
    me = lax.axis_index("ctx")
    low = me < group
    received = Slots((None,) * (group - 1) + received_refs if direct else received_refs, me)
    starts = doc_starts(lengths_ref)
    blocks = 2 * ctx_count
    neighbours = [jnp.minimum(me + 1, ctx_count - 1), jnp.maximum(me - 1, 0)]
    for at, index in enumerate(neighbours):
        rim_scr[index] = rims_ref[at]

    def add(step, carry):
        flip = step + 1
        source = partner(me, flip)
        message = received[flip]
        terms = message[:span].astype(f32)
        if not direct or flip & (flip + 1) == 0:
            rim_scr[source] = joined(message[span:])
        to_early = low & (source > me)
        zero = jnp.zeros_like(terms)
        return carry[0] + jnp.where(to_early, terms, zero), carry[1] + jnp.where(to_early, zero, terms)

    total = near_ref[...] + far_ref[: 2 * span].astype(f32)
    total = (total[:span], total[span:])
    total = add(group - 2, total) if direct else loop(group - 1, add, total, 1)
    for half in range(2):
        dk_ref[half] = total[half][:, :LANES]
        dv_ref[half] = total[half][:, LANES:]
    stores = [
        pltpu.make_async_copy(dk_ref, dk_hbm, sems.at[0]),
        pltpu.make_async_copy(dv_ref, dv_hbm, sems.at[1]),
        pltpu.make_async_copy(dq_ref, dq_hbm.at[:, pl.ds(span - 8, 8)], sems.at[2]),
    ]
    for store in stores[:2]:
        store.start()

    def same(place):
        cut = place >= blocks * span
        for start in starts:
            cut = cut | (place == start)
        return jnp.where(cut, 0.0, 1.0).astype(f32)

    heads = dq_ref.shape[2] // LANES
    taps = [jnp.concatenate([filters_ref[0, tap : tap + 1]] * heads, axis=1) for tap in range(3)]
    row = lax.broadcasted_iota(jnp.int32, dq_ref.shape[1:], 0)
    far_rim = joined(far_ref[2 * span + 16 :])
    crosses = [me == group - 1, me == group]
    first_place = [me * span, (blocks - 1 - me) * span]
    present = [me < ctx_count - 1, me > 0]
    for half in range(2):
        rim = jnp.where(crosses[half], far_rim, rim_scr[neighbours[half]])
        rows = jnp.concatenate([rim[2 * at : 2 * at + 2] for at in range(rim.shape[0] // 2)], axis=1)
        end = first_place[half] + span
        zero, one, two = same(end - 1), same(end), same(end + 1)
        one = jnp.where(present[half], one, 0.0)
        last_but_one = (zero * one) * (taps[2] * rows[0:1])
        last = one * (taps[1] * rows[0:1]) + (one * two) * (taps[2] * rows[1:2])
        extra = jnp.where(row == 6, last_but_one, jnp.where(row == 7, last, 0.0))
        dq_ref[half] = tail_ref[half] + extra
    stores[2].start()
    for store in stores:
        store.wait()


def shards(q_pre, k_pre, value_before_filter, d_out, filters, doc_lengths):
    f32, bf16 = jnp.float32, jnp.bfloat16
    ctx_count = lax.axis_size("ctx")
    span, width = q_pre.shape[1:]
    length = 2 * span * ctx_count
    rim = 4 * width // (2 * LANES)
    vmem = pl.BlockSpec(memory_space=pltpu.VMEM)
    smem = pl.BlockSpec(memory_space=pltpu.SMEM)
    hbm = pl.BlockSpec(memory_space=pltpu.HBM)

    group = ctx_count // 2
    direct = group <= MAX_DIRECT
    halves = [[half * group + at for at in range(group)] for half in range(2)]
    msg_rows = 2 * span + rim

    def whole(shape):
        return pl.BlockSpec(shape, lambda i: (0,) * len(shape))

    def in_hbm(array):
        return pltpu.with_memory_space_constraint(array, pltpu.HBM)

    def flipped(array, flip):
        return lax.ppermute(array, "ctx", [(i, i ^ flip) for i in range(ctx_count)])

    def gathered(array):
        if direct:
            return [flipped(array, flip) for flip in range(1, group)]
        return [lax.all_gather(array, "ctx", axis_index_groups=halves)]

    def delivered(arrays):
        if direct:
            return [flipped(array, step + 1) for step, array in enumerate(arrays)]
        return [lax.all_to_all(arrays[0], "ctx", 0, 0, axis_index_groups=halves, tiled=True)]

    packed = pl.pallas_call(
        pack_kernel,
        out_shape=jax.ShapeDtypeStruct((msg_rows, 2 * LANES), bf16),
        in_specs=[hbm] * 3,
        out_specs=vmem,
        scratch_shapes=[
            pltpu.VMEM(k_pre.shape, bf16),
            pltpu.VMEM(k_pre.shape, bf16),
            pltpu.VMEM((2, TAIL, width), bf16),
            pltpu.SemaphoreType.DMA((3,)),
        ],
        compiler_params=pltpu.CompilerParams(vmem_limit_bytes=4 * MIB),
        name="pack",
    )(*[in_hbm(array) for array in (k_pre, value_before_filter, q_pre)])
    across = flipped(packed, group)
    near = gathered(packed)
    far = gathered(across)
    received = [packed, across] + near + far

    window = span * ctx_count + span
    if direct:
        flips = range(1, group)
        first_shapes = []
        for flip in flips:
            rows = (2 if splits(direct, flip, group) else 3) * span + 16
            rows += 16 if flip == group - 1 or flip & (flip + 1) == 0 else 0
            first_shapes.append((rows, 2 * LANES))
        late_shapes = [(span + 16, 2 * LANES)]
    else:
        first_shapes = [(group, 2 * span + 32, 2 * LANES)]
        late_shapes = [(group, span + 16, 2 * LANES)]
    slots = 4 if direct else 1
    heads = width // LANES
    by_head = (2, span * heads, LANES)
    padded = (2, heads, span + 8, LANES)
    prepared = pl.pallas_call(
        functools.partial(prep_kernel, ctx_count, direct),
        out_shape=[
            jax.ShapeDtypeStruct((length + 16, LANES), f32),
            jax.ShapeDtypeStruct((length + 16, LANES), f32),
            jax.ShapeDtypeStruct(padded, f32),
            jax.ShapeDtypeStruct(by_head, bf16),
            jax.ShapeDtypeStruct(by_head, bf16),
        ],
        in_specs=[smem, vmem, hbm, hbm] + [vmem] * (1 + len(near)),
        out_specs=[vmem] * 5,
        scratch_shapes=[
            pltpu.VMEM((ctx_count, rim, 2 * LANES), f32),
            pltpu.VMEM(q_pre.shape, bf16),
            pltpu.VMEM(q_pre.shape, bf16),
            pltpu.SemaphoreType.DMA((2,)),
        ],
        compiler_params=pltpu.CompilerParams(vmem_limit_bytes=(8 if direct else 32) * MIB),
        name="prep",
    )(doc_lengths, filters, in_hbm(q_pre), in_hbm(d_out), packed, *near)
    scratch = [
        pltpu.VMEM((2, length + 16, LANES), f32),
        pltpu.VMEM((2, length, LANES), bf16),
        pltpu.VMEM((2, length + 8, LANES), f32),
        pltpu.VMEM(padded, f32),
        pltpu.VMEM(by_head, bf16),
        pltpu.VMEM(padded, f32),
        pltpu.VMEM((2, window, LANES), f32),
        pltpu.VMEM((slots, window, 2 * LANES), f32),
        pltpu.VMEM((slots, window, 2 * LANES), f32),
        pltpu.VMEM((2 * ctx_count, span, 2 * LANES), f32),
        pltpu.VMEM((2, window, heads * span) if direct else (2, 16, LANES), bf16),
        pltpu.VMEM((2, window, heads * span) if direct else (2, 16, LANES), bf16),
    ]
    own_shapes = [(2 * span, 2 * LANES), (2 * span + 8, 2 * LANES)]
    d_q_main, d_q_tail, own_near, own_far, *sent = pl.pallas_call(
        functools.partial(grads_kernel, ctx_count, direct),
        out_shape=[jax.ShapeDtypeStruct(q_pre.shape, f32)]
        + [jax.ShapeDtypeStruct(shape, f32) for shape in [(2, 8, width)] + own_shapes]
        + [jax.ShapeDtypeStruct(shape, bf16) for shape in first_shapes + late_shapes],
        in_specs=[smem, vmem] + [vmem] * (len(prepared) + len(received)),
        out_specs=[vmem] * (4 + len(first_shapes + late_shapes)),
        scratch_shapes=scratch,
        compiler_params=pltpu.CompilerParams(vmem_limit_bytes=(20 if direct else 62) * MIB),
        name="grads",
    )(doc_lengths, filters, *prepared, *received)
    d_q_main = pl.pallas_call(
        save_kernel,
        out_shape=jax.ShapeDtypeStruct(q_pre.shape, f32),
        in_specs=[vmem],
        out_specs=hbm,
        scratch_shapes=[pltpu.SemaphoreType.DMA(())],
        compiler_params=pltpu.CompilerParams(vmem_limit_bytes=2 * MIB),
        name="save",
    )(d_q_main)
    half_terms = delivered(sent[: len(first_shapes)])
    d_q_main, *half_terms = lax.optimization_barrier((d_q_main, *half_terms))
    merged_shapes = [
        jax.ShapeDtypeStruct((2 * span, 2 * LANES), f32),
        jax.ShapeDtypeStruct((2 * span + 32, 2 * LANES), bf16),
        jax.ShapeDtypeStruct((8, 2 * LANES), f32),
        jax.ShapeDtypeStruct((2, rim // 2, 2 * LANES), f32),
    ]
    near, far, half_sums, rims = pl.pallas_call(
        functools.partial(merge_kernel, ctx_count, direct),
        out_shape=merged_shapes,
        in_specs=[vmem] * (2 + len(half_terms)),
        out_specs=[vmem] * len(merged_shapes),
        scratch_shapes=[
            pltpu.VMEM((group, 8, 2 * LANES), f32),
            pltpu.VMEM((ctx_count, rim // 2, 2 * LANES), f32),
        ],
        compiler_params=pltpu.CompilerParams(vmem_limit_bytes=(4 if direct else 40) * MIB),
        name="merge",
    )(own_near, own_far, *half_terms)
    from_half = flipped(far, group)
    late_terms = sent[len(first_shapes) :]
    late_terms = [flipped(late_terms[0], group - 1)] if direct else delivered(late_terms)

    sums = pl.pallas_call(
        functools.partial(sums_kernel, span),
        out_shape=jax.ShapeDtypeStruct(filters.shape, f32),
        in_specs=[vmem, vmem],
        out_specs=vmem,
        compiler_params=pltpu.CompilerParams(vmem_limit_bytes=2 * MIB),
        name="sums",
    )(half_sums, from_half)
    count = lax.axis_size("tp")
    all_sums = [sums] + [
        lax.ppermute(sums, "tp", [(i, i ^ flip) for i in range(count)]) for flip in range(1, count)
    ]
    d_q_pre, d_k_pre, d_v_pre = pl.pallas_call(
        functools.partial(finish_kernel, ctx_count, direct),
        out_shape=(
            jax.ShapeDtypeStruct(q_pre.shape, f32),
            jax.ShapeDtypeStruct(k_pre.shape, f32),
            jax.ShapeDtypeStruct(k_pre.shape, f32),
        ),
        in_specs=[smem, vmem, hbm] + [vmem] * (4 + len(late_terms)),
        out_specs=(hbm, hbm, hbm),
        scratch_shapes=[
            pltpu.VMEM((2, 8, width), f32),
            pltpu.VMEM(k_pre.shape, f32),
            pltpu.VMEM(k_pre.shape, f32),
            pltpu.VMEM((ctx_count, rim // 2, 2 * LANES), f32),
            pltpu.SemaphoreType.DMA((3,)),
        ],
        input_output_aliases={2: 0},
        compiler_params=pltpu.CompilerParams(vmem_limit_bytes=(4 if direct else 16) * MIB),
        name="finish",
    )(doc_lengths, filters, d_q_main, d_q_tail, near, from_half, rims, *late_terms)
    while len(all_sums) > 1:
        all_sums = [all_sums[at] + all_sums[at + 1] for at in range(0, len(all_sums), 2)]
    return (d_q_pre, d_k_pre, d_v_pre, all_sums[0])


def solution(mesh):
    split = P(None, "ctx", "tp")
    return jax.shard_map(
        shards,
        mesh=mesh,
        in_specs=(split, split, split, split, P(), P()),
        out_specs=(split, split, split, P()),
        check_vma=False,
    )
```

```python
import functools

import jax
import jax.numpy as jnp
import numpy as np
from jax import lax
from jax.experimental import pallas as pl
from jax.experimental.pallas import tpu as pltpu
from jax.sharding import PartitionSpec as P

LANES = 128
NT = (((1,), (1,)), ((), ()))
NN = (((1,), (0,)), ((), ()))
TN = (((0,), (0,)), ((), ()))
TAIL = 16
MAX_CHUNK = 640
RIM = 8
MAX_DIRECT = 4
WINDOWS = ((2, 2), (4, 4), (2, 9), (6, 6), (8, 4), (4, 9), (6, 9), (8, 9))
MIB = 1 << 20


def loop(count, body, init, unrolled=16):
    if count <= unrolled:
        for step in range(count):
            init = body(step, init)
        return init
    return lax.fori_loop(0, count, body, init)


def aligned(start, multiple):
    return start if isinstance(start, int) else pl.multiple_of(start, multiple)


def doc_starts(lengths_ref):
    starts = [jnp.int32(0)]
    for index in range(lengths_ref.shape[0] - 1):
        starts.append(starts[-1] + lengths_ref[index])
    return starts


def fold_rows(terms):
    rows, lanes = terms.shape
    return jnp.sum(terms.reshape(rows // 8, 8, lanes), axis=0)


def split_bits(values):
    high = values.astype(jnp.bfloat16)
    low = (values - high.astype(jnp.float32)).astype(jnp.bfloat16)
    return high, low


def joined(pair):
    rows = pair.shape[0] // 2
    pair = pair.astype(jnp.float32)
    return pair[:rows] + pair[rows:]


class Slots:
    def __init__(self, refs, me):
        self.refs, self.me = refs, me

    def __getitem__(self, flip):
        if len(self.refs) == 1:
            place = lax.rem(self.me, jnp.int32(self.refs[0].shape[0]))
            return self.refs[0].at[partner(place, flip)]
        return self.refs[flip]


def splits(direct, flip, group):
    return not direct or flip == group - 1


def partner(me, flip):
    return lax.bitwise_xor(me, jnp.int32(flip))


def pack_kernel(k_hbm, v_hbm, q_hbm, out_ref, k_ref, v_ref, q_ref, sems):
    span = k_ref.shape[1]
    loads = [
        pltpu.make_async_copy(k_hbm, k_ref, sems.at[0]),
        pltpu.make_async_copy(v_hbm, v_ref, sems.at[1]),
        pltpu.make_async_copy(q_hbm.at[:, pl.ds(span - TAIL, TAIL)], q_ref, sems.at[2]),
    ]
    for load in loads:
        load.start()
    for load in loads:
        load.wait()
    kv = jnp.concatenate([k_ref[...], v_ref[...]], axis=2).reshape(2 * span, 2 * LANES)
    tails = []
    for half in range(2):
        last = q_ref[half].astype(jnp.float32)[TAIL - 2 :]
        tails += [last[:, at : at + 2 * LANES] for at in range(0, last.shape[1], 2 * LANES)]
    out_ref[: 2 * span] = kv
    out_ref[2 * span :] = jnp.concatenate(tails, axis=0).astype(jnp.bfloat16)


def prep_kernel(ctx_count, direct, lengths_ref, filters_ref, q_hbm, d_out_hbm, own_ref, *refs):
    near_refs, refs = refs[:-9], refs[-9:]
    same_ref, same_two_ref, q_scr, qc_ref, do_ref, rim_scr, q_ref, d_out_ref, sems = refs
    f32, bf16 = jnp.float32, jnp.bfloat16
    loads = [
        pltpu.make_async_copy(q_hbm, q_ref, sems.at[0]),
        pltpu.make_async_copy(d_out_hbm, d_out_ref, sems.at[1]),
    ]
    for load in loads:
        load.start()
    group = ctx_count // 2
    span = q_ref.shape[1]
    heads = q_ref.shape[2] // LANES
    blocks = 2 * ctx_count
    length = span * blocks
    me = lax.axis_index("ctx")
    near = Slots((None,) + near_refs if direct else near_refs, me)
    starts = doc_starts(lengths_ref)

    def fill(index, carry):
        rows = pl.ds(aligned(8 + index * span, 8), span)
        same_ref[rows] = jnp.ones((span, LANES), f32)
        same_two_ref[rows] = jnp.ones((span, LANES), f32)
        return carry

    lax.fori_loop(0, blocks, fill, 0, unroll=2)
    zeros = jnp.zeros((8, LANES), f32)
    for rows in (slice(0, 8), slice(8 + length, 16 + length)):
        same_ref[rows] = zeros
        same_two_ref[rows] = zeros
    for start in starts:
        same_ref[pl.ds(8 + start, 1)] = zeros[:1]
        same_two_ref[pl.ds(8 + start, 1)] = zeros[:1]
        same_two_ref[pl.ds(9 + start, 1)] = zeros[:1]

    before, after = jnp.maximum(me - 1, 0), jnp.minimum(me + 1, ctx_count - 1)
    for index in (before, after):
        rim_scr[index] = jnp.zeros(rim_scr.shape[1:], f32)
    rim_scr[me] = own_ref[2 * span :].astype(f32)

    def place_rims(step, carry):
        flip = step + 1
        if not direct or flip & (flip + 1) == 0:
            rim_scr[partner(me, flip)] = near[flip][2 * span :].astype(f32)
        return carry

    loop(group - 1, place_rims, 0, 16 if direct else 1)
    rim_before, rim_after = rim_scr[before], rim_scr[after]
    late_rim = jnp.where(me == ctx_count - 1, rim_after[:RIM], rim_after[RIM:])
    rims = [rim_before[:RIM], late_rim]
    first_place = [me * span, (blocks - 1 - me) * span]
    taps = [filters_ref[0, tap : tap + 1] for tap in range(3)]

    for load in loads:
        load.wait()
    for half in range(2):
        rows = pl.ds(aligned(first_place[half] + 8, 8), span)
        one, two = same_ref[rows], same_two_ref[rows]
        for head in range(heads):
            at = 2 * (head // 2)
            q_scr[half, head, 6:8] = rims[half][at : at + 2, (head % 2) * LANES : (head % 2 + 1) * LANES]

        def convolve_head(head, carry, half=half, one=one, two=two):
            lanes = pl.ds(pl.multiple_of(head * LANES, LANES), LANES)
            target = pl.ds(pl.multiple_of(head * span, 16), span)
            q_scr[half, head, 8:] = q_ref[half, :, lanes].astype(f32)
            total = taps[0] * q_scr[half, head, 8:]
            total = total + one * (taps[1] * q_scr[half, head, 7 : 7 + span])
            total = total + two * (taps[2] * q_scr[half, head, 6 : 6 + span])
            qc_ref[half, target] = total.astype(bf16)
            do_ref[half, target] = d_out_ref[half, :, lanes]
            return carry

        lax.fori_loop(0, heads, convolve_head, 0, unroll=4)


def grads_kernel(ctx_count, direct, lengths_ref, filters_ref, *refs):
    group = ctx_count // 2
    arrays = group - 1 if direct else 1
    same_scr, same_two_scr, q_in_ref, qc_in_ref, do_scr, own_ref, across_ref = refs[:7]
    refs = refs[7:]
    near_in, far_in, refs = refs[:arrays], refs[arrays : 2 * arrays], refs[2 * arrays :]
    dq_ref, dq_tail_ref, own_near_ref, own_far_ref = refs[:4]
    arrays = group - 1 if direct else 1
    first_out, late_out, refs = refs[4 : 4 + arrays], refs[4 + arrays : 5 + arrays], refs[5 + arrays :]
    kv_scr, conv_scr, dkv_scr, q_scr, qc_scr, dq_scr = refs[:6]
    bias_scr, s_scr, dp_scr, terms_scr, p_scr, ds_scr = refs[6:]
    f32, bf16 = jnp.float32, jnp.bfloat16
    span = own_ref.shape[0] // 2 - TAIL // 2
    heads = q_in_ref.shape[1]
    half_rows = span * ctx_count
    length = 2 * half_rows
    blocks = 2 * ctx_count
    me = lax.axis_index("ctx")
    near_in = Slots((None,) + near_in if direct else near_in, me)
    far_in = Slots((None,) + far_in if direct else far_in, me)
    first_out = Slots((None,) + first_out if direct else first_out, me)
    late_out = Slots((None,) * (group - 1) + late_out if direct else late_out, me)
    scale = LANES**-0.5
    log2_scale = scale * 1.4426950408889634
    starts = doc_starts(lengths_ref)

    def place(index, block):
        for tensor in range(2):
            lanes = slice(tensor * LANES, (tensor + 1) * LANES)
            kv_scr[tensor, pl.ds(aligned(8 + index * span, 8), span)] = block[:, lanes].astype(f32)

    def place_both(message, index):
        place(index, message[:span])
        place(blocks - 1 - index, message[span : 2 * span])

    def place_received(step, carry):
        flip = step + 1
        source = partner(me, flip)
        place_both(near_in[flip], source)
        place_both(far_in[flip], partner(source, group))
        return carry

    zeros = jnp.zeros((8, LANES), f32)
    for tensor in range(2):
        kv_scr[tensor, :8] = zeros
    for block_ref, index in ((own_ref, me), (across_ref, partner(me, group))):
        place_both(block_ref, index)
    loop(group - 1, place_received, 0, 16 if direct else 1)

    def taps(tensor):
        return [filters_ref[tensor, tap : tap + 1] for tap in range(3)]

    def masks(base, ahead):
        one = same_scr[pl.ds(base + 8 + min(ahead, 1), span)]
        return one, same_two_scr[pl.ds(base + 8 + ahead, span)]

    def convolve_kv(index, carry):
        base = index * span
        one, two = masks(base, 0)
        for tensor in range(2):
            zero_tap, one_tap, two_tap = taps(tensor + 1)
            total = zero_tap * kv_scr[tensor, pl.ds(aligned(base + 8, 8), span)]
            total = total + one * (one_tap * kv_scr[tensor, pl.ds(base + 7, span)])
            total = total + two * (two_tap * kv_scr[tensor, pl.ds(base + 6, span)])
            conv_scr[tensor, pl.ds(aligned(base, 16), span)] = total.astype(bf16)
        return carry

    first_place = [me * span, (blocks - 1 - me) * span]
    firsts = []
    for half in range(2):
        lowest = jnp.int32(0)
        for start in starts[1:]:
            lowest = jnp.where(first_place[half] >= start, start, lowest)
        firsts.append(lowest // span)

    def over_needed(body, init):
        carry = lax.fori_loop(firsts[0], me + 1, body, init)
        return lax.fori_loop(jnp.maximum(firsts[1], me + 1), blocks - me, body, carry)

    def clear(index, carry):
        for tensor in range(2):
            rows = pl.ds(pl.multiple_of(index * span, 16), span)
            conv_scr[tensor, rows] = jnp.zeros((span, LANES), bf16)
            dkv_scr[tensor, rows] = jnp.zeros((span, LANES), f32)
        terms_scr[index] = jnp.zeros((span, 2 * LANES), f32)
        return carry

    lax.fori_loop(0, blocks, clear, 0, unroll=2)
    for tensor in range(2):
        dkv_scr[tensor, length:] = zeros
    over_needed(convolve_kv, 0)

    middle = me == ctx_count - 1
    q_scr[...] = q_in_ref[...]
    qc_scr[...] = qc_in_ref[...]
    tails = far_in[group - 1][2 * span :].astype(f32)
    tails = [tails[:RIM], tails[RIM:]]
    for half, crossing in ((0, me == group), (1, me == group - 1)):

        @pl.when(crossing)
        def _(half=half):
            rows = pl.ds(aligned(first_place[half] + 8, 8), TAIL)
            one, two = same_scr[rows], same_two_scr[rows]
            zero_tap, one_tap, two_tap = taps(0)
            for head in range(heads):
                at = 2 * (head // 2)
                q_scr[half, head, 6:8] = tails[half][
                    at : at + 2, (head % 2) * LANES : (head % 2 + 1) * LANES
                ]
                total = zero_tap * q_scr[half, head, 8 : 8 + TAIL]
                total = total + one * (one_tap * q_scr[half, head, 7 : 7 + TAIL])
                total = total + two * (two_tap * q_scr[half, head, 6 : 6 + TAIL])
                qc_scr[half, head * span : head * span + TAIL] = total.astype(bf16)

    wide = 2 * LANES
    parts = heads * span // wide

    def reach(half):
        lane = lax.broadcasted_iota(jnp.int32, (1, LANES), 1)
        query = first_place[half] + lax.rem(lane, jnp.int32(span))
        lowest = jnp.zeros((1, LANES), jnp.int32)
        for start in starts[1:]:
            lowest = jnp.where(query >= start, start, lowest)
        return query, lowest

    def attend_at_once(windows):
        units = [(half, at) for half in range(2) for at in range(parts)]
        keys_rows, tops, scaled = [], [], []
        for half, window in enumerate(windows):
            first_key = pl.multiple_of(jnp.maximum(first_place[half] + span - window, 0), 16)
            keys_rows.append(pl.ds(first_key, window))
            query, lowest = reach(half)
            places = first_key + lax.broadcasted_iota(jnp.int32, (window, LANES), 0)
            allowed = (places >= lowest) & (places <= query)
            bias_scr[half, :window] = jnp.where(allowed, 0.0, -1e30)
        for slot, (half, at) in enumerate(units):
            window = windows[half]
            queries = qc_scr[half, at * wide : (at + 1) * wide]
            scores = lax.dot_general(
                conv_scr[0, keys_rows[half]], queries, NT, preferred_element_type=f32
            )
            bias = bias_scr[half, :window]
            scores = scores * log2_scale + jnp.concatenate([bias, bias], axis=1)
            s_scr[slot, :window] = scores
            tops.append(jnp.max(scores, axis=0, keepdims=True))
        for slot, (half, at) in enumerate(units):
            window = windows[half]
            grads = do_scr[half, at * wide : (at + 1) * wide]
            prob_grads = lax.dot_general(
                conv_scr[1, keys_rows[half]], grads, NT, preferred_element_type=f32
            )
            dp_scr[slot, :window] = prob_grads
            weights = jnp.exp2(s_scr[slot, :window] - tops[slot])
            total = jnp.sum(weights, axis=0, keepdims=True)
            weighted = jnp.sum(weights * prob_grads, axis=0, keepdims=True)
            scaled.append((tops[slot] + jnp.log2(total), weighted / total))
        for slot, (half, at) in enumerate(units):
            window = windows[half]
            log_total, mean = scaled[slot]
            probs = jnp.exp2(s_scr[slot, :window] - log_total)
            cols = slice(at * wide, (at + 1) * wide)
            p_scr[half, :window, cols] = probs.astype(bf16)
            score_grads = probs * (dp_scr[slot, :window] - mean) * scale
            ds_scr[half, :window, cols] = score_grads.astype(bf16)
        for half, window in enumerate(windows):
            score_grads = ds_scr[half, :window]
            keys_t = conv_scr[0, keys_rows[half]].T
            dq = lax.dot_general(keys_t, score_grads, NN, preferred_element_type=f32).T
            for head in range(heads):
                dq_scr[half, head, :span] = dq[head * span : (head + 1) * span]
            dkv_scr[0, keys_rows[half]] += lax.dot_general(
                score_grads, qc_scr[half], NN, preferred_element_type=f32
            )
            dkv_scr[1, keys_rows[half]] += lax.dot_general(
                p_scr[half, :window], do_scr[half], NN, preferred_element_type=f32
            )

    def attend(half, window, first_key):
        chunks = 1
        while window // chunks > MAX_CHUNK or window % (16 * chunks):
            chunks += 1
        size = window // chunks
        query, lowest = reach(half)

        def fill_bias(step, carry):
            places = first_key + step * size + lax.broadcasted_iota(jnp.int32, (size, LANES), 0)
            allowed = (places >= lowest) & (places <= query)
            bias_scr[0, pl.ds(aligned(step * size, 16), size)] = jnp.where(allowed, 0.0, -1e30)
            return carry

        loop(chunks, fill_bias, 0, 1)
        whole_window = pl.ds(aligned(first_key, 16), window)
        keys_t = conv_scr[0, whole_window].T if chunks == 1 else None
        for at in range(parts):
            slot = 0
            cols = slice(at * wide, (at + 1) * wide)
            queries = qc_scr[half, cols]
            grads = do_scr[half, cols]

            def key_rows(step):
                return pl.ds(aligned(first_key + step * size, 16), size)

            def score(step, top):
                keys = conv_scr[0, key_rows(step)]
                scores = lax.dot_general(keys, queries, NT, preferred_element_type=f32)
                bias = bias_scr[0, pl.ds(aligned(step * size, 16), size)]
                scores = scores + jnp.concatenate([bias, bias], axis=1)
                s_scr[slot, pl.ds(aligned(step * size, 16), size)] = scores
                return jnp.maximum(top, jnp.max(scores, axis=0, keepdims=True))

            top = loop(chunks, score, jnp.full((1, wide), -1e30, f32), 1)

            def weigh(step, carry):
                total, weighted = carry
                rows = pl.ds(aligned(step * size, 16), size)
                weights = jnp.exp2((s_scr[slot, rows] - top) * log2_scale)
                values = conv_scr[1, key_rows(step)]
                prob_grads = lax.dot_general(values, grads, NT, preferred_element_type=f32)
                s_scr[slot, rows] = weights
                dp_scr[slot, rows] = prob_grads
                total = total + jnp.sum(weights, axis=0, keepdims=True)
                weighted = weighted + jnp.sum(weights * prob_grads, axis=0, keepdims=True)
                return total, weighted

            zeros = jnp.zeros((1, wide), f32)
            total, weighted = loop(chunks, weigh, (zeros, zeros), 1)
            inverse = 1.0 / total
            mean = weighted * inverse
            slope = inverse * scale

            def accumulate(step, dq):
                rows = pl.ds(aligned(step * size, 16), size)
                weights = s_scr[slot, rows]
                probs = (weights * inverse).astype(bf16)
                score_grads = (weights * slope * (dp_scr[slot, rows] - mean)).astype(bf16)
                dk = lax.dot_general(score_grads, queries, NN, preferred_element_type=f32)
                dv = lax.dot_general(probs, grads, NN, preferred_element_type=f32)
                target = pl.ds(aligned(first_key + step * size, 16), size)
                for tensor, terms in enumerate((dk, dv)):
                    dkv_scr[tensor, target] += terms
                if keys_t is not None:
                    return lax.dot_general(keys_t, score_grads, NN, preferred_element_type=f32)
                keys = conv_scr[0, key_rows(step)]
                return dq + lax.dot_general(keys, score_grads, TN, preferred_element_type=f32)

            dq = loop(chunks, accumulate, jnp.zeros((LANES, wide), f32), 1)
            dq = dq.T
            for part in range(wide // span):
                head = at * (wide // span) + part
                dq_scr[half, head, :span] = dq[part * span : (part + 1) * span]

    needed = [first_place[half] // span - firsts[half] + 1 for half in range(2)]
    if direct:
        done = jnp.bool_(False)
        for sizes in WINDOWS:
            sizes = [min(size, ctx_count + half) for half, size in enumerate(sizes)]
            fits = (needed[0] <= sizes[0]) & (needed[1] <= sizes[1])

            @pl.when(fits & jnp.logical_not(done))
            def _(sizes=sizes):
                attend_at_once([size * span for size in sizes])

            done = done | fits
    else:
        for half in range(2):
            attend(half, half_rows + half * span, half * (ctx_count - 1 - me) * span)

    next_rows = jnp.where(middle, dq_scr[1, :, :8], 0.0)
    dq_scr[0, :, span:] = next_rows
    dq_scr[1, :, span:] = jnp.zeros_like(next_rows)
    sums = [jnp.zeros((8, LANES), f32) for _ in range(3)]
    for half in range(2):
        one, two = masks(first_place[half], 0)
        ahead_one = same_scr[pl.ds(first_place[half] + 9, span)]
        ahead_two = same_two_scr[pl.ds(first_place[half] + 10, span)]
        zero_tap, one_tap, two_tap = taps(0)

        def finish_head(head, carry, half=half, one=one, two=two, ahead_one=ahead_one, ahead_two=ahead_two):
            lanes = pl.ds(pl.multiple_of(head * LANES, LANES), LANES)
            grads = dq_scr[half, head, :span]
            out = zero_tap * grads
            out = out + ahead_one * (one_tap * dq_scr[half, head, 1 : 1 + span])
            out = out + ahead_two * (two_tap * dq_scr[half, head, 2 : 2 + span])
            dq_ref[half, :, lanes] = out
            dq_tail_ref[half, :, lanes] = out[span - 8 :]
            return (
                carry[0] + fold_rows(grads * q_scr[half, head, 8:]),
                carry[1] + fold_rows(grads * one * q_scr[half, head, 7 : 7 + span]),
                carry[2] + fold_rows(grads * two * q_scr[half, head, 6 : 6 + span]),
            )

        sums = lax.fori_loop(0, heads, finish_head, tuple(sums), unroll=4)
    q_sums = [jnp.sum(term, axis=0, keepdims=True) for term in sums]

    def finish_block(index, carry):
        base = pl.multiple_of(index * span, 8)
        one, two = masks(base, 0)
        ahead_one = same_scr[pl.ds(base + 9, span)]
        ahead_two = same_two_scr[pl.ds(base + 10, span)]
        carry = list(carry)
        for tensor in range(2):
            zero_tap, one_tap, two_tap = taps(tensor + 1)
            own = dkv_scr[tensor, pl.ds(base, span)]
            out = zero_tap * own
            out = out + ahead_one * (one_tap * dkv_scr[tensor, pl.ds(base + 1, span)])
            out = out + ahead_two * (two_tap * dkv_scr[tensor, pl.ds(base + 2, span)])
            lanes = slice(tensor * LANES, (tensor + 1) * LANES)
            terms_scr[index, :, lanes] = out
            at = 3 * tensor
            carry[at] += fold_rows(own * kv_scr[tensor, pl.ds(base + 8, span)])
            carry[at + 1] += fold_rows(own * one * kv_scr[tensor, pl.ds(base + 7, span)])
            carry[at + 2] += fold_rows(own * two * kv_scr[tensor, pl.ds(base + 6, span)])
        return tuple(carry)

    low = me < group

    kv_sums = over_needed(finish_block, (zeros,) * 6)
    for target, index in ((own_far_ref, partner(me, group)), (own_near_ref, me)):
        target[:span] = terms_scr[index]
        target[span : 2 * span] = terms_scr[blocks - 1 - index]

    def send(step, carry):
        flip = step + 1
        owner = partner(me, flip)
        far_owner = partner(me, flip + group)
        near_late = blocks - 1 - owner
        second = jnp.where(low, blocks - 1 - far_owner, owner)
        third = jnp.where(low & (me > owner), owner, near_late)
        first_out[flip][:span] = terms_scr[far_owner].astype(bf16)
        first_out[flip][span : 2 * span] = terms_scr[second].astype(bf16)
        if splits(direct, flip, group):
            late_out[flip][:span] = terms_scr[third].astype(bf16)
        else:
            first_out[flip][2 * span : 3 * span] = terms_scr[third].astype(bf16)
        return carry

    loop(group - 1, send, 0, 16 if direct else 1)
    kv_sums = [jnp.sum(term, axis=0, keepdims=True) for term in kv_sums]

    padding = [jnp.zeros((2, LANES), f32)]
    left = jnp.concatenate(q_sums + kv_sums[:3] + padding, axis=0)
    right = jnp.concatenate([jnp.zeros((3, LANES), f32)] + kv_sums[3:] + padding, axis=0)
    sums_tile = jnp.concatenate([left, right], axis=1)
    sums_pair = jnp.concatenate(split_bits(sums_tile), axis=0)
    own_far_ref[2 * span :] = joined(sums_pair)
    rims = []
    for half in range(2):
        rows = [dq_scr[half, head, :2] for head in range(heads)]
        rows = [jnp.concatenate(rows[at : at + 2], axis=1) for at in range(0, heads, 2)]
        rims.append(jnp.concatenate(rows, axis=0))

    def rim_for(index):
        return jnp.concatenate(split_bits(jnp.where(index < me, rims[0], rims[1])), axis=0)

    def store_rims(step, carry):
        flip = step + 1
        owner = partner(me, flip)
        after = (2 if splits(direct, flip, group) else 3) * span
        first_out[flip][after : after + 16] = sums_pair
        if not direct or flip == group - 1:
            first_out[flip][after + 16 :] = rim_for(partner(owner, group))
        if not direct or flip & (flip + 1) == 0:
            if splits(direct, flip, group):
                late_out[flip][span:] = rim_for(owner)
            else:
                first_out[flip][after + 16 :] = rim_for(owner)
        return carry

    loop(group - 1, store_rims, 0, 16 if direct else 1)


def merge_kernel(ctx_count, direct, own_near_ref, own_far_ref, *refs):
    received_refs, refs = refs[:-6], refs[-6:]
    near_ref, far_ref, half_sums_ref, rims_ref, sums_scr, rim_scr = refs
    f32, bf16 = jnp.float32, jnp.bfloat16
    group = ctx_count // 2
    me = lax.axis_index("ctx")
    low = me < group
    received = Slots((own_far_ref,) + received_refs if direct else received_refs, me)
    place = lax.rem(me, jnp.int32(group))
    span = own_near_ref.shape[0] // 2
    rows = 2 * span
    sums_scr[place] = own_far_ref[rows:]
    def add(step, carry):
        flip = step + 1
        source = partner(me, flip)
        message = received[flip]
        early, second = [message[at * span : (at + 1) * span].astype(f32) for at in range(2)]
        near_early, near_late, far_early, far_late = carry
        zero = jnp.zeros_like(second)
        after = (2 if splits(direct, flip, group) else 3) * span
        sums_scr[partner(place, flip)] = joined(message[after : after + 16])
        near_early = near_early + jnp.where(low, zero, second)
        if not splits(direct, flip, group):
            third = message[2 * span : 3 * span].astype(f32)
            to_early = low & (source > me)
            near_early = near_early + jnp.where(to_early, third, zero)
            near_late = near_late + jnp.where(to_early, zero, third)
            if flip & (flip + 1) == 0:
                rim_scr[source] = joined(message[after + 16 :])
        return near_early, near_late, far_early + early, far_late + jnp.where(low, second, zero)

    neighbours = [jnp.minimum(me + 1, ctx_count - 1), jnp.maximum(me - 1, 0)]
    for index in neighbours:
        rim_scr[index] = jnp.zeros(rim_scr.shape[1:], f32)
    init = (own_near_ref[:span], own_near_ref[span:], own_far_ref[:span], own_far_ref[span:rows])
    totals = loop(group - 1, add, init, 16 if direct else 1)
    near_ref[:span] = totals[0]
    near_ref[span:] = totals[1]
    far_ref[:span] = totals[2].astype(bf16)
    far_ref[span:rows] = totals[3].astype(bf16)
    for at, index in enumerate(neighbours):
        rims_ref[at] = rim_scr[index]
    sums = loop(group, lambda index, carry: carry + sums_scr[index], jnp.zeros((8, 2 * LANES), f32))
    pair = jnp.concatenate(split_bits(sums), axis=0)
    half_sums_ref[...] = joined(pair)
    far_ref[rows : rows + 16] = pair
    far_ref[rows + 16 :] = received[group - 1][rows + 16 :]


def save_kernel(source_ref, target_hbm, sem):
    copy = pltpu.make_async_copy(source_ref, target_hbm, sem)
    copy.start()
    copy.wait()


def sums_kernel(span, half_sums_ref, far_ref, out_ref):
    sums = half_sums_ref[...] + joined(far_ref[2 * span : 2 * span + 16])
    out_ref[0] = sums[0:3, :LANES]
    out_ref[1] = sums[3:6, :LANES]
    out_ref[2] = sums[3:6, LANES:]


def finish_kernel(
    ctx_count, direct, lengths_ref, filters_ref, dq_in_hbm, tail_ref, near_ref, far_ref, rims_ref, *refs
):
    received_refs, refs = refs[:-8], refs[-8:]
    dq_hbm, dk_hbm, dv_hbm, dq_ref, dk_ref, dv_ref, rim_scr, sems = refs
    f32 = jnp.float32
    group = ctx_count // 2
    span = dk_ref.shape[1]
    me = lax.axis_index("ctx")
    low = me < group
    received = Slots((None,) * (group - 1) + received_refs if direct else received_refs, me)
    starts = doc_starts(lengths_ref)
    blocks = 2 * ctx_count
    neighbours = [jnp.minimum(me + 1, ctx_count - 1), jnp.maximum(me - 1, 0)]
    for at, index in enumerate(neighbours):
        rim_scr[index] = rims_ref[at]

    def add(step, carry):
        flip = step + 1
        source = partner(me, flip)
        message = received[flip]
        terms = message[:span].astype(f32)
        if not direct or flip & (flip + 1) == 0:
            rim_scr[source] = joined(message[span:])
        to_early = low & (source > me)
        zero = jnp.zeros_like(terms)
        return carry[0] + jnp.where(to_early, terms, zero), carry[1] + jnp.where(to_early, zero, terms)

    total = near_ref[...] + far_ref[: 2 * span].astype(f32)
    total = (total[:span], total[span:])
    total = add(group - 2, total) if direct else loop(group - 1, add, total, 1)
    for half in range(2):
        dk_ref[half] = total[half][:, :LANES]
        dv_ref[half] = total[half][:, LANES:]
    stores = [
        pltpu.make_async_copy(dk_ref, dk_hbm, sems.at[0]),
        pltpu.make_async_copy(dv_ref, dv_hbm, sems.at[1]),
        pltpu.make_async_copy(dq_ref, dq_hbm.at[:, pl.ds(span - 8, 8)], sems.at[2]),
    ]
    for store in stores[:2]:
        store.start()

    def same(place):
        cut = place >= blocks * span
        for start in starts:
            cut = cut | (place == start)
        return jnp.where(cut, 0.0, 1.0).astype(f32)

    heads = dq_ref.shape[2] // LANES
    taps = [jnp.concatenate([filters_ref[0, tap : tap + 1]] * heads, axis=1) for tap in range(3)]
    row = lax.broadcasted_iota(jnp.int32, dq_ref.shape[1:], 0)
    far_rim = joined(far_ref[2 * span + 16 :])
    crosses = [me == group - 1, me == group]
    first_place = [me * span, (blocks - 1 - me) * span]
    present = [me < ctx_count - 1, me > 0]
    for half in range(2):
        rim = jnp.where(crosses[half], far_rim, rim_scr[neighbours[half]])
        rows = jnp.concatenate([rim[2 * at : 2 * at + 2] for at in range(rim.shape[0] // 2)], axis=1)
        end = first_place[half] + span
        zero, one, two = same(end - 1), same(end), same(end + 1)
        one = jnp.where(present[half], one, 0.0)
        last_but_one = (zero * one) * (taps[2] * rows[0:1])
        last = one * (taps[1] * rows[0:1]) + (one * two) * (taps[2] * rows[1:2])
        extra = jnp.where(row == 6, last_but_one, jnp.where(row == 7, last, 0.0))
        dq_ref[half] = tail_ref[half] + extra
    stores[2].start()
    for store in stores:
        store.wait()


def shards(q_pre, k_pre, value_before_filter, d_out, filters, doc_lengths):
    f32, bf16 = jnp.float32, jnp.bfloat16
    ctx_count = lax.axis_size("ctx")
    span, width = q_pre.shape[1:]
    length = 2 * span * ctx_count
    rim = 4 * width // (2 * LANES)
    vmem = pl.BlockSpec(memory_space=pltpu.VMEM)
    smem = pl.BlockSpec(memory_space=pltpu.SMEM)
    hbm = pl.BlockSpec(memory_space=pltpu.HBM)

    group = ctx_count // 2
    direct = group <= MAX_DIRECT
    halves = [[half * group + at for at in range(group)] for half in range(2)]
    msg_rows = 2 * span + rim

    def whole(shape):
        return pl.BlockSpec(shape, lambda i: (0,) * len(shape))

    def in_hbm(array):
        return pltpu.with_memory_space_constraint(array, pltpu.HBM)

    def flipped(array, flip):
        return lax.ppermute(array, "ctx", [(i, i ^ flip) for i in range(ctx_count)])

    def gathered(array):
        if direct:
            return [flipped(array, flip) for flip in range(1, group)]
        return [lax.all_gather(array, "ctx", axis_index_groups=halves)]

    def delivered(arrays):
        if direct:
            return [flipped(array, step + 1) for step, array in enumerate(arrays)]
        return [lax.all_to_all(arrays[0], "ctx", 0, 0, axis_index_groups=halves, tiled=True)]

    packed = pl.pallas_call(
        pack_kernel,
        out_shape=jax.ShapeDtypeStruct((msg_rows, 2 * LANES), bf16),
        in_specs=[hbm] * 3,
        out_specs=vmem,
        scratch_shapes=[
            pltpu.VMEM(k_pre.shape, bf16),
            pltpu.VMEM(k_pre.shape, bf16),
            pltpu.VMEM((2, TAIL, width), bf16),
            pltpu.SemaphoreType.DMA((3,)),
        ],
        compiler_params=pltpu.CompilerParams(vmem_limit_bytes=4 * MIB),
        name="pack",
    )(*[in_hbm(array) for array in (k_pre, value_before_filter, q_pre)])
    across = flipped(packed, group)
    near = gathered(packed)
    far = gathered(across)
    received = [packed, across] + near + far

    window = span * ctx_count + span
    if direct:
        flips = range(1, group)
        first_shapes = []
        for flip in flips:
            rows = (2 if splits(direct, flip, group) else 3) * span + 16
            rows += 16 if flip == group - 1 or flip & (flip + 1) == 0 else 0
            first_shapes.append((rows, 2 * LANES))
        late_shapes = [(span + 16, 2 * LANES)]
    else:
        first_shapes = [(group, 2 * span + 32, 2 * LANES)]
        late_shapes = [(group, span + 16, 2 * LANES)]
    slots = 4 if direct else 1
    heads = width // LANES
    by_head = (2, span * heads, LANES)
    padded = (2, heads, span + 8, LANES)
    prepared = pl.pallas_call(
        functools.partial(prep_kernel, ctx_count, direct),
        out_shape=[
            jax.ShapeDtypeStruct((length + 16, LANES), f32),
            jax.ShapeDtypeStruct((length + 16, LANES), f32),
            jax.ShapeDtypeStruct(padded, f32),
            jax.ShapeDtypeStruct(by_head, bf16),
            jax.ShapeDtypeStruct(by_head, bf16),
        ],
        in_specs=[smem, vmem, hbm, hbm] + [vmem] * (1 + len(near)),
        out_specs=[vmem] * 5,
        scratch_shapes=[
            pltpu.VMEM((ctx_count, rim, 2 * LANES), f32),
            pltpu.VMEM(q_pre.shape, bf16),
            pltpu.VMEM(q_pre.shape, bf16),
            pltpu.SemaphoreType.DMA((2,)),
        ],
        compiler_params=pltpu.CompilerParams(vmem_limit_bytes=(8 if direct else 32) * MIB),
        name="prep",
    )(doc_lengths, filters, in_hbm(q_pre), in_hbm(d_out), packed, *near)
    scratch = [
        pltpu.VMEM((2, length + 16, LANES), f32),
        pltpu.VMEM((2, length, LANES), bf16),
        pltpu.VMEM((2, length + 8, LANES), f32),
        pltpu.VMEM(padded, f32),
        pltpu.VMEM(by_head, bf16),
        pltpu.VMEM(padded, f32),
        pltpu.VMEM((2, window, LANES), f32),
        pltpu.VMEM((slots, window, 2 * LANES), f32),
        pltpu.VMEM((slots, window, 2 * LANES), f32),
        pltpu.VMEM((2 * ctx_count, span, 2 * LANES), f32),
        pltpu.VMEM((2, window, heads * span) if direct else (2, 16, LANES), bf16),
        pltpu.VMEM((2, window, heads * span) if direct else (2, 16, LANES), bf16),
    ]
    own_shapes = [(2 * span, 2 * LANES), (2 * span + 8, 2 * LANES)]
    d_q_main, d_q_tail, own_near, own_far, *sent = pl.pallas_call(
        functools.partial(grads_kernel, ctx_count, direct),
        out_shape=[jax.ShapeDtypeStruct(q_pre.shape, f32)]
        + [jax.ShapeDtypeStruct(shape, f32) for shape in [(2, 8, width)] + own_shapes]
        + [jax.ShapeDtypeStruct(shape, bf16) for shape in first_shapes + late_shapes],
        in_specs=[smem, vmem] + [vmem] * (len(prepared) + len(received)),
        out_specs=[vmem] * (4 + len(first_shapes + late_shapes)),
        scratch_shapes=scratch,
        compiler_params=pltpu.CompilerParams(vmem_limit_bytes=(20 if direct else 62) * MIB),
        name="grads",
    )(doc_lengths, filters, *prepared, *received)
    d_q_main = pl.pallas_call(
        save_kernel,
        out_shape=jax.ShapeDtypeStruct(q_pre.shape, f32),
        in_specs=[vmem],
        out_specs=hbm,
        scratch_shapes=[pltpu.SemaphoreType.DMA(())],
        compiler_params=pltpu.CompilerParams(vmem_limit_bytes=2 * MIB),
        name="save",
    )(d_q_main)
    half_terms = delivered(sent[: len(first_shapes)])
    d_q_main, *half_terms = lax.optimization_barrier((d_q_main, *half_terms))
    merged_shapes = [
        jax.ShapeDtypeStruct((2 * span, 2 * LANES), f32),
        jax.ShapeDtypeStruct((2 * span + 32, 2 * LANES), bf16),
        jax.ShapeDtypeStruct((8, 2 * LANES), f32),
        jax.ShapeDtypeStruct((2, rim // 2, 2 * LANES), f32),
    ]
    near, far, half_sums, rims = pl.pallas_call(
        functools.partial(merge_kernel, ctx_count, direct),
        out_shape=merged_shapes,
        in_specs=[vmem] * (2 + len(half_terms)),
        out_specs=[vmem] * len(merged_shapes),
        scratch_shapes=[
            pltpu.VMEM((group, 8, 2 * LANES), f32),
            pltpu.VMEM((ctx_count, rim // 2, 2 * LANES), f32),
        ],
        compiler_params=pltpu.CompilerParams(vmem_limit_bytes=(4 if direct else 40) * MIB),
        name="merge",
    )(own_near, own_far, *half_terms)
    from_half = flipped(far, group)
    late_terms = sent[len(first_shapes) :]
    late_terms = [flipped(late_terms[0], group - 1)] if direct else delivered(late_terms)

    sums = pl.pallas_call(
        functools.partial(sums_kernel, span),
        out_shape=jax.ShapeDtypeStruct(filters.shape, f32),
        in_specs=[vmem, vmem],
        out_specs=vmem,
        compiler_params=pltpu.CompilerParams(vmem_limit_bytes=2 * MIB),
        name="sums",
    )(half_sums, from_half)
    count = lax.axis_size("tp")
    all_sums = [sums] + [
        lax.ppermute(sums, "tp", [(i, i ^ flip) for i in range(count)]) for flip in range(1, count)
    ]
    d_q_pre, d_k_pre, d_v_pre = pl.pallas_call(
        functools.partial(finish_kernel, ctx_count, direct),
        out_shape=(
            jax.ShapeDtypeStruct(q_pre.shape, f32),
            jax.ShapeDtypeStruct(k_pre.shape, f32),
            jax.ShapeDtypeStruct(k_pre.shape, f32),
        ),
        in_specs=[smem, vmem, hbm] + [vmem] * (4 + len(late_terms)),
        out_specs=(hbm, hbm, hbm),
        scratch_shapes=[
            pltpu.VMEM((2, 8, width), f32),
            pltpu.VMEM(k_pre.shape, f32),
            pltpu.VMEM(k_pre.shape, f32),
            pltpu.VMEM((ctx_count, rim // 2, 2 * LANES), f32),
            pltpu.SemaphoreType.DMA((3,)),
        ],
        input_output_aliases={2: 0},
        compiler_params=pltpu.CompilerParams(vmem_limit_bytes=(4 if direct else 16) * MIB),
        name="finish",
    )(doc_lengths, filters, d_q_main, d_q_tail, near, from_half, rims, *late_terms)
    while len(all_sums) > 1:
        all_sums = [all_sums[at] + all_sums[at + 1] for at in range(0, len(all_sums), 2)]
    return (d_q_pre, d_k_pre, d_v_pre, all_sums[0])


def solution(mesh):
    split = P(None, "ctx", "tp")
    return jax.shard_map(
        shards,
        mesh=mesh,
        in_specs=(split, split, split, split, P(), P()),
        out_specs=(split, split, split, P()),
        check_vma=False,
    )
```

```python
import functools

import jax
import jax.numpy as jnp
import numpy as np
from jax import lax
from jax.experimental import pallas as pl
from jax.experimental.pallas import tpu as pltpu
from jax.sharding import PartitionSpec as P

LANES = 128
NT = (((1,), (1,)), ((), ()))
NN = (((1,), (0,)), ((), ()))
TN = (((0,), (0,)), ((), ()))
TAIL = 16
MAX_CHUNK = 640
RIM = 8
MAX_DIRECT = 4
WINDOWS = ((2, 2), (4, 4), (2, 9), (6, 6), (8, 4), (4, 9), (6, 9), (8, 9))
MIB = 1 << 20


def loop(count, body, init, unrolled=16):
    if count <= unrolled:
        for step in range(count):
            init = body(step, init)
        return init
    return lax.fori_loop(0, count, body, init)


def aligned(start, multiple):
    return start if isinstance(start, int) else pl.multiple_of(start, multiple)


def doc_starts(lengths_ref):
    starts = [jnp.int32(0)]
    for index in range(lengths_ref.shape[0] - 1):
        starts.append(starts[-1] + lengths_ref[index])
    return starts


def fold_rows(terms):
    rows, lanes = terms.shape
    return jnp.sum(terms.reshape(rows // 8, 8, lanes), axis=0)


def split_bits(values):
    high = values.astype(jnp.bfloat16)
    low = (values - high.astype(jnp.float32)).astype(jnp.bfloat16)
    return high, low


def joined(pair):
    rows = pair.shape[0] // 2
    pair = pair.astype(jnp.float32)
    return pair[:rows] + pair[rows:]


class Slots:
    def __init__(self, refs, me):
        self.refs, self.me = refs, me

    def __getitem__(self, flip):
        if len(self.refs) == 1:
            place = lax.rem(self.me, jnp.int32(self.refs[0].shape[0]))
            return self.refs[0].at[partner(place, flip)]
        return self.refs[flip]


def splits(direct, flip, group):
    return not direct or flip == 1


def partner(me, flip):
    return lax.bitwise_xor(me, jnp.int32(flip))


def pack_kernel(k_hbm, v_hbm, q_hbm, out_ref, k_ref, v_ref, q_ref, sems):
    span = k_ref.shape[1]
    loads = [
        pltpu.make_async_copy(k_hbm, k_ref, sems.at[0]),
        pltpu.make_async_copy(v_hbm, v_ref, sems.at[1]),
        pltpu.make_async_copy(q_hbm.at[:, pl.ds(span - TAIL, TAIL)], q_ref, sems.at[2]),
    ]
    for load in loads:
        load.start()
    for load in loads:
        load.wait()
    kv = jnp.concatenate([k_ref[...], v_ref[...]], axis=2).reshape(2 * span, 2 * LANES)
    tails = []
    for half in range(2):
        last = q_ref[half].astype(jnp.float32)[TAIL - 2 :]
        tails += [last[:, at : at + 2 * LANES] for at in range(0, last.shape[1], 2 * LANES)]
    out_ref[: 2 * span] = kv
    out_ref[2 * span :] = jnp.concatenate(tails, axis=0).astype(jnp.bfloat16)


def prep_kernel(ctx_count, direct, lengths_ref, filters_ref, q_hbm, d_out_hbm, own_ref, *refs):
    near_refs, refs = refs[:-9], refs[-9:]
    same_ref, same_two_ref, q_scr, qc_ref, do_ref, rim_scr, q_ref, d_out_ref, sems = refs
    f32, bf16 = jnp.float32, jnp.bfloat16
    loads = [
        pltpu.make_async_copy(q_hbm, q_ref, sems.at[0]),
        pltpu.make_async_copy(d_out_hbm, d_out_ref, sems.at[1]),
    ]
    for load in loads:
        load.start()
    group = ctx_count // 2
    span = q_ref.shape[1]
    heads = q_ref.shape[2] // LANES
    blocks = 2 * ctx_count
    length = span * blocks
    me = lax.axis_index("ctx")
    near = Slots((None,) + near_refs if direct else near_refs, me)
    starts = doc_starts(lengths_ref)

    def fill(index, carry):
        rows = pl.ds(aligned(8 + index * span, 8), span)
        same_ref[rows] = jnp.ones((span, LANES), f32)
        same_two_ref[rows] = jnp.ones((span, LANES), f32)
        return carry

    lax.fori_loop(0, blocks, fill, 0, unroll=2)
    zeros = jnp.zeros((8, LANES), f32)
    for rows in (slice(0, 8), slice(8 + length, 16 + length)):
        same_ref[rows] = zeros
        same_two_ref[rows] = zeros
    for start in starts:
        same_ref[pl.ds(8 + start, 1)] = zeros[:1]
        same_two_ref[pl.ds(8 + start, 1)] = zeros[:1]
        same_two_ref[pl.ds(9 + start, 1)] = zeros[:1]

    before, after = jnp.maximum(me - 1, 0), jnp.minimum(me + 1, ctx_count - 1)
    for index in (before, after):
        rim_scr[index] = jnp.zeros(rim_scr.shape[1:], f32)
    rim_scr[me] = own_ref[2 * span :].astype(f32)

    def place_rims(step, carry):
        flip = step + 1
        if not direct or flip & (flip + 1) == 0:
            rim_scr[partner(me, flip)] = near[flip][2 * span :].astype(f32)
        return carry

    loop(group - 1, place_rims, 0, 16 if direct else 1)
    rim_before, rim_after = rim_scr[before], rim_scr[after]
    late_rim = jnp.where(me == ctx_count - 1, rim_after[:RIM], rim_after[RIM:])
    rims = [rim_before[:RIM], late_rim]
    first_place = [me * span, (blocks - 1 - me) * span]
    taps = [filters_ref[0, tap : tap + 1] for tap in range(3)]

    for load in loads:
        load.wait()
    for half in range(2):
        rows = pl.ds(aligned(first_place[half] + 8, 8), span)
        one, two = same_ref[rows], same_two_ref[rows]
        for head in range(heads):
            at = 2 * (head // 2)
            q_scr[half, head, 6:8] = rims[half][at : at + 2, (head % 2) * LANES : (head % 2 + 1) * LANES]

        def convolve_head(head, carry, half=half, one=one, two=two):
            lanes = pl.ds(pl.multiple_of(head * LANES, LANES), LANES)
            target = pl.ds(pl.multiple_of(head * span, 16), span)
            q_scr[half, head, 8:] = q_ref[half, :, lanes].astype(f32)
            total = taps[0] * q_scr[half, head, 8:]
            total = total + one * (taps[1] * q_scr[half, head, 7 : 7 + span])
            total = total + two * (taps[2] * q_scr[half, head, 6 : 6 + span])
            qc_ref[half, target] = total.astype(bf16)
            do_ref[half, target] = d_out_ref[half, :, lanes]
            return carry

        lax.fori_loop(0, heads, convolve_head, 0, unroll=4)


def grads_kernel(ctx_count, direct, lengths_ref, filters_ref, *refs):
    group = ctx_count // 2
    arrays = group - 1 if direct else 1
    same_scr, same_two_scr, q_in_ref, qc_in_ref, do_scr, own_ref, across_ref = refs[:7]
    refs = refs[7:]
    near_in, far_in, refs = refs[:arrays], refs[arrays : 2 * arrays], refs[2 * arrays :]
    dq_ref, dq_tail_ref, own_near_ref, own_far_ref = refs[:4]
    arrays = group - 1 if direct else 1
    first_out, late_out, refs = refs[4 : 4 + arrays], refs[4 + arrays : 5 + arrays], refs[5 + arrays :]
    kv_scr, conv_scr, dkv_scr, q_scr, qc_scr, dq_scr = refs[:6]
    bias_scr, s_scr, dp_scr, terms_scr, p_scr, ds_scr = refs[6:]
    f32, bf16 = jnp.float32, jnp.bfloat16
    span = own_ref.shape[0] // 2 - TAIL // 2
    heads = q_in_ref.shape[1]
    half_rows = span * ctx_count
    length = 2 * half_rows
    blocks = 2 * ctx_count
    me = lax.axis_index("ctx")
    near_in = Slots((None,) + near_in if direct else near_in, me)
    far_in = Slots((None,) + far_in if direct else far_in, me)
    first_out = Slots((None,) + first_out if direct else first_out, me)
    late_out = Slots((None,) + late_out if direct else late_out, me)
    scale = LANES**-0.5
    log2_scale = scale * 1.4426950408889634
    starts = doc_starts(lengths_ref)

    def place(index, block):
        for tensor in range(2):
            lanes = slice(tensor * LANES, (tensor + 1) * LANES)
            kv_scr[tensor, pl.ds(aligned(8 + index * span, 8), span)] = block[:, lanes].astype(f32)

    def place_both(message, index):
        place(index, message[:span])
        place(blocks - 1 - index, message[span : 2 * span])

    def place_received(step, carry):
        flip = step + 1
        source = partner(me, flip)
        place_both(near_in[flip], source)
        place_both(far_in[flip], partner(source, group))
        return carry

    zeros = jnp.zeros((8, LANES), f32)
    for tensor in range(2):
        kv_scr[tensor, :8] = zeros
    for block_ref, index in ((own_ref, me), (across_ref, partner(me, group))):
        place_both(block_ref, index)
    loop(group - 1, place_received, 0, 16 if direct else 1)

    def taps(tensor):
        return [filters_ref[tensor, tap : tap + 1] for tap in range(3)]

    def masks(base, ahead):
        one = same_scr[pl.ds(base + 8 + min(ahead, 1), span)]
        return one, same_two_scr[pl.ds(base + 8 + ahead, span)]

    def convolve_kv(index, carry):
        base = index * span
        one, two = masks(base, 0)
        for tensor in range(2):
            zero_tap, one_tap, two_tap = taps(tensor + 1)
            total = zero_tap * kv_scr[tensor, pl.ds(aligned(base + 8, 8), span)]
            total = total + one * (one_tap * kv_scr[tensor, pl.ds(base + 7, span)])
            total = total + two * (two_tap * kv_scr[tensor, pl.ds(base + 6, span)])
            conv_scr[tensor, pl.ds(aligned(base, 16), span)] = total.astype(bf16)
        return carry

    first_place = [me * span, (blocks - 1 - me) * span]
    firsts = []
    for half in range(2):
        lowest = jnp.int32(0)
        for start in starts[1:]:
            lowest = jnp.where(first_place[half] >= start, start, lowest)
        firsts.append(lowest // span)

    def over_needed(body, init):
        carry = lax.fori_loop(firsts[0], me + 1, body, init)
        return lax.fori_loop(jnp.maximum(firsts[1], me + 1), blocks - me, body, carry)

    def clear(index, carry):
        for tensor in range(2):
            rows = pl.ds(pl.multiple_of(index * span, 16), span)
            conv_scr[tensor, rows] = jnp.zeros((span, LANES), bf16)
            dkv_scr[tensor, rows] = jnp.zeros((span, LANES), f32)
        terms_scr[index] = jnp.zeros((span, 2 * LANES), f32)
        return carry

    lax.fori_loop(0, blocks, clear, 0, unroll=2)
    for tensor in range(2):
        dkv_scr[tensor, length:] = zeros
    over_needed(convolve_kv, 0)

    middle = me == ctx_count - 1
    q_scr[...] = q_in_ref[...]
    qc_scr[...] = qc_in_ref[...]
    tails = far_in[group - 1][2 * span :].astype(f32)
    tails = [tails[:RIM], tails[RIM:]]
    for half, crossing in ((0, me == group), (1, me == group - 1)):

        @pl.when(crossing)
        def _(half=half):
            rows = pl.ds(aligned(first_place[half] + 8, 8), TAIL)
            one, two = same_scr[rows], same_two_scr[rows]
            zero_tap, one_tap, two_tap = taps(0)
            for head in range(heads):
                at = 2 * (head // 2)
                q_scr[half, head, 6:8] = tails[half][
                    at : at + 2, (head % 2) * LANES : (head % 2 + 1) * LANES
                ]
                total = zero_tap * q_scr[half, head, 8 : 8 + TAIL]
                total = total + one * (one_tap * q_scr[half, head, 7 : 7 + TAIL])
                total = total + two * (two_tap * q_scr[half, head, 6 : 6 + TAIL])
                qc_scr[half, head * span : head * span + TAIL] = total.astype(bf16)

    wide = 2 * LANES
    parts = heads * span // wide

    def reach(half):
        lane = lax.broadcasted_iota(jnp.int32, (1, LANES), 1)
        query = first_place[half] + lax.rem(lane, jnp.int32(span))
        lowest = jnp.zeros((1, LANES), jnp.int32)
        for start in starts[1:]:
            lowest = jnp.where(query >= start, start, lowest)
        return query, lowest

    def attend_at_once(windows):
        units = [(half, at) for half in range(2) for at in range(parts)]
        keys_rows, tops, scaled = [], [], []
        for half, window in enumerate(windows):
            first_key = pl.multiple_of(jnp.maximum(first_place[half] + span - window, 0), 16)
            keys_rows.append(pl.ds(first_key, window))
            query, lowest = reach(half)
            places = first_key + lax.broadcasted_iota(jnp.int32, (window, LANES), 0)
            allowed = (places >= lowest) & (places <= query)
            bias_scr[half, :window] = jnp.where(allowed, 0.0, -1e30)
        for slot, (half, at) in enumerate(units):
            window = windows[half]
            queries = qc_scr[half, at * wide : (at + 1) * wide]
            scores = lax.dot_general(
                conv_scr[0, keys_rows[half]], queries, NT, preferred_element_type=f32
            )
            bias = bias_scr[half, :window]
            scores = scores * log2_scale + jnp.concatenate([bias, bias], axis=1)
            s_scr[slot, :window] = scores
            tops.append(jnp.max(scores, axis=0, keepdims=True))
        for slot, (half, at) in enumerate(units):
            window = windows[half]
            grads = do_scr[half, at * wide : (at + 1) * wide]
            prob_grads = lax.dot_general(
                conv_scr[1, keys_rows[half]], grads, NT, preferred_element_type=f32
            )
            dp_scr[slot, :window] = prob_grads
            weights = jnp.exp2(s_scr[slot, :window] - tops[slot])
            total = jnp.sum(weights, axis=0, keepdims=True)
            weighted = jnp.sum(weights * prob_grads, axis=0, keepdims=True)
            scaled.append((tops[slot] + jnp.log2(total), weighted / total))
        for slot, (half, at) in enumerate(units):
            window = windows[half]
            log_total, mean = scaled[slot]
            probs = jnp.exp2(s_scr[slot, :window] - log_total)
            cols = slice(at * wide, (at + 1) * wide)
            p_scr[half, :window, cols] = probs.astype(bf16)
            score_grads = probs * (dp_scr[slot, :window] - mean) * scale
            ds_scr[half, :window, cols] = score_grads.astype(bf16)
        for half, window in enumerate(windows):
            score_grads = ds_scr[half, :window]
            keys_t = conv_scr[0, keys_rows[half]].T
            dq = lax.dot_general(keys_t, score_grads, NN, preferred_element_type=f32).T
            for head in range(heads):
                dq_scr[half, head, :span] = dq[head * span : (head + 1) * span]
            dkv_scr[0, keys_rows[half]] += lax.dot_general(
                score_grads, qc_scr[half], NN, preferred_element_type=f32
            )
            dkv_scr[1, keys_rows[half]] += lax.dot_general(
                p_scr[half, :window], do_scr[half], NN, preferred_element_type=f32
            )

    def attend(half, window, first_key):
        chunks = 1
        while window // chunks > MAX_CHUNK or window % (16 * chunks):
            chunks += 1
        size = window // chunks
        query, lowest = reach(half)

        def fill_bias(step, carry):
            places = first_key + step * size + lax.broadcasted_iota(jnp.int32, (size, LANES), 0)
            allowed = (places >= lowest) & (places <= query)
            bias_scr[0, pl.ds(aligned(step * size, 16), size)] = jnp.where(allowed, 0.0, -1e30)
            return carry

        loop(chunks, fill_bias, 0, 1)
        whole_window = pl.ds(aligned(first_key, 16), window)
        keys_t = conv_scr[0, whole_window].T if chunks == 1 else None
        for at in range(parts):
            slot = 0
            cols = slice(at * wide, (at + 1) * wide)
            queries = qc_scr[half, cols]
            grads = do_scr[half, cols]

            def key_rows(step):
                return pl.ds(aligned(first_key + step * size, 16), size)

            def score(step, top):
                keys = conv_scr[0, key_rows(step)]
                scores = lax.dot_general(keys, queries, NT, preferred_element_type=f32)
                bias = bias_scr[0, pl.ds(aligned(step * size, 16), size)]
                scores = scores + jnp.concatenate([bias, bias], axis=1)
                s_scr[slot, pl.ds(aligned(step * size, 16), size)] = scores
                return jnp.maximum(top, jnp.max(scores, axis=0, keepdims=True))

            top = loop(chunks, score, jnp.full((1, wide), -1e30, f32), 1)

            def weigh(step, carry):
                total, weighted = carry
                rows = pl.ds(aligned(step * size, 16), size)
                weights = jnp.exp2((s_scr[slot, rows] - top) * log2_scale)
                values = conv_scr[1, key_rows(step)]
                prob_grads = lax.dot_general(values, grads, NT, preferred_element_type=f32)
                s_scr[slot, rows] = weights
                dp_scr[slot, rows] = prob_grads
                total = total + jnp.sum(weights, axis=0, keepdims=True)
                weighted = weighted + jnp.sum(weights * prob_grads, axis=0, keepdims=True)
                return total, weighted

            zeros = jnp.zeros((1, wide), f32)
            total, weighted = loop(chunks, weigh, (zeros, zeros), 1)
            inverse = 1.0 / total
            mean = weighted * inverse
            slope = inverse * scale

            def accumulate(step, dq):
                rows = pl.ds(aligned(step * size, 16), size)
                weights = s_scr[slot, rows]
                probs = (weights * inverse).astype(bf16)
                score_grads = (weights * slope * (dp_scr[slot, rows] - mean)).astype(bf16)
                dk = lax.dot_general(score_grads, queries, NN, preferred_element_type=f32)
                dv = lax.dot_general(probs, grads, NN, preferred_element_type=f32)
                target = pl.ds(aligned(first_key + step * size, 16), size)
                for tensor, terms in enumerate((dk, dv)):
                    dkv_scr[tensor, target] += terms
                if keys_t is not None:
                    return lax.dot_general(keys_t, score_grads, NN, preferred_element_type=f32)
                keys = conv_scr[0, key_rows(step)]
                return dq + lax.dot_general(keys, score_grads, TN, preferred_element_type=f32)

            dq = loop(chunks, accumulate, jnp.zeros((LANES, wide), f32), 1)
            dq = dq.T
            for part in range(wide // span):
                head = at * (wide // span) + part
                dq_scr[half, head, :span] = dq[part * span : (part + 1) * span]

    needed = [first_place[half] // span - firsts[half] + 1 for half in range(2)]
    if direct:
        done = jnp.bool_(False)
        for sizes in WINDOWS:
            sizes = [min(size, ctx_count + half) for half, size in enumerate(sizes)]
            fits = (needed[0] <= sizes[0]) & (needed[1] <= sizes[1])

            @pl.when(fits & jnp.logical_not(done))
            def _(sizes=sizes):
                attend_at_once([size * span for size in sizes])

            done = done | fits
    else:
        for half in range(2):
            attend(half, half_rows + half * span, half * (ctx_count - 1 - me) * span)

    next_rows = jnp.where(middle, dq_scr[1, :, :8], 0.0)
    dq_scr[0, :, span:] = next_rows
    dq_scr[1, :, span:] = jnp.zeros_like(next_rows)
    sums = [jnp.zeros((8, LANES), f32) for _ in range(3)]
    for half in range(2):
        one, two = masks(first_place[half], 0)
        ahead_one = same_scr[pl.ds(first_place[half] + 9, span)]
        ahead_two = same_two_scr[pl.ds(first_place[half] + 10, span)]
        zero_tap, one_tap, two_tap = taps(0)

        def finish_head(head, carry, half=half, one=one, two=two, ahead_one=ahead_one, ahead_two=ahead_two):
            lanes = pl.ds(pl.multiple_of(head * LANES, LANES), LANES)
            grads = dq_scr[half, head, :span]
            out = zero_tap * grads
            out = out + ahead_one * (one_tap * dq_scr[half, head, 1 : 1 + span])
            out = out + ahead_two * (two_tap * dq_scr[half, head, 2 : 2 + span])
            dq_ref[half, :, lanes] = out
            dq_tail_ref[half, :, lanes] = out[span - 8 :]
            return (
                carry[0] + fold_rows(grads * q_scr[half, head, 8:]),
                carry[1] + fold_rows(grads * one * q_scr[half, head, 7 : 7 + span]),
                carry[2] + fold_rows(grads * two * q_scr[half, head, 6 : 6 + span]),
            )

        sums = lax.fori_loop(0, heads, finish_head, tuple(sums), unroll=4)
    q_sums = [jnp.sum(term, axis=0, keepdims=True) for term in sums]

    def finish_block(index, carry):
        base = pl.multiple_of(index * span, 8)
        one, two = masks(base, 0)
        ahead_one = same_scr[pl.ds(base + 9, span)]
        ahead_two = same_two_scr[pl.ds(base + 10, span)]
        carry = list(carry)
        for tensor in range(2):
            zero_tap, one_tap, two_tap = taps(tensor + 1)
            own = dkv_scr[tensor, pl.ds(base, span)]
            out = zero_tap * own
            out = out + ahead_one * (one_tap * dkv_scr[tensor, pl.ds(base + 1, span)])
            out = out + ahead_two * (two_tap * dkv_scr[tensor, pl.ds(base + 2, span)])
            lanes = slice(tensor * LANES, (tensor + 1) * LANES)
            terms_scr[index, :, lanes] = out
            at = 3 * tensor
            carry[at] += fold_rows(own * kv_scr[tensor, pl.ds(base + 8, span)])
            carry[at + 1] += fold_rows(own * one * kv_scr[tensor, pl.ds(base + 7, span)])
            carry[at + 2] += fold_rows(own * two * kv_scr[tensor, pl.ds(base + 6, span)])
        return tuple(carry)

    low = me < group

    kv_sums = over_needed(finish_block, (zeros,) * 6)
    for target, index in ((own_far_ref, partner(me, group)), (own_near_ref, me)):
        target[:span] = terms_scr[index]
        target[span : 2 * span] = terms_scr[blocks - 1 - index]

    def send(step, carry):
        flip = step + 1
        owner = partner(me, flip)
        far_owner = partner(me, flip + group)
        near_late = blocks - 1 - owner
        second = jnp.where(low, blocks - 1 - far_owner, owner)
        third = jnp.where(low & (me > owner), owner, near_late)
        first_out[flip][:span] = terms_scr[far_owner].astype(bf16)
        first_out[flip][span : 2 * span] = terms_scr[second].astype(bf16)
        if splits(direct, flip, group):
            late_out[flip][:span] = terms_scr[third].astype(bf16)
        else:
            first_out[flip][2 * span : 3 * span] = terms_scr[third].astype(bf16)
        return carry

    loop(group - 1, send, 0, 16 if direct else 1)
    kv_sums = [jnp.sum(term, axis=0, keepdims=True) for term in kv_sums]

    padding = [jnp.zeros((2, LANES), f32)]
    left = jnp.concatenate(q_sums + kv_sums[:3] + padding, axis=0)
    right = jnp.concatenate([jnp.zeros((3, LANES), f32)] + kv_sums[3:] + padding, axis=0)
    sums_tile = jnp.concatenate([left, right], axis=1)
    sums_pair = jnp.concatenate(split_bits(sums_tile), axis=0)
    own_far_ref[2 * span :] = joined(sums_pair)
    rims = []
    for half in range(2):
        rows = [dq_scr[half, head, :2] for head in range(heads)]
        rows = [jnp.concatenate(rows[at : at + 2], axis=1) for at in range(0, heads, 2)]
        rims.append(jnp.concatenate(rows, axis=0))

    def rim_for(index):
        return jnp.concatenate(split_bits(jnp.where(index < me, rims[0], rims[1])), axis=0)

    def store_rims(step, carry):
        flip = step + 1
        owner = partner(me, flip)
        after = (2 if splits(direct, flip, group) else 3) * span
        first_out[flip][after : after + 16] = sums_pair
        if not direct:
            first_out[flip][after + 16 :] = rim_for(partner(owner, group))
        elif flip == group - 1:
            target = jnp.where(jnp.abs(owner - me) == 1, owner, partner(owner, group))
            first_out[flip][after + 16 :] = rim_for(target)
        if splits(direct, flip, group):
            late_out[flip][span:] = rim_for(owner)
        return carry

    loop(group - 1, store_rims, 0, 16 if direct else 1)


def merge_kernel(ctx_count, direct, own_near_ref, own_far_ref, *refs):
    received_refs, refs = refs[:-6], refs[-6:]
    near_ref, far_ref, half_sums_ref, rims_ref, sums_scr, rim_scr = refs
    f32, bf16 = jnp.float32, jnp.bfloat16
    group = ctx_count // 2
    me = lax.axis_index("ctx")
    low = me < group
    received = Slots((own_far_ref,) + received_refs if direct else received_refs, me)
    place = lax.rem(me, jnp.int32(group))
    span = own_near_ref.shape[0] // 2
    rows = 2 * span
    sums_scr[place] = own_far_ref[rows:]
    def add(step, carry):
        flip = step + 1
        source = partner(me, flip)
        message = received[flip]
        early, second = [message[at * span : (at + 1) * span].astype(f32) for at in range(2)]
        near_early, near_late, far_early, far_late = carry
        zero = jnp.zeros_like(second)
        after = (2 if splits(direct, flip, group) else 3) * span
        sums_scr[partner(place, flip)] = joined(message[after : after + 16])
        near_early = near_early + jnp.where(low, zero, second)
        if not splits(direct, flip, group):
            third = message[2 * span : 3 * span].astype(f32)
            to_early = low & (source > me)
            near_early = near_early + jnp.where(to_early, third, zero)
            near_late = near_late + jnp.where(to_early, zero, third)
            if flip == group - 1:
                rim_scr[source] = joined(message[after + 16 :])
        return near_early, near_late, far_early + early, far_late + jnp.where(low, second, zero)

    neighbours = [jnp.minimum(me + 1, ctx_count - 1), jnp.maximum(me - 1, 0)]
    for index in neighbours:
        rim_scr[index] = jnp.zeros(rim_scr.shape[1:], f32)
    init = (own_near_ref[:span], own_near_ref[span:], own_far_ref[:span], own_far_ref[span:rows])
    totals = loop(group - 1, add, init, 16 if direct else 1)
    near_ref[:span] = totals[0]
    near_ref[span:] = totals[1]
    far_ref[:span] = totals[2].astype(bf16)
    far_ref[span:rows] = totals[3].astype(bf16)
    for at, index in enumerate(neighbours):
        rims_ref[at] = rim_scr[index]
    sums = loop(group, lambda index, carry: carry + sums_scr[index], jnp.zeros((8, 2 * LANES), f32))
    pair = jnp.concatenate(split_bits(sums), axis=0)
    half_sums_ref[...] = joined(pair)
    far_ref[rows : rows + 16] = pair
    far_ref[rows + 16 :] = received[group - 1][(rows if not direct else 3 * span) + 16 :]


def save_kernel(source_ref, target_hbm, sem):
    copy = pltpu.make_async_copy(source_ref, target_hbm, sem)
    copy.start()
    copy.wait()


def sums_kernel(span, half_sums_ref, far_ref, out_ref):
    sums = half_sums_ref[...] + joined(far_ref[2 * span : 2 * span + 16])
    out_ref[0] = sums[0:3, :LANES]
    out_ref[1] = sums[3:6, :LANES]
    out_ref[2] = sums[3:6, LANES:]


def finish_kernel(
    ctx_count, direct, lengths_ref, filters_ref, dq_in_hbm, tail_ref, near_ref, far_ref, rims_ref, *refs
):
    received_refs, refs = refs[:-8], refs[-8:]
    dq_hbm, dk_hbm, dv_hbm, dq_ref, dk_ref, dv_ref, rim_scr, sems = refs
    f32 = jnp.float32
    group = ctx_count // 2
    span = dk_ref.shape[1]
    me = lax.axis_index("ctx")
    low = me < group
    received = Slots((None,) + received_refs if direct else received_refs, me)
    starts = doc_starts(lengths_ref)
    blocks = 2 * ctx_count
    neighbours = [jnp.minimum(me + 1, ctx_count - 1), jnp.maximum(me - 1, 0)]
    for at, index in enumerate(neighbours):
        rim_scr[index] = rims_ref[at]

    def add(step, carry):
        flip = step + 1
        source = partner(me, flip)
        message = received[flip]
        terms = message[:span].astype(f32)
        rim_scr[source] = joined(message[span:])
        to_early = low & (source > me)
        zero = jnp.zeros_like(terms)
        return carry[0] + jnp.where(to_early, terms, zero), carry[1] + jnp.where(to_early, zero, terms)

    total = near_ref[...] + far_ref[: 2 * span].astype(f32)
    total = (total[:span], total[span:])
    total = add(0, total) if direct else loop(group - 1, add, total, 1)
    for half in range(2):
        dk_ref[half] = total[half][:, :LANES]
        dv_ref[half] = total[half][:, LANES:]
    stores = [
        pltpu.make_async_copy(dk_ref, dk_hbm, sems.at[0]),
        pltpu.make_async_copy(dv_ref, dv_hbm, sems.at[1]),
        pltpu.make_async_copy(dq_ref, dq_hbm.at[:, pl.ds(span - 8, 8)], sems.at[2]),
    ]
    for store in stores[:2]:
        store.start()

    def same(place):
        cut = place >= blocks * span
        for start in starts:
            cut = cut | (place == start)
        return jnp.where(cut, 0.0, 1.0).astype(f32)

    heads = dq_ref.shape[2] // LANES
    taps = [jnp.concatenate([filters_ref[0, tap : tap + 1]] * heads, axis=1) for tap in range(3)]
    row = lax.broadcasted_iota(jnp.int32, dq_ref.shape[1:], 0)
    far_rim = joined(far_ref[2 * span + 16 :])
    crosses = [me == group - 1, me == group]
    first_place = [me * span, (blocks - 1 - me) * span]
    present = [me < ctx_count - 1, me > 0]
    for half in range(2):
        rim = jnp.where(crosses[half], far_rim, rim_scr[neighbours[half]])
        rows = jnp.concatenate([rim[2 * at : 2 * at + 2] for at in range(rim.shape[0] // 2)], axis=1)
        end = first_place[half] + span
        zero, one, two = same(end - 1), same(end), same(end + 1)
        one = jnp.where(present[half], one, 0.0)
        last_but_one = (zero * one) * (taps[2] * rows[0:1])
        last = one * (taps[1] * rows[0:1]) + (one * two) * (taps[2] * rows[1:2])
        extra = jnp.where(row == 6, last_but_one, jnp.where(row == 7, last, 0.0))
        dq_ref[half] = tail_ref[half] + extra
    stores[2].start()
    for store in stores:
        store.wait()


def shards(q_pre, k_pre, value_before_filter, d_out, filters, doc_lengths):
    f32, bf16 = jnp.float32, jnp.bfloat16
    ctx_count = lax.axis_size("ctx")
    span, width = q_pre.shape[1:]
    length = 2 * span * ctx_count
    rim = 4 * width // (2 * LANES)
    vmem = pl.BlockSpec(memory_space=pltpu.VMEM)
    smem = pl.BlockSpec(memory_space=pltpu.SMEM)
    hbm = pl.BlockSpec(memory_space=pltpu.HBM)

    group = ctx_count // 2
    direct = group <= MAX_DIRECT
    halves = [[half * group + at for at in range(group)] for half in range(2)]
    msg_rows = 2 * span + rim

    def whole(shape):
        return pl.BlockSpec(shape, lambda i: (0,) * len(shape))

    def in_hbm(array):
        return pltpu.with_memory_space_constraint(array, pltpu.HBM)

    def flipped(array, flip):
        return lax.ppermute(array, "ctx", [(i, i ^ flip) for i in range(ctx_count)])

    def gathered(array):
        if direct:
            return [flipped(array, flip) for flip in range(1, group)]
        return [lax.all_gather(array, "ctx", axis_index_groups=halves)]

    def delivered(arrays):
        if direct:
            return [flipped(array, step + 1) for step, array in enumerate(arrays)]
        return [lax.all_to_all(arrays[0], "ctx", 0, 0, axis_index_groups=halves, tiled=True)]

    packed = pl.pallas_call(
        pack_kernel,
        out_shape=jax.ShapeDtypeStruct((msg_rows, 2 * LANES), bf16),
        in_specs=[hbm] * 3,
        out_specs=vmem,
        scratch_shapes=[
            pltpu.VMEM(k_pre.shape, bf16),
            pltpu.VMEM(k_pre.shape, bf16),
            pltpu.VMEM((2, TAIL, width), bf16),
            pltpu.SemaphoreType.DMA((3,)),
        ],
        compiler_params=pltpu.CompilerParams(vmem_limit_bytes=4 * MIB),
        name="pack",
    )(*[in_hbm(array) for array in (k_pre, value_before_filter, q_pre)])
    across = flipped(packed, group)
    near = gathered(packed)
    far = gathered(across)
    received = [packed, across] + near + far

    window = span * ctx_count + span
    if direct:
        flips = range(1, group)
        first_shapes = []
        for flip in flips:
            rows = (2 if splits(direct, flip, group) else 3) * span + 16
            rows += 16 if flip == group - 1 else 0
            first_shapes.append((rows, 2 * LANES))
        late_shapes = [(span + 16, 2 * LANES)]
    else:
        first_shapes = [(group, 2 * span + 32, 2 * LANES)]
        late_shapes = [(group, span + 16, 2 * LANES)]
    slots = 4 if direct else 1
    heads = width // LANES
    by_head = (2, span * heads, LANES)
    padded = (2, heads, span + 8, LANES)
    prepared = pl.pallas_call(
        functools.partial(prep_kernel, ctx_count, direct),
        out_shape=[
            jax.ShapeDtypeStruct((length + 16, LANES), f32),
            jax.ShapeDtypeStruct((length + 16, LANES), f32),
            jax.ShapeDtypeStruct(padded, f32),
            jax.ShapeDtypeStruct(by_head, bf16),
            jax.ShapeDtypeStruct(by_head, bf16),
        ],
        in_specs=[smem, vmem, hbm, hbm] + [vmem] * (1 + len(near)),
        out_specs=[vmem] * 5,
        scratch_shapes=[
            pltpu.VMEM((ctx_count, rim, 2 * LANES), f32),
            pltpu.VMEM(q_pre.shape, bf16),
            pltpu.VMEM(q_pre.shape, bf16),
            pltpu.SemaphoreType.DMA((2,)),
        ],
        compiler_params=pltpu.CompilerParams(vmem_limit_bytes=(8 if direct else 32) * MIB),
        name="prep",
    )(doc_lengths, filters, in_hbm(q_pre), in_hbm(d_out), packed, *near)
    scratch = [
        pltpu.VMEM((2, length + 16, LANES), f32),
        pltpu.VMEM((2, length, LANES), bf16),
        pltpu.VMEM((2, length + 8, LANES), f32),
        pltpu.VMEM(padded, f32),
        pltpu.VMEM(by_head, bf16),
        pltpu.VMEM(padded, f32),
        pltpu.VMEM((2, window, LANES), f32),
        pltpu.VMEM((slots, window, 2 * LANES), f32),
        pltpu.VMEM((slots, window, 2 * LANES), f32),
        pltpu.VMEM((2 * ctx_count, span, 2 * LANES), f32),
        pltpu.VMEM((2, window, heads * span) if direct else (2, 16, LANES), bf16),
        pltpu.VMEM((2, window, heads * span) if direct else (2, 16, LANES), bf16),
    ]
    own_shapes = [(2 * span, 2 * LANES), (2 * span + 8, 2 * LANES)]
    d_q_main, d_q_tail, own_near, own_far, *sent = pl.pallas_call(
        functools.partial(grads_kernel, ctx_count, direct),
        out_shape=[jax.ShapeDtypeStruct(q_pre.shape, f32)]
        + [jax.ShapeDtypeStruct(shape, f32) for shape in [(2, 8, width)] + own_shapes]
        + [jax.ShapeDtypeStruct(shape, bf16) for shape in first_shapes + late_shapes],
        in_specs=[smem, vmem] + [vmem] * (len(prepared) + len(received)),
        out_specs=[vmem] * (4 + len(first_shapes + late_shapes)),
        scratch_shapes=scratch,
        compiler_params=pltpu.CompilerParams(vmem_limit_bytes=(20 if direct else 62) * MIB),
        name="grads",
    )(doc_lengths, filters, *prepared, *received)
    d_q_main = pl.pallas_call(
        save_kernel,
        out_shape=jax.ShapeDtypeStruct(q_pre.shape, f32),
        in_specs=[vmem],
        out_specs=hbm,
        scratch_shapes=[pltpu.SemaphoreType.DMA(())],
        compiler_params=pltpu.CompilerParams(vmem_limit_bytes=2 * MIB),
        name="save",
    )(d_q_main)
    half_terms = delivered(sent[: len(first_shapes)])
    d_q_main, *half_terms = lax.optimization_barrier((d_q_main, *half_terms))
    merged_shapes = [
        jax.ShapeDtypeStruct((2 * span, 2 * LANES), f32),
        jax.ShapeDtypeStruct((2 * span + 32, 2 * LANES), bf16),
        jax.ShapeDtypeStruct((8, 2 * LANES), f32),
        jax.ShapeDtypeStruct((2, rim // 2, 2 * LANES), f32),
    ]
    near, far, half_sums, rims = pl.pallas_call(
        functools.partial(merge_kernel, ctx_count, direct),
        out_shape=merged_shapes,
        in_specs=[vmem] * (2 + len(half_terms)),
        out_specs=[vmem] * len(merged_shapes),
        scratch_shapes=[
            pltpu.VMEM((group, 8, 2 * LANES), f32),
            pltpu.VMEM((ctx_count, rim // 2, 2 * LANES), f32),
        ],
        compiler_params=pltpu.CompilerParams(vmem_limit_bytes=(4 if direct else 40) * MIB),
        name="merge",
    )(own_near, own_far, *half_terms)
    from_half = flipped(far, group)
    late_terms = sent[len(first_shapes) :]
    late_terms = [flipped(late_terms[0], 1)] if direct else delivered(late_terms)

    sums = pl.pallas_call(
        functools.partial(sums_kernel, span),
        out_shape=jax.ShapeDtypeStruct(filters.shape, f32),
        in_specs=[vmem, vmem],
        out_specs=vmem,
        compiler_params=pltpu.CompilerParams(vmem_limit_bytes=2 * MIB),
        name="sums",
    )(half_sums, from_half)
    count = lax.axis_size("tp")
    all_sums = [sums] + [
        lax.ppermute(sums, "tp", [(i, i ^ flip) for i in range(count)]) for flip in range(1, count)
    ]
    d_q_pre, d_k_pre, d_v_pre = pl.pallas_call(
        functools.partial(finish_kernel, ctx_count, direct),
        out_shape=(
            jax.ShapeDtypeStruct(q_pre.shape, f32),
            jax.ShapeDtypeStruct(k_pre.shape, f32),
            jax.ShapeDtypeStruct(k_pre.shape, f32),
        ),
        in_specs=[smem, vmem, hbm] + [vmem] * (4 + len(late_terms)),
        out_specs=(hbm, hbm, hbm),
        scratch_shapes=[
            pltpu.VMEM((2, 8, width), f32),
            pltpu.VMEM(k_pre.shape, f32),
            pltpu.VMEM(k_pre.shape, f32),
            pltpu.VMEM((ctx_count, rim // 2, 2 * LANES), f32),
            pltpu.SemaphoreType.DMA((3,)),
        ],
        input_output_aliases={2: 0},
        compiler_params=pltpu.CompilerParams(vmem_limit_bytes=(4 if direct else 16) * MIB),
        name="finish",
    )(doc_lengths, filters, d_q_main, d_q_tail, near, from_half, rims, *late_terms)
    while len(all_sums) > 1:
        all_sums = [all_sums[at] + all_sums[at + 1] for at in range(0, len(all_sums), 2)]
    return (d_q_pre, d_k_pre, d_v_pre, all_sums[0])


def solution(mesh):
    split = P(None, "ctx", "tp")
    return jax.shard_map(
        shards,
        mesh=mesh,
        in_specs=(split, split, split, split, P(), P()),
        out_specs=(split, split, split, P()),
        check_vma=False,
    )
```
